128 devices in a mesh: gx: 8 (over y, core), gy: 16 (over z, x).
Axes of the slice: x: 4, y: 4, z: 4, core: 2. Of those that a mesh axis runs over, the one named last changes fastest.
Arguments:
- pressure: float32 [8, 512, 4096], P(None, 'gx', 'gy'), may hold values from -4 to 4
- sat_water: float32 [8, 512, 4096], P(None, 'gx', 'gy'), may hold values from 0.1 to 0.4
- sat_gas: float32 [8, 512, 4096], P(None, 'gx', 'gy'), may hold values from 0.1 to 0.4
- old_mass: float32 [3, 8, 512, 4096], P(None, None, 'gx', 'gy'), may hold values from 0.02 to 0.2
- perm: bfloat16 [3, 8, 512, 4096], P(None, None, 'gx', 'gy'), may hold values from 0.099609375 to 10
- porosity: float32 [8, 512, 4096], P(None, 'gx', 'gy'), may hold values from 0.1 to 0.3
- perf_well: int32 [32768], P(('gx', 'gy')), may hold values from 0 to 2047, as said below
- perf_cell: int32 [32768], P(('gx', 'gy')), may hold values from 0 to 131071
- perf_index: float32 [32768], P(('gx', 'gy')), may hold values from 0.5 to 5
- well_pressure: float32 [2048], P(('gx', 'gy')), may hold values from -4 to 4
- well_rate: float32 [2048], P(('gx', 'gy')), may hold values from -3 to 3
Outputs:
- residual: float32 [3, 8, 512, 4096], P(None, None, 'gx', 'gy')
- well_residual: float32 [2048], P(('gx', 'gy'))
- update: float32 [3, 8, 512, 4096], P(None, None, 'gx', 'gy')
- well_update: float32 [2048], P(('gx', 'gy'))
The draws below stay inside these ranges and needn't reach their ends.
Inputs may be any that keep to these rules, and one draw needn't show every extreme that they name: Every well has a perforation on the device that holds its state, the one with index perf_well // 16 along gx+gy, and one on the device 2048 // 32 indices after that one, counted cyclically; its other perforations lie on devices at most 39 indices after the holding device along gx+gy, counted cyclically. perf_cell is layer-major within the device's block of 8 x 64 x 256 cells.
All inputs are finite; a program needn't handle non-finite values.
Results may differ from the reference program's by a relative error of at most 0.0003.
Values sent between devices are 32-bit elements; how exact they have to be, the bound alone decides.
No kernel may reach another device: no remote copies, remote signals or barrier semaphores. Data moves between devices by JAX's collectives and lax.ppermute only.
A program may use at most 192 MiB of HBM per device.

```python
import math
import jax
import jax.numpy as jnp
from jax import lax

L = 8
CX = 64
CY = 256
WELL_DEV = 16
PERF_DEV = 256
SWEEPS = 4
NX = 512
NY = 4096
WELLS = 2048
PERFS = 32768
N_GY = 16


reach_tiles = 40


def draw_perf_well(key, part):
    key = jax.random.fold_in(key, 7)
    key_offset, key_first, key_second = jax.random.split(key, 3)
    slot_count = PERFS
    slot_index = jnp.arange(slot_count, dtype=jnp.int32)
    device = slot_index // PERF_DEV
    local_slot = slot_index % PERF_DEV
    devices = PERFS // PERF_DEV
    offset = jax.random.randint(key_offset, (slot_count,), 0, reach_tiles, dtype=jnp.int32)
    home_tile = (device - offset) % devices
    well_pick = jnp.minimum(jax.random.randint(key_first, (slot_count,), 0, WELL_DEV, dtype=jnp.int32), jax.random.randint(key_second, (slot_count,), 0, WELL_DEV, dtype=jnp.int32))
    far_tile = (device - devices // 2) % devices
    far_well = far_tile * WELL_DEV + local_slot - WELL_DEV
    spread_well = jnp.where(local_slot < 2 * WELL_DEV, far_well, home_tile * WELL_DEV + well_pick)
    return jnp.where(local_slot < WELL_DEV, device * WELL_DEV + local_slot, spread_well).astype(jnp.int32)


def place_ends(array, stream_key, low, largest):
    spot = [jax.random.randint(jax.random.fold_in(stream_key, axis), (), 0, length) for axis, length in enumerate(array.shape)]
    longest = array.shape.index(max(array.shape))
    beside = spot[:longest] + [(spot[longest] + 1) % array.shape[longest]] + spot[longest + 1:]
    return array.at[tuple(spot)].set(low).at[tuple(beside)].set(largest)


def level_of(own_key, shape, pieces, least, top_value):
    def one(dim, parts):
        draws = jax.random.uniform(jax.random.fold_in(jax.random.fold_in(own_key, 6), dim), (parts,), jnp.float32, least / len(pieces), top_value / len(pieces))
        return jnp.repeat(jnp.exp(draws), shape[dim] // parts).reshape((-1,) + (1,) * (len(shape) - dim - 1))

    level = one(*pieces[0])
    for cut in pieces[1:]:
        level = level * one(*cut)
    return level


def scatter_about(stream_key, extent, spread, reach, cuts=(), held_as=jnp.bfloat16):
    drawn = jax.random.normal(stream_key, extent, jnp.float32) * spread
    if len(cuts) > 0:
        drawn = level_of(stream_key, extent, cuts, -0.22, 0.18) * drawn
    return jnp.clip(drawn, min=-reach, max=reach).astype(held_as)


def setup_inputs(seed: int = 0) -> dict:
    streams_of = jax.random.split(jax.random.key(seed), 12)
    return {
        "pressure": scatter_about(streams_of[0], (L, NX, NY), 1.0, 4.0, ((1, 8), (2, 16)), jnp.float32),
        "sat_water": jnp.clip(0.1 + 0.3 * jax.random.uniform(streams_of[1], (L, NX, NY), jnp.float32) ** level_of(streams_of[1], (L, NX, NY), ((1, 8), (2, 16)), -0.2, 0.2), 0.1, 0.4),
        "sat_gas": jnp.clip(0.1 + 0.3 * jax.random.uniform(streams_of[2], (L, NX, NY), jnp.float32) ** level_of(streams_of[2], (L, NX, NY), ((1, 8), (2, 16)), -0.2, 0.2), 0.1, 0.4),
        "old_mass": jnp.clip(0.02 + 0.18 * jax.random.uniform(streams_of[3], (3, L, NX, NY), jnp.float32) ** level_of(streams_of[3], (3, L, NX, NY), ((2, 8), (3, 16)), -0.2, 0.2), 0.02, 0.2),
        "perm": jnp.clip(jnp.exp(math.log(10.0) - 4.609084 * jax.random.uniform(streams_of[4], (3, L, NX, NY), jnp.float32) ** level_of(streams_of[4], (3, L, NX, NY), ((2, 8), (3, 16)), -0.2, 0.2)), 0.099609375, 10.0).astype(jnp.bfloat16),
        "porosity": jnp.clip(0.1 + 0.20000001043081284 * jax.random.uniform(streams_of[5], (L, NX, NY), jnp.float32) ** level_of(streams_of[5], (L, NX, NY), ((1, 8), (2, 16)), -0.2, 0.2), 0.1, 0.3),
        "perf_well": draw_perf_well(jax.random.fold_in(streams_of[11], 71), 0),
        "perf_cell": place_ends(jax.random.randint(streams_of[7], (PERFS,), 0, L * CX * CY), jax.random.fold_in(streams_of[7], 1), 0, (L * CX * CY) - 1).astype(jnp.int32),
        "perf_index": jnp.clip(jnp.exp(math.log(5.0) - 2.3025851 * jax.random.uniform(streams_of[8], (PERFS,), jnp.float32) ** level_of(streams_of[8], (PERFS,), ((0, 128),), -0.2, 0.2)), 0.5, 5.0),
        "well_pressure": scatter_about(streams_of[9], (WELLS,), 1.0, 4.0, ((0, 128),), jnp.float32),
        "well_rate": scatter_about(streams_of[10], (WELLS,), 0.5, 3.0, ((0, 128),), jnp.float32),
    }


compress = (0.05, 0.02, 0.2)
viscosity = (0.5, 2.0, 0.1)
volume_scale = 4.0
layer_ratio = 0.1
directions = ((-3, -1, 2, layer_ratio), (-3, 1, 2, layer_ratio), (-2, -1, 0, 1.0), (-2, 1, 0, 1.0), (-1, -1, 1, 1.0), (-1, 1, 1, 1.0))


def phase_coeffs(pressure, sat_water, sat_gas):
    sat_oil = 1.0 - sat_water - sat_gas
    sats = (sat_water, sat_oil, sat_gas)
    return jnp.stack([sats[phase_index] * sats[phase_index] / viscosity[phase_index] * (1.0 + compress[phase_index] * pressure) for phase_index in range(3)])


def shifted(values, dimension, offset):
    dimension = dimension % values.ndim
    length = values.shape[dimension]
    widths = [(0, 0)] * values.ndim
    if offset > 0:
        widths[dimension] = (0, 1)
        padded = jnp.pad(values, widths)
        return lax.slice_in_dim(padded, 1, length + 1, axis=dimension)
    widths[dimension] = (1, 0)
    padded = jnp.pad(values, widths)
    return lax.slice_in_dim(padded, 0, length, axis=dimension)


def face_coefficient(coeffs, perm_here, coeffs_next, perm_next, factor):
    transmit = factor * 2.0 * perm_here * perm_next / (perm_here + perm_next)
    return transmit * 0.5 * (coeffs + coeffs_next)


def block_solve(right_terms, diagonal, inverse_b, inverse_total):
    pressure_step = (right_terms[0] * inverse_b[0] + right_terms[1] * inverse_b[1] + right_terms[2] * inverse_b[2]) * inverse_total
    water_step = (right_terms[0] - diagonal[0] * pressure_step) * inverse_b[0]
    gas_step = (right_terms[2] - diagonal[2] * pressure_step) * inverse_b[2]
    return jnp.stack([pressure_step, water_step, gas_step])


def reference(pressure, sat_water, sat_gas, old_mass, perm, porosity, perf_well, perf_cell, perf_index, well_pressure, well_rate):
    perm_all = perm.astype(jnp.float32)
    coeffs = phase_coeffs(pressure, sat_water, sat_gas)
    saturations = jnp.stack([sat_water, 1.0 - sat_water - sat_gas, sat_gas])
    densities = jnp.stack([1.0 + compress[phase_index] * pressure for phase_index in range(3)])
    diagonal = jnp.stack([volume_scale * porosity * compress[phase_index] * saturations[phase_index] for phase_index in range(3)])
    net_flux = jnp.zeros_like(coeffs)
    face_terms = []
    for dimension, offset, component, factor in directions:
        perm_here = perm_all[component]
        face_term = face_coefficient(coeffs, perm_here, shifted(coeffs, dimension, offset), shifted(perm_here, dimension, offset), factor)
        face_terms.append(face_term)
        net_flux = net_flux + face_term * (pressure - shifted(pressure, dimension, offset))
        diagonal = diagonal + face_term
    cell_count = L * NX * NY
    device = jnp.arange(PERFS, dtype=jnp.int32) // PERF_DEV
    layer_index = perf_cell // (CX * CY)
    row_index = (perf_cell // CY) % CX
    column_index = perf_cell % CY
    global_cell = (layer_index * (NX * NY) + ((device // N_GY) * CX + row_index) * NY + (device % N_GY) * CY + column_index).astype(jnp.int32)
    perf_coeffs = coeffs.reshape(3, -1)[:, global_cell]
    perf_pressure = pressure.reshape(-1)[global_cell]
    perf_rates = perf_index * perf_coeffs * (perf_pressure - well_pressure[perf_well])
    well_rates = jnp.zeros((3, cell_count), jnp.float32).at[:, global_cell].add(perf_rates).reshape(coeffs.shape)
    residual = volume_scale * (porosity * densities * saturations - old_mass) + net_flux + well_rates
    well_residual = jax.ops.segment_sum(jnp.sum(perf_rates, axis=0), perf_well, num_segments=WELLS) - well_rate
    index_sum = jnp.zeros((cell_count,), jnp.float32).at[global_cell].add(perf_index).reshape(pressure.shape)
    diagonal = diagonal + coeffs * index_sum
    inverse_b = 1.0 / (volume_scale * porosity * densities)
    inverse_total = 1.0 / jnp.sum(diagonal * inverse_b, axis=0)
    perf_total = perf_index * jnp.sum(perf_coeffs, axis=0)
    well_total = jax.ops.segment_sum(perf_total, perf_well, num_segments=WELLS)
    update = jnp.zeros_like(coeffs)
    well_update = jnp.zeros((WELLS,), jnp.float32)
    for sweep_number in range(SWEEPS):
        pressure_step = update[0]
        right_terms = -residual
        for direction_index, (dimension, offset, component, factor) in enumerate(directions):
            right_terms = right_terms + face_terms[direction_index] * shifted(pressure_step, dimension, offset)
        well_terms = jnp.zeros((cell_count,), jnp.float32).at[global_cell].add(perf_index * well_update[perf_well]).reshape(pressure.shape)
        right_terms = right_terms + coeffs * well_terms
        well_flow = jax.ops.segment_sum(perf_total * pressure_step.reshape(-1)[global_cell], perf_well, num_segments=WELLS)
        update = block_solve(right_terms, diagonal, inverse_b, inverse_total)
        well_update = (well_flow + well_residual) / well_total
    return residual, well_residual, update, well_update
```

```python
import jax
import jax.numpy as jnp
from jax import lax
from jax.experimental import pallas as pl
from jax.experimental.pallas import tpu as pltpu
from jax.sharding import PartitionSpec as P

f32 = jnp.float32
bf16 = jnp.bfloat16
i32 = jnp.int32

compress = (0.05, 0.02, 0.2)
viscosity = (0.5, 2.0, 0.1)
volume_scale = 4.0
layer_ratio = 0.1
AXES = ("gx", "gy")
DEVICES = 128
WELL_DEV = 16
REACH = 40
FAR = 64
TAIL = REACH * WELL_DEV
WIDTH = TAIL + 128
LANES = 128
L, R, C = 8, 64, 256
PERFS = 256
VM = pl.BlockSpec(memory_space=pltpu.VMEM)
SM = pl.BlockSpec(memory_space=pltpu.SMEM)


def iota(shape, dim):
    return lax.broadcasted_iota(i32, shape, dim)


def split3(x):
    high = x.astype(bf16)
    rest = x - high.astype(f32)
    middle = rest.astype(bf16)
    low = (rest - middle.astype(f32)).astype(bf16)
    return high, middle, low


def dot(a, b):
    return jnp.dot(a, b, preferred_element_type=f32)


def to_column(row):
    n = row.shape[1]
    return jnp.sum(jnp.where(iota((n, n), 0) == iota((n, n), 1), row, 0.0), axis=1, keepdims=True)


def to_row(column):
    n = column.shape[0]
    return jnp.sum(jnp.where(iota((n, n), 0) == iota((n, n), 1), column, 0.0), axis=0, keepdims=True)


def coeffs_of(p, sw, sg):
    so = 1.0 - sw - sg
    return tuple(
        s * s * (1.0 / viscosity[a]) * (1.0 + compress[a] * p) for a, s in enumerate((sw, so, sg))
    )


def scatter(cell_row, values):
    match = iota((L * R, PERFS), 0) == (cell_row >> 8)
    column = to_column(cell_row.astype(f32)).astype(i32) & (C - 1)
    spread = (iota((PERFS, C), 1) == column).astype(bf16)
    return sum(
        dot(jnp.where(match, part.astype(f32), 0.0).astype(bf16), spread) for part in split3(values)
    )


def gather_cells(cells, refs, rows):
    def body(block, carry):
        for u in range(8):
            k = block * 8 + u
            cell = cells[k]
            layer = cell >> 14
            line = (cell >> 8) & (R - 1)
            for n, ref in enumerate(refs):
                rows[n, pl.ds(k, 1), :] = ref[layer, pl.ds(line, 1), :]
        return carry

    lax.fori_loop(0, PERFS // 8, body, 0)


def pick_columns(rows, n, column):
    return jnp.sum(jnp.where(iota((PERFS, C), 1) == column, rows[n], 0.0), axis=1, keepdims=True)


def gather_wells(table, holder, slot):
    onehot = (iota((DEVICES, PERFS), 0) == holder).astype(bf16)
    wide = sum(dot(part, onehot) for part in split3(table.T))
    return jnp.sum(jnp.where(iota((LANES, PERFS), 0) == slot, wide, 0.0), axis=0, keepdims=True)


def to_holders(holder, slot_column, columns):
    lane = iota((PERFS, LANES), 1)
    group = lane >> 4
    values = jnp.zeros((PERFS, LANES), f32)
    for g, column in columns:
        values = jnp.where(group == g, column, values)
    values = jnp.where((lane & 15) == slot_column, values, 0.0)
    onehot = (iota((DEVICES, PERFS), 0) == holder).astype(bf16)
    return sum(dot(onehot, part) for part in split3(values))


def parts_by_offset(me, well_row, values):
    offset = (me - (well_row >> 4)) & (DEVICES - 1)
    lane = jnp.where(offset == FAR, TAIL, offset * WELL_DEV) + (well_row & 15)
    column = to_column(lane.astype(f32)).astype(i32)
    onehot = (iota((PERFS, WIDTH), 1) == column).astype(bf16)
    high, middle, low = split3(values)
    rows = jnp.concatenate([high.astype(f32), middle.astype(f32), low.astype(f32), jnp.zeros((5, PERFS), f32)], axis=0)
    return jnp.sum(dot(rows.astype(bf16), onehot), axis=0, keepdims=True)


def sum_parts(got):
    aligned = got[:, :LANES]
    for t in range(1, TAIL // LANES):
        aligned = aligned + pltpu.roll(got[:, t * LANES : (t + 1) * LANES], DEVICES - 8 * t, 0)
    total = aligned + pltpu.roll(got[:, TAIL:], DEVICES - FAR, 0)
    for u in range(1, 8):
        total = total + pltpu.roll(pltpu.roll(aligned, DEVICES - u, 0), LANES - 16 * u, 1)
    return total


def shift_rows(x, first, last):
    return (
        jnp.concatenate([first, x[:-1]], axis=0),
        jnp.concatenate([x[1:], last], axis=0),
    )


def shift_columns(x, first, last):
    lane = iota(x.shape, 1)
    return (
        jnp.where(lane == 0, first, pltpu.roll(x, 1, 1)),
        jnp.where(lane == C - 1, last, pltpu.roll(x, C - 1, 1)),
    )


def lane_of(ref, index):
    return pltpu.roll(ref, (LANES - index) % LANES, 1)[:, 0:1]


def write_faces(read, outs):
    row_lo, row_hi, col_lo, col_hi = outs
    lane = iota((R, LANES), 1)
    low = jnp.zeros((R, LANES), f32)
    high = jnp.zeros((R, LANES), f32)
    for l in range(L):
        x = read(l)
        row_lo[l : l + 1, :] = x[0:1]
        row_hi[l : l + 1, :] = x[R - 1 : R]
        low = jnp.where(lane == l, x[:, 0:1], low)
        high = jnp.where(lane == l, x[:, C - 1 : C], high)
    col_lo[...] = low
    col_hi[...] = high


def start_kernel(cells, info, own, p, sw, sg, perm, row_lo, row_hi, col_lo, col_hi, pay, perf, rows):
    lane = iota((R, LANES), 1)
    low = jnp.zeros((R, LANES), f32)
    high = jnp.zeros((R, LANES), f32)
    for l in range(L):
        for f, ref in enumerate((p, sw, sg)):
            x = ref[l]
            n = f * L + l
            row_lo[n : n + 1, :] = x[0:1]
            row_hi[n : n + 1, :] = x[R - 1 : R]
            low = jnp.where(lane == n, x[:, 0:1], low)
            high = jnp.where(lane == n, x[:, C - 1 : C], high)
        n = 3 * L + l
        row_lo[n : n + 1, :] = perm[0, l, 0:16, :].astype(f32)[0:1]
        row_hi[n : n + 1, :] = perm[0, l, R - 16 : R, :].astype(f32)[15:16]
        k = perm[1, l].astype(f32)
        low = jnp.where(lane == n, k[:, 0:1], low)
        high = jnp.where(lane == n, k[:, C - 1 : C], high)
    col_lo[...] = low
    col_hi[...] = high
    gather_cells(cells, (p, sw, sg), rows)
    cell_row = info[0:1].astype(i32)
    well_row = info[1:2].astype(i32)
    index_row = info[2:3]
    column = to_column(info[0:1]).astype(i32) & (C - 1)
    here = [pick_columns(rows, n, column) for n in range(3)]
    coeffs = coeffs_of(*here)
    total = to_column(index_row) * (coeffs[0] + coeffs[1] + coeffs[2])
    slot_column = to_column(info[1:2]).astype(i32) & 15
    sums = to_holders(well_row >> 4, slot_column, ((0, total), (1, total * here[0])))
    wide = pltpu.roll(jnp.broadcast_to(own[0:1], (8, LANES)), 32, 1)[0:1]
    pay[...] = sums + wide
    perf[...] = jnp.broadcast_to(to_row(total), (8, PERFS))


def transmit(k, k_next):
    return k * k_next / (k + k_next)


def setup_kernel(
    info, p, sw, sg, por, mass, perm, row_lo, row_hi, col_lo, col_hi,
    coef, coef_row, coef_col, tx, ty, tz, base, head, weight, res, diag, index_sum,
):
    for side, ref in enumerate((row_lo, row_hi)):
        for a, c in enumerate(coeffs_of(ref[0:L], ref[L : 2 * L], ref[2 * L : 3 * L])):
            coef_row[side, a] = c
    for side, ref in enumerate((col_lo, col_hi)):
        x = ref[...]
        for a, c in enumerate(coeffs_of(x, pltpu.roll(x, LANES - L, 1), pltpu.roll(x, LANES - 2 * L, 1))):
            coef_col[side, a] = c
    index_sum[...] = scatter(info[0:1].astype(i32), info[2:3]).reshape(L, R, C)
    lane = iota((R, C), 1)

    def first(l, carry):
        for a, c in enumerate(coeffs_of(p[l], sw[l], sg[l])):
            coef[a, l] = c
        k = perm[0, l].astype(f32)
        n = 3 * L + l
        before = transmit(k, jnp.concatenate([row_lo[pl.ds(n, 1), :], k[:-1]], axis=0))
        tx[0, l] = before
        tx[1, l] = jnp.concatenate([before[1:], transmit(k[R - 1 : R], row_hi[pl.ds(n, 1), :])], axis=0)
        k = perm[1, l].astype(f32)
        before = transmit(k, jnp.where(lane == 0, lane_of(col_lo[...], n), pltpu.roll(k, 1, 1)))
        ty[0, l] = before
        last = transmit(k[:, C - 1 : C], lane_of(col_hi[...], n))
        ty[1, l] = jnp.where(lane == C - 1, last, pltpu.roll(before, C - 1, 1))
        k = perm[2, l].astype(f32)
        under = perm[2, jnp.maximum(l - 1, 0)].astype(f32)
        tz[l] = jnp.where(l > 0, layer_ratio, 0.0) * transmit(k, under)
        return carry

    lax.fori_loop(0, L, first, 0)
    tz[L] = jnp.zeros((R, C), f32)

    def second(l, carry):
        down, up = (jnp.maximum(l - 1, 0), jnp.minimum(l + 1, L - 1))
        here = p[l]
        nexts = shift_rows(here, row_lo[pl.ds(l, 1), :], row_hi[pl.ds(l, 1), :])
        nexts += shift_columns(here, lane_of(col_lo[...], l), lane_of(col_hi[...], l))
        nexts += (p[down], p[up])
        faces = (tx[0, l], tx[1, l], ty[0, l], ty[1, l], tz[l], tz[l + 1])
        drops = [t * (here - q) for t, q in zip(faces, nexts)]
        face_sum = sum(faces)
        drop_sum = sum(drops)
        porous = volume_scale * por[l]
        sats = (sw[l], 1.0 - sw[l] - sg[l], sg[l])
        indices = index_sum[l]
        diagonals, residuals, inverses, cs = [], [], [], []
        for a in range(3):
            c = coef[a, l]
            sides = shift_rows(c, coef_row[0, a, pl.ds(l, 1), :], coef_row[1, a, pl.ds(l, 1), :])
            sides += shift_columns(c, lane_of(coef_col[0, a], l), lane_of(coef_col[1, a], l))
            sides += (coef[a, down], coef[a, up])
            ab = c * face_sum
            net = c * drop_sum
            for t, d, s in zip(faces, drops, sides):
                ab = ab + t * s
                net = net + d * s
            b = 1.0 + compress[a] * here
            stored = porous * sats[a]
            diagonals.append(compress[a] * stored + ab + c * indices)
            residuals.append(b * stored - volume_scale * mass[a, l] + net + c * (indices * here))
            inverses.append(1.0 / (porous * b))
            cs.append(c)
        inverse_total = 1.0 / sum(d * v for d, v in zip(diagonals, inverses))
        weights = [v * inverse_total for v in inverses]
        base[l] = -sum(w * r for w, r in zip(weights, residuals))
        head[l] = sum(w * c for w, c in zip(weights, cs))
        for a in range(3):
            weight[a, l] = weights[a]
            res[a, l] = residuals[a]
        diag[0, l] = diagonals[0]
        diag[1, l] = diagonals[2]
        return carry

    lax.fori_loop(0, L, second, 0)


def first_kernel(
    cells, me, got, info, own, perf, base, head,
    spread, step, row_lo, row_hi, col_lo, col_hi, pay, mine, rows,
):
    lane = iota((1, LANES), 1)
    sums = jnp.sum(got[...], axis=0, keepdims=True)
    total = jnp.where(lane < WELL_DEV, sums, 1.0)
    flow = pltpu.roll(jnp.broadcast_to(sums, (8, LANES)), LANES - 16, 1)[0:1]
    residual = jnp.where(lane < WELL_DEV, flow - total * own[0:1] - own[1:2], 0.0)
    inverse = jnp.where(lane < WELL_DEV, 1.0 / total, 0.0)
    mine[0:1] = residual
    mine[1:2] = inverse
    cell_row = info[0:1].astype(i32)
    well_row = info[1:2].astype(i32)
    heads = gather_wells(got[...], well_row >> 4, (well_row & 15) + 32)
    wells = scatter(cell_row, info[2:3] * heads).reshape(L, R, C)
    spread[...] = wells
    step[...] = base[...] + head[...] * wells
    write_faces(lambda l: step[l], (row_lo, row_hi, col_lo, col_hi))
    gather_cells(cells, (step,), rows)
    column = to_column(info[0:1]).astype(i32) & (C - 1)
    here = to_row(pick_columns(rows, 0, column))
    parts = parts_by_offset(me[0], well_row, perf[0:1] * here)
    pay[:, :TAIL] = jnp.broadcast_to(parts[:, :TAIL], (DEVICES, TAIL))
    packed = parts[:, TAIL:]
    for n, row in enumerate((residual * inverse, residual, inverse)):
        packed = packed + pltpu.roll(jnp.broadcast_to(row, (8, LANES)), 16 * (n + 1), 1)[0:1]
    pay[:, TAIL:] = jnp.broadcast_to(packed, (DEVICES, LANES))


def step_faces(l, down, up, refs, halo):
    step = refs
    row_lo, row_hi, col_lo, col_hi = halo
    here = step[l]
    nexts = shift_rows(here, row_lo[pl.ds(l, 1), :], row_hi[pl.ds(l, 1), :])
    nexts += shift_columns(here, lane_of(col_lo[...], l), lane_of(col_hi[...], l))
    return nexts + (step[down], step[up])


def grid_kernel(
    coef, coef_row, coef_col, tx, ty, tz, head, weight, res, spread, step, row_lo, row_hi, col_lo, col_hi,
    residual, gain, ahead,
):
    def layer(l, carry):
        down, up = (jnp.maximum(l - 1, 0), jnp.minimum(l + 1, L - 1))
        nexts = step_faces(l, down, up, step, (row_lo, row_hi, col_lo, col_hi))
        faces = (tx[0, l], tx[1, l], ty[0, l], ty[1, l], tz[l], tz[l + 1])
        wells = spread[l]
        mixes = [head[l]] * 6
        for a in range(3):
            c = coef[a, l]
            w = weight[a, l]
            sides = shift_rows(c, coef_row[0, a, pl.ds(l, 1), :], coef_row[1, a, pl.ds(l, 1), :])
            sides += shift_columns(c, lane_of(coef_col[0, a], l), lane_of(coef_col[1, a], l))
            sides += (coef[a, down], coef[a, up])
            mixes = [m + w * s for m, s in zip(mixes, sides)]
            residual[a, l] = res[a, l] - c * wells
        total = step[l]
        for j in range(6):
            g = faces[j] * mixes[j]
            gain[j, l] = g
            total = total + g * nexts[j]
        ahead[l] = total
        return carry

    lax.fori_loop(0, L, layer, 0)


def second_kernel(got, info, ahead, head, step, row_lo, row_hi, col_lo, col_hi):
    cell_row = info[0:1].astype(i32)
    well_row = info[1:2].astype(i32)
    moves = gather_wells(got[:, TAIL:], well_row >> 4, (well_row & 15) + 16)
    wells = scatter(cell_row, info[2:3] * moves).reshape(L, R, C)
    step[...] = ahead[...] + head[...] * wells
    write_faces(lambda l: step[l], (row_lo, row_hi, col_lo, col_hi))


def wells_kernel(cells, me, got, info, perf, step, table, spread, parts, rows):
    tail = got[:, TAIL:]
    residuals = pltpu.roll(tail, LANES - 32, 1)
    inverses = pltpu.roll(tail, LANES - 48, 1)
    table[0] = residuals
    table[1] = inverses
    cell_row = info[0:1].astype(i32)
    well_row = info[1:2].astype(i32)
    valid = iota((DEVICES, LANES), 1) < WELL_DEV
    moves = jnp.where(valid, (sum_parts(got[...]) + residuals) * inverses, 0.0)
    values = gather_wells(moves, well_row >> 4, well_row & 15)
    spread[...] = scatter(cell_row, info[2:3] * values).reshape(L, R, C)
    gather_cells(cells, (step,), rows)
    column = to_column(info[0:1]).astype(i32) & (C - 1)
    here = to_row(pick_columns(rows, 0, column))
    parts[...] = jnp.broadcast_to(parts_by_offset(me[0], well_row, perf[0:1] * here), (8, WIDTH))


def third_kernel(
    cells, info, perf, parts, base, gain, head, spread, old, row_lo, row_hi, col_lo, col_hi,
    step, out_row_lo, out_row_hi, out_col_lo, out_col_hi, pay, rows,
):
    def layer(l, carry):
        down, up = (jnp.maximum(l - 1, 0), jnp.minimum(l + 1, L - 1))
        nexts = step_faces(l, down, up, old, (row_lo, row_hi, col_lo, col_hi))
        total = base[l] + head[l] * spread[l]
        for j in range(6):
            total = total + gain[j, l] * nexts[j]
        step[l] = total
        return carry

    lax.fori_loop(0, L, layer, 0)
    write_faces(lambda l: step[l], (out_row_lo, out_row_hi, out_col_lo, out_col_hi))
    gather_cells(cells, (step,), rows)
    column = to_column(info[0:1]).astype(i32) & (C - 1)
    here = pick_columns(rows, 0, column)
    well_row = info[1:2].astype(i32)
    slot_column = to_column(info[1:2]).astype(i32) & 15
    flows = to_holders(well_row >> 4, slot_column, ((1, to_column(perf[0:1]) * here),))
    pay[:, :TAIL] = jnp.broadcast_to(parts[0:1, :TAIL], (DEVICES, TAIL))
    pay[:, TAIL:] = parts[0:1, TAIL:] + flows


def last_grid_kernel(
    p, por, coef, coef_row, coef_col, tx, ty, tz, head, weight, diag, residual, step, row_lo, row_hi, col_lo, col_hi,
    ahead, slope,
):
    def layer(l, carry):
        down, up = (jnp.maximum(l - 1, 0), jnp.minimum(l + 1, L - 1))
        nexts = step_faces(l, down, up, step, (row_lo, row_hi, col_lo, col_hi))
        faces = (tx[0, l], tx[1, l], ty[0, l], ty[1, l], tz[l], tz[l + 1])
        flows = [t * q for t, q in zip(faces, nexts)]
        flow_sum = sum(flows)
        rights, cs = [], []
        for a in range(3):
            c = coef[a, l]
            sides = shift_rows(c, coef_row[0, a, pl.ds(l, 1), :], coef_row[1, a, pl.ds(l, 1), :])
            sides += shift_columns(c, lane_of(coef_col[0, a], l), lane_of(coef_col[1, a], l))
            sides += (coef[a, down], coef[a, up])
            total = c * flow_sum - residual[a, l]
            for v, s in zip(flows, sides):
                total = total + v * s
            rights.append(total)
            cs.append(c)
        z = sum(weight[a, l] * rights[a] for a in range(3))
        h = head[l]
        porous = volume_scale * por[l]
        inverse_water = 1.0 / (porous * (1.0 + compress[0] * p[l]))
        inverse_gas = 1.0 / (porous * (1.0 + compress[2] * p[l]))
        ahead[0, l] = z
        ahead[1, l] = (rights[0] - diag[0, l] * z) * inverse_water
        ahead[2, l] = (rights[2] - diag[1, l] * z) * inverse_gas
        slope[0, l] = (cs[0] - diag[0, l] * h) * inverse_water
        slope[1, l] = (cs[2] - diag[1, l] * h) * inverse_gas
        return carry

    lax.fori_loop(0, L, layer, 0)


def final_kernel(got, info, table, mine, ahead, head, slope, update, moved):
    cell_row = info[0:1].astype(i32)
    well_row = info[1:2].astype(i32)
    valid = iota((DEVICES, LANES), 1) < WELL_DEV
    moves = jnp.where(valid, (sum_parts(got[...]) + table[0]) * table[1], 0.0)
    values = gather_wells(moves, well_row >> 4, well_row & 15)
    wells = scatter(cell_row, info[2:3] * values).reshape(L, R, C)
    update[0] = ahead[0] + head[...] * wells
    update[1] = ahead[1] + slope[0] * wells
    update[2] = ahead[2] + slope[1] * wells
    flow = jnp.sum(got[:, TAIL:], axis=0, keepdims=True)
    flow = pltpu.roll(jnp.broadcast_to(flow, (8, LANES)), LANES - 16, 1)[0:1]
    moved[...] = jnp.broadcast_to((flow + mine[0:1]) * mine[1:2], (8, LANES))


def call(kernel, outs, ins, operands, scratch=(), flops=0, hbm=()):
    shapes = tuple(
        jax.ShapeDtypeStruct(s, f32) if n in hbm else pltpu.VMEM(s, f32) for n, s in enumerate(outs)
    )
    moved = 4 * sum(int(x.size) for x in operands)
    return pl.pallas_call(
        kernel,
        out_shape=shapes,
        in_specs=ins,
        out_specs=tuple(VM for _ in outs),
        scratch_shapes=list(scratch),
        compiler_params=pltpu.CompilerParams(vmem_limit_bytes=40 * 1024 * 1024),
        cost_estimate=pl.CostEstimate(flops=flops, bytes_accessed=moved, transcendentals=0),
    )(*operands)


FIELD = (L, R, C)
ROW, COLUMN = ((L, C), (R, LANES))
FACES = (ROW, ROW, COLUMN, COLUMN)
GATHERED = pltpu.VMEM((1, PERFS, C), f32)


def exchange(array):
    return lax.all_to_all(array, AXES, split_axis=0, concat_axis=0, tiled=True)


def halo_of(faces):
    row_lo, row_hi, col_lo, col_hi = faces
    got = []
    for axis, low, high in (("gx", row_lo, row_hi), ("gy", col_lo, col_hi)):
        count = lax.axis_size(axis)
        up = [(i, i + 1) for i in range(count - 1)]
        got.append(lax.ppermute(high, axis, up))
        got.append(lax.ppermute(low, axis, [(j, i) for i, j in up]))
    return got


def local(
    pressure, sat_water, sat_gas, old_mass, perm, porosity,
    perf_well, perf_cell, perf_index, well_pressure, well_rate,
):
    me = (lax.axis_index("gx") * lax.axis_size("gy") + lax.axis_index("gy")).astype(i32).reshape(1)
    info = jnp.pad(
        jnp.stack([perf_cell.astype(f32), perf_well.astype(f32), perf_index]), ((0, 5), (0, 0))
    )
    own = jnp.pad(jnp.stack([well_pressure, well_rate]), ((0, 6), (0, LANES - WELL_DEV)))
    wide_row, wide_column = ((4 * L, C), (R, LANES))
    *faces, pay, perf = call(
        start_kernel,
        (wide_row, wide_row, wide_column, wide_column, (DEVICES, LANES), (8, PERFS)),
        [SM] + [VM] * 6,
        (perf_cell, info, own, pressure, sat_water, sat_gas, perm),
        [pltpu.VMEM((3, PERFS, C), f32)],
    )
    halo = halo_of(faces)
    got = exchange(pay)
    coef, coef_row, coef_col, tx, ty, tz, base, head, weight, res, diag, _ = call(
        setup_kernel,
        (
            (3,) + FIELD, (2, 3) + ROW, (2, 3) + COLUMN, (2,) + FIELD, (2,) + FIELD, (L + 1, R, C),
            FIELD, FIELD, (3,) + FIELD, (3,) + FIELD, (2,) + FIELD, FIELD,
        ),
        [VM] * 11,
        (info, pressure, sat_water, sat_gas, porosity, old_mass, perm, *halo),
        flops=400 * L * R * C,
    )
    spread, start, *faces, pay, mine = call(
        first_kernel,
        (FIELD, FIELD) + FACES + ((DEVICES, WIDTH), (8, LANES)),
        [SM, SM] + [VM] * 6,
        (perf_cell, me, got, info, own, perf, base, head),
        [GATHERED],
    )
    halo = halo_of(faces)
    got = exchange(pay)
    fields = (coef, coef_row, coef_col, tx, ty, tz, head, weight)
    residual, gain, ahead = call(
        grid_kernel,
        ((3,) + FIELD, (6,) + FIELD, FIELD),
        [VM] * 15,
        (*fields, res, spread, start, *halo),
        flops=100 * L * R * C,
        hbm=(0,),
    )
    step, *faces = call(second_kernel, (FIELD,) + FACES, [VM] * 4, (got, info, ahead, head))
    halo = halo_of(faces)
    table, spread, parts = call(
        wells_kernel,
        ((2, DEVICES, LANES), FIELD, (8, WIDTH)),
        [SM, SM] + [VM] * 4,
        (perf_cell, me, got, info, perf, step),
        [GATHERED],
    )
    step, *faces, pay = call(
        third_kernel,
        (FIELD,) + FACES + ((DEVICES, WIDTH),),
        [SM] + [VM] * 12,
        (perf_cell, info, perf, parts, start, gain, head, spread, step, *halo),
        [GATHERED],
    )
    halo = halo_of(faces)
    got = exchange(pay)
    ahead, slope = call(
        last_grid_kernel,
        ((3,) + FIELD, (2,) + FIELD),
        [VM] * 17,
        (pressure, porosity, *fields, diag, residual, step, *halo),
        flops=150 * L * R * C,
    )
    update, moved = call(
        final_kernel,
        ((3,) + FIELD, (8, LANES)),
        [VM] * 7,
        (got, info, table, mine, ahead, head, slope),
        hbm=(0, 1),
    )
    return residual, mine[0, :WELL_DEV], update, moved[0, :WELL_DEV]


def solution(mesh):
    return jax.shard_map(
        local,
        mesh=mesh,
        in_specs=(
            P(None, "gx", "gy"),
            P(None, "gx", "gy"),
            P(None, "gx", "gy"),
            P(None, None, "gx", "gy"),
            P(None, None, "gx", "gy"),
            P(None, "gx", "gy"),
            P(("gx", "gy")),
            P(("gx", "gy")),
            P(("gx", "gy")),
            P(("gx", "gy")),
            P(("gx", "gy")),
        ),
        out_specs=(
            P(None, None, "gx", "gy"),
            P(("gx", "gy")),
            P(None, None, "gx", "gy"),
            P(("gx", "gy")),
        ),
        check_vma=False,
    )
```

```python
import jax
import jax.numpy as jnp
from jax import lax
from jax.experimental import pallas as pl
from jax.experimental.pallas import tpu as pltpu
from jax.sharding import PartitionSpec as P

f32 = jnp.float32
bf16 = jnp.bfloat16
i32 = jnp.int32

compress = (0.05, 0.02, 0.2)
viscosity = (0.5, 2.0, 0.1)
volume_scale = 4.0
layer_ratio = 0.1
AXES = ("gx", "gy")
DEVICES = 128
WELL_DEV = 16
REACH = 40
FAR = 64
TAIL = REACH * WELL_DEV
WIDTH = TAIL + 128
LANES = 128
L, R, C = 8, 64, 256
PERFS = 256
VM = pl.BlockSpec(memory_space=pltpu.VMEM)
SM = pl.BlockSpec(memory_space=pltpu.SMEM)
HB = pl.BlockSpec(memory_space=pltpu.HBM)


def iota(shape, dim):
    return lax.broadcasted_iota(i32, shape, dim)


def split3(x):
    high = x.astype(bf16)
    rest = x - high.astype(f32)
    middle = rest.astype(bf16)
    low = (rest - middle.astype(f32)).astype(bf16)
    return high, middle, low


def dot(a, b):
    return jnp.dot(a, b, preferred_element_type=f32)


def to_column(row):
    n = row.shape[1]
    return jnp.sum(jnp.where(iota((n, n), 0) == iota((n, n), 1), row, 0.0), axis=1, keepdims=True)


def to_row(column):
    n = column.shape[0]
    return jnp.sum(jnp.where(iota((n, n), 0) == iota((n, n), 1), column, 0.0), axis=0, keepdims=True)


def coeffs_of(p, sw, sg):
    so = 1.0 - sw - sg
    return tuple(
        s * s * (1.0 / viscosity[a]) * (1.0 + compress[a] * p) for a, s in enumerate((sw, so, sg))
    )


def scatter(cell_row, values):
    match = iota((L * R, PERFS), 0) == (cell_row >> 8)
    column = to_column(cell_row.astype(f32)).astype(i32) & (C - 1)
    spread = (iota((PERFS, C), 1) == column).astype(bf16)
    return sum(
        dot(jnp.where(match, part.astype(f32), 0.0).astype(bf16), spread) for part in split3(values)
    )


def gather_cells(cells, refs, rows):
    def body(block, carry):
        for u in range(8):
            k = block * 8 + u
            cell = cells[k]
            layer = cell >> 14
            line = (cell >> 8) & (R - 1)
            for n, ref in enumerate(refs):
                rows[n, pl.ds(k, 1), :] = ref[layer, pl.ds(line, 1), :]
        return carry

    lax.fori_loop(0, PERFS // 8, body, 0)


def pick_columns(rows, n, column):
    return jnp.sum(jnp.where(iota((PERFS, C), 1) == column, rows[n], 0.0), axis=1, keepdims=True)


def gather_wells(table, holder, slot):
    onehot = (iota((DEVICES, PERFS), 0) == holder).astype(bf16)
    wide = sum(dot(part, onehot) for part in split3(table.T))
    return jnp.sum(jnp.where(iota((LANES, PERFS), 0) == slot, wide, 0.0), axis=0, keepdims=True)


def to_holders(holder, slot_column, columns):
    lane = iota((PERFS, LANES), 1)
    group = lane >> 4
    values = jnp.zeros((PERFS, LANES), f32)
    for g, column in columns:
        values = jnp.where(group == g, column, values)
    values = jnp.where((lane & 15) == slot_column, values, 0.0)
    onehot = (iota((DEVICES, PERFS), 0) == holder).astype(bf16)
    return sum(dot(onehot, part) for part in split3(values))


def parts_by_offset(me, well_row, values):
    offset = (me - (well_row >> 4)) & (DEVICES - 1)
    lane = jnp.where(offset == FAR, TAIL, offset * WELL_DEV) + (well_row & 15)
    column = to_column(lane.astype(f32)).astype(i32)
    onehot = (iota((PERFS, WIDTH), 1) == column).astype(bf16)
    high, middle, low = split3(values)
    rows = jnp.concatenate([high.astype(f32), middle.astype(f32), low.astype(f32), jnp.zeros((5, PERFS), f32)], axis=0)
    return jnp.sum(dot(rows.astype(bf16), onehot), axis=0, keepdims=True)


def tile_of(got, t):
    return got[pl.ds(t, DEVICES, stride=8), :]


def sum_parts(got):
    aligned = tile_of(got, 0)
    for t in range(1, TAIL // LANES):
        aligned = aligned + pltpu.roll(tile_of(got, t), DEVICES - 8 * t, 0)
    total = aligned + pltpu.roll(tile_of(got, 5), DEVICES - FAR, 0)
    for u in range(1, 8):
        total = total + pltpu.roll(pltpu.roll(aligned, DEVICES - u, 0), LANES - 16 * u, 1)
    return total


def to_everyone(tile):
    return jnp.broadcast_to(tile[None], (DEVICES, 8, LANES)).reshape(8 * DEVICES, LANES)


def rolled_row(row, shift):
    return pltpu.roll(jnp.broadcast_to(row, (8, LANES)), shift, 1)[0:1]


def shift_rows(x, first, last):
    return (
        jnp.concatenate([first, x[:-1]], axis=0),
        jnp.concatenate([x[1:], last], axis=0),
    )


def shift_columns(x, first, last):
    lane = iota(x.shape, 1)
    return (
        jnp.where(lane == 0, first, pltpu.roll(x, 1, 1)),
        jnp.where(lane == C - 1, last, pltpu.roll(x, C - 1, 1)),
    )


def lane_of(x, index):
    return pltpu.roll(x, (LANES - index) % LANES, 1)[:, 0:1]


def pack_columns(columns, low, high):
    n = low.shape[0]
    turned = jnp.concatenate([columns, jnp.zeros((LANES - R, LANES), f32)], axis=0).T
    low[...] = turned[0:n]
    high[...] = turned[n : 2 * n]


def unpack_columns(low, high):
    n = low.shape[0]
    rows = jnp.concatenate([low[...], high[...], jnp.zeros((LANES - 2 * n, LANES), f32)], axis=0)
    return rows.T[0:R]


def write_faces(step, outs):
    row_lo, row_hi, col_lo, col_hi = outs
    lane = iota((R, LANES), 1)
    columns = jnp.zeros((R, LANES), f32)
    for l in range(L):
        x = step[l]
        row_lo[l : l + 1, :] = x[0:1]
        row_hi[l : l + 1, :] = x[R - 1 : R]
        columns = jnp.where(lane == l, x[:, 0:1], columns)
        columns = jnp.where(lane == L + l, x[:, C - 1 : C], columns)
    pack_columns(columns, col_lo, col_hi)


def start_copies(pairs, sems):
    copies = [pltpu.make_async_copy(a, b, sems.at[n]) for n, (a, b) in enumerate(pairs)]
    for c in copies:
        c.start()
    return copies


def wait_copies(copies):
    for c in copies:
        c.wait()


def layer_copies(pairs, sems, l):
    return [pltpu.make_async_copy(a, b, sems.at[n, l]) for n, (a, b) in enumerate(pairs(l))]


def start_kernel(
    cells, cell_in, well_in, index_in, pressure_in, rate_in, p_h, sw_h, sg_h, perm_h,
    row_lo, row_hi, col_lo, col_hi, pay, perf, info, own,
    p, sw, sg, perm, rows, sems,
):
    copies = start_copies(
        ((p_h, p), (sw_h, sw), (sg_h, sg), (perm_h.at[0:2], perm)), sems
    )
    cell_row = cell_in[...]
    well_row = well_in[...]
    index_row = index_in[...]
    cell_float = cell_row.astype(f32)
    well_float = well_row.astype(f32)
    info[...] = jnp.concatenate([cell_float, well_float, index_row, jnp.zeros((5, PERFS), f32)], axis=0)
    blank = jnp.zeros((1, LANES - WELL_DEV), f32)
    heads = jnp.concatenate([pressure_in[...], blank], axis=1)
    rates = jnp.concatenate([rate_in[...], blank], axis=1)
    own[...] = jnp.concatenate([heads, rates, jnp.zeros((6, LANES), f32)], axis=0)
    column = to_column(cell_float).astype(i32) & (C - 1)
    slot_column = to_column(well_float).astype(i32) & 15
    index_column = to_column(index_row)
    wait_copies(copies)
    lane = iota((R, LANES), 1)
    columns = jnp.zeros((R, LANES), f32)
    for l in range(L):
        for f, ref in enumerate((p, sw, sg)):
            x = ref[l]
            n = f * L + l
            row_lo[n : n + 1, :] = x[0:1]
            row_hi[n : n + 1, :] = x[R - 1 : R]
            columns = jnp.where(lane == n, x[:, 0:1], columns)
            columns = jnp.where(lane == 4 * L + n, x[:, C - 1 : C], columns)
        n = 3 * L + l
        row_lo[n : n + 1, :] = perm[0, l, 0:16, :].astype(f32)[0:1]
        row_hi[n : n + 1, :] = perm[0, l, R - 16 : R, :].astype(f32)[15:16]
        k = perm[1, l].astype(f32)
        columns = jnp.where(lane == n, k[:, 0:1], columns)
        columns = jnp.where(lane == 4 * L + n, k[:, C - 1 : C], columns)
    pack_columns(columns, col_lo, col_hi)
    gather_cells(cells, (p, sw, sg), rows)
    here = [pick_columns(rows, n, column) for n in range(3)]
    coeffs = coeffs_of(*here)
    total = index_column * (coeffs[0] + coeffs[1] + coeffs[2])
    sums = to_holders(well_row >> 4, slot_column, ((0, total), (1, total * here[0])))
    pay[...] = sums + rolled_row(heads, 32)
    perf[...] = jnp.broadcast_to(to_row(total), (8, PERFS))


def transmit(k, k_next):
    return k * k_next / (k + k_next)


def neighbours(field, l, rows, columns, first, last):
    here = field(l)
    nexts = shift_rows(here, *rows)
    nexts += shift_columns(here, lane_of(columns, first), lane_of(columns, last))
    return nexts + (field(jnp.maximum(l - 1, 0)), field(jnp.minimum(l + 1, L - 1)))


def coeff_neighbours(coef, coef_row, coef_col, a, l):
    rows = (coef_row[0, a, pl.ds(l, 1), :], coef_row[1, a, pl.ds(l, 1), :])
    return neighbours(lambda m: coef[a, m], l, rows, coef_col[a], l, 4 * L + l)


def step_neighbours(step, row_lo, row_hi, columns, l):
    rows = (row_lo[pl.ds(l, 1), :], row_hi[pl.ds(l, 1), :])
    return neighbours(lambda m: step[m], l, rows, columns, l, L + l)


def setup_kernel(
    me, info, row_lo, row_hi, col_lo, col_hi, p_h, sw_h, sg_h, por_h, mass_h, perm_h,
    coef_row, coef_col, coef_h, tx_h, ty_h, tz_h, base_h, head_h, weight_h, res_h, diag_h,
    p, sw, sg, por, mass, perm, coef, tx, ty, tz, base, head, weight, res, diag, index_sum,
    sems, sems_t, sems_out,
):
    copies = start_copies(
        ((p_h, p), (sw_h, sw), (sg_h, sg), (perm_h, perm), (por_h, por), (mass_h, mass)), sems
    )
    index_sum[...] = scatter(info[0:1].astype(i32), info[2:3]).reshape(L, R, C)
    for side, ref in enumerate((row_lo, row_hi)):
        for a, c in enumerate(coeffs_of(ref[0:L], ref[L : 2 * L], ref[2 * L : 3 * L])):
            coef_row[side, a] = c
    columns = unpack_columns(col_lo, col_hi)
    for a, c in enumerate(
        coeffs_of(columns, pltpu.roll(columns, LANES - L, 1), pltpu.roll(columns, LANES - 2 * L, 1))
    ):
        coef_col[a] = c
    lane = iota((R, C), 1)
    gx = me[0] >> 4
    gy = me[0] & 15
    inside = [jnp.where(t, 1.0, 0.0) for t in (gx > 0, gx < 7, gy > 0, gy < 15)]
    wait_copies(copies[:4])

    def first(l, carry):
        for a, c in enumerate(coeffs_of(p[l], sw[l], sg[l])):
            coef[a, l] = c
        k = perm[0, l].astype(f32)
        n = 3 * L + l
        edge = row_lo[pl.ds(n, 1), :] * inside[0]
        before = transmit(k, jnp.concatenate([edge, k[:-1]], axis=0))
        edge = row_hi[pl.ds(n, 1), :] * inside[1]
        tx[0, l] = before
        tx[1, l] = jnp.concatenate([before[1:], transmit(k[R - 1 : R], edge)], axis=0)
        k = perm[1, l].astype(f32)
        edge = lane_of(columns, n) * inside[2]
        before = transmit(k, jnp.where(lane == 0, edge, pltpu.roll(k, 1, 1)))
        edge = lane_of(columns, 4 * L + n) * inside[3]
        ty[0, l] = before
        ty[1, l] = jnp.where(lane == C - 1, transmit(k[:, C - 1 : C], edge), pltpu.roll(before, C - 1, 1))
        k = perm[2, l].astype(f32)
        under = perm[2, jnp.maximum(l - 1, 0)].astype(f32)
        tz[l] = jnp.where(l > 0, layer_ratio, 0.0) * transmit(k, under)
        return carry

    lax.fori_loop(0, L, first, 0)
    tz[L] = jnp.zeros((R, C), f32)
    saved = start_copies(((coef, coef_h), (tx, tx_h), (ty, ty_h), (tz, tz_h)), sems_t)
    wait_copies(copies[4:])

    def outs(l):
        return (
            (base.at[l], base_h.at[l]), (head.at[l], head_h.at[l]), (weight.at[:, l], weight_h.at[:, l]),
            (res.at[:, l], res_h.at[:, l]), (diag.at[:, l], diag_h.at[:, l]),
        )

    def second(l, carry):
        here = p[l]
        rows = (row_lo[pl.ds(l, 1), :], row_hi[pl.ds(l, 1), :])
        nexts = neighbours(lambda m: p[m], l, rows, columns, l, 4 * L + l)
        faces = (tx[0, l], tx[1, l], ty[0, l], ty[1, l], tz[l], tz[l + 1])
        drops = [t * (here - q) for t, q in zip(faces, nexts)]
        face_sum = sum(faces)
        drop_sum = sum(drops)
        porous = volume_scale * por[l]
        sats = (sw[l], 1.0 - sw[l] - sg[l], sg[l])
        indices = index_sum[l]
        diagonals, residuals, inverses, cs = [], [], [], []
        for a in range(3):
            c = coef[a, l]
            ab = c * face_sum
            net = c * drop_sum
            for t, d, s in zip(faces, drops, coeff_neighbours(coef, coef_row, coef_col, a, l)):
                ab = ab + t * s
                net = net + d * s
            b = 1.0 + compress[a] * here
            stored = porous * sats[a]
            diagonals.append(compress[a] * stored + ab + c * indices)
            residuals.append(b * stored - volume_scale * mass[a, l] + net + c * (indices * here))
            inverses.append(1.0 / (porous * b))
            cs.append(c)
        inverse_total = 1.0 / sum(d * v for d, v in zip(diagonals, inverses))
        weights = [v * inverse_total for v in inverses]
        base[l] = -sum(w * r for w, r in zip(weights, residuals))
        head[l] = sum(w * c for w, c in zip(weights, cs))
        for a in range(3):
            weight[a, l] = weights[a]
            res[a, l] = residuals[a]
        diag[0, l] = diagonals[0]
        diag[1, l] = diagonals[2]
        for c in layer_copies(outs, sems_out, l):
            c.start()
        return carry

    lax.fori_loop(0, L, second, 0)
    wait_copies(saved)
    for l in range(L):
        wait_copies(layer_copies(outs, sems_out, l))


def first_kernel(
    cells, me, got, info, own, perf, base_h, head_h,
    row_lo, row_hi, col_lo, col_hi, pay, mine, well_residual, spread_h, step_h,
    base, head, spread, step, rows, sems,
):
    copies = start_copies(((base_h, base), (head_h, head)), sems)
    lane = iota((1, LANES), 1)
    sums = jnp.sum(got[...], axis=0, keepdims=True)
    total = jnp.where(lane < WELL_DEV, sums, 1.0)
    flow = rolled_row(sums, LANES - 16)
    residual = jnp.where(lane < WELL_DEV, flow - total * own[0:1] - own[1:2], 0.0)
    inverse = jnp.where(lane < WELL_DEV, 1.0 / total, 0.0)
    mine[...] = jnp.concatenate([residual, inverse, jnp.zeros((6, LANES), f32)], axis=0)
    well_residual[...] = residual[:, 0:WELL_DEV]
    cell_row = info[0:1].astype(i32)
    well_row = info[1:2].astype(i32)
    heads = gather_wells(got[...], well_row >> 4, (well_row & 15) + 32)
    spread[...] = scatter(cell_row, info[2:3] * heads).reshape(L, R, C)
    wait_copies(copies)
    step[...] = base[...] + head[...] * spread[...]
    copies = start_copies(((spread, spread_h), (step, step_h)), sems)
    write_faces(step, (row_lo, row_hi, col_lo, col_hi))
    gather_cells(cells, (step,), rows)
    column = to_column(info[0:1]).astype(i32) & (C - 1)
    here = to_row(pick_columns(rows, 0, column))
    parts = parts_by_offset(me[0], well_row, perf[0:1] * here)
    packed = parts[:, TAIL:]
    for n, row in enumerate((residual * inverse, residual, inverse)):
        packed = packed + rolled_row(row, 16 * (n + 1))
    tiles = [parts[:, LANES * t : LANES * (t + 1)] for t in range(5)]
    pay[...] = to_everyone(jnp.concatenate(tiles + [packed, jnp.zeros((2, LANES), f32)], axis=0))
    wait_copies(copies)


def grid_kernel(
    coef_row, coef_col, row_lo, row_hi, col_lo, col_hi,
    coef_h, tx_h, ty_h, tz_h, head_h, weight_h, res_h, spread_h, step_h,
    residual_h, gain_h, ahead_h,
    coef, tx, ty, tz, head, weight, res, spread, step, residual, gain, ahead, sems, sems_out,
):
    copies = start_copies(
        (
            (coef_h, coef), (tx_h, tx), (ty_h, ty), (tz_h, tz), (head_h, head), (weight_h, weight),
            (res_h, res), (spread_h, spread), (step_h, step),
        ),
        sems,
    )
    columns = unpack_columns(col_lo, col_hi)
    wait_copies(copies)

    def outs(l):
        return (
            (residual.at[:, l], residual_h.at[:, l]), (gain.at[:, l], gain_h.at[:, l]),
            (ahead.at[l], ahead_h.at[l]),
        )

    def layer(l, carry):
        nexts = step_neighbours(step, row_lo, row_hi, columns, l)
        faces = (tx[0, l], tx[1, l], ty[0, l], ty[1, l], tz[l], tz[l + 1])
        wells = spread[l]
        mixes = [head[l]] * 6
        for a in range(3):
            w = weight[a, l]
            sides = coeff_neighbours(coef, coef_row, coef_col, a, l)
            mixes = [m + w * s for m, s in zip(mixes, sides)]
            residual[a, l] = res[a, l] - coef[a, l] * wells
        total = step[l]
        for j in range(6):
            g = faces[j] * mixes[j]
            gain[j, l] = g
            total = total + g * nexts[j]
        ahead[l] = total
        for c in layer_copies(outs, sems_out, l):
            c.start()
        return carry

    lax.fori_loop(0, L, layer, 0)
    for l in range(L):
        wait_copies(layer_copies(outs, sems_out, l))


def second_kernel(got, info, ahead_h, head_h, row_lo, row_hi, col_lo, col_hi, step, ahead, head, sems):
    copies = start_copies(((ahead_h, ahead), (head_h, head)), sems)
    cell_row = info[0:1].astype(i32)
    well_row = info[1:2].astype(i32)
    moves = gather_wells(tile_of(got, 5), well_row >> 4, (well_row & 15) + 16)
    wells = scatter(cell_row, info[2:3] * moves).reshape(L, R, C)
    wait_copies(copies)
    step[...] = ahead[...] + head[...] * wells
    write_faces(step, (row_lo, row_hi, col_lo, col_hi))


def wells_kernel(
    cells, me, got, info, perf, step, base_h, gain_h, head_h, table, parts, spread, base, gain, head, rows, sems,
):
    copies = start_copies(((base_h, base), (gain_h, gain), (head_h, head)), sems)
    tail = tile_of(got, 5)
    residuals = pltpu.roll(tail, LANES - 32, 1)
    inverses = pltpu.roll(tail, LANES - 48, 1)
    table[0] = residuals
    table[1] = inverses
    cell_row = info[0:1].astype(i32)
    well_row = info[1:2].astype(i32)
    valid = iota((DEVICES, LANES), 1) < WELL_DEV
    moves = jnp.where(valid, (sum_parts(got) + residuals) * inverses, 0.0)
    values = gather_wells(moves, well_row >> 4, well_row & 15)
    spread[...] = scatter(cell_row, info[2:3] * values).reshape(L, R, C)
    gather_cells(cells, (step,), rows)
    column = to_column(info[0:1]).astype(i32) & (C - 1)
    here = to_row(pick_columns(rows, 0, column))
    flows = parts_by_offset(me[0], well_row, perf[0:1] * here)
    tiles = [flows[:, LANES * t : LANES * (t + 1)] for t in range(6)]
    parts[...] = jnp.concatenate(tiles + [jnp.zeros((2, LANES), f32)], axis=0)
    wait_copies(copies)


def third_kernel(
    cells, info, perf, parts, spread, old, base, gain, head, row_lo, row_hi, col_lo, col_hi,
    out_row_lo, out_row_hi, out_col_lo, out_col_hi, pay, step_h, step, rows, sems,
):
    columns = unpack_columns(col_lo, col_hi)

    def layer(l, carry):
        nexts = step_neighbours(old, row_lo, row_hi, columns, l)
        total = base[l] + head[l] * spread[l]
        for j in range(6):
            total = total + gain[j, l] * nexts[j]
        step[l] = total
        return carry

    lax.fori_loop(0, L, layer, 0)
    copies = start_copies(((step, step_h),), sems)
    write_faces(step, (out_row_lo, out_row_hi, out_col_lo, out_col_hi))
    gather_cells(cells, (step,), rows)
    column = to_column(info[0:1]).astype(i32) & (C - 1)
    here = pick_columns(rows, 0, column)
    well_row = info[1:2].astype(i32)
    slot_column = to_column(info[1:2]).astype(i32) & 15
    pay[...] = to_everyone(parts[...])
    pay[pl.ds(6, DEVICES, stride=8), :] = to_holders(
        well_row >> 4, slot_column, ((0, to_column(perf[0:1]) * here),)
    )
    wait_copies(copies)


def last_grid_kernel(
    coef_row, coef_col, row_lo, row_hi, col_lo, col_hi,
    p_h, por_h, coef_h, tx_h, ty_h, tz_h, head_h, weight_h, diag_h, residual_h, step_h,
    ahead_h, slope_h,
    p, por, coef, tx, ty, tz, head, weight, diag, residual, step, ahead, slope, sems, sems_out,
):
    copies = start_copies(
        (
            (p_h, p), (por_h, por), (coef_h, coef), (tx_h, tx), (ty_h, ty), (tz_h, tz), (head_h, head),
            (weight_h, weight), (diag_h, diag), (residual_h, residual), (step_h, step),
        ),
        sems,
    )
    columns = unpack_columns(col_lo, col_hi)
    wait_copies(copies)

    def outs(l):
        return ((ahead.at[:, l], ahead_h.at[:, l]), (slope.at[:, l], slope_h.at[:, l]))

    def layer(l, carry):
        nexts = step_neighbours(step, row_lo, row_hi, columns, l)
        faces = (tx[0, l], tx[1, l], ty[0, l], ty[1, l], tz[l], tz[l + 1])
        flows = [t * q for t, q in zip(faces, nexts)]
        flow_sum = sum(flows)
        rights, cs = [], []
        for a in range(3):
            c = coef[a, l]
            total = c * flow_sum - residual[a, l]
            for v, s in zip(flows, coeff_neighbours(coef, coef_row, coef_col, a, l)):
                total = total + v * s
            rights.append(total)
            cs.append(c)
        z = sum(weight[a, l] * rights[a] for a in range(3))
        h = head[l]
        porous = volume_scale * por[l]
        inverse_water = 1.0 / (porous * (1.0 + compress[0] * p[l]))
        inverse_gas = 1.0 / (porous * (1.0 + compress[2] * p[l]))
        ahead[0, l] = z
        ahead[1, l] = (rights[0] - diag[0, l] * z) * inverse_water
        ahead[2, l] = (rights[2] - diag[1, l] * z) * inverse_gas
        slope[0, l] = (cs[0] - diag[0, l] * h) * inverse_water
        slope[1, l] = (cs[2] - diag[1, l] * h) * inverse_gas
        for c in layer_copies(outs, sems_out, l):
            c.start()
        return carry

    lax.fori_loop(0, L, layer, 0)
    for l in range(L):
        wait_copies(layer_copies(outs, sems_out, l))


def final_kernel(
    got, info, table, mine, ahead_h, head_h, slope_h, update_h, moved, ahead, head, slope, update, sems, sems_out,
):
    copies = start_copies(((head_h, head), (ahead_h, ahead), (slope_h, slope)), sems)
    flow = jnp.sum(tile_of(got, 6), axis=0, keepdims=True)
    moved[...] = ((flow + mine[0:1]) * mine[1:2])[:, 0:WELL_DEV]
    cell_row = info[0:1].astype(i32)
    well_row = info[1:2].astype(i32)
    valid = iota((DEVICES, LANES), 1) < WELL_DEV
    moves = jnp.where(valid, (sum_parts(got) + table[0]) * table[1], 0.0)
    values = gather_wells(moves, well_row >> 4, well_row & 15)
    wells = scatter(cell_row, info[2:3] * values).reshape(L, R, C)
    wait_copies(copies)

    def outs(l):
        return ((update.at[:, l], update_h.at[:, l]),)

    for l in range(L):
        update[0, l] = ahead[0, l] + head[l] * wells[l]
        update[1, l] = ahead[1, l] + slope[0, l] * wells[l]
        update[2, l] = ahead[2, l] + slope[1, l] * wells[l]
        layer_copies(outs, sems_out, l)[0].start()
    for l in range(L):
        wait_copies(layer_copies(outs, sems_out, l))


def call(kernel, outs, ins, operands, scratch=(), flops=0):
    shapes = tuple(pltpu.VMEM(s, f32) if w is VM else jax.ShapeDtypeStruct(s, f32) for s, w in outs)
    moved = 4 * sum(int(x.size) for x in operands)
    return pl.pallas_call(
        kernel,
        out_shape=shapes,
        in_specs=ins,
        out_specs=tuple(w or VM for _, w in outs),
        scratch_shapes=[pltpu.VMEM(x, f32) if type(x) is tuple else x for x in scratch],
        compiler_params=pltpu.CompilerParams(vmem_limit_bytes=40 * 1024 * 1024),
        cost_estimate=pl.CostEstimate(flops=flops, bytes_accessed=moved, transcendentals=0),
    )(*operands)


FIELD = (L, R, C)
TWO, THREE, SIX, FACED = ((2,) + FIELD, (3,) + FIELD, (6,) + FIELD, (L + 1, R, C))
FACES = (((L, C), VM), ((L, C), VM), ((L, LANES), VM), ((L, LANES), VM))
WIDE_FACES = (((4 * L, C), VM), ((4 * L, C), VM), ((4 * L, LANES), VM), ((4 * L, LANES), VM))
SMALL = (8, LANES)
ROWS = (1, PERFS, C)
PAY = ((8 * DEVICES, LANES), None)
sem = pltpu.SemaphoreType.DMA


def exchange(array):
    return lax.all_to_all(array, AXES, split_axis=0, concat_axis=0, tiled=True)


def exchange_tiles(array):
    return exchange(array.reshape(DEVICES, 8, LANES)).reshape(8 * DEVICES, LANES)


def halo_of(faces):
    row_lo, row_hi, col_lo, col_hi = faces
    got = []
    for axis, low, high in (("gx", row_lo, row_hi), ("gy", col_lo, col_hi)):
        count = lax.axis_size(axis)
        up = [(i, (i + 1) % count) for i in range(count)]
        got.append(lax.ppermute(high, axis, up))
        got.append(lax.ppermute(low, axis, [(j, i) for i, j in up]))
    return got


def local(
    pressure, sat_water, sat_gas, old_mass, perm, porosity,
    perf_well, perf_cell, perf_index, well_pressure, well_rate,
):
    me = (lax.axis_index("gx") * lax.axis_size("gy") + lax.axis_index("gy")).astype(i32).reshape(1)
    *faces, pay, perf, info, own = call(
        start_kernel,
        WIDE_FACES + (((DEVICES, LANES), None), ((8, PERFS), VM), ((8, PERFS), VM), (SMALL, VM)),
        [SM] + [VM] * 5 + [HB] * 4,
        (
            perf_cell, perf_cell.reshape(1, PERFS), perf_well.reshape(1, PERFS), perf_index.reshape(1, PERFS),
            well_pressure.reshape(1, WELL_DEV), well_rate.reshape(1, WELL_DEV), pressure, sat_water, sat_gas, perm,
        ),
        [FIELD, FIELD, FIELD, pltpu.VMEM(TWO, bf16), (3, PERFS, C), sem((4,))],
    )
    halo = halo_of(faces)
    got = exchange(pay)
    coef_row, coef_col, coef, tx, ty, tz, base, head, weight, res, diag = call(
        setup_kernel,
        (
            ((2, 3, L, C), VM), ((3, R, LANES), VM), (THREE, HB), (TWO, HB), (TWO, HB), (FACED, HB),
            (FIELD, HB), (FIELD, HB), (THREE, HB), (THREE, HB), (TWO, HB),
        ),
        [SM] + [VM] * 5 + [HB] * 6,
        (me, info, *halo, pressure, sat_water, sat_gas, porosity, old_mass, perm),
        [
            FIELD, FIELD, FIELD, FIELD, THREE, pltpu.VMEM(THREE, bf16), THREE, TWO, TWO, FACED,
            FIELD, FIELD, THREE, THREE, TWO, FIELD, sem((6,)), sem((4,)), sem((5, L)),
        ],
        flops=400 * L * R * C,
    )
    *faces, pay, mine, well_residual, spread, start = call(
        first_kernel,
        FACES + (PAY, (SMALL, VM), ((1, WELL_DEV), None), (FIELD, HB), (FIELD, HB)),
        [SM, SM] + [VM] * 4 + [HB] * 2,
        (perf_cell, me, got, info, own, perf, base, head),
        [FIELD, FIELD, FIELD, FIELD, ROWS, sem((2,))],
    )
    halo = halo_of(faces)
    got = exchange_tiles(pay)
    fields = (coef, tx, ty, tz, head, weight)
    residual, gain, ahead = call(
        grid_kernel,
        ((THREE, HB), (SIX, HB), (FIELD, HB)),
        [VM] * 6 + [HB] * 9,
        (coef_row, coef_col, *halo, *fields, res, spread, start),
        [
            THREE, TWO, TWO, FACED, FIELD, THREE, THREE, FIELD, FIELD, THREE, SIX, FIELD,
            sem((9,)), sem((3, L)),
        ],
        flops=100 * L * R * C,
    )
    *faces, step = call(
        second_kernel,
        FACES + ((FIELD, VM),),
        [VM] * 2 + [HB] * 2,
        (got, info, ahead, head),
        [FIELD, FIELD, sem((2,))],
    )
    halo = halo_of(faces)
    table, parts, spread, base, gain_near, head_near = call(
        wells_kernel,
        (((2, DEVICES, LANES), None), (SMALL, VM), (FIELD, VM), (FIELD, VM), (SIX, VM), (FIELD, VM)),
        [SM, SM] + [VM] * 4 + [HB] * 3,
        (perf_cell, me, got, info, perf, step, start, gain, head),
        [ROWS, sem((3,))],
    )
    *faces, pay, step = call(
        third_kernel,
        FACES + (PAY, (FIELD, HB)),
        [SM] + [VM] * 12,
        (perf_cell, info, perf, parts, spread, step, base, gain_near, head_near, *halo),
        [FIELD, ROWS, sem((1,))],
    )
    halo = halo_of(faces)
    got = exchange_tiles(pay)
    ahead, slope = call(
        last_grid_kernel,
        ((THREE, HB), (TWO, HB)),
        [VM] * 6 + [HB] * 11,
        (coef_row, coef_col, *halo, pressure, porosity, *fields, diag, residual, step),
        [
            FIELD, FIELD, THREE, TWO, TWO, FACED, FIELD, THREE, TWO, THREE, FIELD, THREE, TWO,
            sem((11,)), sem((2, L)),
        ],
        flops=150 * L * R * C,
    )
    update, moved = call(
        final_kernel,
        ((THREE, HB), ((1, WELL_DEV), None)),
        [VM] * 4 + [HB] * 3,
        (got, info, table, mine, ahead, head, slope),
        [THREE, FIELD, TWO, THREE, sem((3,)), sem((1, L))],
    )
    return residual, well_residual.reshape(WELL_DEV), update, moved.reshape(WELL_DEV)


def solution(mesh):
    return jax.shard_map(
        local,
        mesh=mesh,
        in_specs=(
            P(None, "gx", "gy"),
            P(None, "gx", "gy"),
            P(None, "gx", "gy"),
            P(None, None, "gx", "gy"),
            P(None, None, "gx", "gy"),
            P(None, "gx", "gy"),
            P(("gx", "gy")),
            P(("gx", "gy")),
            P(("gx", "gy")),
            P(("gx", "gy")),
            P(("gx", "gy")),
        ),
        out_specs=(
            P(None, None, "gx", "gy"),
            P(("gx", "gy")),
            P(None, None, "gx", "gy"),
            P(("gx", "gy")),
        ),
        check_vma=False,
    )
```

```python
import jax
import jax.numpy as jnp
from jax import lax
from jax.experimental import pallas as pl
from jax.experimental.pallas import tpu as pltpu
from jax.sharding import PartitionSpec as P

f32 = jnp.float32
bf16 = jnp.bfloat16
i32 = jnp.int32

compress = (0.05, 0.02, 0.2)
viscosity = (0.5, 2.0, 0.1)
volume_scale = 4.0
layer_ratio = 0.1
AXES = ("gx", "gy")
DEVICES = 128
WELL_DEV = 16
REACH = 40
FAR = 64
TAIL = REACH * WELL_DEV
WIDTH = TAIL + 128
LANES = 128
L, R, C = 8, 64, 256
PERFS = 256
VM = pl.BlockSpec(memory_space=pltpu.VMEM)
SM = pl.BlockSpec(memory_space=pltpu.SMEM)
HB = pl.BlockSpec(memory_space=pltpu.HBM)


def iota(shape, dim):
    return lax.broadcasted_iota(i32, shape, dim)


def split3(x):
    high = x.astype(bf16)
    rest = x - high.astype(f32)
    middle = rest.astype(bf16)
    low = (rest - middle.astype(f32)).astype(bf16)
    return high, middle, low


def dot(a, b):
    return jnp.dot(a, b, preferred_element_type=f32)


def to_column(row):
    n = row.shape[1]
    return jnp.sum(jnp.where(iota((n, n), 0) == iota((n, n), 1), row, 0.0), axis=1, keepdims=True)


def to_row(column):
    n = column.shape[0]
    return jnp.sum(jnp.where(iota((n, n), 0) == iota((n, n), 1), column, 0.0), axis=0, keepdims=True)


def coeffs_of(p, sw, sg):
    so = 1.0 - sw - sg
    return tuple(
        s * s * (1.0 / viscosity[a]) * (1.0 + compress[a] * p) for a, s in enumerate((sw, so, sg))
    )


def scatter(cell_row, values):
    match = iota((L * R, PERFS), 0) == (cell_row >> 8)
    column = to_column(cell_row.astype(f32)).astype(i32) & (C - 1)
    spread = (iota((PERFS, C), 1) == column).astype(bf16)
    return sum(
        dot(jnp.where(match, part.astype(f32), 0.0).astype(bf16), spread) for part in split3(values)
    )


def gather_cells(cells, refs, rows):
    def body(block, carry):
        for u in range(8):
            k = block * 8 + u
            cell = cells[0, k]
            layer = cell >> 14
            line = (cell >> 8) & (R - 1)
            for n, ref in enumerate(refs):
                rows[n, pl.ds(k, 1), :] = ref[layer, pl.ds(line, 1), :]
        return carry

    lax.fori_loop(0, PERFS // 8, body, 0)


def pick_columns(rows, n, column):
    return jnp.sum(jnp.where(iota((PERFS, C), 1) == column, rows[n], 0.0), axis=1, keepdims=True)


def gather_wells(table, holder, slot):
    onehot = (iota((DEVICES, PERFS), 0) == holder).astype(bf16)
    wide = sum(dot(part, onehot) for part in split3(table.T))
    return jnp.sum(jnp.where(iota((LANES, PERFS), 0) == slot, wide, 0.0), axis=0, keepdims=True)


def to_holders(holder, slot_column, columns):
    lane = iota((PERFS, LANES), 1)
    group = lane >> 4
    values = jnp.zeros((PERFS, LANES), f32)
    for g, column in columns:
        values = jnp.where(group == g, column, values)
    values = jnp.where((lane & 15) == slot_column, values, 0.0)
    onehot = (iota((DEVICES, PERFS), 0) == holder).astype(bf16)
    return sum(dot(onehot, part) for part in split3(values))


def parts_by_offset(me, well_row, values):
    offset = (me - (well_row >> 4)) & (DEVICES - 1)
    lane = jnp.where(offset == FAR, TAIL, offset * WELL_DEV) + (well_row & 15)
    column = to_column(lane.astype(f32)).astype(i32)
    onehot = (iota((PERFS, WIDTH), 1) == column).astype(bf16)
    high, middle, low = split3(values)
    rows = jnp.concatenate([high.astype(f32), middle.astype(f32), low.astype(f32), jnp.zeros((5, PERFS), f32)], axis=0)
    return jnp.sum(dot(rows.astype(bf16), onehot), axis=0, keepdims=True)


def tile_of(got, t):
    return got[pl.ds(t, DEVICES, stride=8), :]


def sum_parts(got):
    aligned = tile_of(got, 0)
    for t in range(1, TAIL // LANES):
        aligned = aligned + pltpu.roll(tile_of(got, t), DEVICES - 8 * t, 0)
    total = aligned + pltpu.roll(tile_of(got, 5), DEVICES - FAR, 0)
    for u in range(1, 8):
        total = total + pltpu.roll(pltpu.roll(aligned, DEVICES - u, 0), LANES - 16 * u, 1)
    return total


def to_everyone(tile):
    return jnp.broadcast_to(tile[None], (DEVICES, 8, LANES)).reshape(8 * DEVICES, LANES)


def rolled_row(row, shift):
    return pltpu.roll(jnp.broadcast_to(row, (8, LANES)), shift, 1)[0:1]


def shift_rows(x, first, last):
    return (
        jnp.concatenate([first, x[:-1]], axis=0),
        jnp.concatenate([x[1:], last], axis=0),
    )


def shift_columns(x, first, last):
    lane = iota(x.shape, 1)
    return (
        jnp.where(lane == 0, first, pltpu.roll(x, 1, 1)),
        jnp.where(lane == C - 1, last, pltpu.roll(x, C - 1, 1)),
    )


def lane_of(x, index):
    return pltpu.roll(x, (LANES - index) % LANES, 1)[:, 0:1]


def pack_columns(columns, low, high):
    n = low.shape[0]
    turned = jnp.concatenate([columns, jnp.zeros((LANES - R, LANES), f32)], axis=0).T
    low[...] = turned[0:n]
    high[...] = turned[n : 2 * n]


def unpack_columns(low, high):
    n = low.shape[0]
    rows = jnp.concatenate([low[...], high[...], jnp.zeros((LANES - 2 * n, LANES), f32)], axis=0)
    return rows.T[0:R]


def write_faces(step, outs):
    row_lo, row_hi, col_lo, col_hi = outs
    lane = iota((R, LANES), 1)
    columns = jnp.zeros((R, LANES), f32)
    for l in range(L):
        x = step[l]
        row_lo[l : l + 1, :] = x[0:1]
        row_hi[l : l + 1, :] = x[R - 1 : R]
        columns = jnp.where(lane == l, x[:, 0:1], columns)
        columns = jnp.where(lane == L + l, x[:, C - 1 : C], columns)
    pack_columns(columns, col_lo, col_hi)


def start_copies(pairs, sems):
    copies = [pltpu.make_async_copy(a, b, sems.at[n]) for n, (a, b) in enumerate(pairs)]
    for c in copies:
        c.start()
    return copies


def wait_copies(copies):
    for c in copies:
        c.wait()


def layer_copies(pairs, sems, l):
    return [pltpu.make_async_copy(a, b, sems.at[n, l]) for n, (a, b) in enumerate(pairs(l))]


def start_kernel(
    cell_h, well_h, index_h, pressure_h, rate_h, p_h, sw_h, sg_h, perm_h,
    row_lo, row_hi, col_lo, col_hi, pay, perf, info, own,
    cells, cell_in, well_in, index_in, pressure_in, rate_in, p, sw, sg, perm, rows, sems,
):
    copies = start_copies(
        (
            (cell_h, cells), (cell_h, cell_in), (well_h, well_in), (index_h, index_in),
            (pressure_h, pressure_in), (rate_h, rate_in),
            (p_h, p), (sw_h, sw), (sg_h, sg), (perm_h.at[0:2], perm),
        ),
        sems,
    )
    wait_copies(copies[:6])
    cell_row = cell_in[...]
    well_row = well_in[...]
    index_row = index_in[...]
    cell_float = cell_row.astype(f32)
    well_float = well_row.astype(f32)
    info[...] = jnp.concatenate([cell_float, well_float, index_row, jnp.zeros((5, PERFS), f32)], axis=0)
    blank = jnp.zeros((1, LANES - WELL_DEV), f32)
    heads = jnp.concatenate([pressure_in[...], blank], axis=1)
    rates = jnp.concatenate([rate_in[...], blank], axis=1)
    own[...] = jnp.concatenate([heads, rates, jnp.zeros((6, LANES), f32)], axis=0)
    column = to_column(cell_float).astype(i32) & (C - 1)
    slot_column = to_column(well_float).astype(i32) & 15
    index_column = to_column(index_row)
    wait_copies(copies[6:])
    lane = iota((R, LANES), 1)
    columns = jnp.zeros((R, LANES), f32)
    for l in range(L):
        for f, ref in enumerate((p, sw, sg)):
            x = ref[l]
            n = f * L + l
            row_lo[n : n + 1, :] = x[0:1]
            row_hi[n : n + 1, :] = x[R - 1 : R]
            columns = jnp.where(lane == n, x[:, 0:1], columns)
            columns = jnp.where(lane == 4 * L + n, x[:, C - 1 : C], columns)
        n = 3 * L + l
        row_lo[n : n + 1, :] = perm[0, l, 0:16, :].astype(f32)[0:1]
        row_hi[n : n + 1, :] = perm[0, l, R - 16 : R, :].astype(f32)[15:16]
        k = perm[1, l].astype(f32)
        columns = jnp.where(lane == n, k[:, 0:1], columns)
        columns = jnp.where(lane == 4 * L + n, k[:, C - 1 : C], columns)
    pack_columns(columns, col_lo, col_hi)
    gather_cells(cells, (p, sw, sg), rows)
    here = [pick_columns(rows, n, column) for n in range(3)]
    coeffs = coeffs_of(*here)
    total = index_column * (coeffs[0] + coeffs[1] + coeffs[2])
    sums = to_holders(well_row >> 4, slot_column, ((0, total), (1, total * here[0])))
    pay[...] = sums + rolled_row(heads, 32)
    perf[...] = jnp.broadcast_to(to_row(total), (8, PERFS))


def transmit(k, k_next):
    return k * k_next / (k + k_next)


def neighbours(field, l, rows, columns, first, last):
    here = field(l)
    nexts = shift_rows(here, *rows)
    nexts += shift_columns(here, lane_of(columns, first), lane_of(columns, last))
    return nexts + (field(jnp.maximum(l - 1, 0)), field(jnp.minimum(l + 1, L - 1)))


def coeff_neighbours(coef, coef_row, coef_col, a, l):
    rows = (coef_row[0, a, pl.ds(l, 1), :], coef_row[1, a, pl.ds(l, 1), :])
    return neighbours(lambda m: coef[a, m], l, rows, coef_col[a], l, 4 * L + l)


def step_neighbours(step, row_lo, row_hi, columns, l):
    rows = (row_lo[pl.ds(l, 1), :], row_hi[pl.ds(l, 1), :])
    return neighbours(lambda m: step[m], l, rows, columns, l, L + l)


def setup_kernel(
    me, info, row_lo, row_hi, col_lo, col_hi, p_h, sw_h, sg_h, por_h, mass_h, perm_h,
    coef_row, coef_col, coef_h, tx_h, ty_h, tz_h, base_h, head_h, weight_h, res_h, diag_h,
    p, sw, sg, por, mass, perm, coef, tx, ty, tz, base, head, weight, res, diag, index_sum,
    sems, sems_t, sems_out,
):
    copies = start_copies(
        ((p_h, p), (sw_h, sw), (sg_h, sg), (perm_h, perm), (por_h, por), (mass_h, mass)), sems
    )
    index_sum[...] = scatter(info[0:1].astype(i32), info[2:3]).reshape(L, R, C)
    for side, ref in enumerate((row_lo, row_hi)):
        for a, c in enumerate(coeffs_of(ref[0:L], ref[L : 2 * L], ref[2 * L : 3 * L])):
            coef_row[side, a] = c
    columns = unpack_columns(col_lo, col_hi)
    for a, c in enumerate(
        coeffs_of(columns, pltpu.roll(columns, LANES - L, 1), pltpu.roll(columns, LANES - 2 * L, 1))
    ):
        coef_col[a] = c
    lane = iota((R, C), 1)
    gx = me[0] >> 4
    gy = me[0] & 15
    inside = [jnp.where(t, 1.0, 0.0) for t in (gx > 0, gx < 7, gy > 0, gy < 15)]
    wait_copies(copies[:4])

    def first(l, carry):
        for a, c in enumerate(coeffs_of(p[l], sw[l], sg[l])):
            coef[a, l] = c
        k = perm[0, l].astype(f32)
        n = 3 * L + l
        edge = row_lo[pl.ds(n, 1), :] * inside[0]
        before = transmit(k, jnp.concatenate([edge, k[:-1]], axis=0))
        edge = row_hi[pl.ds(n, 1), :] * inside[1]
        tx[0, l] = before
        tx[1, l] = jnp.concatenate([before[1:], transmit(k[R - 1 : R], edge)], axis=0)
        k = perm[1, l].astype(f32)
        edge = lane_of(columns, n) * inside[2]
        before = transmit(k, jnp.where(lane == 0, edge, pltpu.roll(k, 1, 1)))
        edge = lane_of(columns, 4 * L + n) * inside[3]
        ty[0, l] = before
        ty[1, l] = jnp.where(lane == C - 1, transmit(k[:, C - 1 : C], edge), pltpu.roll(before, C - 1, 1))
        k = perm[2, l].astype(f32)
        under = perm[2, jnp.maximum(l - 1, 0)].astype(f32)
        tz[l] = jnp.where(l > 0, layer_ratio, 0.0) * transmit(k, under)
        return carry

    lax.fori_loop(0, L, first, 0)
    tz[L] = jnp.zeros((R, C), f32)
    saved = start_copies(((coef, coef_h), (tx, tx_h), (ty, ty_h), (tz, tz_h)), sems_t)
    wait_copies(copies[4:])

    def outs(l):
        return (
            (base.at[l], base_h.at[l]), (head.at[l], head_h.at[l]), (weight.at[:, l], weight_h.at[:, l]),
            (res.at[:, l], res_h.at[:, l]), (diag.at[:, l], diag_h.at[:, l]),
        )

    def second(l, carry):
        here = p[l]
        rows = (row_lo[pl.ds(l, 1), :], row_hi[pl.ds(l, 1), :])
        nexts = neighbours(lambda m: p[m], l, rows, columns, l, 4 * L + l)
        faces = (tx[0, l], tx[1, l], ty[0, l], ty[1, l], tz[l], tz[l + 1])
        drops = [t * (here - q) for t, q in zip(faces, nexts)]
        face_sum = sum(faces)
        drop_sum = sum(drops)
        porous = volume_scale * por[l]
        sats = (sw[l], 1.0 - sw[l] - sg[l], sg[l])
        indices = index_sum[l]
        diagonals, residuals, inverses, cs = [], [], [], []
        for a in range(3):
            c = coef[a, l]
            ab = c * face_sum
            net = c * drop_sum
            for t, d, s in zip(faces, drops, coeff_neighbours(coef, coef_row, coef_col, a, l)):
                ab = ab + t * s
                net = net + d * s
            b = 1.0 + compress[a] * here
            stored = porous * sats[a]
            diagonals.append(compress[a] * stored + ab + c * indices)
            residuals.append(b * stored - volume_scale * mass[a, l] + net + c * (indices * here))
            inverses.append(1.0 / (porous * b))
            cs.append(c)
        inverse_total = 1.0 / sum(d * v for d, v in zip(diagonals, inverses))
        weights = [v * inverse_total for v in inverses]
        base[l] = -sum(w * r for w, r in zip(weights, residuals))
        head[l] = sum(w * c for w, c in zip(weights, cs))
        for a in range(3):
            weight[a, l] = weights[a]
            res[a, l] = residuals[a]
        diag[0, l] = diagonals[0]
        diag[1, l] = diagonals[2]
        for c in layer_copies(outs, sems_out, l):
            c.start()
        return carry

    lax.fori_loop(0, L, second, 0)
    wait_copies(saved)
    for l in range(L):
        wait_copies(layer_copies(outs, sems_out, l))


def first_kernel(
    cells, me, got, info, own, perf, base_h, head_h,
    row_lo, row_hi, col_lo, col_hi, pay, mine, well_residual, spread_h, step_h,
    base, head, spread, step, rows, sems,
):
    copies = start_copies(((base_h, base), (head_h, head)), sems)
    lane = iota((1, LANES), 1)
    sums = jnp.sum(got[...], axis=0, keepdims=True)
    total = jnp.where(lane < WELL_DEV, sums, 1.0)
    flow = rolled_row(sums, LANES - 16)
    residual = jnp.where(lane < WELL_DEV, flow - total * own[0:1] - own[1:2], 0.0)
    inverse = jnp.where(lane < WELL_DEV, 1.0 / total, 0.0)
    mine[...] = jnp.concatenate([residual, inverse, jnp.zeros((6, LANES), f32)], axis=0)
    well_residual[...] = residual[:, 0:WELL_DEV]
    cell_row = info[0:1].astype(i32)
    well_row = info[1:2].astype(i32)
    heads = gather_wells(got[...], well_row >> 4, (well_row & 15) + 32)
    spread[...] = scatter(cell_row, info[2:3] * heads).reshape(L, R, C)
    wait_copies(copies)
    step[...] = base[...] + head[...] * spread[...]
    copies = start_copies(((spread, spread_h), (step, step_h)), sems)
    write_faces(step, (row_lo, row_hi, col_lo, col_hi))
    gather_cells(cells, (step,), rows)
    column = to_column(info[0:1]).astype(i32) & (C - 1)
    here = to_row(pick_columns(rows, 0, column))
    parts = parts_by_offset(me[0], well_row, perf[0:1] * here)
    packed = parts[:, TAIL:]
    for n, row in enumerate((residual * inverse, residual, inverse)):
        packed = packed + rolled_row(row, 16 * (n + 1))
    tiles = [parts[:, LANES * t : LANES * (t + 1)] for t in range(5)]
    pay[...] = to_everyone(jnp.concatenate(tiles + [packed, jnp.zeros((2, LANES), f32)], axis=0))
    wait_copies(copies)


def grid_kernel(
    coef_row, coef_col, row_lo, row_hi, col_lo, col_hi,
    coef_h, tx_h, ty_h, tz_h, head_h, weight_h, res_h, spread_h, step_h,
    residual_h, gain_h, ahead_h,
    coef, tx, ty, tz, head, weight, res, spread, step, residual, gain, ahead, sems, sems_out,
):
    copies = start_copies(
        (
            (coef_h, coef), (tx_h, tx), (ty_h, ty), (tz_h, tz), (head_h, head), (weight_h, weight),
            (res_h, res), (spread_h, spread), (step_h, step),
        ),
        sems,
    )
    columns = unpack_columns(col_lo, col_hi)
    wait_copies(copies)

    def outs(l):
        return (
            (residual.at[:, l], residual_h.at[:, l]), (gain.at[:, l], gain_h.at[:, l]),
            (ahead.at[l], ahead_h.at[l]),
        )

    def layer(l, carry):
        nexts = step_neighbours(step, row_lo, row_hi, columns, l)
        faces = (tx[0, l], tx[1, l], ty[0, l], ty[1, l], tz[l], tz[l + 1])
        wells = spread[l]
        mixes = [head[l]] * 6
        for a in range(3):
            w = weight[a, l]
            sides = coeff_neighbours(coef, coef_row, coef_col, a, l)
            mixes = [m + w * s for m, s in zip(mixes, sides)]
            residual[a, l] = res[a, l] - coef[a, l] * wells
        total = step[l]
        for j in range(6):
            g = faces[j] * mixes[j]
            gain[j, l] = g
            total = total + g * nexts[j]
        ahead[l] = total
        for c in layer_copies(outs, sems_out, l):
            c.start()
        return carry

    lax.fori_loop(0, L, layer, 0)
    for l in range(L):
        wait_copies(layer_copies(outs, sems_out, l))


def second_kernel(got, info, ahead_h, head_h, row_lo, row_hi, col_lo, col_hi, step, ahead, head, sems):
    copies = start_copies(((ahead_h, ahead), (head_h, head)), sems)
    cell_row = info[0:1].astype(i32)
    well_row = info[1:2].astype(i32)
    moves = gather_wells(tile_of(got, 5), well_row >> 4, (well_row & 15) + 16)
    wells = scatter(cell_row, info[2:3] * moves).reshape(L, R, C)
    wait_copies(copies)
    step[...] = ahead[...] + head[...] * wells
    write_faces(step, (row_lo, row_hi, col_lo, col_hi))


def wells_kernel(
    cells, me, got, info, perf, step, base_h, gain_h, head_h, table, parts, spread, base, gain, head, rows, sems,
):
    copies = start_copies(((base_h, base), (gain_h, gain), (head_h, head)), sems)
    tail = tile_of(got, 5)
    residuals = pltpu.roll(tail, LANES - 32, 1)
    inverses = pltpu.roll(tail, LANES - 48, 1)
    table[0] = residuals
    table[1] = inverses
    cell_row = info[0:1].astype(i32)
    well_row = info[1:2].astype(i32)
    valid = iota((DEVICES, LANES), 1) < WELL_DEV
    moves = jnp.where(valid, (sum_parts(got) + residuals) * inverses, 0.0)
    values = gather_wells(moves, well_row >> 4, well_row & 15)
    spread[...] = scatter(cell_row, info[2:3] * values).reshape(L, R, C)
    gather_cells(cells, (step,), rows)
    column = to_column(info[0:1]).astype(i32) & (C - 1)
    here = to_row(pick_columns(rows, 0, column))
    flows = parts_by_offset(me[0], well_row, perf[0:1] * here)
    tiles = [flows[:, LANES * t : LANES * (t + 1)] for t in range(6)]
    parts[...] = jnp.concatenate(tiles + [jnp.zeros((2, LANES), f32)], axis=0)
    wait_copies(copies)


def third_kernel(
    cells, info, perf, parts, spread, old, base, gain, head, row_lo, row_hi, col_lo, col_hi,
    out_row_lo, out_row_hi, out_col_lo, out_col_hi, pay, step_h, step, rows, sems,
):
    columns = unpack_columns(col_lo, col_hi)

    def layer(l, carry):
        nexts = step_neighbours(old, row_lo, row_hi, columns, l)
        total = base[l] + head[l] * spread[l]
        for j in range(6):
            total = total + gain[j, l] * nexts[j]
        step[l] = total
        return carry

    lax.fori_loop(0, L, layer, 0)
    copies = start_copies(((step, step_h),), sems)
    write_faces(step, (out_row_lo, out_row_hi, out_col_lo, out_col_hi))
    gather_cells(cells, (step,), rows)
    column = to_column(info[0:1]).astype(i32) & (C - 1)
    here = pick_columns(rows, 0, column)
    well_row = info[1:2].astype(i32)
    slot_column = to_column(info[1:2]).astype(i32) & 15
    pay[...] = to_everyone(parts[...])
    pay[pl.ds(6, DEVICES, stride=8), :] = to_holders(
        well_row >> 4, slot_column, ((0, to_column(perf[0:1]) * here),)
    )
    wait_copies(copies)


def last_grid_kernel(
    coef_row, coef_col, row_lo, row_hi, col_lo, col_hi,
    p_h, por_h, coef_h, tx_h, ty_h, tz_h, head_h, weight_h, diag_h, residual_h, step_h,
    ahead_h, slope_h,
    p, por, coef, tx, ty, tz, head, weight, diag, residual, step, ahead, slope, sems, sems_out,
):
    copies = start_copies(
        (
            (p_h, p), (por_h, por), (coef_h, coef), (tx_h, tx), (ty_h, ty), (tz_h, tz), (head_h, head),
            (weight_h, weight), (diag_h, diag), (residual_h, residual), (step_h, step),
        ),
        sems,
    )
    columns = unpack_columns(col_lo, col_hi)
    wait_copies(copies)

    def outs(l):
        return ((ahead.at[:, l], ahead_h.at[:, l]), (slope.at[:, l], slope_h.at[:, l]))

    def layer(l, carry):
        nexts = step_neighbours(step, row_lo, row_hi, columns, l)
        faces = (tx[0, l], tx[1, l], ty[0, l], ty[1, l], tz[l], tz[l + 1])
        flows = [t * q for t, q in zip(faces, nexts)]
        flow_sum = sum(flows)
        rights, cs = [], []
        for a in range(3):
            c = coef[a, l]
            total = c * flow_sum - residual[a, l]
            for v, s in zip(flows, coeff_neighbours(coef, coef_row, coef_col, a, l)):
                total = total + v * s
            rights.append(total)
            cs.append(c)
        z = sum(weight[a, l] * rights[a] for a in range(3))
        h = head[l]
        porous = volume_scale * por[l]
        inverse_water = 1.0 / (porous * (1.0 + compress[0] * p[l]))
        inverse_gas = 1.0 / (porous * (1.0 + compress[2] * p[l]))
        ahead[0, l] = z
        ahead[1, l] = (rights[0] - diag[0, l] * z) * inverse_water
        ahead[2, l] = (rights[2] - diag[1, l] * z) * inverse_gas
        slope[0, l] = (cs[0] - diag[0, l] * h) * inverse_water
        slope[1, l] = (cs[2] - diag[1, l] * h) * inverse_gas
        for c in layer_copies(outs, sems_out, l):
            c.start()
        return carry

    lax.fori_loop(0, L, layer, 0)
    for l in range(L):
        wait_copies(layer_copies(outs, sems_out, l))


def final_kernel(
    got, info, table, mine, ahead_h, head_h, slope_h, update_h, moved, ahead, head, slope, update, sems, sems_out,
):
    copies = start_copies(((head_h, head), (ahead_h, ahead), (slope_h, slope)), sems)
    flow = jnp.sum(tile_of(got, 6), axis=0, keepdims=True)
    moved[...] = ((flow + mine[0:1]) * mine[1:2])[:, 0:WELL_DEV]
    cell_row = info[0:1].astype(i32)
    well_row = info[1:2].astype(i32)
    valid = iota((DEVICES, LANES), 1) < WELL_DEV
    moves = jnp.where(valid, (sum_parts(got) + table[0]) * table[1], 0.0)
    values = gather_wells(moves, well_row >> 4, well_row & 15)
    wells = scatter(cell_row, info[2:3] * values).reshape(L, R, C)
    wait_copies(copies)

    def outs(l):
        return ((update.at[:, l], update_h.at[:, l]),)

    for l in range(L):
        update[0, l] = ahead[0, l] + head[l] * wells[l]
        update[1, l] = ahead[1, l] + slope[0, l] * wells[l]
        update[2, l] = ahead[2, l] + slope[1, l] * wells[l]
        layer_copies(outs, sems_out, l)[0].start()
    for l in range(L):
        wait_copies(layer_copies(outs, sems_out, l))


def call(kernel, outs, ins, operands, scratch=(), flops=0):
    shapes = tuple(
        pltpu.VMEM(s, f32) if w is VM else pltpu.HBM(s, f32) if w is HB else jax.ShapeDtypeStruct(s, f32)
        for s, w in outs
    )
    moved = 4 * sum(int(x.size) for x in operands)
    operands = [
        pltpu.with_memory_space_constraint(x, pltpu.HBM) if w is HB else x for x, w in zip(operands, ins)
    ]
    return pl.pallas_call(
        kernel,
        out_shape=shapes,
        in_specs=ins,
        out_specs=tuple(w or VM for _, w in outs),
        scratch_shapes=[pltpu.VMEM(x, f32) if type(x) is tuple else x for x in scratch],
        compiler_params=pltpu.CompilerParams(vmem_limit_bytes=40 * 1024 * 1024),
        cost_estimate=pl.CostEstimate(flops=flops, bytes_accessed=moved, transcendentals=0),
    )(*operands)


FIELD = (L, R, C)
TWO, THREE, SIX, FACED = ((2,) + FIELD, (3,) + FIELD, (6,) + FIELD, (L + 1, R, C))
FACES = (((L, C), VM), ((L, C), VM), ((L, LANES), VM), ((L, LANES), VM))
WIDE_FACES = (((4 * L, C), VM), ((4 * L, C), VM), ((4 * L, LANES), VM), ((4 * L, LANES), VM))
SMALL = (8, LANES)
ROWS = (1, PERFS, C)
PAY = ((8 * DEVICES, LANES), None)
sem = pltpu.SemaphoreType.DMA


def exchange(array):
    return lax.all_to_all(array, AXES, split_axis=0, concat_axis=0, tiled=True)


def exchange_tiles(array):
    return exchange(array.reshape(DEVICES, 8, LANES)).reshape(8 * DEVICES, LANES)


def halo_of(faces):
    row_lo, row_hi, col_lo, col_hi = faces
    got = []
    for axis, low, high in (("gx", row_lo, row_hi), ("gy", col_lo, col_hi)):
        count = lax.axis_size(axis)
        up = [(i, (i + 1) % count) for i in range(count)]
        got.append(lax.ppermute(high, axis, up))
        got.append(lax.ppermute(low, axis, [(j, i) for i, j in up]))
    return got


def local(
    pressure, sat_water, sat_gas, old_mass, perm, porosity,
    perf_well, perf_cell, perf_index, well_pressure, well_rate,
):
    me = (lax.axis_index("gx") * lax.axis_size("gy") + lax.axis_index("gy")).astype(i32).reshape(1)
    cells = perf_cell.reshape(1, PERFS)
    *faces, pay, perf, info, own = call(
        start_kernel,
        WIDE_FACES + (((DEVICES, LANES), None), ((8, PERFS), VM), ((8, PERFS), VM), (SMALL, VM)),
        [HB] * 9,
        (
            cells, perf_well.reshape(1, PERFS), perf_index.reshape(1, PERFS),
            well_pressure.reshape(1, WELL_DEV), well_rate.reshape(1, WELL_DEV), pressure, sat_water, sat_gas, perm,
        ),
        [
            pltpu.SMEM((1, PERFS), i32), pltpu.VMEM((1, PERFS), i32), pltpu.VMEM((1, PERFS), i32), (1, PERFS),
            (1, WELL_DEV), (1, WELL_DEV), FIELD, FIELD, FIELD, pltpu.VMEM(TWO, bf16), (3, PERFS, C), sem((10,)),
        ],
    )
    halo = halo_of(faces)
    got = exchange(pay)
    coef_row, coef_col, coef, tx, ty, tz, base, head, weight, res, diag = call(
        setup_kernel,
        (
            ((2, 3, L, C), VM), ((3, R, LANES), VM), (THREE, HB), (TWO, HB), (TWO, HB), (FACED, HB),
            (FIELD, HB), (FIELD, HB), (THREE, HB), (THREE, HB), (TWO, HB),
        ),
        [SM] + [VM] * 5 + [HB] * 6,
        (me, info, *halo, pressure, sat_water, sat_gas, porosity, old_mass, perm),
        [
            FIELD, FIELD, FIELD, FIELD, THREE, pltpu.VMEM(THREE, bf16), THREE, TWO, TWO, FACED,
            FIELD, FIELD, THREE, THREE, TWO, FIELD, sem((6,)), sem((4,)), sem((5, L)),
        ],
        flops=400 * L * R * C,
    )
    *faces, pay, mine, well_residual, spread, start = call(
        first_kernel,
        FACES + (PAY, (SMALL, VM), ((1, WELL_DEV), None), (FIELD, HB), (FIELD, HB)),
        [SM, SM] + [VM] * 4 + [HB] * 2,
        (cells, me, got, info, own, perf, base, head),
        [FIELD, FIELD, FIELD, FIELD, ROWS, sem((2,))],
    )
    halo = halo_of(faces)
    got = exchange_tiles(pay)
    fields = (coef, tx, ty, tz, head, weight)
    residual, gain, ahead = call(
        grid_kernel,
        ((THREE, HB), (SIX, HB), (FIELD, HB)),
        [VM] * 6 + [HB] * 9,
        (coef_row, coef_col, *halo, *fields, res, spread, start),
        [
            THREE, TWO, TWO, FACED, FIELD, THREE, THREE, FIELD, FIELD, THREE, SIX, FIELD,
            sem((9,)), sem((3, L)),
        ],
        flops=100 * L * R * C,
    )
    *faces, step = call(
        second_kernel,
        FACES + ((FIELD, VM),),
        [VM] * 2 + [HB] * 2,
        (got, info, ahead, head),
        [FIELD, FIELD, sem((2,))],
    )
    halo = halo_of(faces)
    table, parts, spread, base, gain_near, head_near = call(
        wells_kernel,
        (((2, DEVICES, LANES), None), (SMALL, VM), (FIELD, VM), (FIELD, VM), (SIX, VM), (FIELD, VM)),
        [SM, SM] + [VM] * 4 + [HB] * 3,
        (cells, me, got, info, perf, step, start, gain, head),
        [ROWS, sem((3,))],
    )
    *faces, pay, step = call(
        third_kernel,
        FACES + (PAY, (FIELD, HB)),
        [SM] + [VM] * 12,
        (cells, info, perf, parts, spread, step, base, gain_near, head_near, *halo),
        [FIELD, ROWS, sem((1,))],
    )
    halo = halo_of(faces)
    got = exchange_tiles(pay)
    ahead, slope = call(
        last_grid_kernel,
        ((THREE, HB), (TWO, HB)),
        [VM] * 6 + [HB] * 11,
        (coef_row, coef_col, *halo, pressure, porosity, *fields, diag, residual, step),
        [
            FIELD, FIELD, THREE, TWO, TWO, FACED, FIELD, THREE, TWO, THREE, FIELD, THREE, TWO,
            sem((11,)), sem((2, L)),
        ],
        flops=150 * L * R * C,
    )
    update, moved = call(
        final_kernel,
        ((THREE, HB), ((1, WELL_DEV), None)),
        [VM] * 4 + [HB] * 3,
        (got, info, table, mine, ahead, head, slope),
        [THREE, FIELD, TWO, THREE, sem((3,)), sem((1, L))],
    )
    return residual, well_residual.reshape(WELL_DEV), update, moved.reshape(WELL_DEV)


def solution(mesh):
    return jax.shard_map(
        local,
        mesh=mesh,
        in_specs=(
            P(None, "gx", "gy"),
            P(None, "gx", "gy"),
            P(None, "gx", "gy"),
            P(None, None, "gx", "gy"),
            P(None, None, "gx", "gy"),
            P(None, "gx", "gy"),
            P(("gx", "gy")),
            P(("gx", "gy")),
            P(("gx", "gy")),
            P(("gx", "gy")),
            P(("gx", "gy")),
        ),
        out_specs=(
            P(None, None, "gx", "gy"),
            P(("gx", "gy")),
            P(None, None, "gx", "gy"),
            P(("gx", "gy")),
        ),
        check_vma=False,
    )
```

```python
import jax
import jax.numpy as jnp
from jax import lax
from jax.experimental import pallas as pl
from jax.experimental.pallas import tpu as pltpu
from jax.sharding import PartitionSpec as P

f32 = jnp.float32
bf16 = jnp.bfloat16
i32 = jnp.int32

compress = (0.05, 0.02, 0.2)
viscosity = (0.5, 2.0, 0.1)
volume_scale = 4.0
layer_ratio = 0.1
AXES = ("gx", "gy")
DEVICES = 128
WELL_DEV = 16
REACH = 40
FAR = 64
TAIL = REACH * WELL_DEV
WIDTH = TAIL + 128
LANES = 128
L, R, C = 8, 64, 256
PERFS = 256
VM = pl.BlockSpec(memory_space=pltpu.VMEM)
SM = pl.BlockSpec(memory_space=pltpu.SMEM)
HB = pl.BlockSpec(memory_space=pltpu.HBM)


def iota(shape, dim):
    return lax.broadcasted_iota(i32, shape, dim)


def split3(x):
    high = x.astype(bf16)
    rest = x - high.astype(f32)
    middle = rest.astype(bf16)
    low = (rest - middle.astype(f32)).astype(bf16)
    return high, middle, low


def dot(a, b):
    return jnp.dot(a, b, preferred_element_type=f32)


def to_column(row):
    n = row.shape[1]
    return jnp.sum(jnp.where(iota((n, n), 0) == iota((n, n), 1), row, 0.0), axis=1, keepdims=True)


def to_row(column):
    n = column.shape[0]
    return jnp.sum(jnp.where(iota((n, n), 0) == iota((n, n), 1), column, 0.0), axis=0, keepdims=True)


def coeffs_of(p, sw, sg):
    so = 1.0 - sw - sg
    return tuple(
        s * s * (1.0 / viscosity[a]) * (1.0 + compress[a] * p) for a, s in enumerate((sw, so, sg))
    )


def scatter(cell_row, values):
    match = iota((L * R, PERFS), 0) == (cell_row >> 8)
    column = to_column(cell_row.astype(f32)).astype(i32) & (C - 1)
    spread = (iota((PERFS, C), 1) == column).astype(bf16)
    return sum(
        dot(jnp.where(match, part.astype(f32), 0.0).astype(bf16), spread) for part in split3(values)
    )


def gather_cells(cells, refs, rows):
    def body(block, carry):
        for u in range(8):
            k = block * 8 + u
            cell = cells[0, k]
            layer = cell >> 14
            line = (cell >> 8) & (R - 1)
            for n, ref in enumerate(refs):
                rows[n, pl.ds(k, 1), :] = ref[layer, pl.ds(line, 1), :]
        return carry

    lax.fori_loop(0, PERFS // 8, body, 0)


def pick_columns(rows, n, column):
    return jnp.sum(jnp.where(iota((PERFS, C), 1) == column, rows[n], 0.0), axis=1, keepdims=True)


def gather_wells(table, holder, slot):
    onehot = (iota((DEVICES, PERFS), 0) == holder).astype(bf16)
    wide = sum(dot(part, onehot) for part in split3(table.T))
    return jnp.sum(jnp.where(iota((LANES, PERFS), 0) == slot, wide, 0.0), axis=0, keepdims=True)


def to_holders(holder, slot_column, columns):
    lane = iota((PERFS, LANES), 1)
    group = lane >> 4
    values = jnp.zeros((PERFS, LANES), f32)
    for g, column in columns:
        values = jnp.where(group == g, column, values)
    values = jnp.where((lane & 15) == slot_column, values, 0.0)
    onehot = (iota((DEVICES, PERFS), 0) == holder).astype(bf16)
    return sum(dot(onehot, part) for part in split3(values))


def parts_by_offset(me, well_row, values):
    offset = (me - (well_row >> 4)) & (DEVICES - 1)
    lane = jnp.where(offset == FAR, TAIL, offset * WELL_DEV) + (well_row & 15)
    column = to_column(lane.astype(f32)).astype(i32)
    onehot = (iota((PERFS, WIDTH), 1) == column).astype(bf16)
    high, middle, low = split3(values)
    rows = jnp.concatenate([high.astype(f32), middle.astype(f32), low.astype(f32), jnp.zeros((5, PERFS), f32)], axis=0)
    return jnp.sum(dot(rows.astype(bf16), onehot), axis=0, keepdims=True)


def tile_of(got, t):
    return got[pl.ds(t, DEVICES, stride=8), :]


def sum_parts(got):
    aligned = tile_of(got, 0)
    for t in range(1, TAIL // LANES):
        aligned = aligned + pltpu.roll(tile_of(got, t), DEVICES - 8 * t, 0)
    total = aligned + pltpu.roll(tile_of(got, 5), DEVICES - FAR, 0)
    for u in range(1, 8):
        total = total + pltpu.roll(pltpu.roll(aligned, DEVICES - u, 0), LANES - 16 * u, 1)
    return total


def to_everyone(tile):
    return jnp.broadcast_to(tile[None], (DEVICES, 8, LANES)).reshape(8 * DEVICES, LANES)


def rolled_row(row, shift):
    return pltpu.roll(jnp.broadcast_to(row, (8, LANES)), shift, 1)[0:1]


def shift_rows(x, first, last):
    return (
        jnp.concatenate([first, x[:-1]], axis=0),
        jnp.concatenate([x[1:], last], axis=0),
    )


def shift_columns(x, first, last):
    lane = iota(x.shape, 1)
    return (
        jnp.where(lane == 0, first, pltpu.roll(x, 1, 1)),
        jnp.where(lane == C - 1, last, pltpu.roll(x, C - 1, 1)),
    )


def lane_of(x, index):
    return pltpu.roll(x, (LANES - index) % LANES, 1)[:, 0:1]


def pack_columns(columns, low, high):
    n = low.shape[0]
    turned = jnp.concatenate([columns, jnp.zeros((LANES - R, LANES), f32)], axis=0).T
    low[...] = turned[0:n]
    high[...] = turned[n : 2 * n]


def unpack_columns(low, high):
    n = low.shape[0]
    rows = jnp.concatenate([low[...], high[...], jnp.zeros((LANES - 2 * n, LANES), f32)], axis=0)
    return rows.T[0:R]


def write_faces(step, outs):
    row_lo, row_hi, col_lo, col_hi = outs
    lane = iota((R, LANES), 1)
    columns = jnp.zeros((R, LANES), f32)
    for l in range(L):
        x = step[l]
        row_lo[l : l + 1, :] = x[0:1]
        row_hi[l : l + 1, :] = x[R - 1 : R]
        columns = jnp.where(lane == l, x[:, 0:1], columns)
        columns = jnp.where(lane == L + l, x[:, C - 1 : C], columns)
    pack_columns(columns, col_lo, col_hi)


def start_copies(pairs, sems):
    copies = [pltpu.make_async_copy(a, b, sems.at[n]) for n, (a, b) in enumerate(pairs)]
    for c in copies:
        c.start()
    return copies


def wait_copies(copies):
    for c in copies:
        c.wait()


def layer_copies(pairs, sems, l):
    return [pltpu.make_async_copy(a, b, sems.at[n, l]) for n, (a, b) in enumerate(pairs(l))]


def faces_kernel(
    p_h, sw_h, sg_h, perm_h, row_lo, row_hi, col_lo, col_hi, p, sw, sg, perm, sems,
):
    copies = start_copies(((perm_h.at[0:2], perm), (p_h, p), (sw_h, sw), (sg_h, sg)), sems)
    lane = iota((R, LANES), 1)
    columns = jnp.zeros((R, LANES), f32)
    wait_copies(copies[:1])
    for l in range(L):
        n = 3 * L + l
        row_lo[n : n + 1, :] = perm[0, l, 0:16, :].astype(f32)[0:1]
        row_hi[n : n + 1, :] = perm[0, l, R - 16 : R, :].astype(f32)[15:16]
        k = perm[1, l].astype(f32)
        columns = jnp.where(lane == n, k[:, 0:1], columns)
        columns = jnp.where(lane == 4 * L + n, k[:, C - 1 : C], columns)
    wait_copies(copies[1:])
    for l in range(L):
        for f, ref in enumerate((p, sw, sg)):
            x = ref[l]
            n = f * L + l
            row_lo[n : n + 1, :] = x[0:1]
            row_hi[n : n + 1, :] = x[R - 1 : R]
            columns = jnp.where(lane == n, x[:, 0:1], columns)
            columns = jnp.where(lane == 4 * L + n, x[:, C - 1 : C], columns)
    pack_columns(columns, col_lo, col_hi)


def start_kernel(
    cell_h, well_h, index_h, pressure_h, rate_h, p, sw, sg,
    pay, perf, info, own,
    cells, cell_in, well_in, index_in, pressure_in, rate_in, rows, sems,
):
    copies = start_copies(
        (
            (cell_h, cells), (cell_h, cell_in), (well_h, well_in), (index_h, index_in),
            (pressure_h, pressure_in), (rate_h, rate_in),
        ),
        sems,
    )
    wait_copies(copies)
    cell_row = cell_in[...]
    well_row = well_in[...]
    index_row = index_in[...]
    cell_float = cell_row.astype(f32)
    well_float = well_row.astype(f32)
    info[...] = jnp.concatenate([cell_float, well_float, index_row, jnp.zeros((5, PERFS), f32)], axis=0)
    blank = jnp.zeros((1, LANES - WELL_DEV), f32)
    heads = jnp.concatenate([pressure_in[...], blank], axis=1)
    rates = jnp.concatenate([rate_in[...], blank], axis=1)
    own[...] = jnp.concatenate([heads, rates, jnp.zeros((6, LANES), f32)], axis=0)
    column = to_column(cell_float).astype(i32) & (C - 1)
    slot_column = to_column(well_float).astype(i32) & 15
    index_column = to_column(index_row)
    gather_cells(cells, (p, sw, sg), rows)
    here = [pick_columns(rows, n, column) for n in range(3)]
    coeffs = coeffs_of(*here)
    total = index_column * (coeffs[0] + coeffs[1] + coeffs[2])
    sums = to_holders(well_row >> 4, slot_column, ((0, total), (1, total * here[0])))
    pay[...] = sums + rolled_row(heads, 32)
    perf[...] = jnp.broadcast_to(to_row(total), (8, PERFS))


def transmit(k, k_next):
    return k * k_next / (k + k_next)


def neighbours(field, l, rows, columns, first, last):
    here = field(l)
    nexts = shift_rows(here, *rows)
    nexts += shift_columns(here, lane_of(columns, first), lane_of(columns, last))
    return nexts + (field(jnp.maximum(l - 1, 0)), field(jnp.minimum(l + 1, L - 1)))


def coeff_neighbours(coef, coef_row, coef_col, a, l):
    rows = (coef_row[0, a, pl.ds(l, 1), :], coef_row[1, a, pl.ds(l, 1), :])
    return neighbours(lambda m: coef[a, m], l, rows, coef_col[a], l, 4 * L + l)


def step_neighbours(step, row_lo, row_hi, columns, l):
    rows = (row_lo[pl.ds(l, 1), :], row_hi[pl.ds(l, 1), :])
    return neighbours(lambda m: step[m], l, rows, columns, l, L + l)


def setup_kernel(
    me, info, row_lo, row_hi, col_lo, col_hi, p, sw, sg, por_h, mass_h, perm_h,
    coef_row, coef_col, base, head, coef_h, tx_h, ty_h, tz_h, weight_h, res_h, diag_h,
    por, mass, perm, coef, tx, ty, tz, weight, res, diag, index_sum,
    sems, sems_t, sems_out,
):
    copies = start_copies(((perm_h, perm), (por_h, por), (mass_h, mass)), sems)
    index_sum[...] = scatter(info[0:1].astype(i32), info[2:3]).reshape(L, R, C)
    for side, ref in enumerate((row_lo, row_hi)):
        for a, c in enumerate(coeffs_of(ref[0:L], ref[L : 2 * L], ref[2 * L : 3 * L])):
            coef_row[side, a] = c
    columns = unpack_columns(col_lo, col_hi)
    for a, c in enumerate(
        coeffs_of(columns, pltpu.roll(columns, LANES - L, 1), pltpu.roll(columns, LANES - 2 * L, 1))
    ):
        coef_col[a] = c
    lane = iota((R, C), 1)
    gx = me[0] >> 4
    gy = me[0] & 15
    inside = [jnp.where(t, 1.0, 0.0) for t in (gx > 0, gx < 7, gy > 0, gy < 15)]
    wait_copies(copies[:1])

    def first(l, carry):
        for a, c in enumerate(coeffs_of(p[l], sw[l], sg[l])):
            coef[a, l] = c
        k = perm[0, l].astype(f32)
        n = 3 * L + l
        edge = row_lo[pl.ds(n, 1), :] * inside[0]
        before = transmit(k, jnp.concatenate([edge, k[:-1]], axis=0))
        edge = row_hi[pl.ds(n, 1), :] * inside[1]
        tx[0, l] = before
        tx[1, l] = jnp.concatenate([before[1:], transmit(k[R - 1 : R], edge)], axis=0)
        k = perm[1, l].astype(f32)
        edge = lane_of(columns, n) * inside[2]
        before = transmit(k, jnp.where(lane == 0, edge, pltpu.roll(k, 1, 1)))
        edge = lane_of(columns, 4 * L + n) * inside[3]
        ty[0, l] = before
        ty[1, l] = jnp.where(lane == C - 1, transmit(k[:, C - 1 : C], edge), pltpu.roll(before, C - 1, 1))
        k = perm[2, l].astype(f32)
        under = perm[2, jnp.maximum(l - 1, 0)].astype(f32)
        tz[l] = jnp.where(l > 0, layer_ratio, 0.0) * transmit(k, under)
        return carry

    lax.fori_loop(0, L, first, 0)
    tz[L] = jnp.zeros((R, C), f32)
    saved = start_copies(((coef, coef_h), (tx, tx_h), (ty, ty_h), (tz, tz_h)), sems_t)
    wait_copies(copies[1:])

    def outs(l):
        return (
            (weight.at[:, l], weight_h.at[:, l]),
            (res.at[:, l], res_h.at[:, l]), (diag.at[:, l], diag_h.at[:, l]),
        )

    def second(l, carry):
        here = p[l]
        rows = (row_lo[pl.ds(l, 1), :], row_hi[pl.ds(l, 1), :])
        nexts = neighbours(lambda m: p[m], l, rows, columns, l, 4 * L + l)
        faces = (tx[0, l], tx[1, l], ty[0, l], ty[1, l], tz[l], tz[l + 1])
        drops = [t * (here - q) for t, q in zip(faces, nexts)]
        face_sum = sum(faces)
        drop_sum = sum(drops)
        porous = volume_scale * por[l]
        sats = (sw[l], 1.0 - sw[l] - sg[l], sg[l])
        indices = index_sum[l]
        diagonals, residuals, inverses, cs = [], [], [], []
        for a in range(3):
            c = coef[a, l]
            ab = c * face_sum
            net = c * drop_sum
            for t, d, s in zip(faces, drops, coeff_neighbours(coef, coef_row, coef_col, a, l)):
                ab = ab + t * s
                net = net + d * s
            b = 1.0 + compress[a] * here
            stored = porous * sats[a]
            diagonals.append(compress[a] * stored + ab + c * indices)
            residuals.append(b * stored - volume_scale * mass[a, l] + net + c * (indices * here))
            inverses.append(1.0 / (porous * b))
            cs.append(c)
        inverse_total = 1.0 / sum(d * v for d, v in zip(diagonals, inverses))
        weights = [v * inverse_total for v in inverses]
        base[l] = -sum(w * r for w, r in zip(weights, residuals))
        head[l] = sum(w * c for w, c in zip(weights, cs))
        for a in range(3):
            weight[a, l] = weights[a]
            res[a, l] = residuals[a]
        diag[0, l] = diagonals[0]
        diag[1, l] = diagonals[2]
        for c in layer_copies(outs, sems_out, l):
            c.start()
        return carry

    lax.fori_loop(0, L, second, 0)
    wait_copies(saved)
    for l in range(L):
        wait_copies(layer_copies(outs, sems_out, l))


def first_kernel(
    got, info, own, base, head, row_lo, row_hi, col_lo, col_hi, mine, well_residual, spread, step,
):
    lane = iota((1, LANES), 1)
    sums = jnp.sum(got[...], axis=0, keepdims=True)
    total = jnp.where(lane < WELL_DEV, sums, 1.0)
    flow = rolled_row(sums, LANES - 16)
    residual = jnp.where(lane < WELL_DEV, flow - total * own[0:1] - own[1:2], 0.0)
    inverse = jnp.where(lane < WELL_DEV, 1.0 / total, 0.0)
    mine[...] = jnp.concatenate([residual, inverse, jnp.zeros((6, LANES), f32)], axis=0)
    well_residual[...] = residual[:, 0:WELL_DEV]
    cell_row = info[0:1].astype(i32)
    well_row = info[1:2].astype(i32)
    heads = gather_wells(got[...], well_row >> 4, (well_row & 15) + 32)
    spread[...] = scatter(cell_row, info[2:3] * heads).reshape(L, R, C)
    step[...] = base[...] + head[...] * spread[...]
    write_faces(step, (row_lo, row_hi, col_lo, col_hi))


def first_flow_kernel(cells, me, info, perf, mine, step, pay, rows):
    gather_cells(cells, (step,), rows)
    well_row = info[1:2].astype(i32)
    column = to_column(info[0:1]).astype(i32) & (C - 1)
    here = to_row(pick_columns(rows, 0, column))
    parts = parts_by_offset(me[0], well_row, perf[0:1] * here)
    packed = parts[:, TAIL:]
    residual = mine[0:1]
    inverse = mine[1:2]
    for n, row in enumerate((residual * inverse, residual, inverse)):
        packed = packed + rolled_row(row, 16 * (n + 1))
    tiles = [parts[:, LANES * t : LANES * (t + 1)] for t in range(5)]
    pay[...] = to_everyone(jnp.concatenate(tiles + [packed, jnp.zeros((2, LANES), f32)], axis=0))


def grid_kernel(
    coef_row, coef_col, row_lo, row_hi, col_lo, col_hi, head, spread, step,
    coef_h, tx_h, ty_h, tz_h, weight_h, res_h,
    ahead, residual_h, gain_h,
    coef, tx, ty, tz, weight, res, residual, gain, sems, sems_out,
):
    copies = start_copies(
        ((coef_h, coef), (tx_h, tx), (ty_h, ty), (tz_h, tz), (weight_h, weight), (res_h, res)), sems
    )
    columns = unpack_columns(col_lo, col_hi)
    wait_copies(copies)

    def outs(l):
        return (
            (residual.at[:, l], residual_h.at[:, l]), (gain.at[:, l], gain_h.at[:, l]),
        )

    def layer(l, carry):
        nexts = step_neighbours(step, row_lo, row_hi, columns, l)
        faces = (tx[0, l], tx[1, l], ty[0, l], ty[1, l], tz[l], tz[l + 1])
        wells = spread[l]
        mixes = [head[l]] * 6
        for a in range(3):
            w = weight[a, l]
            sides = coeff_neighbours(coef, coef_row, coef_col, a, l)
            mixes = [m + w * s for m, s in zip(mixes, sides)]
            residual[a, l] = res[a, l] - coef[a, l] * wells
        total = step[l]
        for j in range(6):
            g = faces[j] * mixes[j]
            gain[j, l] = g
            total = total + g * nexts[j]
        ahead[l] = total
        for c in layer_copies(outs, sems_out, l):
            c.start()
        return carry

    lax.fori_loop(0, L, layer, 0)
    for l in range(L):
        wait_copies(layer_copies(outs, sems_out, l))


def second_kernel(got, info, ahead, head, row_lo, row_hi, col_lo, col_hi, step):
    cell_row = info[0:1].astype(i32)
    well_row = info[1:2].astype(i32)
    moves = gather_wells(tile_of(got, 5), well_row >> 4, (well_row & 15) + 16)
    wells = scatter(cell_row, info[2:3] * moves).reshape(L, R, C)
    step[...] = ahead[...] + head[...] * wells
    write_faces(step, (row_lo, row_hi, col_lo, col_hi))


def wells_kernel(
    cells, me, got, info, perf, step, gain_h, table, parts, spread, gain, rows, sems,
):
    copies = start_copies(((gain_h, gain),), sems)
    tail = tile_of(got, 5)
    residuals = pltpu.roll(tail, LANES - 32, 1)
    inverses = pltpu.roll(tail, LANES - 48, 1)
    table[0] = residuals
    table[1] = inverses
    cell_row = info[0:1].astype(i32)
    well_row = info[1:2].astype(i32)
    valid = iota((DEVICES, LANES), 1) < WELL_DEV
    moves = jnp.where(valid, (sum_parts(got) + residuals) * inverses, 0.0)
    values = gather_wells(moves, well_row >> 4, well_row & 15)
    spread[...] = scatter(cell_row, info[2:3] * values).reshape(L, R, C)
    gather_cells(cells, (step,), rows)
    column = to_column(info[0:1]).astype(i32) & (C - 1)
    here = to_row(pick_columns(rows, 0, column))
    flows = parts_by_offset(me[0], well_row, perf[0:1] * here)
    tiles = [flows[:, LANES * t : LANES * (t + 1)] for t in range(6)]
    parts[...] = jnp.concatenate(tiles + [jnp.zeros((2, LANES), f32)], axis=0)
    wait_copies(copies)


def third_kernel(
    spread, old, base, gain, head, row_lo, row_hi, col_lo, col_hi,
    out_row_lo, out_row_hi, out_col_lo, out_col_hi, step,
):
    columns = unpack_columns(col_lo, col_hi)

    def layer(l, carry):
        nexts = step_neighbours(old, row_lo, row_hi, columns, l)
        total = base[l] + head[l] * spread[l]
        for j in range(6):
            total = total + gain[j, l] * nexts[j]
        step[l] = total
        return carry

    lax.fori_loop(0, L, layer, 0)
    write_faces(step, (out_row_lo, out_row_hi, out_col_lo, out_col_hi))


def third_flow_kernel(cells, info, perf, parts, step, pay, rows):
    gather_cells(cells, (step,), rows)
    column = to_column(info[0:1]).astype(i32) & (C - 1)
    here = pick_columns(rows, 0, column)
    well_row = info[1:2].astype(i32)
    slot_column = to_column(info[1:2]).astype(i32) & 15
    pay[...] = to_everyone(parts[...])
    pay[pl.ds(6, DEVICES, stride=8), :] = to_holders(
        well_row >> 4, slot_column, ((0, to_column(perf[0:1]) * here),)
    )


def last_grid_kernel(
    coef_row, coef_col, row_lo, row_hi, col_lo, col_hi, head, step,
    p_h, por_h, coef_h, tx_h, ty_h, tz_h, weight_h, diag_h, residual_h,
    ahead_h, slope_h,
    p, por, coef, tx, ty, tz, weight, diag, residual, ahead, slope, sems, sems_out,
):
    copies = start_copies(
        (
            (p_h, p), (por_h, por), (coef_h, coef), (tx_h, tx), (ty_h, ty), (tz_h, tz),
            (weight_h, weight), (diag_h, diag), (residual_h, residual),
        ),
        sems,
    )
    columns = unpack_columns(col_lo, col_hi)
    wait_copies(copies)

    def outs(l):
        return ((ahead.at[:, l], ahead_h.at[:, l]), (slope.at[:, l], slope_h.at[:, l]))

    def layer(l, carry):
        nexts = step_neighbours(step, row_lo, row_hi, columns, l)
        faces = (tx[0, l], tx[1, l], ty[0, l], ty[1, l], tz[l], tz[l + 1])
        flows = [t * q for t, q in zip(faces, nexts)]
        flow_sum = sum(flows)
        rights, cs = [], []
        for a in range(3):
            c = coef[a, l]
            total = c * flow_sum - residual[a, l]
            for v, s in zip(flows, coeff_neighbours(coef, coef_row, coef_col, a, l)):
                total = total + v * s
            rights.append(total)
            cs.append(c)
        z = sum(weight[a, l] * rights[a] for a in range(3))
        h = head[l]
        porous = volume_scale * por[l]
        inverse_water = 1.0 / (porous * (1.0 + compress[0] * p[l]))
        inverse_gas = 1.0 / (porous * (1.0 + compress[2] * p[l]))
        ahead[0, l] = z
        ahead[1, l] = (rights[0] - diag[0, l] * z) * inverse_water
        ahead[2, l] = (rights[2] - diag[1, l] * z) * inverse_gas
        slope[0, l] = (cs[0] - diag[0, l] * h) * inverse_water
        slope[1, l] = (cs[2] - diag[1, l] * h) * inverse_gas
        for c in layer_copies(outs, sems_out, l):
            c.start()
        return carry

    lax.fori_loop(0, L, layer, 0)
    for l in range(L):
        wait_copies(layer_copies(outs, sems_out, l))


def final_kernel(
    got, info, table, mine, head, ahead_h, slope_h, update_h, moved, ahead, slope, update, sems, sems_out,
):
    copies = start_copies(((ahead_h, ahead), (slope_h, slope)), sems)
    flow = jnp.sum(tile_of(got, 6), axis=0, keepdims=True)
    moved[...] = ((flow + mine[0:1]) * mine[1:2])[:, 0:WELL_DEV]
    cell_row = info[0:1].astype(i32)
    well_row = info[1:2].astype(i32)
    valid = iota((DEVICES, LANES), 1) < WELL_DEV
    moves = jnp.where(valid, (sum_parts(got) + table[0]) * table[1], 0.0)
    values = gather_wells(moves, well_row >> 4, well_row & 15)
    wells = scatter(cell_row, info[2:3] * values).reshape(L, R, C)
    wait_copies(copies)

    def outs(l):
        return ((update.at[:, l], update_h.at[:, l]),)

    for l in range(L):
        update[0, l] = ahead[0, l] + head[l] * wells[l]
        update[1, l] = ahead[1, l] + slope[0, l] * wells[l]
        update[2, l] = ahead[2, l] + slope[1, l] * wells[l]
        layer_copies(outs, sems_out, l)[0].start()
    for l in range(L):
        wait_copies(layer_copies(outs, sems_out, l))


def call(kernel, outs, ins, operands, scratch=(), flops=0):
    shapes = tuple(
        pltpu.VMEM(s, f32) if w is VM else pltpu.HBM(s, f32) if w is HB else jax.ShapeDtypeStruct(s, f32)
        for s, w in outs
    )
    moved = 4 * sum(int(x.size) for x in operands)
    operands = [
        pltpu.with_memory_space_constraint(x, pltpu.HBM) if w is HB else x for x, w in zip(operands, ins)
    ]
    return pl.pallas_call(
        kernel,
        out_shape=shapes,
        in_specs=ins,
        out_specs=tuple(w or VM for _, w in outs),
        scratch_shapes=[pltpu.VMEM(x, f32) if type(x) is tuple else x for x in scratch],
        compiler_params=pltpu.CompilerParams(vmem_limit_bytes=40 * 1024 * 1024),
        cost_estimate=pl.CostEstimate(flops=flops, bytes_accessed=moved, transcendentals=0),
    )(*operands)


FIELD = (L, R, C)
TWO, THREE, SIX, FACED = ((2,) + FIELD, (3,) + FIELD, (6,) + FIELD, (L + 1, R, C))
FACES = (((L, C), VM), ((L, C), VM), ((L, LANES), VM), ((L, LANES), VM))
WIDE_FACES = (((4 * L, C), VM), ((4 * L, C), VM), ((4 * L, LANES), VM), ((4 * L, LANES), VM))
SMALL = (8, LANES)
ROWS = (1, PERFS, C)
PAY = ((8 * DEVICES, LANES), None)
sem = pltpu.SemaphoreType.DMA


def exchange(array):
    return lax.all_to_all(array, AXES, split_axis=0, concat_axis=0, tiled=True)


def exchange_tiles(array):
    return exchange(array.reshape(DEVICES, 8, LANES)).reshape(8 * DEVICES, LANES)


def halo_of(faces):
    row_lo, row_hi, col_lo, col_hi = faces
    got = []
    for axis, low, high in (("gx", row_lo, row_hi), ("gy", col_lo, col_hi)):
        count = lax.axis_size(axis)
        up = [(i, (i + 1) % count) for i in range(count)]
        got.append(lax.ppermute(high, axis, up))
        got.append(lax.ppermute(low, axis, [(j, i) for i, j in up]))
    return got


def local(
    pressure, sat_water, sat_gas, old_mass, perm, porosity,
    perf_well, perf_cell, perf_index, well_pressure, well_rate,
):
    me = (lax.axis_index("gx") * lax.axis_size("gy") + lax.axis_index("gy")).astype(i32).reshape(1)
    cells = perf_cell.reshape(1, PERFS)
    *faces, p, sw, sg = call(
        faces_kernel,
        WIDE_FACES + ((FIELD, VM), (FIELD, VM), (FIELD, VM)),
        [HB] * 4,
        (pressure, sat_water, sat_gas, perm),
        [pltpu.VMEM(TWO, bf16), sem((4,))],
    )
    halo = halo_of(faces)
    pay, perf, info, own = call(
        start_kernel,
        (((DEVICES, LANES), None), ((8, PERFS), VM), ((8, PERFS), VM), (SMALL, VM)),
        [HB] * 5 + [VM] * 3,
        (
            cells, perf_well.reshape(1, PERFS), perf_index.reshape(1, PERFS),
            well_pressure.reshape(1, WELL_DEV), well_rate.reshape(1, WELL_DEV), p, sw, sg,
        ),
        [
            pltpu.SMEM((1, PERFS), i32), pltpu.VMEM((1, PERFS), i32), pltpu.VMEM((1, PERFS), i32), (1, PERFS),
            (1, WELL_DEV), (1, WELL_DEV), (3, PERFS, C), sem((6,)),
        ],
    )
    got = exchange(pay)
    coef_row, coef_col, base, head, coef, tx, ty, tz, weight, res, diag = call(
        setup_kernel,
        (
            ((2, 3, L, C), VM), ((3, R, LANES), VM), (FIELD, VM), (FIELD, VM), (THREE, HB), (TWO, HB), (TWO, HB),
            (FACED, HB), (THREE, HB), (THREE, HB), (TWO, HB),
        ),
        [SM] + [VM] * 8 + [HB] * 3,
        (me, info, *halo, p, sw, sg, porosity, old_mass, perm),
        [
            FIELD, THREE, pltpu.VMEM(THREE, bf16), THREE, TWO, TWO, FACED,
            THREE, THREE, TWO, FIELD, sem((3,)), sem((4,)), sem((3, L)),
        ],
        flops=400 * L * R * C,
    )
    *faces, mine, well_residual, spread, start = call(
        first_kernel,
        FACES + ((SMALL, VM), ((1, WELL_DEV), None), (FIELD, VM), (FIELD, VM)),
        [VM] * 5,
        (got, info, own, base, head),
    )
    halo = halo_of(faces)
    (pay,) = call(
        first_flow_kernel, (PAY,), [SM] * 2 + [VM] * 4, (cells, me, info, perf, mine, start), [ROWS]
    )
    got = exchange_tiles(pay)
    fields = (coef, tx, ty, tz, weight)
    ahead, residual, gain = call(
        grid_kernel,
        ((FIELD, VM), (THREE, HB), (SIX, HB)),
        [VM] * 9 + [HB] * 6,
        (coef_row, coef_col, *halo, head, spread, start, *fields, res),
        [THREE, TWO, TWO, FACED, THREE, THREE, THREE, SIX, sem((6,)), sem((2, L))],
        flops=100 * L * R * C,
    )
    *faces, step = call(second_kernel, FACES + ((FIELD, VM),), [VM] * 4, (got, info, ahead, head))
    halo = halo_of(faces)
    table, parts, spread, gain_near = call(
        wells_kernel,
        (((2, DEVICES, LANES), VM), (SMALL, VM), (FIELD, VM), (SIX, VM)),
        [SM, SM] + [VM] * 4 + [HB],
        (cells, me, got, info, perf, step, gain),
        [ROWS, sem((1,))],
    )
    *faces, step = call(
        third_kernel,
        FACES + ((FIELD, VM),),
        [VM] * 9,
        (spread, step, start, gain_near, head, *halo),
    )
    halo = halo_of(faces)
    (pay,) = call(
        third_flow_kernel, (PAY,), [SM] + [VM] * 4, (cells, info, perf, parts, step), [ROWS]
    )
    got = exchange_tiles(pay)
    ahead, slope = call(
        last_grid_kernel,
        ((THREE, HB), (TWO, HB)),
        [VM] * 8 + [HB] * 9,
        (coef_row, coef_col, *halo, head, step, pressure, porosity, *fields, diag, residual),
        [FIELD, FIELD, THREE, TWO, TWO, FACED, THREE, TWO, THREE, THREE, TWO, sem((9,)), sem((2, L))],
        flops=150 * L * R * C,
    )
    update, moved = call(
        final_kernel,
        ((THREE, HB), ((1, WELL_DEV), None)),
        [VM] * 5 + [HB] * 2,
        (got, info, table, mine, head, ahead, slope),
        [THREE, TWO, THREE, sem((2,)), sem((1, L))],
    )
    return residual, well_residual.reshape(WELL_DEV), update, moved.reshape(WELL_DEV)


def solution(mesh):
    return jax.shard_map(
        local,
        mesh=mesh,
        in_specs=(
            P(None, "gx", "gy"),
            P(None, "gx", "gy"),
            P(None, "gx", "gy"),
            P(None, None, "gx", "gy"),
            P(None, None, "gx", "gy"),
            P(None, "gx", "gy"),
            P(("gx", "gy")),
            P(("gx", "gy")),
            P(("gx", "gy")),
            P(("gx", "gy")),
            P(("gx", "gy")),
        ),
        out_specs=(
            P(None, None, "gx", "gy"),
            P(("gx", "gy")),
            P(None, None, "gx", "gy"),
            P(("gx", "gy")),
        ),
        check_vma=False,
    )
```

```python
import jax
import jax.numpy as jnp
from jax import lax
from jax.experimental import pallas as pl
from jax.experimental.pallas import tpu as pltpu
from jax.sharding import PartitionSpec as P

f32 = jnp.float32
bf16 = jnp.bfloat16
i32 = jnp.int32

compress = (0.05, 0.02, 0.2)
viscosity = (0.5, 2.0, 0.1)
volume_scale = 4.0
layer_ratio = 0.1
AXES = ("gx", "gy")
DEVICES = 128
WELL_DEV = 16
REACH = 40
FAR = 64
TAIL = REACH * WELL_DEV
WIDTH = TAIL + 128
LANES = 128
L, R, C = 8, 64, 256
PERFS = 256
VM = pl.BlockSpec(memory_space=pltpu.VMEM)
HB = pl.BlockSpec(memory_space=pltpu.HBM)


def iota(shape, dim):
    return lax.broadcasted_iota(i32, shape, dim)


def split3(x):
    high = x.astype(bf16)
    rest = x - high.astype(f32)
    middle = rest.astype(bf16)
    low = (rest - middle.astype(f32)).astype(bf16)
    return high, middle, low


def dot(a, b):
    return jnp.dot(a, b, preferred_element_type=f32)


def to_column(row):
    n = row.shape[1]
    return jnp.sum(jnp.where(iota((n, n), 0) == iota((n, n), 1), row, 0.0), axis=1, keepdims=True)


def to_row(column):
    n = column.shape[0]
    return jnp.sum(jnp.where(iota((n, n), 0) == iota((n, n), 1), column, 0.0), axis=0, keepdims=True)


def coeffs_of(p, sw, sg):
    so = 1.0 - sw - sg
    return tuple(
        s * s * (1.0 / viscosity[a]) * (1.0 + compress[a] * p) for a, s in enumerate((sw, so, sg))
    )


def scatter(cell_row, values):
    match = iota((L * R, PERFS), 0) == (cell_row >> 8)
    column = to_column(cell_row.astype(f32)).astype(i32) & (C - 1)
    spread = (iota((PERFS, C), 1) == column).astype(bf16)
    return sum(
        dot(jnp.where(match, part.astype(f32), 0.0).astype(bf16), spread) for part in split3(values)
    )


def gather_cells(cell_column, fields):
    onehot = (iota((PERFS, L * R), 1) == (cell_column >> 8)).astype(bf16)
    here = iota((PERFS, C), 1) == (cell_column & (C - 1))
    picked = []
    for field in fields:
        rows = sum(dot(onehot, part) for part in split3(field))
        picked.append(jnp.sum(jnp.where(here, rows, 0.0), axis=1, keepdims=True))
    return picked


def flat(field):
    return field[...].reshape(L * R, C)


def gather_wells(table, holder, slot):
    onehot = (iota((DEVICES, PERFS), 0) == holder).astype(bf16)
    wide = sum(dot(part, onehot) for part in split3(table.T))
    return jnp.sum(jnp.where(iota((LANES, PERFS), 0) == slot, wide, 0.0), axis=0, keepdims=True)


def to_holders(holder, slot_column, columns):
    lane = iota((PERFS, LANES), 1)
    group = lane >> 4
    values = jnp.zeros((PERFS, LANES), f32)
    for g, column in columns:
        values = jnp.where(group == g, column, values)
    values = jnp.where((lane & 15) == slot_column, values, 0.0)
    onehot = (iota((DEVICES, PERFS), 0) == holder).astype(bf16)
    return sum(dot(onehot, part) for part in split3(values))


def parts_by_offset(me, well_row, values):
    offset = (me - (well_row >> 4)) & (DEVICES - 1)
    lane = jnp.where(offset == FAR, TAIL, offset * WELL_DEV) + (well_row & 15)
    column = to_column(lane.astype(f32)).astype(i32)
    onehot = (iota((PERFS, WIDTH), 1) == column).astype(bf16)
    high, middle, low = split3(values)
    rows = jnp.concatenate([high.astype(f32), middle.astype(f32), low.astype(f32), jnp.zeros((5, PERFS), f32)], axis=0)
    return jnp.sum(dot(rows.astype(bf16), onehot), axis=0, keepdims=True)


def tile_of(got, t):
    return got[pl.ds(t, DEVICES, stride=8), :]


def sum_parts(got):
    aligned = tile_of(got, 0)
    for t in range(1, TAIL // LANES):
        aligned = aligned + pltpu.roll(tile_of(got, t), DEVICES - 8 * t, 0)
    total = aligned + pltpu.roll(tile_of(got, 5), DEVICES - FAR, 0)
    for u in range(1, 8):
        total = total + pltpu.roll(pltpu.roll(aligned, DEVICES - u, 0), LANES - 16 * u, 1)
    return total


def to_everyone(tile):
    return jnp.broadcast_to(tile[None], (DEVICES, 8, LANES)).reshape(8 * DEVICES, LANES)


def rolled_row(row, shift):
    return pltpu.roll(jnp.broadcast_to(row, (8, LANES)), shift, 1)[0:1]


def shift_rows(x, first, last):
    return (
        jnp.concatenate([first, x[:-1]], axis=0),
        jnp.concatenate([x[1:], last], axis=0),
    )


def shift_columns(x, first, last):
    lane = iota(x.shape, 1)
    return (
        jnp.where(lane == 0, first, pltpu.roll(x, 1, 1)),
        jnp.where(lane == C - 1, last, pltpu.roll(x, C - 1, 1)),
    )


def lane_of(x, index):
    return pltpu.roll(x, (LANES - index) % LANES, 1)[:, 0:1]


def pack_columns(columns, low, high):
    n = low.shape[0]
    turned = jnp.concatenate([columns, jnp.zeros((LANES - R, LANES), f32)], axis=0).T
    low[...] = turned[0:n]
    high[...] = turned[n : 2 * n]


def unpack_columns(low, high):
    n = low.shape[0]
    rows = jnp.concatenate([low[...], high[...], jnp.zeros((LANES - 2 * n, LANES), f32)], axis=0)
    return rows.T[0:R]


def write_faces(step, outs):
    row_lo, row_hi, col_lo, col_hi = outs
    lane = iota((R, LANES), 1)
    columns = jnp.zeros((R, LANES), f32)
    for l in range(L):
        x = step[l]
        row_lo[l : l + 1, :] = x[0:1]
        row_hi[l : l + 1, :] = x[R - 1 : R]
        columns = jnp.where(lane == l, x[:, 0:1], columns)
        columns = jnp.where(lane == L + l, x[:, C - 1 : C], columns)
    pack_columns(columns, col_lo, col_hi)


def start_copies(pairs, sems):
    copies = [pltpu.make_async_copy(a, b, sems.at[n]) for n, (a, b) in enumerate(pairs)]
    for c in copies:
        c.start()
    return copies


def wait_copies(copies):
    for c in copies:
        c.wait()


def layer_copies(pairs, sems, l):
    return [pltpu.make_async_copy(a, b, sems.at[n, l]) for n, (a, b) in enumerate(pairs(l))]


def faces_kernel(
    p_h, sw_h, sg_h, perm_h, row_lo, row_hi, col_lo, col_hi, p, sw, sg, perm, sems,
):
    copies = start_copies(((perm_h.at[0:2], perm), (p_h, p), (sw_h, sw), (sg_h, sg)), sems)
    lane = iota((R, LANES), 1)
    columns = jnp.zeros((R, LANES), f32)
    wait_copies(copies[:1])
    for l in range(L):
        n = 3 * L + l
        row_lo[n : n + 1, :] = perm[0, l, 0:16, :].astype(f32)[0:1]
        row_hi[n : n + 1, :] = perm[0, l, R - 16 : R, :].astype(f32)[15:16]
        k = perm[1, l].astype(f32)
        columns = jnp.where(lane == n, k[:, 0:1], columns)
        columns = jnp.where(lane == 4 * L + n, k[:, C - 1 : C], columns)
    wait_copies(copies[1:])
    for l in range(L):
        for f, ref in enumerate((p, sw, sg)):
            x = ref[l]
            n = f * L + l
            row_lo[n : n + 1, :] = x[0:1]
            row_hi[n : n + 1, :] = x[R - 1 : R]
            columns = jnp.where(lane == n, x[:, 0:1], columns)
            columns = jnp.where(lane == 4 * L + n, x[:, C - 1 : C], columns)
    pack_columns(columns, col_lo, col_hi)


def start_kernel(
    cell_h, well_h, index_h, pressure_h, rate_h, p, sw, sg,
    pay, perf, info, own,
    cell_in, well_in, index_in, pressure_in, rate_in, sems,
):
    copies = start_copies(
        (
            (cell_h, cell_in), (well_h, well_in), (index_h, index_in),
            (pressure_h, pressure_in), (rate_h, rate_in),
        ),
        sems,
    )
    me = lax.axis_index("gx") * 16 + lax.axis_index("gy")
    device = jnp.full((1, PERFS), me, i32).astype(f32)
    wait_copies(copies)
    well_row = well_in[...]
    index_row = index_in[...]
    cell_float = cell_in[...].astype(f32)
    well_float = well_row.astype(f32)
    info[...] = jnp.concatenate([cell_float, well_float, index_row, device, jnp.zeros((4, PERFS), f32)], axis=0)
    blank = jnp.zeros((1, LANES - WELL_DEV), f32)
    heads = jnp.concatenate([pressure_in[...], blank], axis=1)
    rates = jnp.concatenate([rate_in[...], blank], axis=1)
    own[...] = jnp.concatenate([heads, rates, jnp.zeros((6, LANES), f32)], axis=0)
    slot_column = to_column(well_float).astype(i32) & 15
    here = gather_cells(to_column(cell_float).astype(i32), (flat(p), flat(sw), flat(sg)))
    coeffs = coeffs_of(*here)
    total = to_column(index_row) * (coeffs[0] + coeffs[1] + coeffs[2])
    sums = to_holders(well_row >> 4, slot_column, ((0, total), (1, total * here[0])))
    pay[...] = sums + rolled_row(heads, 32)
    perf[...] = jnp.broadcast_to(to_row(total), (8, PERFS))


def after_kernel(pay, *refs):
    pass


def transmit(k, k_next):
    return k * k_next / (k + k_next)


def neighbours(field, l, rows, columns, first, last):
    here = field(l)
    nexts = shift_rows(here, *rows)
    nexts += shift_columns(here, lane_of(columns, first), lane_of(columns, last))
    return nexts + (field(jnp.maximum(l - 1, 0)), field(jnp.minimum(l + 1, L - 1)))


def coeff_neighbours(coef, coef_row, coef_col, a, l):
    rows = (coef_row[0, a, pl.ds(l, 1), :], coef_row[1, a, pl.ds(l, 1), :])
    return neighbours(lambda m: coef[a, m], l, rows, coef_col[a], l, 4 * L + l)


def inner_neighbours(step, l):
    blank = jnp.zeros((1, C), f32)
    here = step[l]
    nexts = shift_rows(here, blank, blank) + shift_columns(here, 0.0, 0.0)
    return nexts + (step[jnp.maximum(l - 1, 0)], step[jnp.minimum(l + 1, L - 1)])


def step_neighbours(step, row_lo, row_hi, columns, l):
    rows = (row_lo[pl.ds(l, 1), :], row_hi[pl.ds(l, 1), :])
    return neighbours(lambda m: step[m], l, rows, columns, l, L + l)


def add_faces(field, l, low, high, columns):
    lane = iota((R, LANES), 1)
    field[l, :, 0:LANES] += jnp.where(lane == 0, columns[:, l : l + 1], 0.0)
    field[l, :, C - LANES : C] += jnp.where(lane == LANES - 1, columns[:, L + l : L + l + 1], 0.0)
    field[l, 0:1, :] += low
    field[l, R - 1 : R, :] += high


def end_columns(columns, l, first, last):
    lane = iota((R, LANES), 1)
    return jnp.where(lane == l, first, jnp.where(lane == L + l, last, columns))


def setup_kernel(
    info, row_lo, row_hi, col_lo, col_hi, p, sw, sg, por_h, mass_h, perm_h,
    coef_row, coef_col, base, head, coef_h, tx_h, ty_h, tz_h, weight_h, res_h, diag_h,
    por, mass, perm, coef, tx, ty, tz, weight, res, diag, index_sum,
    sems, sems_t, sems_out,
):
    copies = start_copies(((perm_h, perm), (por_h, por), (mass_h, mass)), sems)
    index_sum[...] = scatter(info[0:1].astype(i32), info[2:3]).reshape(L, R, C)
    for side, ref in enumerate((row_lo, row_hi)):
        for a, c in enumerate(coeffs_of(ref[0:L], ref[L : 2 * L], ref[2 * L : 3 * L])):
            coef_row[side, a] = c
    columns = unpack_columns(col_lo, col_hi)
    for a, c in enumerate(
        coeffs_of(columns, pltpu.roll(columns, LANES - L, 1), pltpu.roll(columns, LANES - 2 * L, 1))
    ):
        coef_col[a] = c
    lane = iota((R, C), 1)
    me = info[3:4, 0:1].astype(i32)
    gx = me >> 4
    gy = me & 15
    inside = [jnp.where(t, 1.0, 0.0) for t in (gx > 0, gx < 7, gy > 0, gy < 15)]
    wait_copies(copies[:1])

    def first(l, carry):
        for a, c in enumerate(coeffs_of(p[l], sw[l], sg[l])):
            coef[a, l] = c
        k = perm[0, l].astype(f32)
        n = 3 * L + l
        edge = row_lo[pl.ds(n, 1), :] * inside[0]
        before = transmit(k, jnp.concatenate([edge, k[:-1]], axis=0))
        edge = row_hi[pl.ds(n, 1), :] * inside[1]
        tx[0, l] = before
        tx[1, l] = jnp.concatenate([before[1:], transmit(k[R - 1 : R], edge)], axis=0)
        k = perm[1, l].astype(f32)
        edge = lane_of(columns, n) * inside[2]
        before = transmit(k, jnp.where(lane == 0, edge, pltpu.roll(k, 1, 1)))
        edge = lane_of(columns, 4 * L + n) * inside[3]
        ty[0, l] = before
        ty[1, l] = jnp.where(lane == C - 1, transmit(k[:, C - 1 : C], edge), pltpu.roll(before, C - 1, 1))
        k = perm[2, l].astype(f32)
        under = perm[2, jnp.maximum(l - 1, 0)].astype(f32)
        tz[l] = jnp.where(l > 0, layer_ratio, 0.0) * transmit(k, under)
        return carry

    lax.fori_loop(0, L, first, 0)
    tz[L] = jnp.zeros((R, C), f32)
    saved = start_copies(((coef, coef_h), (tx, tx_h), (ty, ty_h), (tz, tz_h)), sems_t)
    wait_copies(copies[1:])

    def outs(l):
        return (
            (weight.at[:, l], weight_h.at[:, l]),
            (res.at[:, l], res_h.at[:, l]), (diag.at[:, l], diag_h.at[:, l]),
        )

    def second(l, carry):
        here = p[l]
        rows = (row_lo[pl.ds(l, 1), :], row_hi[pl.ds(l, 1), :])
        nexts = neighbours(lambda m: p[m], l, rows, columns, l, 4 * L + l)
        faces = (tx[0, l], tx[1, l], ty[0, l], ty[1, l], tz[l], tz[l + 1])
        drops = [t * (here - q) for t, q in zip(faces, nexts)]
        face_sum = sum(faces)
        drop_sum = sum(drops)
        porous = volume_scale * por[l]
        sats = (sw[l], 1.0 - sw[l] - sg[l], sg[l])
        indices = index_sum[l]
        diagonals, residuals, inverses, cs = [], [], [], []
        for a in range(3):
            c = coef[a, l]
            ab = c * face_sum
            net = c * drop_sum
            for t, d, s in zip(faces, drops, coeff_neighbours(coef, coef_row, coef_col, a, l)):
                ab = ab + t * s
                net = net + d * s
            b = 1.0 + compress[a] * here
            stored = porous * sats[a]
            diagonals.append(compress[a] * stored + ab + c * indices)
            residuals.append(b * stored - volume_scale * mass[a, l] + net + c * (indices * here))
            inverses.append(1.0 / (porous * b))
            cs.append(c)
        inverse_total = 1.0 / sum(d * v for d, v in zip(diagonals, inverses))
        weights = [v * inverse_total for v in inverses]
        base[l] = -sum(w * r for w, r in zip(weights, residuals))
        head[l] = sum(w * c for w, c in zip(weights, cs))
        for a in range(3):
            weight[a, l] = weights[a]
            res[a, l] = residuals[a]
        diag[0, l] = diagonals[0]
        diag[1, l] = diagonals[2]
        for c in layer_copies(outs, sems_out, l):
            c.start()
        return carry

    lax.fori_loop(0, L, second, 0)
    wait_copies(saved)
    for l in range(L):
        wait_copies(layer_copies(outs, sems_out, l))


def first_kernel(
    got, info, own, base, head, row_lo, row_hi, col_lo, col_hi, mine, well_residual, spread, step,
):
    lane = iota((1, LANES), 1)
    sums = jnp.sum(got[...], axis=0, keepdims=True)
    total = jnp.where(lane < WELL_DEV, sums, 1.0)
    flow = rolled_row(sums, LANES - 16)
    residual = jnp.where(lane < WELL_DEV, flow - total * own[0:1] - own[1:2], 0.0)
    inverse = jnp.where(lane < WELL_DEV, 1.0 / total, 0.0)
    mine[...] = jnp.concatenate([residual, inverse, jnp.zeros((6, LANES), f32)], axis=0)
    well_residual[...] = residual[:, 0:WELL_DEV]
    cell_row = info[0:1].astype(i32)
    well_row = info[1:2].astype(i32)
    heads = gather_wells(got[...], well_row >> 4, (well_row & 15) + 32)
    spread[...] = scatter(cell_row, info[2:3] * heads).reshape(L, R, C)
    step[...] = base[...] + head[...] * spread[...]
    write_faces(step, (row_lo, row_hi, col_lo, col_hi))


def first_flow_kernel(info, perf, mine, step, pay):
    well_row = info[1:2].astype(i32)
    here = to_row(gather_cells(to_column(info[0:1]).astype(i32), (flat(step),))[0])
    parts = parts_by_offset(info[3:4].astype(i32), well_row, perf[0:1] * here)
    packed = parts[:, TAIL:]
    residual = mine[0:1]
    inverse = mine[1:2]
    for n, row in enumerate((residual * inverse, residual, inverse)):
        packed = packed + rolled_row(row, 16 * (n + 1))
    tiles = [parts[:, LANES * t : LANES * (t + 1)] for t in range(5)]
    pay[...] = to_everyone(jnp.concatenate(tiles + [packed, jnp.zeros((2, LANES), f32)], axis=0))


def grid_kernel(
    coef_row, coef_col, head, spread, step,
    coef_h, tx_h, ty_h, tz_h, weight_h, res_h,
    ahead, end_row, end_col, residual_h, gain_h,
    coef, tx, ty, tz, weight, res, residual, gain, sems, sems_out,
):
    copies = start_copies(
        ((coef_h, coef), (tx_h, tx), (ty_h, ty), (tz_h, tz), (weight_h, weight), (res_h, res)), sems
    )
    wait_copies(copies)

    def outs(l):
        return (
            (residual.at[:, l], residual_h.at[:, l]), (gain.at[:, l], gain_h.at[:, l]),
        )

    def layer(l, ends):
        nexts = inner_neighbours(step, l)
        faces = (tx[0, l], tx[1, l], ty[0, l], ty[1, l], tz[l], tz[l + 1])
        wells = spread[l]
        mixes = [head[l]] * 6
        for a in range(3):
            w = weight[a, l]
            sides = coeff_neighbours(coef, coef_row, coef_col, a, l)
            mixes = [m + w * s for m, s in zip(mixes, sides)]
            residual[a, l] = res[a, l] - coef[a, l] * wells
        total = step[l]
        gains = []
        for j in range(6):
            g = faces[j] * mixes[j]
            gain[j, l] = g
            total = total + g * nexts[j]
            gains.append(g)
        ahead[l] = total
        end_row[0, pl.ds(l, 1), :] = gains[0][0:1]
        end_row[1, pl.ds(l, 1), :] = gains[1][R - 1 : R]
        for c in layer_copies(outs, sems_out, l):
            c.start()
        return end_columns(ends, l, gains[2][:, 0:1], gains[3][:, C - 1 : C])

    end_col[...] = lax.fori_loop(0, L, layer, jnp.zeros((R, LANES), f32))
    for l in range(L):
        wait_copies(layer_copies(outs, sems_out, l))


def second_kernel(
    got, info, ahead, head, end_row, end_col, row_lo, row_hi, col_lo, col_hi,
    out_row_lo, out_row_hi, out_col_lo, out_col_hi, step,
):
    cell_row = info[0:1].astype(i32)
    well_row = info[1:2].astype(i32)
    moves = gather_wells(tile_of(got, 5), well_row >> 4, (well_row & 15) + 16)
    wells = scatter(cell_row, info[2:3] * moves).reshape(L, R, C)
    step[...] = ahead[...] + head[...] * wells
    columns = end_col[...] * unpack_columns(col_lo, col_hi)
    for l in range(L):
        low = end_row[0, l : l + 1, :] * row_lo[l : l + 1, :]
        high = end_row[1, l : l + 1, :] * row_hi[l : l + 1, :]
        add_faces(step, l, low, high, columns)
    write_faces(step, (out_row_lo, out_row_hi, out_col_lo, out_col_hi))


def wells_kernel(
    got, info, perf, step, gain_h, table, parts, spread, gain, sems,
):
    copies = start_copies(((gain_h, gain),), sems)
    tail = tile_of(got, 5)
    residuals = pltpu.roll(tail, LANES - 32, 1)
    inverses = pltpu.roll(tail, LANES - 48, 1)
    table[0] = residuals
    table[1] = inverses
    cell_row = info[0:1].astype(i32)
    well_row = info[1:2].astype(i32)
    valid = iota((DEVICES, LANES), 1) < WELL_DEV
    moves = jnp.where(valid, (sum_parts(got) + residuals) * inverses, 0.0)
    values = gather_wells(moves, well_row >> 4, well_row & 15)
    spread[...] = scatter(cell_row, info[2:3] * values).reshape(L, R, C)
    here = to_row(gather_cells(to_column(info[0:1]).astype(i32), (flat(step),))[0])
    flows = parts_by_offset(info[3:4].astype(i32), well_row, perf[0:1] * here)
    tiles = [flows[:, LANES * t : LANES * (t + 1)] for t in range(6)]
    parts[...] = jnp.concatenate(tiles + [jnp.zeros((2, LANES), f32)], axis=0)
    wait_copies(copies)


def third_kernel(
    spread, old, base, gain, head, row_lo, row_hi, col_lo, col_hi,
    out_row_lo, out_row_hi, out_col_lo, out_col_hi, step,
):
    columns = unpack_columns(col_lo, col_hi)

    def layer(l, carry):
        nexts = step_neighbours(old, row_lo, row_hi, columns, l)
        total = base[l] + head[l] * spread[l]
        for j in range(6):
            total = total + gain[j, l] * nexts[j]
        step[l] = total
        return carry

    lax.fori_loop(0, L, layer, 0)
    write_faces(step, (out_row_lo, out_row_hi, out_col_lo, out_col_hi))


def third_flow_kernel(info, perf, parts, step, pay):
    here = gather_cells(to_column(info[0:1]).astype(i32), (flat(step),))[0]
    well_row = info[1:2].astype(i32)
    slot_column = to_column(info[1:2]).astype(i32) & 15
    pay[...] = to_everyone(parts[...])
    pay[pl.ds(6, DEVICES, stride=8), :] = to_holders(
        well_row >> 4, slot_column, ((0, to_column(perf[0:1]) * here),)
    )


def last_grid_kernel(
    coef_row, coef_col, head, step, gain_row, gain_col,
    p_h, por_h, coef_h, tx_h, ty_h, tz_h, weight_h, diag_h, residual_h,
    end_row, end_col, ahead_h, slope_h,
    p, por, coef, tx, ty, tz, weight, diag, residual, ahead, slope, sems, sems_out,
):
    copies = start_copies(
        (
            (p_h, p), (por_h, por), (coef_h, coef), (tx_h, tx), (ty_h, ty), (tz_h, tz),
            (weight_h, weight), (diag_h, diag), (residual_h, residual),
        ),
        sems,
    )
    wait_copies(copies)

    def outs(l):
        return ((ahead.at[:, l], ahead_h.at[:, l]), (slope.at[:, l], slope_h.at[:, l]))

    def layer(l, ends):
        nexts = inner_neighbours(step, l)
        faces = (tx[0, l], tx[1, l], ty[0, l], ty[1, l], tz[l], tz[l + 1])
        flows = [t * q for t, q in zip(faces, nexts)]
        flow_sum = sum(flows)
        rights, cs, sides = [], [], []
        for a in range(3):
            c = coef[a, l]
            total = c * flow_sum - residual[a, l]
            sides.append(coeff_neighbours(coef, coef_row, coef_col, a, l))
            for v, s in zip(flows, sides[a]):
                total = total + v * s
            rights.append(total)
            cs.append(c)
        z = sum(weight[a, l] * rights[a] for a in range(3))
        h = head[l]
        porous = volume_scale * por[l]
        inverse_water = 1.0 / (porous * (1.0 + compress[0] * p[l]))
        inverse_gas = 1.0 / (porous * (1.0 + compress[2] * p[l]))
        ahead[0, l] = z
        ahead[1, l] = (rights[0] - diag[0, l] * z) * inverse_water
        ahead[2, l] = (rights[2] - diag[1, l] * z) * inverse_gas
        slope[0, l] = (cs[0] - diag[0, l] * h) * inverse_water
        slope[1, l] = (cs[2] - diag[1, l] * h) * inverse_gas
        for c in layer_copies(outs, sems_out, l):
            c.start()
        columns = lane_of(gain_col[...], l), lane_of(gain_col[...], L + l)
        done = []
        for n, (a, inverse) in enumerate(((0, inverse_water), (2, inverse_gas))):
            d = diag[n, l]
            for side, row in enumerate((slice(0, 1), slice(R - 1, R))):
                face = faces[side][row] * (cs[a][row] + sides[a][side][row])
                end_row[side, n, pl.ds(l, 1), :] = (
                    face - d[row] * gain_row[side, pl.ds(l, 1), :]
                ) * inverse[row]
            pair = []
            for side, col in enumerate((slice(0, 1), slice(C - 1, C))):
                face = faces[2 + side][:, col] * (cs[a][:, col] + sides[a][2 + side][:, col])
                pair.append((face - d[:, col] * columns[side]) * inverse[:, col])
            done.append(end_columns(ends[n], l, *pair))
        return tuple(done)

    blank = jnp.zeros((R, LANES), f32)
    end_col[0], end_col[1] = lax.fori_loop(0, L, layer, (blank, blank))
    for l in range(L):
        wait_copies(layer_copies(outs, sems_out, l))


def final_kernel(
    got, info, table, mine, head, gain_row, gain_col, end_row, end_col, row_lo, row_hi, col_lo, col_hi,
    ahead_h, slope_h, update_h, moved, ahead, slope, update, sems, sems_out,
):
    copies = start_copies(((ahead_h, ahead), (slope_h, slope)), sems)
    flow = jnp.sum(tile_of(got, 6), axis=0, keepdims=True)
    moved[...] = ((flow + mine[0:1]) * mine[1:2])[:, 0:WELL_DEV]
    cell_row = info[0:1].astype(i32)
    well_row = info[1:2].astype(i32)
    valid = iota((DEVICES, LANES), 1) < WELL_DEV
    moves = jnp.where(valid, (sum_parts(got) + table[0]) * table[1], 0.0)
    values = gather_wells(moves, well_row >> 4, well_row & 15)
    wells = scatter(cell_row, info[2:3] * values).reshape(L, R, C)
    halo = unpack_columns(col_lo, col_hi)
    columns = (gain_col[...] * halo, end_col[0] * halo, end_col[1] * halo)
    wait_copies(copies)

    def outs(l):
        return ((update.at[:, l], update_h.at[:, l]),)

    for l in range(L):
        low = row_lo[l : l + 1, :]
        high = row_hi[l : l + 1, :]
        for n in range(3):
            rows = [gain_row[side, l : l + 1, :] if n == 0 else end_row[side, n - 1, l : l + 1, :] for side in range(2)]
            update[n, l] = ahead[n, l] + (head[l] if n == 0 else slope[n - 1, l]) * wells[l]
            add_faces(update.at[n], l, rows[0] * low, rows[1] * high, columns[n])
        layer_copies(outs, sems_out, l)[0].start()
    for l in range(L):
        wait_copies(layer_copies(outs, sems_out, l))


def call(kernel, outs, ins, operands, scratch=(), flops=0):
    shapes = tuple(
        pltpu.VMEM(s, f32) if w is VM else pltpu.HBM(s, f32) if w is HB else jax.ShapeDtypeStruct(s, f32)
        for s, w in outs
    )
    moved = 4 * sum(int(x.size) for x in operands)
    operands = [
        pltpu.with_memory_space_constraint(x, pltpu.HBM) if w is HB else x for x, w in zip(operands, ins)
    ]
    return pl.pallas_call(
        kernel,
        out_shape=shapes,
        in_specs=ins,
        out_specs=tuple(w or VM for _, w in outs),
        scratch_shapes=[pltpu.VMEM(x, f32) if type(x) is tuple else x for x in scratch],
        compiler_params=pltpu.CompilerParams(vmem_limit_bytes=40 * 1024 * 1024),
        cost_estimate=pl.CostEstimate(flops=flops, bytes_accessed=moved, transcendentals=0),
    )(*operands)


FIELD = (L, R, C)
TWO, THREE, SIX, FACED = ((2,) + FIELD, (3,) + FIELD, (6,) + FIELD, (L + 1, R, C))
FACES = (((L, C), VM), ((L, C), VM), ((L, LANES), VM), ((L, LANES), VM))
WIDE_FACES = (((4 * L, C), VM), ((4 * L, C), VM), ((4 * L, LANES), VM), ((4 * L, LANES), VM))
SMALL = (8, LANES)
PAY = ((8 * DEVICES, LANES), None)
sem = pltpu.SemaphoreType.DMA


def exchange(array):
    return lax.all_to_all(array, AXES, split_axis=0, concat_axis=0, tiled=True)


def exchange_tiles(array):
    return exchange(array.reshape(DEVICES, 8, LANES)).reshape(8 * DEVICES, LANES)


def halo_of(faces):
    row_lo, row_hi, col_lo, col_hi = faces
    got = []
    for axis, low, high in (("gx", row_lo, row_hi), ("gy", col_lo, col_hi)):
        count = lax.axis_size(axis)
        up = [(i, (i + 1) % count) for i in range(count)]
        got.append(lax.ppermute(high, axis, up))
        got.append(lax.ppermute(low, axis, [(j, i) for i, j in up]))
    return got


def local(
    pressure, sat_water, sat_gas, old_mass, perm, porosity,
    perf_well, perf_cell, perf_index, well_pressure, well_rate,
):
    *faces, p, sw, sg = call(
        faces_kernel,
        WIDE_FACES + ((FIELD, VM), (FIELD, VM), (FIELD, VM)),
        [HB] * 4,
        (pressure, sat_water, sat_gas, perm),
        [pltpu.VMEM(TWO, bf16), sem((4,))],
    )
    halo = halo_of(faces)
    pay, perf, info, own = call(
        start_kernel,
        (((DEVICES, LANES), None), ((8, PERFS), VM), ((8, PERFS), VM), (SMALL, VM)),
        [HB] * 5 + [VM] * 3,
        (
            perf_cell.reshape(1, PERFS), perf_well.reshape(1, PERFS), perf_index.reshape(1, PERFS),
            well_pressure.reshape(1, WELL_DEV), well_rate.reshape(1, WELL_DEV), p, sw, sg,
        ),
        [
            pltpu.VMEM((1, PERFS), i32), pltpu.VMEM((1, PERFS), i32), (1, PERFS),
            (1, WELL_DEV), (1, WELL_DEV), sem((5,)),
        ],
    )
    pay = pl.pallas_call(
        after_kernel,
        out_shape=jax.ShapeDtypeStruct(pay.shape, f32),
        in_specs=[pl.BlockSpec(memory_space=pl.ANY)] * 5,
        out_specs=pl.BlockSpec(memory_space=pl.ANY),
        input_output_aliases={0: 0},
    )(pay, *halo)
    got = exchange(pay)
    coef_row, coef_col, base, head, coef, tx, ty, tz, weight, res, diag = call(
        setup_kernel,
        (
            ((2, 3, L, C), VM), ((3, R, LANES), VM), (FIELD, VM), (FIELD, VM), (THREE, HB), (TWO, HB), (TWO, HB),
            (FACED, HB), (THREE, HB), (THREE, HB), (TWO, HB),
        ),
        [VM] * 8 + [HB] * 3,
        (info, *halo, p, sw, sg, porosity, old_mass, perm),
        [
            FIELD, THREE, pltpu.VMEM(THREE, bf16), THREE, TWO, TWO, FACED,
            THREE, THREE, TWO, FIELD, sem((3,)), sem((4,)), sem((3, L)),
        ],
        flops=400 * L * R * C,
    )
    *faces, mine, well_residual, spread, start = call(
        first_kernel,
        FACES + ((SMALL, VM), ((1, WELL_DEV), None), (FIELD, VM), (FIELD, VM)),
        [VM] * 5,
        (got, info, own, base, head),
    )
    halo = halo_of(faces)
    (pay,) = call(first_flow_kernel, (PAY,), [VM] * 4, (info, perf, mine, start))
    got = exchange_tiles(pay)
    fields = (coef, tx, ty, tz, weight)
    ahead, gain_row, gain_col, residual, gain = call(
        grid_kernel,
        ((FIELD, VM), ((2, L, C), VM), ((R, LANES), VM), (THREE, HB), (SIX, HB)),
        [VM] * 5 + [HB] * 6,
        (coef_row, coef_col, head, spread, start, *fields, res),
        [THREE, TWO, TWO, FACED, THREE, THREE, THREE, SIX, sem((6,)), sem((2, L))],
        flops=100 * L * R * C,
    )
    *faces, step = call(
        second_kernel,
        FACES + ((FIELD, VM),),
        [VM] * 10,
        (got, info, ahead, head, gain_row, gain_col, *halo),
    )
    halo = halo_of(faces)
    table, parts, spread, gain_near = call(
        wells_kernel,
        (((2, DEVICES, LANES), VM), (SMALL, VM), (FIELD, VM), (SIX, VM)),
        [VM] * 4 + [HB],
        (got, info, perf, step, gain),
        [sem((1,))],
    )
    *faces, step = call(
        third_kernel,
        FACES + ((FIELD, VM),),
        [VM] * 9,
        (spread, step, start, gain_near, head, *halo),
    )
    halo = halo_of(faces)
    (pay,) = call(third_flow_kernel, (PAY,), [VM] * 4, (info, perf, parts, step))
    got = exchange_tiles(pay)
    end_row, end_col, ahead, slope = call(
        last_grid_kernel,
        (((2, 2, L, C), VM), ((2, R, LANES), VM), (THREE, HB), (TWO, HB)),
        [VM] * 6 + [HB] * 9,
        (coef_row, coef_col, head, step, gain_row, gain_col, pressure, porosity, *fields, diag, residual),
        [FIELD, FIELD, THREE, TWO, TWO, FACED, THREE, TWO, THREE, THREE, TWO, sem((9,)), sem((2, L))],
        flops=150 * L * R * C,
    )
    update, moved = call(
        final_kernel,
        ((THREE, HB), ((1, WELL_DEV), None)),
        [VM] * 13 + [HB] * 2,
        (got, info, table, mine, head, gain_row, gain_col, end_row, end_col, *halo, ahead, slope),
        [THREE, TWO, THREE, sem((2,)), sem((1, L))],
    )
    return residual, well_residual.reshape(WELL_DEV), update, moved.reshape(WELL_DEV)


def solution(mesh):
    return jax.shard_map(
        local,
        mesh=mesh,
        in_specs=(
            P(None, "gx", "gy"),
            P(None, "gx", "gy"),
            P(None, "gx", "gy"),
            P(None, None, "gx", "gy"),
            P(None, None, "gx", "gy"),
            P(None, "gx", "gy"),
            P(("gx", "gy")),
            P(("gx", "gy")),
            P(("gx", "gy")),
            P(("gx", "gy")),
            P(("gx", "gy")),
        ),
        out_specs=(
            P(None, None, "gx", "gy"),
            P(("gx", "gy")),
            P(None, None, "gx", "gy"),
            P(("gx", "gy")),
        ),
        check_vma=False,
    )
```

```python
import jax
import jax.numpy as jnp
from jax import lax
from jax.experimental import pallas as pl
from jax.experimental.pallas import tpu as pltpu
from jax.sharding import PartitionSpec as P

f32 = jnp.float32
bf16 = jnp.bfloat16
i32 = jnp.int32

compress = (0.05, 0.02, 0.2)
viscosity = (0.5, 2.0, 0.1)
volume_scale = 4.0
layer_ratio = 0.1
AXES = ("gx", "gy")
DEVICES = 128
WELL_DEV = 16
REACH = 40
FAR = 64
TAIL = REACH * WELL_DEV
WIDTH = TAIL + 128
LANES = 128
L, R, C = 8, 64, 256
PERFS = 256
BLOCK = 8
VM = pl.BlockSpec(memory_space=pltpu.VMEM)
HB = pl.BlockSpec(memory_space=pltpu.HBM)


def iota(shape, dim):
    return lax.broadcasted_iota(i32, shape, dim)


def split3(x):
    high = x.astype(bf16)
    rest = x - high.astype(f32)
    middle = rest.astype(bf16)
    low = (rest - middle.astype(f32)).astype(bf16)
    return high, middle, low


def dot(a, b):
    return jnp.dot(a, b, preferred_element_type=f32)


def to_column(row):
    n = row.shape[1]
    return jnp.sum(jnp.where(iota((n, n), 0) == iota((n, n), 1), row, 0.0), axis=1, keepdims=True)


def to_row(column):
    n = column.shape[0]
    return jnp.sum(jnp.where(iota((n, n), 0) == iota((n, n), 1), column, 0.0), axis=0, keepdims=True)


def coeffs_of(p, sw, sg):
    so = 1.0 - sw - sg
    return tuple(
        s * s * (1.0 / viscosity[a]) * (1.0 + compress[a] * p) for a, s in enumerate((sw, so, sg))
    )


def scatter(cell_row, values):
    match = iota((L * R, PERFS), 0) == (cell_row >> 8)
    column = to_column(cell_row.astype(f32)).astype(i32) & (C - 1)
    spread = (iota((PERFS, C), 1) == column).astype(bf16)
    return sum(
        dot(jnp.where(match, part.astype(f32), 0.0).astype(bf16), spread) for part in split3(values)
    )


def gather_cells(cell_column, fields):
    onehot = (iota((PERFS, L * R), 1) == (cell_column >> 8)).astype(bf16)
    here = iota((PERFS, C), 1) == (cell_column & (C - 1))
    picked = []
    for field in fields:
        rows = sum(dot(onehot, part) for part in split3(field))
        picked.append(jnp.sum(jnp.where(here, rows, 0.0), axis=1, keepdims=True))
    return picked


def flat(field):
    return field[...].reshape(L * R, C)


def gather_wells(table, holder, slot):
    onehot = (iota((DEVICES, PERFS), 0) == holder).astype(bf16)
    wide = sum(dot(part, onehot) for part in split3(table.T))
    return jnp.sum(jnp.where(iota((LANES, PERFS), 0) == slot, wide, 0.0), axis=0, keepdims=True)


def to_holders(holder, slot_column, columns):
    lane = iota((PERFS, LANES), 1)
    group = lane >> 4
    values = jnp.zeros((PERFS, LANES), f32)
    for g, column in columns:
        values = jnp.where(group == g, column, values)
    values = jnp.where((lane & 15) == slot_column, values, 0.0)
    onehot = (iota((DEVICES, PERFS), 0) == holder).astype(bf16)
    return sum(dot(onehot, part) for part in split3(values))


def parts_by_offset(me, well_row, values):
    offset = (me - (well_row >> 4)) & (DEVICES - 1)
    lane = jnp.where(offset == FAR, TAIL, offset * WELL_DEV) + (well_row & 15)
    column = to_column(lane.astype(f32)).astype(i32)
    onehot = (iota((PERFS, WIDTH), 1) == column).astype(bf16)
    high, middle, low = split3(values)
    rows = jnp.concatenate([high.astype(f32), middle.astype(f32), low.astype(f32), jnp.zeros((5, PERFS), f32)], axis=0)
    return jnp.sum(dot(rows.astype(bf16), onehot), axis=0, keepdims=True)


def tile_of(got, t):
    return got[pl.ds(t, DEVICES, stride=8), :]


def sum_parts(got):
    aligned = tile_of(got, 0)
    for t in range(1, TAIL // LANES):
        aligned = aligned + pltpu.roll(tile_of(got, t), DEVICES - 8 * t, 0)
    total = aligned + pltpu.roll(tile_of(got, 5), DEVICES - FAR, 0)
    for u in range(1, 8):
        total = total + pltpu.roll(pltpu.roll(aligned, DEVICES - u, 0), LANES - 16 * u, 1)
    return total


def to_everyone(tile):
    return jnp.broadcast_to(tile[None], (DEVICES, 8, LANES)).reshape(8 * DEVICES, LANES)


def rolled_row(row, shift):
    return pltpu.roll(jnp.broadcast_to(row, (8, LANES)), shift, 1)[0:1]


def shift_rows(x, first, last):
    return (
        jnp.concatenate([first, x[:-1]], axis=0),
        jnp.concatenate([x[1:], last], axis=0),
    )


def shift_columns(x, first, last):
    lane = iota(x.shape, 1)
    return (
        jnp.where(lane == 0, first, pltpu.roll(x, 1, 1)),
        jnp.where(lane == C - 1, last, pltpu.roll(x, C - 1, 1)),
    )


def lane_of(x, index):
    return pltpu.roll(x, (LANES - index) % LANES, 1)[:, 0:1]


def is_even(axis):
    return lax.axis_index(axis) % 2 == 0


def by_partner(axis, low, high):
    even = is_even(axis)
    return jnp.where(even, high, low), jnp.where(even, low, high)


def from_partner(axis, first, second):
    even = is_even(axis)
    return jnp.where(even, second, first), jnp.where(even, first, second)


def pack_columns(columns, first, second):
    n = first.shape[0]
    turned = jnp.concatenate([columns, jnp.zeros((LANES - R, LANES), f32)], axis=0).T
    first[...], second[...] = by_partner("gy", turned[0:n], turned[n : 2 * n])


def unpack_columns(first, second):
    n = first.shape[0]
    low, high = from_partner("gy", first[...], second[...])
    rows = jnp.concatenate([low, high, jnp.zeros((LANES - 2 * n, LANES), f32)], axis=0)
    return rows.T[0:R]


def write_faces(step, outs):
    row_first, row_second, col_first, col_second = outs
    lane = iota((R, LANES), 1)
    columns = jnp.zeros((R, LANES), f32)
    for l in range(L):
        x = step[l]
        pair = by_partner("gx", x[0:1], x[R - 1 : R])
        row_first[l : l + 1, :], row_second[l : l + 1, :] = pair
        columns = jnp.where(lane == l, x[:, 0:1], columns)
        columns = jnp.where(lane == L + l, x[:, C - 1 : C], columns)
    pack_columns(columns, col_first, col_second)


def start_copies(pairs, sems):
    copies = [pltpu.make_async_copy(a, b, sems.at[n]) for n, (a, b) in enumerate(pairs)]
    for c in copies:
        c.start()
    return copies


def wait_copies(copies):
    for c in copies:
        c.wait()


def layer_copies(pairs, sems, l):
    return [pltpu.make_async_copy(a, b, sems.at[n, l]) for n, (a, b) in enumerate(pairs(l))]


def faces_kernel(
    p_h, sw_h, sg_h, perm_h, row_first, row_second, col_first, col_second, p, sw, sg, perm, sems,
):
    copies = start_copies(((perm_h.at[0:2], perm), (p_h, p), (sw_h, sw), (sg_h, sg)), sems)
    lane = iota((R, LANES), 1)
    columns = jnp.zeros((R, LANES), f32)
    wait_copies(copies[:1])
    for l in range(L):
        n = 3 * L + l
        low = perm[0, l, 0:16, :].astype(f32)[0:1]
        high = perm[0, l, R - 16 : R, :].astype(f32)[15:16]
        row_first[n : n + 1, :], row_second[n : n + 1, :] = by_partner("gx", low, high)
        k = perm[1, l].astype(f32)
        columns = jnp.where(lane == n, k[:, 0:1], columns)
        columns = jnp.where(lane == 4 * L + n, k[:, C - 1 : C], columns)
    wait_copies(copies[1:])
    for l in range(L):
        for f, ref in enumerate((p, sw, sg)):
            x = ref[l]
            n = f * L + l
            pair = by_partner("gx", x[0:1], x[R - 1 : R])
            row_first[n : n + 1, :], row_second[n : n + 1, :] = pair
            columns = jnp.where(lane == n, x[:, 0:1], columns)
            columns = jnp.where(lane == 4 * L + n, x[:, C - 1 : C], columns)
    pack_columns(columns, col_first, col_second)


def start_kernel(
    cell_h, well_h, index_h, pressure_h, rate_h, p, sw, sg,
    pay, perf, info, own,
    cell_in, well_in, index_in, pressure_in, rate_in, sems,
):
    copies = start_copies(
        (
            (cell_h, cell_in), (well_h, well_in), (index_h, index_in),
            (pressure_h, pressure_in), (rate_h, rate_in),
        ),
        sems,
    )
    me = lax.axis_index("gx") * 16 + lax.axis_index("gy")
    device = jnp.full((1, PERFS), me, i32).astype(f32)
    wait_copies(copies)
    well_row = well_in[...]
    index_row = index_in[...]
    cell_float = cell_in[...].astype(f32)
    well_float = well_row.astype(f32)
    info[...] = jnp.concatenate([cell_float, well_float, index_row, device, jnp.zeros((4, PERFS), f32)], axis=0)
    blank = jnp.zeros((1, LANES - WELL_DEV), f32)
    heads = jnp.concatenate([pressure_in[...], blank], axis=1)
    rates = jnp.concatenate([rate_in[...], blank], axis=1)
    own[...] = jnp.concatenate([heads, rates, jnp.zeros((6, LANES), f32)], axis=0)
    slot_column = to_column(well_float).astype(i32) & 15
    here = gather_cells(to_column(cell_float).astype(i32), (flat(p), flat(sw), flat(sg)))
    coeffs = coeffs_of(*here)
    total = to_column(index_row) * (coeffs[0] + coeffs[1] + coeffs[2])
    sums = to_holders(well_row >> 4, slot_column, ((0, total), (1, total * here[0])))
    pay[...] = sums + rolled_row(heads, 32)
    perf[...] = jnp.broadcast_to(to_row(total), (8, PERFS))


def after_kernel(pay, *refs):
    pass


def reciprocal(x):
    r = pl.reciprocal(x, approx=True)
    return r * (2.0 - x * r)


def transmit(k, k_next):
    return k * k_next * reciprocal(k + k_next)


def neighbours(field, l, lo, rows, columns):
    hi = lo + BLOCK
    here = field[l, lo:hi, :]
    if lo > 0:
        before = field[l, lo - 1 : hi - 1, :]
    else:
        before = jnp.concatenate([rows[0], field[l, 0 : hi - 1, :]], axis=0)
    if hi < R:
        after = field[l, lo + 1 : hi + 1, :]
    else:
        after = jnp.concatenate([field[l, lo + 1 : R, :], rows[1]], axis=0)
    sides = (field[jnp.maximum(l - 1, 0), lo:hi, :], field[jnp.minimum(l + 1, L - 1), lo:hi, :])
    return (before, after) + shift_columns(here, *columns) + sides


def coeff_neighbours(coef, coef_row, a, l, lo, columns):
    rows = (coef_row[0, a, pl.ds(l, 1), :], coef_row[1, a, pl.ds(l, 1), :])
    ends = [c[lo : lo + BLOCK] for c in columns[a]]
    return neighbours(coef.at[a], l, lo, rows, ends)


def coeff_columns(coef_col, l):
    return [(lane_of(coef_col[a], l), lane_of(coef_col[a], 4 * L + l)) for a in range(3)]


def inner_neighbours(step, l, lo):
    blank = jnp.zeros((1, C), f32)
    return neighbours(step, l, lo, (blank, blank), (0.0, 0.0))


def step_neighbours(step, row_lo, row_hi, columns, l, lo):
    rows = (row_lo[pl.ds(l, 1), :], row_hi[pl.ds(l, 1), :])
    ends = [lane_of(columns, n)[lo : lo + BLOCK] for n in (l, L + l)]
    return neighbours(step, l, lo, rows, ends)


def face_terms(tx, ty, tz, l, rows):
    return (tx[0, l, rows, :], tx[1, l, rows, :], ty[0, l, rows, :], ty[1, l, rows, :], tz[l, rows, :], tz[l + 1, rows, :])


def halves(pairs):
    parts = []
    for half in range(2):
        for a, b, dim in pairs:
            count = a.shape[dim]
            middle = L // 2 + 1
            span = pl.ds(0, middle) if half == 0 else pl.ds(middle, count - middle)
            index = (slice(None),) * dim + (span,)
            parts.append((a.at[index], b.at[index]))
    return parts


def add_faces(field, l, low, high, columns):
    lane = iota((R, LANES), 1)
    field[l, :, 0:LANES] += jnp.where(lane == 0, columns[:, l : l + 1], 0.0)
    field[l, :, C - LANES : C] += jnp.where(lane == LANES - 1, columns[:, L + l : L + l + 1], 0.0)
    field[l, 0:1, :] += low
    field[l, R - 1 : R, :] += high


def end_columns(columns, l, first, last):
    lane = iota((R, LANES), 1)
    return jnp.where(lane == l, first, jnp.where(lane == L + l, last, columns))


def setup_kernel(
    info, row_first, row_second, col_first, col_second, p, sw, sg, por_h, mass_h, perm_h,
    coef_row, coef_col, base, head, coef_h, tx_h, ty_h, tz_h, weight_h, res_h, diag_h,
    por, mass, perm, coef, tx, ty, tz, weight, res, diag, index_sum, row_lo, row_hi,
    sems, sems_t, sems_out,
):
    copies = start_copies(((perm_h, perm), (por_h, por), (mass_h, mass)), sems)
    index_sum[...] = scatter(info[0:1].astype(i32), info[2:3]).reshape(L, R, C)
    row_lo[...], row_hi[...] = from_partner("gx", row_first[...], row_second[...])
    for side, ref in enumerate((row_lo, row_hi)):
        for a, c in enumerate(coeffs_of(ref[0:L], ref[L : 2 * L], ref[2 * L : 3 * L])):
            coef_row[side, a] = c
    columns = unpack_columns(col_first, col_second)
    for a, c in enumerate(
        coeffs_of(columns, pltpu.roll(columns, LANES - L, 1), pltpu.roll(columns, LANES - 2 * L, 1))
    ):
        coef_col[a] = c
    lane = iota((R, C), 1)
    me = info[3:4, 0:1].astype(i32)
    gx = me >> 4
    gy = me & 15
    inside = [jnp.where(t, 1.0, 0.0) for t in (gx > 0, gx < 7, gy > 0, gy < 15)]
    wait_copies(copies[:1])

    def first(l, carry):
        for a, c in enumerate(coeffs_of(p[l], sw[l], sg[l])):
            coef[a, l] = c
        k = perm[0, l].astype(f32)
        n = 3 * L + l
        edge = row_lo[pl.ds(n, 1), :] * inside[0]
        before = transmit(k, jnp.concatenate([edge, k[:-1]], axis=0))
        edge = row_hi[pl.ds(n, 1), :] * inside[1]
        tx[0, l] = before
        tx[1, l] = jnp.concatenate([before[1:], transmit(k[R - 1 : R], edge)], axis=0)
        k = perm[1, l].astype(f32)
        edge = lane_of(columns, n) * inside[2]
        before = transmit(k, jnp.where(lane == 0, edge, pltpu.roll(k, 1, 1)))
        edge = lane_of(columns, 4 * L + n) * inside[3]
        ty[0, l] = before
        ty[1, l] = jnp.where(lane == C - 1, transmit(k[:, C - 1 : C], edge), pltpu.roll(before, C - 1, 1))
        k = perm[2, l].astype(f32)
        under = perm[2, jnp.maximum(l - 1, 0)].astype(f32)
        tz[l] = jnp.where(l > 0, layer_ratio, 0.0) * transmit(k, under)
        return carry

    lax.fori_loop(0, L, first, 0)
    tz[L] = jnp.zeros((R, C), f32)
    saved = start_copies(((coef, coef_h), (tx, tx_h), (ty, ty_h), (tz, tz_h)), sems_t)
    wait_copies(copies[1:])

    def outs(l):
        return (
            (weight.at[:, l], weight_h.at[:, l]),
            (res.at[:, l], res_h.at[:, l]), (diag.at[:, l], diag_h.at[:, l]),
        )

    def second(l, carry):
        rows = (row_lo[pl.ds(l, 1), :], row_hi[pl.ds(l, 1), :])
        ends = lane_of(columns, l), lane_of(columns, 4 * L + l)
        sides_of = coeff_columns(coef_col, l)
        for lo in range(0, R, BLOCK):
            at = slice(lo, lo + BLOCK)
            here = p[l, at, :]
            nexts = neighbours(p, l, lo, rows, [e[at] for e in ends])
            faces = face_terms(tx, ty, tz, l, at)
            drops = [t * (here - q) for t, q in zip(faces, nexts)]
            face_sum = sum(faces)
            drop_sum = sum(drops)
            porous = volume_scale * por[l, at, :]
            water, gas = (sw[l, at, :], sg[l, at, :])
            sats = (water, 1.0 - water - gas, gas)
            indices = index_sum[l, at, :]
            diagonals, residuals, inverses, cs = [], [], [], []
            for a in range(3):
                c = coef[a, l, at, :]
                ab = c * face_sum
                net = c * drop_sum
                for t, d, s in zip(faces, drops, coeff_neighbours(coef, coef_row, a, l, lo, sides_of)):
                    ab = ab + t * s
                    net = net + d * s
                b = 1.0 + compress[a] * here
                stored = porous * sats[a]
                diagonals.append(compress[a] * stored + ab + c * indices)
                residuals.append(b * stored - volume_scale * mass[a, l, at, :] + net + c * (indices * here))
                inverses.append(reciprocal(porous * b))
                cs.append(c)
            inverse_total = reciprocal(sum(d * v for d, v in zip(diagonals, inverses)))
            weights = [v * inverse_total for v in inverses]
            base[l, at, :] = -sum(w * r for w, r in zip(weights, residuals))
            head[l, at, :] = sum(w * c for w, c in zip(weights, cs))
            for a in range(3):
                weight[a, l, at, :] = weights[a]
                res[a, l, at, :] = residuals[a]
            diag[0, l, at, :] = diagonals[0]
            diag[1, l, at, :] = diagonals[2]
        for c in layer_copies(outs, sems_out, l):
            c.start()
        return carry

    lax.fori_loop(0, L, second, 0)
    wait_copies(saved)
    for l in range(L):
        wait_copies(layer_copies(outs, sems_out, l))


def first_kernel(
    got, info, own, base, head, row_first, row_second, col_first, col_second, mine, well_residual, spread, step,
):
    lane = iota((1, LANES), 1)
    sums = jnp.sum(got[...], axis=0, keepdims=True)
    total = jnp.where(lane < WELL_DEV, sums, 1.0)
    flow = rolled_row(sums, LANES - 16)
    residual = jnp.where(lane < WELL_DEV, flow - total * own[0:1] - own[1:2], 0.0)
    inverse = jnp.where(lane < WELL_DEV, 1.0 / total, 0.0)
    mine[...] = jnp.concatenate([residual, inverse, jnp.zeros((6, LANES), f32)], axis=0)
    well_residual[...] = residual[:, 0:WELL_DEV]
    cell_row = info[0:1].astype(i32)
    well_row = info[1:2].astype(i32)
    heads = gather_wells(got[...], well_row >> 4, (well_row & 15) + 32)
    spread[...] = scatter(cell_row, info[2:3] * heads).reshape(L, R, C)
    step[...] = base[...] + head[...] * spread[...]
    write_faces(step, (row_first, row_second, col_first, col_second))


def first_flow_kernel(info, perf, mine, step, pay):
    well_row = info[1:2].astype(i32)
    here = to_row(gather_cells(to_column(info[0:1]).astype(i32), (flat(step),))[0])
    parts = parts_by_offset(info[3:4].astype(i32), well_row, perf[0:1] * here)
    packed = parts[:, TAIL:]
    residual = mine[0:1]
    inverse = mine[1:2]
    for n, row in enumerate((residual * inverse, residual, inverse)):
        packed = packed + rolled_row(row, 16 * (n + 1))
    tiles = [parts[:, LANES * t : LANES * (t + 1)] for t in range(5)]
    pay[...] = to_everyone(jnp.concatenate(tiles + [packed, jnp.zeros((2, LANES), f32)], axis=0))


def grid_kernel(
    coef_row, coef_col, head, spread, step,
    coef_h, tx_h, ty_h, tz_h, weight_h, res_h,
    ahead, end_row, end_col, residual_h, gain_h,
    coef, tx, ty, tz, weight, res, residual, gain, sems, sems_out,
):
    copies = start_copies(
        halves(((coef_h, coef, 1), (tx_h, tx, 1), (ty_h, ty, 1), (tz_h, tz, 0), (weight_h, weight, 1), (res_h, res, 1))),
        sems,
    )
    wait_copies(copies[:6])

    def outs(l):
        return (
            (residual.at[:, l], residual_h.at[:, l]), (gain.at[:, l], gain_h.at[:, l]),
        )

    def layer(l, ends):
        sides_of = coeff_columns(coef_col, l)
        for lo in range(0, R, BLOCK):
            at = slice(lo, lo + BLOCK)
            nexts = inner_neighbours(step, l, lo)
            faces = face_terms(tx, ty, tz, l, at)
            wells = spread[l, at, :]
            mixes = [head[l, at, :]] * 6
            for a in range(3):
                w = weight[a, l, at, :]
                sides = coeff_neighbours(coef, coef_row, a, l, lo, sides_of)
                mixes = [m + w * s for m, s in zip(mixes, sides)]
                residual[a, l, at, :] = res[a, l, at, :] - coef[a, l, at, :] * wells
            total = step[l, at, :]
            for j in range(6):
                g = faces[j] * mixes[j]
                gain[j, l, at, :] = g
                total = total + g * nexts[j]
            ahead[l, at, :] = total
        end_row[0, pl.ds(l, 1), :] = gain[0, l, 0:1, :]
        end_row[1, pl.ds(l, 1), :] = gain[1, l, R - 1 : R, :]
        for c in layer_copies(outs, sems_out, l):
            c.start()
        return end_columns(ends, l, gain[2, l, :, 0:LANES][:, 0:1], gain[3, l, :, C - LANES : C][:, LANES - 1 : LANES])

    ends = lax.fori_loop(0, L // 2, layer, jnp.zeros((R, LANES), f32))
    wait_copies(copies[6:])
    end_col[...] = lax.fori_loop(L // 2, L, layer, ends)
    for l in range(L):
        wait_copies(layer_copies(outs, sems_out, l))


def second_kernel(
    got, info, ahead, head, end_row, end_col, row_first, row_second, col_first, col_second,
    out_row_first, out_row_second, out_col_first, out_col_second, step,
):
    cell_row = info[0:1].astype(i32)
    well_row = info[1:2].astype(i32)
    moves = gather_wells(tile_of(got, 5), well_row >> 4, (well_row & 15) + 16)
    wells = scatter(cell_row, info[2:3] * moves).reshape(L, R, C)
    step[...] = ahead[...] + head[...] * wells
    columns = end_col[...] * unpack_columns(col_first, col_second)
    low, high = from_partner("gx", row_first[...], row_second[...])
    low = end_row[0] * low
    high = end_row[1] * high
    for l in range(L):
        add_faces(step, l, low[l : l + 1], high[l : l + 1], columns)
    write_faces(step, (out_row_first, out_row_second, out_col_first, out_col_second))


def wells_kernel(
    got, info, perf, step, gain_h, table, parts, spread, gain, sems,
):
    copies = start_copies(((gain_h, gain),), sems)
    tail = tile_of(got, 5)
    residuals = pltpu.roll(tail, LANES - 32, 1)
    inverses = pltpu.roll(tail, LANES - 48, 1)
    table[0] = residuals
    table[1] = inverses
    cell_row = info[0:1].astype(i32)
    well_row = info[1:2].astype(i32)
    valid = iota((DEVICES, LANES), 1) < WELL_DEV
    moves = jnp.where(valid, (sum_parts(got) + residuals) * inverses, 0.0)
    values = gather_wells(moves, well_row >> 4, well_row & 15)
    spread[...] = scatter(cell_row, info[2:3] * values).reshape(L, R, C)
    here = to_row(gather_cells(to_column(info[0:1]).astype(i32), (flat(step),))[0])
    flows = parts_by_offset(info[3:4].astype(i32), well_row, perf[0:1] * here)
    tiles = [flows[:, LANES * t : LANES * (t + 1)] for t in range(6)]
    parts[...] = jnp.concatenate(tiles + [jnp.zeros((2, LANES), f32)], axis=0)
    wait_copies(copies)


def third_kernel(
    spread, old, base, gain, head, row_first, row_second, col_first, col_second,
    out_row_first, out_row_second, out_col_first, out_col_second, step, row_lo, row_hi,
):
    columns = unpack_columns(col_first, col_second)
    row_lo[...], row_hi[...] = from_partner("gx", row_first[...], row_second[...])

    def layer(l, carry):
        for lo in range(0, R, BLOCK):
            at = slice(lo, lo + BLOCK)
            nexts = step_neighbours(old, row_lo, row_hi, columns, l, lo)
            total = base[l, at, :] + head[l, at, :] * spread[l, at, :]
            for j in range(6):
                total = total + gain[j, l, at, :] * nexts[j]
            step[l, at, :] = total
        return carry

    lax.fori_loop(0, L, layer, 0)
    write_faces(step, (out_row_first, out_row_second, out_col_first, out_col_second))


def third_flow_kernel(info, perf, parts, step, pay):
    here = gather_cells(to_column(info[0:1]).astype(i32), (flat(step),))[0]
    well_row = info[1:2].astype(i32)
    slot_column = to_column(info[1:2]).astype(i32) & 15
    pay[...] = to_everyone(parts[...])
    pay[pl.ds(6, DEVICES, stride=8), :] = to_holders(
        well_row >> 4, slot_column, ((0, to_column(perf[0:1]) * here),)
    )


def last_grid_kernel(
    coef_row, coef_col, head, step, gain_row, gain_col,
    p_h, por_h, coef_h, tx_h, ty_h, tz_h, weight_h, diag_h, residual_h,
    end_row, end_col, ahead_h, slope_h,
    p, por, coef, tx, ty, tz, weight, diag, residual, ahead, slope, sems, sems_out,
):
    copies = start_copies(
        halves(
            (
                (p_h, p, 0), (por_h, por, 0), (coef_h, coef, 1), (tx_h, tx, 1), (ty_h, ty, 1), (tz_h, tz, 0),
                (weight_h, weight, 1), (diag_h, diag, 1), (residual_h, residual, 1),
            )
        ),
        sems,
    )
    wait_copies(copies[:9])

    def outs(l):
        return ((ahead.at[:, l], ahead_h.at[:, l]), (slope.at[:, l], slope_h.at[:, l]))

    def layer(l, ends):
        sides_of = coeff_columns(coef_col, l)
        gains = lane_of(gain_col[...], l), lane_of(gain_col[...], L + l)
        pairs = [([], []), ([], [])]
        for lo in range(0, R, BLOCK):
            at = slice(lo, lo + BLOCK)
            nexts = inner_neighbours(step, l, lo)
            faces = face_terms(tx, ty, tz, l, at)
            flows = [t * q for t, q in zip(faces, nexts)]
            flow_sum = sum(flows)
            rights, cs, sides = [], [], []
            for a in range(3):
                c = coef[a, l, at, :]
                total = c * flow_sum - residual[a, l, at, :]
                sides.append(coeff_neighbours(coef, coef_row, a, l, lo, sides_of))
                for v, s in zip(flows, sides[a]):
                    total = total + v * s
                rights.append(total)
                cs.append(c)
            z = sum(weight[a, l, at, :] * rights[a] for a in range(3))
            h = head[l, at, :]
            porous = volume_scale * por[l, at, :]
            inverses = [reciprocal(porous * (1.0 + compress[a] * p[l, at, :])) for a in (0, 2)]
            ahead[0, l, at, :] = z
            for n, a in enumerate((0, 2)):
                d = diag[n, l, at, :]
                inverse = inverses[n]
                ahead[1 + n, l, at, :] = (rights[a] - d * z) * inverse
                slope[n, l, at, :] = (cs[a] - d * h) * inverse
                for side in range(2):
                    if lo == (0, R - BLOCK)[side]:
                        row = slice(0, 1) if side == 0 else slice(BLOCK - 1, BLOCK)
                        face = faces[side][row] * (cs[a][row] + sides[a][side][row])
                        end_row[side, n, pl.ds(l, 1), :] = (
                            face - d[row] * gain_row[side, pl.ds(l, 1), :]
                        ) * inverse[row]
                    col = slice(0, 1) if side == 0 else slice(C - 1, C)
                    face = faces[2 + side][:, col] * (cs[a][:, col] + sides_of[a][side][at])
                    pairs[n][side].append((face - d[:, col] * gains[side][at]) * inverse[:, col])
        for c in layer_copies(outs, sems_out, l):
            c.start()
        return tuple(
            end_columns(ends[n], l, *(jnp.concatenate(part, axis=0) for part in pairs[n])) for n in range(2)
        )

    blank = jnp.zeros((R, LANES), f32)
    ends = lax.fori_loop(0, L // 2, layer, (blank, blank))
    wait_copies(copies[9:])
    end_col[0], end_col[1] = lax.fori_loop(L // 2, L, layer, ends)
    for l in range(L):
        wait_copies(layer_copies(outs, sems_out, l))


def final_kernel(
    got, info, table, mine, head, gain_row, gain_col, end_row, end_col, row_first, row_second, col_first, col_second,
    ahead_h, slope_h, update_h, moved, ahead, slope, update, sems, sems_out,
):
    copies = start_copies(((ahead_h, ahead), (slope_h, slope)), sems)
    flow = jnp.sum(tile_of(got, 6), axis=0, keepdims=True)
    moved[...] = ((flow + mine[0:1]) * mine[1:2])[:, 0:WELL_DEV]
    cell_row = info[0:1].astype(i32)
    well_row = info[1:2].astype(i32)
    valid = iota((DEVICES, LANES), 1) < WELL_DEV
    moves = jnp.where(valid, (sum_parts(got) + table[0]) * table[1], 0.0)
    values = gather_wells(moves, well_row >> 4, well_row & 15)
    wells = scatter(cell_row, info[2:3] * values).reshape(L, R, C)
    halo = unpack_columns(col_first, col_second)
    lows, highs = from_partner("gx", row_first[...], row_second[...])
    columns = (gain_col[...] * halo, end_col[0] * halo, end_col[1] * halo)
    wait_copies(copies)

    def outs(l):
        return ((update.at[:, l], update_h.at[:, l]),)

    for l in range(L):
        low = lows[l : l + 1]
        high = highs[l : l + 1]
        for n in range(3):
            rows = [gain_row[side, l : l + 1, :] if n == 0 else end_row[side, n - 1, l : l + 1, :] for side in range(2)]
            update[n, l] = ahead[n, l] + (head[l] if n == 0 else slope[n - 1, l]) * wells[l]
            add_faces(update.at[n], l, rows[0] * low, rows[1] * high, columns[n])
        layer_copies(outs, sems_out, l)[0].start()
    for l in range(L):
        wait_copies(layer_copies(outs, sems_out, l))


def call(kernel, outs, ins, operands, scratch=(), flops=0):
    shapes = tuple(
        pltpu.VMEM(s, f32) if w is VM else pltpu.HBM(s, f32) if w is HB else jax.ShapeDtypeStruct(s, f32)
        for s, w in outs
    )
    moved = 4 * sum(int(x.size) for x in operands)
    operands = [
        pltpu.with_memory_space_constraint(x, pltpu.HBM) if w is HB else x for x, w in zip(operands, ins)
    ]
    return pl.pallas_call(
        kernel,
        out_shape=shapes,
        in_specs=ins,
        out_specs=tuple(w or VM for _, w in outs),
        scratch_shapes=[pltpu.VMEM(x, f32) if type(x) is tuple else x for x in scratch],
        compiler_params=pltpu.CompilerParams(vmem_limit_bytes=40 * 1024 * 1024),
        cost_estimate=pl.CostEstimate(flops=flops, bytes_accessed=moved, transcendentals=0),
    )(*operands)


FIELD = (L, R, C)
TWO, THREE, SIX, FACED = ((2,) + FIELD, (3,) + FIELD, (6,) + FIELD, (L + 1, R, C))
FACES = (((L, C), VM), ((L, C), VM), ((L, LANES), VM), ((L, LANES), VM))
WIDE_FACES = (((4 * L, C), VM), ((4 * L, C), VM), ((4 * L, LANES), VM), ((4 * L, LANES), VM))
SMALL = (8, LANES)
PAY = ((8 * DEVICES, LANES), None)
sem = pltpu.SemaphoreType.DMA


def exchange(array):
    return lax.all_to_all(array, AXES, split_axis=0, concat_axis=0, tiled=True)


def exchange_tiles(array):
    return exchange(array.reshape(DEVICES, 8, LANES)).reshape(8 * DEVICES, LANES)


def halo_of(faces):
    row_first, row_second, col_first, col_second = faces
    got = []
    for axis, first, second in (("gx", row_first, row_second), ("gy", col_first, col_second)):
        count = lax.axis_size(axis)
        got.append(lax.ppermute(first, axis, [(i, i ^ 1) for i in range(count)]))
        got.append(lax.ppermute(second, axis, [(i, (i - 1 + 2 * (i % 2)) % count) for i in range(count)]))
    return got


def local(
    pressure, sat_water, sat_gas, old_mass, perm, porosity,
    perf_well, perf_cell, perf_index, well_pressure, well_rate,
):
    *faces, p, sw, sg = call(
        faces_kernel,
        WIDE_FACES + ((FIELD, VM), (FIELD, VM), (FIELD, VM)),
        [HB] * 4,
        (pressure, sat_water, sat_gas, perm),
        [pltpu.VMEM(TWO, bf16), sem((4,))],
    )
    halo = halo_of(faces)
    pay, perf, info, own = call(
        start_kernel,
        (((DEVICES, LANES), VM), ((8, PERFS), VM), ((8, PERFS), VM), (SMALL, VM)),
        [HB] * 5 + [VM] * 3,
        (
            perf_cell.reshape(1, PERFS), perf_well.reshape(1, PERFS), perf_index.reshape(1, PERFS),
            well_pressure.reshape(1, WELL_DEV), well_rate.reshape(1, WELL_DEV), p, sw, sg,
        ),
        [
            pltpu.VMEM((1, PERFS), i32), pltpu.VMEM((1, PERFS), i32), (1, PERFS),
            (1, WELL_DEV), (1, WELL_DEV), sem((5,)),
        ],
    )
    pay, *halo = pl.pallas_call(
        after_kernel,
        out_shape=tuple(pltpu.VMEM(x.shape, f32) for x in (pay, *halo)),
        in_specs=[pl.BlockSpec(memory_space=pl.ANY)] * 5,
        out_specs=(pl.BlockSpec(memory_space=pl.ANY),) * 5,
        input_output_aliases={n: n for n in range(5)},
    )(pay, *halo)
    got = exchange(pay)
    coef_row, coef_col, base, head, coef, tx, ty, tz, weight, res, diag = call(
        setup_kernel,
        (
            ((2, 3, L, C), VM), ((3, R, LANES), VM), (FIELD, VM), (FIELD, VM), (THREE, HB), (TWO, HB), (TWO, HB),
            (FACED, HB), (THREE, HB), (THREE, HB), (TWO, HB),
        ),
        [VM] * 8 + [HB] * 3,
        (info, *halo, p, sw, sg, porosity, old_mass, perm),
        [
            FIELD, THREE, pltpu.VMEM(THREE, bf16), THREE, TWO, TWO, FACED,
            THREE, THREE, TWO, FIELD, (4 * L, C), (4 * L, C), sem((3,)), sem((4,)), sem((3, L)),
        ],
        flops=400 * L * R * C,
    )
    *faces, mine, well_residual, spread, start = call(
        first_kernel,
        FACES + ((SMALL, VM), ((1, WELL_DEV), None), (FIELD, VM), (FIELD, VM)),
        [VM] * 5,
        (got, info, own, base, head),
    )
    halo = halo_of(faces)
    (pay,) = call(first_flow_kernel, (PAY,), [VM] * 4, (info, perf, mine, start))
    got = exchange_tiles(pay)
    fields = (coef, tx, ty, tz, weight)
    ahead, gain_row, gain_col, residual, gain = call(
        grid_kernel,
        ((FIELD, VM), ((2, L, C), VM), ((R, LANES), VM), (THREE, HB), (SIX, HB)),
        [VM] * 5 + [HB] * 6,
        (coef_row, coef_col, head, spread, start, *fields, res),
        [THREE, TWO, TWO, FACED, THREE, THREE, THREE, SIX, sem((12,)), sem((2, L))],
        flops=100 * L * R * C,
    )
    *faces, step = call(
        second_kernel,
        FACES + ((FIELD, VM),),
        [VM] * 10,
        (got, info, ahead, head, gain_row, gain_col, *halo),
    )
    halo = halo_of(faces)
    table, parts, spread, gain_near = call(
        wells_kernel,
        (((2, DEVICES, LANES), VM), (SMALL, VM), (FIELD, VM), (SIX, VM)),
        [VM] * 4 + [HB],
        (got, info, perf, step, gain),
        [sem((1,))],
    )
    *faces, step = call(
        third_kernel,
        FACES + ((FIELD, VM),),
        [VM] * 9,
        (spread, step, start, gain_near, head, *halo),
        [(L, C), (L, C)],
    )
    halo = halo_of(faces)
    (pay,) = call(third_flow_kernel, (PAY,), [VM] * 4, (info, perf, parts, step))
    got = exchange_tiles(pay)
    end_row, end_col, ahead, slope = call(
        last_grid_kernel,
        (((2, 2, L, C), VM), ((2, R, LANES), VM), (THREE, HB), (TWO, HB)),
        [VM] * 6 + [HB] * 9,
        (coef_row, coef_col, head, step, gain_row, gain_col, pressure, porosity, *fields, diag, residual),
        [FIELD, FIELD, THREE, TWO, TWO, FACED, THREE, TWO, THREE, THREE, TWO, sem((18,)), sem((2, L))],
        flops=150 * L * R * C,
    )
    update, moved = call(
        final_kernel,
        ((THREE, HB), ((1, WELL_DEV), None)),
        [VM] * 13 + [HB] * 2,
        (got, info, table, mine, head, gain_row, gain_col, end_row, end_col, *halo, ahead, slope),
        [THREE, TWO, THREE, sem((2,)), sem((1, L))],
    )
    return residual, well_residual.reshape(WELL_DEV), update, moved.reshape(WELL_DEV)


def solution(mesh):
    return jax.shard_map(
        local,
        mesh=mesh,
        in_specs=(
            P(None, "gx", "gy"),
            P(None, "gx", "gy"),
            P(None, "gx", "gy"),
            P(None, None, "gx", "gy"),
            P(None, None, "gx", "gy"),
            P(None, "gx", "gy"),
            P(("gx", "gy")),
            P(("gx", "gy")),
            P(("gx", "gy")),
            P(("gx", "gy")),
            P(("gx", "gy")),
        ),
        out_specs=(
            P(None, None, "gx", "gy"),
            P(("gx", "gy")),
            P(None, None, "gx", "gy"),
            P(("gx", "gy")),
        ),
        check_vma=False,
    )
```

```python
import jax
import jax.numpy as jnp
from jax import lax
from jax.experimental import pallas as pl
from jax.experimental.pallas import tpu as pltpu
from jax.sharding import PartitionSpec as P

f32 = jnp.float32
bf16 = jnp.bfloat16
i32 = jnp.int32

compress = (0.05, 0.02, 0.2)
viscosity = (0.5, 2.0, 0.1)
volume_scale = 4.0
layer_ratio = 0.1
AXES = ("gx", "gy")
DEVICES = 128
WELL_DEV = 16
REACH = 40
FAR = 64
TAIL = REACH * WELL_DEV
WIDTH = TAIL + 128
LANES = 128
L, R, C = 8, 64, 256
PERFS = 256
BLOCK = 8
VM = pl.BlockSpec(memory_space=pltpu.VMEM)
HB = pl.BlockSpec(memory_space=pltpu.HBM)


def iota(shape, dim):
    return lax.broadcasted_iota(i32, shape, dim)


def split3(x):
    high = x.astype(bf16)
    rest = x - high.astype(f32)
    middle = rest.astype(bf16)
    low = (rest - middle.astype(f32)).astype(bf16)
    return high, middle, low


def dot(a, b):
    return jnp.dot(a, b, preferred_element_type=f32)


def to_column(row):
    n = row.shape[1]
    return jnp.sum(jnp.where(iota((n, n), 0) == iota((n, n), 1), row, 0.0), axis=1, keepdims=True)


def to_row(column):
    n = column.shape[0]
    return jnp.sum(jnp.where(iota((n, n), 0) == iota((n, n), 1), column, 0.0), axis=0, keepdims=True)


def coeffs_of(p, sw, sg):
    so = 1.0 - sw - sg
    return tuple(
        s * s * (1.0 / viscosity[a]) * (1.0 + compress[a] * p) for a, s in enumerate((sw, so, sg))
    )


def scatter(cell_row, values):
    match = iota((L * R, PERFS), 0) == (cell_row >> 8)
    column = to_column(cell_row.astype(f32)).astype(i32) & (C - 1)
    spread = (iota((PERFS, C), 1) == column).astype(bf16)
    return sum(
        dot(jnp.where(match, part.astype(f32), 0.0).astype(bf16), spread) for part in split3(values)
    )


def gather_cells(cell_column, fields):
    onehot = (iota((PERFS, L * R), 1) == (cell_column >> 8)).astype(bf16)
    here = iota((PERFS, C), 1) == (cell_column & (C - 1))
    picked = []
    for field in fields:
        rows = sum(dot(onehot, part) for part in split3(field))
        picked.append(jnp.sum(jnp.where(here, rows, 0.0), axis=1, keepdims=True))
    return picked


def flat(field):
    return field[...].reshape(L * R, C)


def gather_wells(table, holder, slot):
    onehot = (iota((DEVICES, PERFS), 0) == holder).astype(bf16)
    wide = sum(dot(part, onehot) for part in split3(table.T))
    return jnp.sum(jnp.where(iota((LANES, PERFS), 0) == slot, wide, 0.0), axis=0, keepdims=True)


def to_holders(holder, slot_column, columns):
    lane = iota((PERFS, LANES), 1)
    group = lane >> 4
    values = jnp.zeros((PERFS, LANES), f32)
    for g, column in columns:
        values = jnp.where(group == g, column, values)
    values = jnp.where((lane & 15) == slot_column, values, 0.0)
    onehot = (iota((DEVICES, PERFS), 0) == holder).astype(bf16)
    return sum(dot(onehot, part) for part in split3(values))


def parts_by_offset(me, well_row, values):
    offset = (me - (well_row >> 4)) & (DEVICES - 1)
    lane = jnp.where(offset == FAR, TAIL, offset * WELL_DEV) + (well_row & 15)
    column = to_column(lane.astype(f32)).astype(i32)
    onehot = (iota((PERFS, WIDTH), 1) == column).astype(bf16)
    high, middle, low = split3(values)
    rows = jnp.concatenate([high.astype(f32), middle.astype(f32), low.astype(f32), jnp.zeros((5, PERFS), f32)], axis=0)
    return jnp.sum(dot(rows.astype(bf16), onehot), axis=0, keepdims=True)


def tile_of(got, t):
    return got[pl.ds(t, DEVICES, stride=8), :]


def sum_parts(got):
    aligned = tile_of(got, 0)
    for t in range(1, TAIL // LANES):
        aligned = aligned + pltpu.roll(tile_of(got, t), DEVICES - 8 * t, 0)
    total = aligned + pltpu.roll(tile_of(got, 5), DEVICES - FAR, 0)
    for u in range(1, 8):
        total = total + pltpu.roll(pltpu.roll(aligned, DEVICES - u, 0), LANES - 16 * u, 1)
    return total


def to_everyone(tile):
    return jnp.broadcast_to(tile[None], (DEVICES, 8, LANES)).reshape(8 * DEVICES, LANES)


def rolled_row(row, shift):
    return pltpu.roll(jnp.broadcast_to(row, (8, LANES)), shift, 1)[0:1]


def shift_rows(x, first, last):
    return (
        jnp.concatenate([first, x[:-1]], axis=0),
        jnp.concatenate([x[1:], last], axis=0),
    )


def shift_columns(x, first, last):
    lane = iota(x.shape, 1)
    return (
        jnp.where(lane == 0, first, pltpu.roll(x, 1, 1)),
        jnp.where(lane == C - 1, last, pltpu.roll(x, C - 1, 1)),
    )


def lane_of(x, index):
    return pltpu.roll(x, (LANES - index) % LANES, 1)[:, 0:1]


def is_even(axis):
    return lax.axis_index(axis) % 2 == 0


def by_partner(axis, low, high):
    even = is_even(axis)
    return jnp.where(even, high, low), jnp.where(even, low, high)


def from_partner(axis, first, second):
    even = is_even(axis)
    return jnp.where(even, second, first), jnp.where(even, first, second)


def pack_columns(columns, first, second):
    n = first.shape[0]
    turned = jnp.concatenate([columns, jnp.zeros((LANES - R, LANES), f32)], axis=0).T
    first[...], second[...] = by_partner("gy", turned[0:n], turned[n : 2 * n])


def unpack_columns(first, second):
    n = first.shape[0]
    low, high = from_partner("gy", first[...], second[...])
    rows = jnp.concatenate([low, high, jnp.zeros((LANES - 2 * n, LANES), f32)], axis=0)
    return rows.T[0:R]


def write_faces(step, outs):
    row_first, row_second, col_first, col_second = outs
    lane = iota((R, LANES), 1)
    columns = jnp.zeros((R, LANES), f32)
    for l in range(L):
        x = step[l]
        pair = by_partner("gx", x[0:1], x[R - 1 : R])
        row_first[l : l + 1, :], row_second[l : l + 1, :] = pair
        columns = jnp.where(lane == l, x[:, 0:1], columns)
        columns = jnp.where(lane == L + l, x[:, C - 1 : C], columns)
    pack_columns(columns, col_first, col_second)


def start_copies(pairs, sems):
    copies = [pltpu.make_async_copy(a, b, sems.at[n]) for n, (a, b) in enumerate(pairs)]
    for c in copies:
        c.start()
    return copies


def wait_copies(copies):
    for c in copies:
        c.wait()


def layer_copies(pairs, sems, l):
    return [pltpu.make_async_copy(a, b, sems.at[n, l]) for n, (a, b) in enumerate(pairs(l))]


def faces_kernel(
    p_h, sw_h, sg_h, perm_h, row_first, row_second, col_first, col_second, p, sw, sg, perm, sems,
):
    copies = start_copies(((perm_h.at[0:2], perm), (p_h, p), (sw_h, sw), (sg_h, sg)), sems)
    lane = iota((R, LANES), 1)
    columns = jnp.zeros((R, LANES), f32)
    wait_copies(copies[:1])
    for l in range(L):
        n = 3 * L + l
        low = perm[0, l, 0:16, :].astype(f32)[0:1]
        high = perm[0, l, R - 16 : R, :].astype(f32)[15:16]
        row_first[n : n + 1, :], row_second[n : n + 1, :] = by_partner("gx", low, high)
        k = perm[1, l].astype(f32)
        columns = jnp.where(lane == n, k[:, 0:1], columns)
        columns = jnp.where(lane == 4 * L + n, k[:, C - 1 : C], columns)
    wait_copies(copies[1:])
    for l in range(L):
        for f, ref in enumerate((p, sw, sg)):
            x = ref[l]
            n = f * L + l
            pair = by_partner("gx", x[0:1], x[R - 1 : R])
            row_first[n : n + 1, :], row_second[n : n + 1, :] = pair
            columns = jnp.where(lane == n, x[:, 0:1], columns)
            columns = jnp.where(lane == 4 * L + n, x[:, C - 1 : C], columns)
    pack_columns(columns, col_first, col_second)


def start_kernel(
    cell_h, well_h, index_h, pressure_h, rate_h, p, sw, sg,
    pay, perf, info, own,
    cell_in, well_in, index_in, pressure_in, rate_in, sems,
):
    copies = start_copies(
        (
            (cell_h, cell_in), (well_h, well_in), (index_h, index_in),
            (pressure_h, pressure_in), (rate_h, rate_in),
        ),
        sems,
    )
    me = lax.axis_index("gx") * 16 + lax.axis_index("gy")
    device = jnp.full((1, PERFS), me, i32).astype(f32)
    wait_copies(copies)
    well_row = well_in[...]
    index_row = index_in[...]
    cell_float = cell_in[...].astype(f32)
    well_float = well_row.astype(f32)
    info[...] = jnp.concatenate([cell_float, well_float, index_row, device, jnp.zeros((4, PERFS), f32)], axis=0)
    blank = jnp.zeros((1, LANES - WELL_DEV), f32)
    heads = jnp.concatenate([pressure_in[...], blank], axis=1)
    rates = jnp.concatenate([rate_in[...], blank], axis=1)
    own[...] = jnp.concatenate([heads, rates, jnp.zeros((6, LANES), f32)], axis=0)
    slot_column = to_column(well_float).astype(i32) & 15
    here = gather_cells(to_column(cell_float).astype(i32), (flat(p), flat(sw), flat(sg)))
    coeffs = coeffs_of(*here)
    total = to_column(index_row) * (coeffs[0] + coeffs[1] + coeffs[2])
    sums = to_holders(well_row >> 4, slot_column, ((0, total), (1, total * here[0])))
    pay[...] = sums + rolled_row(heads, 32)
    perf[...] = jnp.broadcast_to(to_row(total), (8, PERFS))


def after_kernel(pay, *refs):
    pass


def reciprocal(x):
    r = pl.reciprocal(x, approx=True)
    return r * (2.0 - x * r)


def transmit(k, k_next):
    return k * k_next * reciprocal(k + k_next)


def neighbours(field, l, lo, rows, columns):
    hi = lo + BLOCK
    here = field[l, lo:hi, :]
    if lo > 0:
        before = field[l, lo - 1 : hi - 1, :]
    else:
        before = jnp.concatenate([rows[0], field[l, 0 : hi - 1, :]], axis=0)
    if hi < R:
        after = field[l, lo + 1 : hi + 1, :]
    else:
        after = jnp.concatenate([field[l, lo + 1 : R, :], rows[1]], axis=0)
    sides = (field[jnp.maximum(l - 1, 0), lo:hi, :], field[jnp.minimum(l + 1, L - 1), lo:hi, :])
    return (before, after) + shift_columns(here, *columns) + sides


def coeff_neighbours(coef, coef_row, a, l, lo, columns):
    rows = (coef_row[0, a, pl.ds(l, 1), :], coef_row[1, a, pl.ds(l, 1), :])
    ends = [c[lo : lo + BLOCK] for c in columns[a]]
    return neighbours(coef.at[a], l, lo, rows, ends)


def coeff_columns(coef_col, l):
    return [(lane_of(coef_col[a], l), lane_of(coef_col[a], 4 * L + l)) for a in range(3)]


def inner_neighbours(step, l, lo):
    blank = jnp.zeros((1, C), f32)
    return neighbours(step, l, lo, (blank, blank), (0.0, 0.0))


def step_neighbours(step, row_lo, row_hi, columns, l, lo):
    rows = (row_lo[pl.ds(l, 1), :], row_hi[pl.ds(l, 1), :])
    ends = [lane_of(columns, n)[lo : lo + BLOCK] for n in (l, L + l)]
    return neighbours(step, l, lo, rows, ends)


def face_terms(tx, ty, tz, l, rows):
    return (tx[0, l, rows, :], tx[1, l, rows, :], ty[0, l, rows, :], ty[1, l, rows, :], tz[l, rows, :], tz[l + 1, rows, :])


def halves(pairs):
    parts = []
    for half in range(2):
        for a, b, dim in pairs:
            count = a.shape[dim]
            middle = L // 2 + 1
            span = pl.ds(0, middle) if half == 0 else pl.ds(middle, count - middle)
            index = (slice(None),) * dim + (span,)
            parts.append((a.at[index], b.at[index]))
    return parts


def add_faces(field, l, low, high, columns):
    lane = iota((R, LANES), 1)
    field[l, :, 0:LANES] += jnp.where(lane == 0, columns[:, l : l + 1], 0.0)
    field[l, :, C - LANES : C] += jnp.where(lane == LANES - 1, columns[:, L + l : L + l + 1], 0.0)
    field[l, 0:1, :] += low
    field[l, R - 1 : R, :] += high


def end_columns(columns, l, first, last):
    lane = iota((R, LANES), 1)
    return jnp.where(lane == l, first, jnp.where(lane == L + l, last, columns))


def setup_kernel(
    info, row_first, row_second, col_first, col_second, p, sw, sg, por_h, mass_h, perm_h,
    coef_row, coef_col, base, head, coef_h, tx_h, ty_h, tz_h, weight_h, res_h, diag_h,
    por, mass, perm, coef, tx, ty, tz, weight, res, diag, index_sum, row_lo, row_hi,
    sems, sems_t, sems_out,
):
    copies = start_copies(((perm_h, perm), (por_h, por), (mass_h, mass)), sems)
    index_sum[...] = scatter(info[0:1].astype(i32), info[2:3]).reshape(L, R, C)
    row_lo[...], row_hi[...] = from_partner("gx", row_first[...], row_second[...])
    for side, ref in enumerate((row_lo, row_hi)):
        for a, c in enumerate(coeffs_of(ref[0:L], ref[L : 2 * L], ref[2 * L : 3 * L])):
            coef_row[side, a] = c
    columns = unpack_columns(col_first, col_second)
    for a, c in enumerate(
        coeffs_of(columns, pltpu.roll(columns, LANES - L, 1), pltpu.roll(columns, LANES - 2 * L, 1))
    ):
        coef_col[a] = c
    lane = iota((R, C), 1)
    me = info[3:4, 0:1].astype(i32)
    gx = me >> 4
    gy = me & 15
    inside = [jnp.where(t, 1.0, 0.0) for t in (gx > 0, gx < 7, gy > 0, gy < 15)]
    wait_copies(copies[:1])

    def first(l, carry):
        for a, c in enumerate(coeffs_of(p[l], sw[l], sg[l])):
            coef[a, l] = c
        k = perm[0, l].astype(f32)
        n = 3 * L + l
        edge = row_lo[pl.ds(n, 1), :] * inside[0]
        before = transmit(k, jnp.concatenate([edge, k[:-1]], axis=0))
        edge = row_hi[pl.ds(n, 1), :] * inside[1]
        tx[0, l] = before
        tx[1, l] = jnp.concatenate([before[1:], transmit(k[R - 1 : R], edge)], axis=0)
        k = perm[1, l].astype(f32)
        edge = lane_of(columns, n) * inside[2]
        before = transmit(k, jnp.where(lane == 0, edge, pltpu.roll(k, 1, 1)))
        edge = lane_of(columns, 4 * L + n) * inside[3]
        ty[0, l] = before
        ty[1, l] = jnp.where(lane == C - 1, transmit(k[:, C - 1 : C], edge), pltpu.roll(before, C - 1, 1))
        k = perm[2, l].astype(f32)
        under = perm[2, jnp.maximum(l - 1, 0)].astype(f32)
        tz[l] = jnp.where(l > 0, layer_ratio, 0.0) * transmit(k, under)
        return carry

    lax.fori_loop(0, L, first, 0)
    tz[L] = jnp.zeros((R, C), f32)
    saved = start_copies(((coef, coef_h), (tx, tx_h), (ty, ty_h), (tz, tz_h)), sems_t)
    wait_copies(copies[1:])

    def outs(l):
        return (
            (weight.at[:, l], weight_h.at[:, l]),
            (res.at[:, l], res_h.at[:, l]), (diag.at[:, l], diag_h.at[:, l]),
        )

    def second(l, carry):
        rows = (row_lo[pl.ds(l, 1), :], row_hi[pl.ds(l, 1), :])
        ends = lane_of(columns, l), lane_of(columns, 4 * L + l)
        sides_of = coeff_columns(coef_col, l)
        for lo in range(0, R, BLOCK):
            at = slice(lo, lo + BLOCK)
            here = p[l, at, :]
            nexts = neighbours(p, l, lo, rows, [e[at] for e in ends])
            faces = face_terms(tx, ty, tz, l, at)
            drops = [t * (here - q) for t, q in zip(faces, nexts)]
            face_sum = sum(faces)
            drop_sum = sum(drops)
            porous = volume_scale * por[l, at, :]
            water, gas = (sw[l, at, :], sg[l, at, :])
            sats = (water, 1.0 - water - gas, gas)
            indices = index_sum[l, at, :]
            diagonals, residuals, inverses, cs = [], [], [], []
            for a in range(3):
                c = coef[a, l, at, :]
                ab = c * face_sum
                net = c * drop_sum
                for t, d, s in zip(faces, drops, coeff_neighbours(coef, coef_row, a, l, lo, sides_of)):
                    ab = ab + t * s
                    net = net + d * s
                b = 1.0 + compress[a] * here
                stored = porous * sats[a]
                diagonals.append(compress[a] * stored + ab + c * indices)
                residuals.append(b * stored - volume_scale * mass[a, l, at, :] + net + c * (indices * here))
                inverses.append(reciprocal(porous * b))
                cs.append(c)
            inverse_total = reciprocal(sum(d * v for d, v in zip(diagonals, inverses)))
            weights = [v * inverse_total for v in inverses]
            base[l, at, :] = -sum(w * r for w, r in zip(weights, residuals))
            head[l, at, :] = sum(w * c for w, c in zip(weights, cs))
            for a in range(3):
                weight[a, l, at, :] = weights[a]
                res[a, l, at, :] = residuals[a]
            diag[0, l, at, :] = diagonals[0]
            diag[1, l, at, :] = diagonals[2]
        for c in layer_copies(outs, sems_out, l):
            c.start()
        return carry

    lax.fori_loop(0, L, second, 0)
    wait_copies(saved)
    for l in range(L):
        wait_copies(layer_copies(outs, sems_out, l))


def first_kernel(
    got, info, own, base, head, row_first, row_second, col_first, col_second, mine, well_residual, spread, step,
):
    lane = iota((1, LANES), 1)
    sums = jnp.sum(got[...], axis=0, keepdims=True)
    total = jnp.where(lane < WELL_DEV, sums, 1.0)
    flow = rolled_row(sums, LANES - 16)
    residual = jnp.where(lane < WELL_DEV, flow - total * own[0:1] - own[1:2], 0.0)
    inverse = jnp.where(lane < WELL_DEV, 1.0 / total, 0.0)
    mine[...] = jnp.concatenate([residual, inverse, jnp.zeros((6, LANES), f32)], axis=0)
    well_residual[...] = residual[:, 0:WELL_DEV]
    cell_row = info[0:1].astype(i32)
    well_row = info[1:2].astype(i32)
    heads = gather_wells(got[...], well_row >> 4, (well_row & 15) + 32)
    spread[...] = scatter(cell_row, info[2:3] * heads).reshape(L, R, C)
    step[...] = base[...] + head[...] * spread[...]
    write_faces(step, (row_first, row_second, col_first, col_second))


def first_flow_kernel(info, perf, mine, step, pay):
    well_row = info[1:2].astype(i32)
    here = to_row(gather_cells(to_column(info[0:1]).astype(i32), (flat(step),))[0])
    parts = parts_by_offset(info[3:4].astype(i32), well_row, perf[0:1] * here)
    packed = parts[:, TAIL:]
    residual = mine[0:1]
    inverse = mine[1:2]
    for n, row in enumerate((residual * inverse, residual, inverse)):
        packed = packed + rolled_row(row, 16 * (n + 1))
    tiles = [parts[:, LANES * t : LANES * (t + 1)] for t in range(5)]
    pay[...] = to_everyone(jnp.concatenate(tiles + [packed, jnp.zeros((2, LANES), f32)], axis=0))


def grid_kernel(
    coef_row, coef_col, head, spread, step,
    coef_h, tx_h, ty_h, tz_h, weight_h, res_h,
    ahead, end_row, end_col, residual_h, gain_h,
    coef, tx, ty, tz, weight, res, residual, gain, sems, sems_out,
):
    copies = start_copies(
        halves(((coef_h, coef, 1), (tx_h, tx, 1), (ty_h, ty, 1), (tz_h, tz, 0), (weight_h, weight, 1), (res_h, res, 1))),
        sems,
    )
    wait_copies(copies[:6])

    def outs(l):
        return (
            (residual.at[:, l], residual_h.at[:, l]), (gain.at[:, l], gain_h.at[:, l]),
        )

    def layer(l, ends):
        sides_of = coeff_columns(coef_col, l)
        for lo in range(0, R, BLOCK):
            at = slice(lo, lo + BLOCK)
            nexts = inner_neighbours(step, l, lo)
            faces = face_terms(tx, ty, tz, l, at)
            wells = spread[l, at, :]
            mixes = [head[l, at, :]] * 6
            for a in range(3):
                w = weight[a, l, at, :]
                sides = coeff_neighbours(coef, coef_row, a, l, lo, sides_of)
                mixes = [m + w * s for m, s in zip(mixes, sides)]
                residual[a, l, at, :] = res[a, l, at, :] - coef[a, l, at, :] * wells
            total = step[l, at, :]
            for j in range(6):
                g = faces[j] * mixes[j]
                gain[j, l, at, :] = g
                total = total + g * nexts[j]
            ahead[l, at, :] = total
        end_row[0, pl.ds(l, 1), :] = gain[0, l, 0:1, :]
        end_row[1, pl.ds(l, 1), :] = gain[1, l, R - 1 : R, :]
        for c in layer_copies(outs, sems_out, l):
            c.start()
        return end_columns(ends, l, gain[2, l, :, 0:LANES][:, 0:1], gain[3, l, :, C - LANES : C][:, LANES - 1 : LANES])

    ends = lax.fori_loop(0, L // 2, layer, jnp.zeros((R, LANES), f32))
    wait_copies(copies[6:])
    end_col[...] = lax.fori_loop(L // 2, L, layer, ends)
    for l in range(L):
        wait_copies(layer_copies(outs, sems_out, l))


def second_kernel(
    got, info, ahead, head, end_row, end_col, row_first, row_second, col_first, col_second,
    out_row_first, out_row_second, out_col_first, out_col_second, step,
):
    cell_row = info[0:1].astype(i32)
    well_row = info[1:2].astype(i32)
    moves = gather_wells(tile_of(got, 5), well_row >> 4, (well_row & 15) + 16)
    wells = scatter(cell_row, info[2:3] * moves).reshape(L, R, C)
    step[...] = ahead[...] + head[...] * wells
    columns = end_col[...] * unpack_columns(col_first, col_second)
    low, high = from_partner("gx", row_first[...], row_second[...])
    low = end_row[0] * low
    high = end_row[1] * high
    for l in range(L):
        add_faces(step, l, low[l : l + 1], high[l : l + 1], columns)
    write_faces(step, (out_row_first, out_row_second, out_col_first, out_col_second))


def wells_kernel(
    got, info, perf, step, gain_h, table, parts, spread, gain, sems,
):
    copies = start_copies(((gain_h, gain),), sems)
    tail = tile_of(got, 5)
    residuals = pltpu.roll(tail, LANES - 32, 1)
    inverses = pltpu.roll(tail, LANES - 48, 1)
    table[0] = residuals
    table[1] = inverses
    cell_row = info[0:1].astype(i32)
    well_row = info[1:2].astype(i32)
    valid = iota((DEVICES, LANES), 1) < WELL_DEV
    moves = jnp.where(valid, (sum_parts(got) + residuals) * inverses, 0.0)
    values = gather_wells(moves, well_row >> 4, well_row & 15)
    spread[...] = scatter(cell_row, info[2:3] * values).reshape(L, R, C)
    here = to_row(gather_cells(to_column(info[0:1]).astype(i32), (flat(step),))[0])
    flows = parts_by_offset(info[3:4].astype(i32), well_row, perf[0:1] * here)
    tiles = [flows[:, LANES * t : LANES * (t + 1)] for t in range(6)]
    parts[...] = jnp.concatenate(tiles + [jnp.zeros((2, LANES), f32)], axis=0)
    wait_copies(copies)


def third_kernel(
    spread, old, base, gain, head, row_first, row_second, col_first, col_second,
    out_row_first, out_row_second, out_col_first, out_col_second, step, row_lo, row_hi,
):
    columns = unpack_columns(col_first, col_second)
    row_lo[...], row_hi[...] = from_partner("gx", row_first[...], row_second[...])

    def layer(l, carry):
        for lo in range(0, R, BLOCK):
            at = slice(lo, lo + BLOCK)
            nexts = step_neighbours(old, row_lo, row_hi, columns, l, lo)
            total = base[l, at, :] + head[l, at, :] * spread[l, at, :]
            for j in range(6):
                total = total + gain[j, l, at, :] * nexts[j]
            step[l, at, :] = total
        return carry

    lax.fori_loop(0, L, layer, 0)
    write_faces(step, (out_row_first, out_row_second, out_col_first, out_col_second))


def third_flow_kernel(info, perf, parts, step, pay):
    here = gather_cells(to_column(info[0:1]).astype(i32), (flat(step),))[0]
    well_row = info[1:2].astype(i32)
    slot_column = to_column(info[1:2]).astype(i32) & 15
    pay[...] = to_everyone(parts[...])
    pay[pl.ds(6, DEVICES, stride=8), :] = to_holders(
        well_row >> 4, slot_column, ((0, to_column(perf[0:1]) * here),)
    )


def last_grid_kernel(
    coef_row, coef_col, head, step, gain_row, gain_col,
    p_h, por_h, coef_h, tx_h, ty_h, tz_h, weight_h, diag_h, residual_h,
    end_row, end_col, ahead_h, slope_h,
    p, por, coef, tx, ty, tz, weight, diag, residual, ahead, slope, sems, sems_out,
):
    copies = start_copies(
        halves(
            (
                (p_h, p, 0), (por_h, por, 0), (coef_h, coef, 1), (tx_h, tx, 1), (ty_h, ty, 1), (tz_h, tz, 0),
                (weight_h, weight, 1), (diag_h, diag, 1), (residual_h, residual, 1),
            )
        ),
        sems,
    )
    wait_copies(copies[:9])

    def outs(l):
        return ((ahead.at[:, l], ahead_h.at[:, l]), (slope.at[:, l], slope_h.at[:, l]))

    def layer(l, ends):
        sides_of = coeff_columns(coef_col, l)
        gains = lane_of(gain_col[...], l), lane_of(gain_col[...], L + l)
        pairs = [([], []), ([], [])]
        for lo in range(0, R, BLOCK):
            at = slice(lo, lo + BLOCK)
            nexts = inner_neighbours(step, l, lo)
            faces = face_terms(tx, ty, tz, l, at)
            flows = [t * q for t, q in zip(faces, nexts)]
            flow_sum = sum(flows)
            rights, cs, sides = [], [], []
            for a in range(3):
                c = coef[a, l, at, :]
                total = c * flow_sum - residual[a, l, at, :]
                sides.append(coeff_neighbours(coef, coef_row, a, l, lo, sides_of))
                for v, s in zip(flows, sides[a]):
                    total = total + v * s
                rights.append(total)
                cs.append(c)
            z = sum(weight[a, l, at, :] * rights[a] for a in range(3))
            h = head[l, at, :]
            porous = volume_scale * por[l, at, :]
            inverses = [reciprocal(porous * (1.0 + compress[a] * p[l, at, :])) for a in (0, 2)]
            ahead[0, l, at, :] = z
            for n, a in enumerate((0, 2)):
                d = diag[n, l, at, :]
                inverse = inverses[n]
                ahead[1 + n, l, at, :] = (rights[a] - d * z) * inverse
                slope[n, l, at, :] = (cs[a] - d * h) * inverse
                for side in range(2):
                    if lo == (0, R - BLOCK)[side]:
                        row = slice(0, 1) if side == 0 else slice(BLOCK - 1, BLOCK)
                        face = faces[side][row] * (cs[a][row] + sides[a][side][row])
                        end_row[side, n, pl.ds(l, 1), :] = (
                            face - d[row] * gain_row[side, pl.ds(l, 1), :]
                        ) * inverse[row]
                    col = slice(0, 1) if side == 0 else slice(C - 1, C)
                    face = faces[2 + side][:, col] * (cs[a][:, col] + sides_of[a][side][at])
                    pairs[n][side].append((face - d[:, col] * gains[side][at]) * inverse[:, col])
        for c in layer_copies(outs, sems_out, l):
            c.start()
        return tuple(
            end_columns(ends[n], l, *(jnp.concatenate(part, axis=0) for part in pairs[n])) for n in range(2)
        )

    blank = jnp.zeros((R, LANES), f32)
    ends = lax.fori_loop(0, L // 2, layer, (blank, blank))
    wait_copies(copies[9:])
    end_col[0], end_col[1] = lax.fori_loop(L // 2, L, layer, ends)
    for l in range(L):
        wait_copies(layer_copies(outs, sems_out, l))


def final_kernel(
    got, info, table, mine, head, gain_row, gain_col, end_row, end_col, row_first, row_second, col_first, col_second,
    ahead_h, slope_h, update_h, moved, ahead, slope, update, sems, sems_out,
):
    copies = start_copies(((ahead_h, ahead), (slope_h, slope)), sems)
    flow = jnp.sum(tile_of(got, 6), axis=0, keepdims=True)
    moved[...] = ((flow + mine[0:1]) * mine[1:2])[:, 0:WELL_DEV]
    cell_row = info[0:1].astype(i32)
    well_row = info[1:2].astype(i32)
    valid = iota((DEVICES, LANES), 1) < WELL_DEV
    moves = jnp.where(valid, (sum_parts(got) + table[0]) * table[1], 0.0)
    values = gather_wells(moves, well_row >> 4, well_row & 15)
    wells = scatter(cell_row, info[2:3] * values).reshape(L, R, C)
    halo = unpack_columns(col_first, col_second)
    lows, highs = from_partner("gx", row_first[...], row_second[...])
    columns = (gain_col[...] * halo, end_col[0] * halo, end_col[1] * halo)
    wait_copies(copies)

    def outs(l):
        return ((update.at[:, l], update_h.at[:, l]),)

    for l in range(L):
        low = lows[l : l + 1]
        high = highs[l : l + 1]
        for n in range(3):
            rows = [gain_row[side, l : l + 1, :] if n == 0 else end_row[side, n - 1, l : l + 1, :] for side in range(2)]
            update[n, l] = ahead[n, l] + (head[l] if n == 0 else slope[n - 1, l]) * wells[l]
            add_faces(update.at[n], l, rows[0] * low, rows[1] * high, columns[n])
        layer_copies(outs, sems_out, l)[0].start()
    for l in range(L):
        wait_copies(layer_copies(outs, sems_out, l))


def call(kernel, outs, ins, operands, scratch=(), flops=0):
    shapes = tuple(
        pltpu.VMEM(s, f32) if w is VM else pltpu.HBM(s, f32) if w is HB else jax.ShapeDtypeStruct(s, f32)
        for s, w in outs
    )
    moved = 4 * sum(int(x.size) for x in operands)
    operands = [
        pltpu.with_memory_space_constraint(x, pltpu.HBM) if w is HB else x for x, w in zip(operands, ins)
    ]
    return pl.pallas_call(
        kernel,
        out_shape=shapes,
        in_specs=ins,
        out_specs=tuple(w or VM for _, w in outs),
        scratch_shapes=[pltpu.VMEM(x, f32) if type(x) is tuple else x for x in scratch],
        compiler_params=pltpu.CompilerParams(vmem_limit_bytes=40 * 1024 * 1024),
        cost_estimate=pl.CostEstimate(flops=flops, bytes_accessed=moved, transcendentals=0),
    )(*operands)


FIELD = (L, R, C)
TWO, THREE, SIX, FACED = ((2,) + FIELD, (3,) + FIELD, (6,) + FIELD, (L + 1, R, C))
FACES = (((L, C), VM), ((L, C), VM), ((L, LANES), VM), ((L, LANES), VM))
WIDE_FACES = (((4 * L, C), VM), ((4 * L, C), VM), ((4 * L, LANES), VM), ((4 * L, LANES), VM))
SMALL = (8, LANES)
PAY = ((8 * DEVICES, LANES), None)
sem = pltpu.SemaphoreType.DMA


def exchange(array):
    return lax.all_to_all(array, AXES, split_axis=0, concat_axis=0, tiled=True)


def exchange_tiles(array):
    return exchange(array.reshape(DEVICES, 8, LANES)).reshape(8 * DEVICES, LANES)


def partners():
    rows, columns = (lax.axis_size(axis) for axis in AXES)
    swaps = [[], [], [], []]
    for x in range(rows):
        for y in range(columns):
            here = x * columns + y
            x_next = x - 1 + 2 * (x % 2)
            y_next = y - 1 + 2 * (y % 2)
            swaps[0].append((here, (x ^ 1) * columns + y))
            swaps[1].append((here, x_next * columns + y if 0 <= x_next < rows else x * columns + (y ^ 1)))
            swaps[2].append((here, x * columns + (y ^ 1)))
            swaps[3].append((here, x * columns + y_next if 0 <= y_next < columns else (x ^ 1) * columns + y))
    return swaps


def halo_of(faces):
    swaps = partners()
    got = {n: lax.ppermute(faces[n], AXES, swaps[n]) for n in (3, 1, 2, 0)}
    return [got[n] for n in range(4)]


def local(
    pressure, sat_water, sat_gas, old_mass, perm, porosity,
    perf_well, perf_cell, perf_index, well_pressure, well_rate,
):
    *faces, p, sw, sg = call(
        faces_kernel,
        WIDE_FACES + ((FIELD, VM), (FIELD, VM), (FIELD, VM)),
        [HB] * 4,
        (pressure, sat_water, sat_gas, perm),
        [pltpu.VMEM(TWO, bf16), sem((4,))],
    )
    halo = halo_of(faces)
    pay, perf, info, own = call(
        start_kernel,
        (((DEVICES, LANES), VM), ((8, PERFS), VM), ((8, PERFS), VM), (SMALL, VM)),
        [HB] * 5 + [VM] * 3,
        (
            perf_cell.reshape(1, PERFS), perf_well.reshape(1, PERFS), perf_index.reshape(1, PERFS),
            well_pressure.reshape(1, WELL_DEV), well_rate.reshape(1, WELL_DEV), p, sw, sg,
        ),
        [
            pltpu.VMEM((1, PERFS), i32), pltpu.VMEM((1, PERFS), i32), (1, PERFS),
            (1, WELL_DEV), (1, WELL_DEV), sem((5,)),
        ],
    )
    pay, *halo = pl.pallas_call(
        after_kernel,
        out_shape=tuple(pltpu.VMEM(x.shape, f32) for x in (pay, *halo)),
        in_specs=[pl.BlockSpec(memory_space=pl.ANY)] * 5,
        out_specs=(pl.BlockSpec(memory_space=pl.ANY),) * 5,
        input_output_aliases={n: n for n in range(5)},
    )(pay, *halo)
    got = exchange(pay)
    coef_row, coef_col, base, head, coef, tx, ty, tz, weight, res, diag = call(
        setup_kernel,
        (
            ((2, 3, L, C), VM), ((3, R, LANES), VM), (FIELD, VM), (FIELD, VM), (THREE, HB), (TWO, HB), (TWO, HB),
            (FACED, HB), (THREE, HB), (THREE, HB), (TWO, HB),
        ),
        [VM] * 8 + [HB] * 3,
        (info, *halo, p, sw, sg, porosity, old_mass, perm),
        [
            FIELD, THREE, pltpu.VMEM(THREE, bf16), THREE, TWO, TWO, FACED,
            THREE, THREE, TWO, FIELD, (4 * L, C), (4 * L, C), sem((3,)), sem((4,)), sem((3, L)),
        ],
        flops=400 * L * R * C,
    )
    *faces, mine, well_residual, spread, start = call(
        first_kernel,
        FACES + ((SMALL, VM), ((1, WELL_DEV), None), (FIELD, VM), (FIELD, VM)),
        [VM] * 5,
        (got, info, own, base, head),
    )
    halo = halo_of(faces)
    (pay,) = call(first_flow_kernel, (PAY,), [VM] * 4, (info, perf, mine, start))
    got = exchange_tiles(pay)
    fields = (coef, tx, ty, tz, weight)
    ahead, gain_row, gain_col, residual, gain = call(
        grid_kernel,
        ((FIELD, VM), ((2, L, C), VM), ((R, LANES), VM), (THREE, HB), (SIX, HB)),
        [VM] * 5 + [HB] * 6,
        (coef_row, coef_col, head, spread, start, *fields, res),
        [THREE, TWO, TWO, FACED, THREE, THREE, THREE, SIX, sem((12,)), sem((2, L))],
        flops=100 * L * R * C,
    )
    *faces, step = call(
        second_kernel,
        FACES + ((FIELD, VM),),
        [VM] * 10,
        (got, info, ahead, head, gain_row, gain_col, *halo),
    )
    halo = halo_of(faces)
    table, parts, spread, gain_near = call(
        wells_kernel,
        (((2, DEVICES, LANES), VM), (SMALL, VM), (FIELD, VM), (SIX, VM)),
        [VM] * 4 + [HB],
        (got, info, perf, step, gain),
        [sem((1,))],
    )
    *faces, step = call(
        third_kernel,
        FACES + ((FIELD, VM),),
        [VM] * 9,
        (spread, step, start, gain_near, head, *halo),
        [(L, C), (L, C)],
    )
    halo = halo_of(faces)
    (pay,) = call(third_flow_kernel, (PAY,), [VM] * 4, (info, perf, parts, step))
    got = exchange_tiles(pay)
    end_row, end_col, ahead, slope = call(
        last_grid_kernel,
        (((2, 2, L, C), VM), ((2, R, LANES), VM), (THREE, HB), (TWO, HB)),
        [VM] * 6 + [HB] * 9,
        (coef_row, coef_col, head, step, gain_row, gain_col, pressure, porosity, *fields, diag, residual),
        [FIELD, FIELD, THREE, TWO, TWO, FACED, THREE, TWO, THREE, THREE, TWO, sem((18,)), sem((2, L))],
        flops=150 * L * R * C,
    )
    update, moved = call(
        final_kernel,
        ((THREE, HB), ((1, WELL_DEV), None)),
        [VM] * 13 + [HB] * 2,
        (got, info, table, mine, head, gain_row, gain_col, end_row, end_col, *halo, ahead, slope),
        [THREE, TWO, THREE, sem((2,)), sem((1, L))],
    )
    return residual, well_residual.reshape(WELL_DEV), update, moved.reshape(WELL_DEV)


def solution(mesh):
    return jax.shard_map(
        local,
        mesh=mesh,
        in_specs=(
            P(None, "gx", "gy"),
            P(None, "gx", "gy"),
            P(None, "gx", "gy"),
            P(None, None, "gx", "gy"),
            P(None, None, "gx", "gy"),
            P(None, "gx", "gy"),
            P(("gx", "gy")),
            P(("gx", "gy")),
            P(("gx", "gy")),
            P(("gx", "gy")),
            P(("gx", "gy")),
        ),
        out_specs=(
            P(None, None, "gx", "gy"),
            P(("gx", "gy")),
            P(None, None, "gx", "gy"),
            P(("gx", "gy")),
        ),
        check_vma=False,
    )
```

```python
import jax
import jax.numpy as jnp
from jax import lax
from jax.experimental import pallas as pl
from jax.experimental.pallas import tpu as pltpu
from jax.sharding import PartitionSpec as P

f32 = jnp.float32
bf16 = jnp.bfloat16
i32 = jnp.int32

compress = (0.05, 0.02, 0.2)
viscosity = (0.5, 2.0, 0.1)
volume_scale = 4.0
layer_ratio = 0.1
AXES = ("gx", "gy")
DEVICES = 128
WELL_DEV = 16
REACH = 40
FAR = 64
TAIL = REACH * WELL_DEV
WIDTH = TAIL + 128
TILES = WIDTH // 128
LANES = 128
L, R, C = 8, 64, 256
PERFS = 256
BLOCK = 8
VM = pl.BlockSpec(memory_space=pltpu.VMEM)
HB = pl.BlockSpec(memory_space=pltpu.HBM)


def iota(shape, dim):
    return lax.broadcasted_iota(i32, shape, dim)


def split3(x):
    high = x.astype(bf16)
    rest = x - high.astype(f32)
    middle = rest.astype(bf16)
    low = (rest - middle.astype(f32)).astype(bf16)
    return high, middle, low


def dot(a, b):
    return jnp.dot(a, b, preferred_element_type=f32)


def to_column(row):
    n = row.shape[1]
    return jnp.sum(jnp.where(iota((n, n), 0) == iota((n, n), 1), row, 0.0), axis=1, keepdims=True)


def to_row(column):
    n = column.shape[0]
    return jnp.sum(jnp.where(iota((n, n), 0) == iota((n, n), 1), column, 0.0), axis=0, keepdims=True)


def coeffs_of(p, sw, sg):
    so = 1.0 - sw - sg
    return tuple(
        s * s * (1.0 / viscosity[a]) * (1.0 + compress[a] * p) for a, s in enumerate((sw, so, sg))
    )


def scatter(cell_row, values):
    match = iota((L * R, PERFS), 0) == (cell_row >> 8)
    column = to_column(cell_row.astype(f32)).astype(i32) & (C - 1)
    spread = (iota((PERFS, C), 1) == column).astype(bf16)
    return sum(
        dot(jnp.where(match, part.astype(f32), 0.0).astype(bf16), spread) for part in split3(values)
    )


def gather_cells(cell_column, fields):
    onehot = (iota((PERFS, L * R), 1) == (cell_column >> 8)).astype(bf16)
    here = iota((PERFS, C), 1) == (cell_column & (C - 1))
    picked = []
    for field in fields:
        rows = sum(dot(onehot, part) for part in split3(field))
        picked.append(jnp.sum(jnp.where(here, rows, 0.0), axis=1, keepdims=True))
    return picked


def flat(field):
    return field[...].reshape(L * R, C)


def gather_wells(table, holder, slot):
    onehot = (iota((DEVICES, PERFS), 0) == holder).astype(bf16)
    wide = sum(dot(part, onehot) for part in split3(table.T))
    return jnp.sum(jnp.where(iota((LANES, PERFS), 0) == slot, wide, 0.0), axis=0, keepdims=True)


def to_holders(holder, slot_column, columns):
    lane = iota((PERFS, LANES), 1)
    group = lane >> 4
    values = jnp.zeros((PERFS, LANES), f32)
    for g, column in columns:
        values = jnp.where(group == g, column, values)
    values = jnp.where((lane & 15) == slot_column, values, 0.0)
    onehot = (iota((DEVICES, PERFS), 0) == holder).astype(bf16)
    return sum(dot(onehot, part) for part in split3(values))


def parts_by_offset(me, well_row, values):
    offset = (me - (well_row >> 4)) & (DEVICES - 1)
    lane = jnp.where(offset == FAR, TAIL, offset * WELL_DEV) + (well_row & 15)
    column = to_column(lane.astype(f32)).astype(i32)
    onehot = (iota((PERFS, WIDTH), 1) == column).astype(bf16)
    high, middle, low = split3(values)
    rows = jnp.concatenate([high.astype(f32), middle.astype(f32), low.astype(f32), jnp.zeros((5, PERFS), f32)], axis=0)
    return jnp.sum(dot(rows.astype(bf16), onehot), axis=0, keepdims=True)


def tile_of(got, t):
    return got[pl.ds(t, DEVICES, stride=TILES), :]


def sum_parts(got):
    aligned = tile_of(got, 0)
    for t in range(1, TAIL // LANES):
        aligned = aligned + pltpu.roll(tile_of(got, t), DEVICES - 8 * t, 0)
    total = aligned + pltpu.roll(tile_of(got, 5), DEVICES - FAR, 0)
    for u in range(1, 8):
        total = total + pltpu.roll(pltpu.roll(aligned, DEVICES - u, 0), LANES - 16 * u, 1)
    return total


def to_everyone(pay, rows):
    four = jnp.concatenate([rows] * 4, axis=0)
    pay[...] = jnp.broadcast_to(four[None], (DEVICES // 4, 4 * TILES, LANES)).reshape(TILES * DEVICES, LANES)


def rolled_row(row, shift):
    return pltpu.roll(jnp.broadcast_to(row, (8, LANES)), shift, 1)[0:1]


def shift_rows(x, first, last):
    return (
        jnp.concatenate([first, x[:-1]], axis=0),
        jnp.concatenate([x[1:], last], axis=0),
    )


def shift_columns(x, first, last):
    lane = iota(x.shape, 1)
    return (
        jnp.where(lane == 0, first, pltpu.roll(x, 1, 1)),
        jnp.where(lane == C - 1, last, pltpu.roll(x, C - 1, 1)),
    )


def lane_of(x, index):
    return pltpu.roll(x, (LANES - index) % LANES, 1)[:, 0:1]


def is_even(axis):
    return lax.axis_index(axis) % 2 == 0


def by_partner(axis, low, high):
    even = is_even(axis)
    return jnp.where(even, high, low), jnp.where(even, low, high)


def from_partner(axis, first, second):
    even = is_even(axis)
    return jnp.where(even, second, first), jnp.where(even, first, second)


def pack_columns(columns, first, second):
    n = first.shape[0]
    turned = jnp.concatenate([columns, jnp.zeros((LANES - R, LANES), f32)], axis=0).T
    first[...], second[...] = by_partner("gy", turned[0:n], turned[n : 2 * n])


def unpack_columns(first, second):
    n = first.shape[0]
    low, high = from_partner("gy", first[...], second[...])
    rows = jnp.concatenate([low, high, jnp.zeros((LANES - 2 * n, LANES), f32)], axis=0)
    return rows.T[0:R]


def write_faces(step, outs):
    row_first, row_second, col_first, col_second = outs
    lane = iota((R, LANES), 1)
    columns = jnp.zeros((R, LANES), f32)
    for l in range(L):
        x = step[l]
        pair = by_partner("gx", x[0:1], x[R - 1 : R])
        row_first[l : l + 1, :], row_second[l : l + 1, :] = pair
        columns = jnp.where(lane == l, x[:, 0:1], columns)
        columns = jnp.where(lane == L + l, x[:, C - 1 : C], columns)
    pack_columns(columns, col_first, col_second)


def start_copies(pairs, sems):
    copies = [pltpu.make_async_copy(a, b, sems.at[n]) for n, (a, b) in enumerate(pairs)]
    for c in copies:
        c.start()
    return copies


def wait_copies(copies):
    for c in copies:
        c.wait()


def layer_copies(pairs, sems, l):
    return [pltpu.make_async_copy(a, b, sems.at[n, l]) for n, (a, b) in enumerate(pairs(l))]


def faces_kernel(
    cell_h, well_h, index_h, pressure_h, rate_h, p_h, sw_h, sg_h, perm_h,
    row_first, row_second, col_first, col_second, p, sw, sg, info, own,
    cell_in, well_in, index_in, pressure_in, rate_in, perm, sems, sems_in,
):
    copies = start_copies(((perm_h.at[0:2], perm), (p_h, p), (sw_h, sw), (sg_h, sg)), sems)
    small = start_copies(
        (
            (cell_h, cell_in), (well_h, well_in), (index_h, index_in),
            (pressure_h, pressure_in), (rate_h, rate_in),
        ),
        sems_in,
    )
    me = lax.axis_index("gx") * 16 + lax.axis_index("gy")
    device = jnp.full((1, PERFS), me, i32).astype(f32)
    wait_copies(small)
    numbers = [cell_in[...].astype(f32), well_in[...].astype(f32), index_in[...], device]
    info[...] = jnp.concatenate(numbers + [jnp.zeros((4, PERFS), f32)], axis=0)
    blank = jnp.zeros((1, LANES - WELL_DEV), f32)
    heads = jnp.concatenate([pressure_in[...], blank], axis=1)
    rates = jnp.concatenate([rate_in[...], blank], axis=1)
    own[...] = jnp.concatenate([heads, rates, jnp.zeros((6, LANES), f32)], axis=0)
    lane = iota((R, LANES), 1)
    columns = jnp.zeros((R, LANES), f32)
    wait_copies(copies[:1])
    for l in range(L):
        n = 3 * L + l
        low = perm[0, l, 0:16, :].astype(f32)[0:1]
        high = perm[0, l, R - 16 : R, :].astype(f32)[15:16]
        row_first[n : n + 1, :], row_second[n : n + 1, :] = by_partner("gx", low, high)
        k = perm[1, l].astype(f32)
        columns = jnp.where(lane == n, k[:, 0:1], columns)
        columns = jnp.where(lane == 4 * L + n, k[:, C - 1 : C], columns)
    wait_copies(copies[1:])
    for l in range(L):
        for f, ref in enumerate((p, sw, sg)):
            x = ref[l]
            n = f * L + l
            pair = by_partner("gx", x[0:1], x[R - 1 : R])
            row_first[n : n + 1, :], row_second[n : n + 1, :] = pair
            columns = jnp.where(lane == n, x[:, 0:1], columns)
            columns = jnp.where(lane == 4 * L + n, x[:, C - 1 : C], columns)
    pack_columns(columns, col_first, col_second)


def start_kernel(info, own, p, sw, sg, pay, perf):
    well_row = info[1:2].astype(i32)
    slot_column = to_column(info[1:2]).astype(i32) & 15
    here = gather_cells(to_column(info[0:1]).astype(i32), (flat(p), flat(sw), flat(sg)))
    coeffs = coeffs_of(*here)
    total = to_column(info[2:3]) * (coeffs[0] + coeffs[1] + coeffs[2])
    sums = to_holders(well_row >> 4, slot_column, ((0, total), (1, total * here[0])))
    pay[...] = sums + rolled_row(own[0:1], 32)
    perf[...] = jnp.broadcast_to(to_row(total), (8, PERFS))


def after_kernel(pay, *refs):
    pass


def reciprocal(x):
    r = pl.reciprocal(x, approx=True)
    return r * (2.0 - x * r)


def transmit(k, k_next):
    return k * k_next * reciprocal(k + k_next)


def neighbours(field, l, lo, rows, columns):
    hi = lo + BLOCK
    here = field[l, lo:hi, :]
    if lo > 0:
        before = field[l, lo - 1 : hi - 1, :]
    else:
        before = jnp.concatenate([rows[0], field[l, 0 : hi - 1, :]], axis=0)
    if hi < R:
        after = field[l, lo + 1 : hi + 1, :]
    else:
        after = jnp.concatenate([field[l, lo + 1 : R, :], rows[1]], axis=0)
    sides = (field[jnp.maximum(l - 1, 0), lo:hi, :], field[jnp.minimum(l + 1, L - 1), lo:hi, :])
    return (before, after) + shift_columns(here, *columns) + sides


def coeff_neighbours(coef, coef_row, a, l, lo, columns):
    rows = (coef_row[0, a, pl.ds(l, 1), :], coef_row[1, a, pl.ds(l, 1), :])
    ends = [c[lo : lo + BLOCK] for c in columns[a]]
    return neighbours(coef.at[a], l, lo, rows, ends)


def coeff_columns(coef_col, l):
    return [(lane_of(coef_col[a], l), lane_of(coef_col[a], 4 * L + l)) for a in range(3)]


def inner_neighbours(step, l, lo):
    blank = jnp.zeros((1, C), f32)
    return neighbours(step, l, lo, (blank, blank), (0.0, 0.0))


def step_neighbours(step, row_lo, row_hi, columns, l, lo):
    rows = (row_lo[pl.ds(l, 1), :], row_hi[pl.ds(l, 1), :])
    ends = [lane_of(columns, n)[lo : lo + BLOCK] for n in (l, L + l)]
    return neighbours(step, l, lo, rows, ends)


def face_terms(tx, ty, tz, l, rows):
    return (tx[0, l, rows, :], tx[1, l, rows, :], ty[0, l, rows, :], ty[1, l, rows, :], tz[l, rows, :], tz[l + 1, rows, :])


def halves(pairs):
    parts = []
    for half in range(2):
        for a, b, dim in pairs:
            count = a.shape[dim]
            middle = L // 2 + 1
            span = pl.ds(0, middle) if half == 0 else pl.ds(middle, count - middle)
            index = (slice(None),) * dim + (span,)
            parts.append((a.at[index], b.at[index]))
    return parts


def add_faces(field, l, low, high, columns):
    lane = iota((R, LANES), 1)
    field[l, :, 0:LANES] += jnp.where(lane == 0, columns[:, l : l + 1], 0.0)
    field[l, :, C - LANES : C] += jnp.where(lane == LANES - 1, columns[:, L + l : L + l + 1], 0.0)
    field[l, 0:1, :] += low
    field[l, R - 1 : R, :] += high


def end_columns(columns, l, first, last):
    lane = iota((R, LANES), 1)
    return jnp.where(lane == l, first, jnp.where(lane == L + l, last, columns))


def setup_kernel(
    info, row_first, row_second, col_first, col_second, p, sw, sg, por_h, mass_h, perm_h,
    coef_row, coef_col, base, head, coef_h, tx_h, ty_h, tz_h, weight_h, res_h, diag_h,
    por, mass, perm, coef, tx, ty, tz, weight, res, diag, index_sum, row_lo, row_hi,
    sems, sems_t, sems_out,
):
    copies = start_copies(((perm_h, perm), (por_h, por), (mass_h, mass)), sems)
    index_sum[...] = scatter(info[0:1].astype(i32), info[2:3]).reshape(L, R, C)
    row_lo[...], row_hi[...] = from_partner("gx", row_first[...], row_second[...])
    for side, ref in enumerate((row_lo, row_hi)):
        for a, c in enumerate(coeffs_of(ref[0:L], ref[L : 2 * L], ref[2 * L : 3 * L])):
            coef_row[side, a] = c
    columns = unpack_columns(col_first, col_second)
    for a, c in enumerate(
        coeffs_of(columns, pltpu.roll(columns, LANES - L, 1), pltpu.roll(columns, LANES - 2 * L, 1))
    ):
        coef_col[a] = c
    lane = iota((R, C), 1)
    me = info[3:4, 0:1].astype(i32)
    gx = me >> 4
    gy = me & 15
    inside = [jnp.where(t, 1.0, 0.0) for t in (gx > 0, gx < 7, gy > 0, gy < 15)]
    wait_copies(copies[:1])

    def first(l, carry):
        for a, c in enumerate(coeffs_of(p[l], sw[l], sg[l])):
            coef[a, l] = c
        k = perm[0, l].astype(f32)
        n = 3 * L + l
        edge = row_lo[pl.ds(n, 1), :] * inside[0]
        before = transmit(k, jnp.concatenate([edge, k[:-1]], axis=0))
        edge = row_hi[pl.ds(n, 1), :] * inside[1]
        tx[0, l] = before
        tx[1, l] = jnp.concatenate([before[1:], transmit(k[R - 1 : R], edge)], axis=0)
        k = perm[1, l].astype(f32)
        edge = lane_of(columns, n) * inside[2]
        before = transmit(k, jnp.where(lane == 0, edge, pltpu.roll(k, 1, 1)))
        edge = lane_of(columns, 4 * L + n) * inside[3]
        ty[0, l] = before
        ty[1, l] = jnp.where(lane == C - 1, transmit(k[:, C - 1 : C], edge), pltpu.roll(before, C - 1, 1))
        k = perm[2, l].astype(f32)
        under = perm[2, jnp.maximum(l - 1, 0)].astype(f32)
        tz[l] = jnp.where(l > 0, layer_ratio, 0.0) * transmit(k, under)
        return carry

    lax.fori_loop(0, L, first, 0)
    tz[L] = jnp.zeros((R, C), f32)
    saved = start_copies(((coef, coef_h), (tx, tx_h), (ty, ty_h), (tz, tz_h)), sems_t)
    wait_copies(copies[1:])

    def outs(l):
        return (
            (weight.at[:, l], weight_h.at[:, l]),
            (res.at[:, l], res_h.at[:, l]), (diag.at[:, l], diag_h.at[:, l]),
        )

    def second(l, carry):
        rows = (row_lo[pl.ds(l, 1), :], row_hi[pl.ds(l, 1), :])
        ends = lane_of(columns, l), lane_of(columns, 4 * L + l)
        sides_of = coeff_columns(coef_col, l)
        for lo in range(0, R, BLOCK):
            at = slice(lo, lo + BLOCK)
            here = p[l, at, :]
            nexts = neighbours(p, l, lo, rows, [e[at] for e in ends])
            faces = face_terms(tx, ty, tz, l, at)
            drops = [t * (here - q) for t, q in zip(faces, nexts)]
            face_sum = sum(faces)
            drop_sum = sum(drops)
            porous = volume_scale * por[l, at, :]
            water, gas = (sw[l, at, :], sg[l, at, :])
            sats = (water, 1.0 - water - gas, gas)
            indices = index_sum[l, at, :]
            diagonals, residuals, inverses, cs = [], [], [], []
            for a in range(3):
                c = coef[a, l, at, :]
                ab = c * face_sum
                net = c * drop_sum
                for t, d, s in zip(faces, drops, coeff_neighbours(coef, coef_row, a, l, lo, sides_of)):
                    ab = ab + t * s
                    net = net + d * s
                b = 1.0 + compress[a] * here
                stored = porous * sats[a]
                diagonals.append(compress[a] * stored + ab + c * indices)
                residuals.append(b * stored - volume_scale * mass[a, l, at, :] + net + c * (indices * here))
                inverses.append(reciprocal(porous * b))
                cs.append(c)
            inverse_total = reciprocal(sum(d * v for d, v in zip(diagonals, inverses)))
            weights = [v * inverse_total for v in inverses]
            base[l, at, :] = -sum(w * r for w, r in zip(weights, residuals))
            head[l, at, :] = sum(w * c for w, c in zip(weights, cs))
            for a in range(3):
                weight[a, l, at, :] = weights[a]
                res[a, l, at, :] = residuals[a]
            diag[0, l, at, :] = diagonals[0]
            diag[1, l, at, :] = diagonals[2]
        for c in layer_copies(outs, sems_out, l):
            c.start()
        return carry

    lax.fori_loop(0, L, second, 0)
    wait_copies(saved)
    for l in range(L):
        wait_copies(layer_copies(outs, sems_out, l))


def first_kernel(
    got, info, own, perf, base, head, mine, well_residual, spread, step, pay,
):
    lane = iota((1, LANES), 1)
    sums = jnp.sum(got[...], axis=0, keepdims=True)
    total = jnp.where(lane < WELL_DEV, sums, 1.0)
    flow = rolled_row(sums, LANES - 16)
    residual = jnp.where(lane < WELL_DEV, flow - total * own[0:1] - own[1:2], 0.0)
    inverse = jnp.where(lane < WELL_DEV, 1.0 / total, 0.0)
    mine[...] = jnp.concatenate([residual, inverse, jnp.zeros((6, LANES), f32)], axis=0)
    well_residual[...] = residual[:, 0:WELL_DEV]
    cell_row = info[0:1].astype(i32)
    well_row = info[1:2].astype(i32)
    heads = gather_wells(got[...], well_row >> 4, (well_row & 15) + 32)
    spread[...] = scatter(cell_row, info[2:3] * heads).reshape(L, R, C)
    step[...] = base[...] + head[...] * spread[...]
    here = to_row(gather_cells(to_column(info[0:1]).astype(i32), (flat(step),))[0])
    parts = parts_by_offset(info[3:4].astype(i32), well_row, perf[0:1] * here)
    packed = parts[:, TAIL:]
    for n, row in enumerate((residual * inverse, residual, inverse)):
        packed = packed + rolled_row(row, 16 * (n + 1))
    tiles = [parts[:, LANES * t : LANES * (t + 1)] for t in range(5)]
    to_everyone(pay, jnp.concatenate(tiles + [packed], axis=0))


def step_faces_kernel(step, row_first, row_second, col_first, col_second):
    write_faces(step, (row_first, row_second, col_first, col_second))


def grid_kernel(
    coef_row, coef_col, head, spread, step,
    coef_h, tx_h, ty_h, tz_h, weight_h, res_h,
    ahead, end_row, end_col, residual_h, gain_h,
    coef, tx, ty, tz, weight, res, residual, gain, sems, sems_out,
):
    copies = start_copies(
        halves(((coef_h, coef, 1), (tx_h, tx, 1), (ty_h, ty, 1), (tz_h, tz, 0), (weight_h, weight, 1), (res_h, res, 1))),
        sems,
    )
    wait_copies(copies[:6])

    def outs(l):
        return (
            (residual.at[:, l], residual_h.at[:, l]), (gain.at[:, l], gain_h.at[:, l]),
        )

    def layer(l, ends):
        sides_of = coeff_columns(coef_col, l)
        for lo in range(0, R, BLOCK):
            at = slice(lo, lo + BLOCK)
            nexts = inner_neighbours(step, l, lo)
            faces = face_terms(tx, ty, tz, l, at)
            wells = spread[l, at, :]
            mixes = [head[l, at, :]] * 6
            for a in range(3):
                w = weight[a, l, at, :]
                sides = coeff_neighbours(coef, coef_row, a, l, lo, sides_of)
                mixes = [m + w * s for m, s in zip(mixes, sides)]
                residual[a, l, at, :] = res[a, l, at, :] - coef[a, l, at, :] * wells
            total = step[l, at, :]
            for j in range(6):
                g = faces[j] * mixes[j]
                gain[j, l, at, :] = g
                total = total + g * nexts[j]
            ahead[l, at, :] = total
        end_row[0, pl.ds(l, 1), :] = gain[0, l, 0:1, :]
        end_row[1, pl.ds(l, 1), :] = gain[1, l, R - 1 : R, :]
        for c in layer_copies(outs, sems_out, l):
            c.start()
        return end_columns(ends, l, gain[2, l, :, 0:LANES][:, 0:1], gain[3, l, :, C - LANES : C][:, LANES - 1 : LANES])

    ends = lax.fori_loop(0, L // 2, layer, jnp.zeros((R, LANES), f32))
    wait_copies(copies[6:])
    end_col[...] = lax.fori_loop(L // 2, L, layer, ends)
    for l in range(L):
        wait_copies(layer_copies(outs, sems_out, l))


def second_kernel(
    got, info, ahead, head, end_row, end_col, row_first, row_second, col_first, col_second,
    out_row_first, out_row_second, out_col_first, out_col_second, step,
):
    cell_row = info[0:1].astype(i32)
    well_row = info[1:2].astype(i32)
    moves = gather_wells(tile_of(got, 5), well_row >> 4, (well_row & 15) + 16)
    wells = scatter(cell_row, info[2:3] * moves).reshape(L, R, C)
    step[...] = ahead[...] + head[...] * wells
    columns = end_col[...] * unpack_columns(col_first, col_second)
    low, high = from_partner("gx", row_first[...], row_second[...])
    low = end_row[0] * low
    high = end_row[1] * high
    for l in range(L):
        add_faces(step, l, low[l : l + 1], high[l : l + 1], columns)
    write_faces(step, (out_row_first, out_row_second, out_col_first, out_col_second))


def wells_kernel(
    got, info, perf, step, gain_h, table, parts, spread, gain, sems,
):
    copies = start_copies(((gain_h, gain),), sems)
    tail = tile_of(got, 5)
    residuals = pltpu.roll(tail, LANES - 32, 1)
    inverses = pltpu.roll(tail, LANES - 48, 1)
    table[0] = residuals
    table[1] = inverses
    cell_row = info[0:1].astype(i32)
    well_row = info[1:2].astype(i32)
    valid = iota((DEVICES, LANES), 1) < WELL_DEV
    moves = jnp.where(valid, (sum_parts(got) + residuals) * inverses, 0.0)
    values = gather_wells(moves, well_row >> 4, well_row & 15)
    spread[...] = scatter(cell_row, info[2:3] * values).reshape(L, R, C)
    here = to_row(gather_cells(to_column(info[0:1]).astype(i32), (flat(step),))[0])
    flows = parts_by_offset(info[3:4].astype(i32), well_row, perf[0:1] * here)
    tiles = [flows[:, LANES * t : LANES * (t + 1)] for t in range(6)]
    parts[...] = jnp.concatenate(tiles + [jnp.zeros((2, LANES), f32)], axis=0)
    wait_copies(copies)


def third_kernel(
    info, perf, parts, spread, old, base, gain, head, row_first, row_second, col_first, col_second,
    step, pay, row_lo, row_hi,
):
    columns = unpack_columns(col_first, col_second)
    row_lo[...], row_hi[...] = from_partner("gx", row_first[...], row_second[...])

    def layer(l, carry):
        for lo in range(0, R, BLOCK):
            at = slice(lo, lo + BLOCK)
            nexts = step_neighbours(old, row_lo, row_hi, columns, l, lo)
            total = base[l, at, :] + head[l, at, :] * spread[l, at, :]
            for j in range(6):
                total = total + gain[j, l, at, :] * nexts[j]
            step[l, at, :] = total
        return carry

    lax.fori_loop(0, L, layer, 0)
    here = gather_cells(to_column(info[0:1]).astype(i32), (flat(step),))[0]
    well_row = info[1:2].astype(i32)
    slot_column = to_column(info[1:2]).astype(i32) & 15
    sums = to_holders(well_row >> 4, slot_column, ((1, to_column(perf[0:1]) * here),))
    to_everyone(pay, parts[0:TILES])
    pay[pl.ds(TILES - 1, DEVICES, stride=TILES), :] = sums + parts[TILES - 1 : TILES]


def last_grid_kernel(
    coef_row, coef_col, head, step, gain_row, gain_col,
    p_h, por_h, coef_h, tx_h, ty_h, tz_h, weight_h, diag_h, residual_h,
    end_row, end_col, ahead_h, slope_h,
    p, por, coef, tx, ty, tz, weight, diag, residual, ahead, slope, sems, sems_out,
):
    copies = start_copies(
        halves(
            (
                (p_h, p, 0), (por_h, por, 0), (coef_h, coef, 1), (tx_h, tx, 1), (ty_h, ty, 1), (tz_h, tz, 0),
                (weight_h, weight, 1), (diag_h, diag, 1), (residual_h, residual, 1),
            )
        ),
        sems,
    )
    wait_copies(copies[:9])

    def outs(l):
        return ((ahead.at[:, l], ahead_h.at[:, l]), (slope.at[:, l], slope_h.at[:, l]))

    def layer(l, ends):
        sides_of = coeff_columns(coef_col, l)
        gains = lane_of(gain_col[...], l), lane_of(gain_col[...], L + l)
        pairs = [([], []), ([], [])]
        for lo in range(0, R, BLOCK):
            at = slice(lo, lo + BLOCK)
            nexts = inner_neighbours(step, l, lo)
            faces = face_terms(tx, ty, tz, l, at)
            flows = [t * q for t, q in zip(faces, nexts)]
            flow_sum = sum(flows)
            rights, cs, sides = [], [], []
            for a in range(3):
                c = coef[a, l, at, :]
                total = c * flow_sum - residual[a, l, at, :]
                sides.append(coeff_neighbours(coef, coef_row, a, l, lo, sides_of))
                for v, s in zip(flows, sides[a]):
                    total = total + v * s
                rights.append(total)
                cs.append(c)
            z = sum(weight[a, l, at, :] * rights[a] for a in range(3))
            h = head[l, at, :]
            porous = volume_scale * por[l, at, :]
            inverses = [reciprocal(porous * (1.0 + compress[a] * p[l, at, :])) for a in (0, 2)]
            ahead[0, l, at, :] = z
            for n, a in enumerate((0, 2)):
                d = diag[n, l, at, :]
                inverse = inverses[n]
                ahead[1 + n, l, at, :] = (rights[a] - d * z) * inverse
                slope[n, l, at, :] = (cs[a] - d * h) * inverse
                for side in range(2):
                    if lo == (0, R - BLOCK)[side]:
                        row = slice(0, 1) if side == 0 else slice(BLOCK - 1, BLOCK)
                        face = faces[side][row] * (cs[a][row] + sides[a][side][row])
                        end_row[side, n, pl.ds(l, 1), :] = (
                            face - d[row] * gain_row[side, pl.ds(l, 1), :]
                        ) * inverse[row]
                    col = slice(0, 1) if side == 0 else slice(C - 1, C)
                    face = faces[2 + side][:, col] * (cs[a][:, col] + sides_of[a][side][at])
                    pairs[n][side].append((face - d[:, col] * gains[side][at]) * inverse[:, col])
        for c in layer_copies(outs, sems_out, l):
            c.start()
        return tuple(
            end_columns(ends[n], l, *(jnp.concatenate(part, axis=0) for part in pairs[n])) for n in range(2)
        )

    blank = jnp.zeros((R, LANES), f32)
    ends = lax.fori_loop(0, L // 2, layer, (blank, blank))
    wait_copies(copies[9:])
    end_col[0], end_col[1] = lax.fori_loop(L // 2, L, layer, ends)
    for l in range(L):
        wait_copies(layer_copies(outs, sems_out, l))


def final_kernel(
    got, info, table, mine, head, gain_row, gain_col, end_row, end_col, row_first, row_second, col_first, col_second,
    ahead_h, slope_h, update_h, moved, ahead, slope, update, sems, sems_out,
):
    copies = start_copies(((ahead_h, ahead), (slope_h, slope)), sems)
    flow = rolled_row(jnp.sum(tile_of(got, TILES - 1), axis=0, keepdims=True), LANES - 16)
    moved[...] = ((flow + mine[0:1]) * mine[1:2])[:, 0:WELL_DEV]
    cell_row = info[0:1].astype(i32)
    well_row = info[1:2].astype(i32)
    valid = iota((DEVICES, LANES), 1) < WELL_DEV
    moves = jnp.where(valid, (sum_parts(got) + table[0]) * table[1], 0.0)
    values = gather_wells(moves, well_row >> 4, well_row & 15)
    wells = scatter(cell_row, info[2:3] * values).reshape(L, R, C)
    halo = unpack_columns(col_first, col_second)
    lows, highs = from_partner("gx", row_first[...], row_second[...])
    columns = (gain_col[...] * halo, end_col[0] * halo, end_col[1] * halo)
    wait_copies(copies)

    def outs(l):
        return ((update.at[:, l], update_h.at[:, l]),)

    for l in range(L):
        low = lows[l : l + 1]
        high = highs[l : l + 1]
        for n in range(3):
            rows = [gain_row[side, l : l + 1, :] if n == 0 else end_row[side, n - 1, l : l + 1, :] for side in range(2)]
            update[n, l] = ahead[n, l] + (head[l] if n == 0 else slope[n - 1, l]) * wells[l]
            add_faces(update.at[n], l, rows[0] * low, rows[1] * high, columns[n])
        layer_copies(outs, sems_out, l)[0].start()
    for l in range(L):
        wait_copies(layer_copies(outs, sems_out, l))


def call(kernel, outs, ins, operands, scratch=(), flops=0):
    shapes = tuple(
        pltpu.VMEM(s, f32) if w is VM else pltpu.HBM(s, f32) if w is HB else jax.ShapeDtypeStruct(s, f32)
        for s, w in outs
    )
    moved = 4 * sum(int(x.size) for x in operands)
    operands = [
        pltpu.with_memory_space_constraint(x, pltpu.HBM) if w is HB else x for x, w in zip(operands, ins)
    ]
    return pl.pallas_call(
        kernel,
        out_shape=shapes,
        in_specs=ins,
        out_specs=tuple(w or VM for _, w in outs),
        scratch_shapes=[pltpu.VMEM(x, f32) if type(x) is tuple else x for x in scratch],
        compiler_params=pltpu.CompilerParams(vmem_limit_bytes=40 * 1024 * 1024),
        cost_estimate=pl.CostEstimate(flops=flops, bytes_accessed=moved, transcendentals=0),
    )(*operands)


FIELD = (L, R, C)
TWO, THREE, SIX, FACED = ((2,) + FIELD, (3,) + FIELD, (6,) + FIELD, (L + 1, R, C))
FACES = (((L, C), VM), ((L, C), VM), ((L, LANES), VM), ((L, LANES), VM))
WIDE_FACES = (((4 * L, C), VM), ((4 * L, C), VM), ((4 * L, LANES), VM), ((4 * L, LANES), VM))
SMALL = (8, LANES)
PAY = ((TILES * DEVICES, LANES), None)
sem = pltpu.SemaphoreType.DMA


def exchange(array):
    return lax.all_to_all(array, AXES, split_axis=0, concat_axis=0, tiled=True)


def exchange_tiles(array):
    return exchange(array.reshape(DEVICES, WIDTH)).reshape(TILES * DEVICES, LANES)


def partners():
    rows, columns = (lax.axis_size(axis) for axis in AXES)
    swaps = [[], [], [], []]
    for x in range(rows):
        for y in range(columns):
            here = x * columns + y
            x_next = x - 1 + 2 * (x % 2)
            y_next = y - 1 + 2 * (y % 2)
            swaps[0].append((here, (x ^ 1) * columns + y))
            swaps[1].append((here, x_next * columns + y if 0 <= x_next < rows else x * columns + (y ^ 1)))
            swaps[2].append((here, x * columns + (y ^ 1)))
            swaps[3].append((here, x * columns + y_next if 0 <= y_next < columns else (x ^ 1) * columns + y))
    return swaps


def halo_of(faces):
    swaps = partners()
    got = {n: lax.ppermute(faces[n], AXES, swaps[n]) for n in (3, 1, 2, 0)}
    return [got[n] for n in range(4)]


def local(
    pressure, sat_water, sat_gas, old_mass, perm, porosity,
    perf_well, perf_cell, perf_index, well_pressure, well_rate,
):
    *faces, p, sw, sg, info, own = call(
        faces_kernel,
        WIDE_FACES + ((FIELD, VM), (FIELD, VM), (FIELD, VM), ((8, PERFS), VM), (SMALL, VM)),
        [HB] * 9,
        (
            perf_cell.reshape(1, PERFS), perf_well.reshape(1, PERFS), perf_index.reshape(1, PERFS),
            well_pressure.reshape(1, WELL_DEV), well_rate.reshape(1, WELL_DEV), pressure, sat_water, sat_gas, perm,
        ),
        [
            pltpu.VMEM((1, PERFS), i32), pltpu.VMEM((1, PERFS), i32), (1, PERFS),
            (1, WELL_DEV), (1, WELL_DEV), pltpu.VMEM(TWO, bf16), sem((4,)), sem((5,)),
        ],
    )
    halo = halo_of(faces)
    pay, perf = call(
        start_kernel, (((DEVICES, LANES), VM), ((8, PERFS), VM)), [VM] * 5, (info, own, p, sw, sg)
    )
    pay, *halo = pl.pallas_call(
        after_kernel,
        out_shape=tuple(pltpu.VMEM(x.shape, f32) for x in (pay, *halo)),
        in_specs=[pl.BlockSpec(memory_space=pl.ANY)] * 5,
        out_specs=(pl.BlockSpec(memory_space=pl.ANY),) * 5,
        input_output_aliases={n: n for n in range(5)},
    )(pay, *halo)
    got = exchange(pay)
    coef_row, coef_col, base, head, coef, tx, ty, tz, weight, res, diag = call(
        setup_kernel,
        (
            ((2, 3, L, C), VM), ((3, R, LANES), VM), (FIELD, VM), (FIELD, VM), (THREE, HB), (TWO, HB), (TWO, HB),
            (FACED, HB), (THREE, HB), (THREE, HB), (TWO, HB),
        ),
        [VM] * 8 + [HB] * 3,
        (info, *halo, p, sw, sg, porosity, old_mass, perm),
        [
            FIELD, THREE, pltpu.VMEM(THREE, bf16), THREE, TWO, TWO, FACED,
            THREE, THREE, TWO, FIELD, (4 * L, C), (4 * L, C), sem((3,)), sem((4,)), sem((3, L)),
        ],
        flops=400 * L * R * C,
    )
    mine, well_residual, spread, start, pay = call(
        first_kernel,
        ((SMALL, VM), ((1, WELL_DEV), None), (FIELD, VM), (FIELD, VM), PAY),
        [VM] * 6,
        (got, info, own, perf, base, head),
    )
    got = exchange_tiles(pay)
    halo = halo_of(call(step_faces_kernel, FACES, [VM], (start,)))
    fields = (coef, tx, ty, tz, weight)
    ahead, gain_row, gain_col, residual, gain = call(
        grid_kernel,
        ((FIELD, VM), ((2, L, C), VM), ((R, LANES), VM), (THREE, HB), (SIX, HB)),
        [VM] * 5 + [HB] * 6,
        (coef_row, coef_col, head, spread, start, *fields, res),
        [THREE, TWO, TWO, FACED, THREE, THREE, THREE, SIX, sem((12,)), sem((2, L))],
        flops=100 * L * R * C,
    )
    *faces, step = call(
        second_kernel,
        FACES + ((FIELD, VM),),
        [VM] * 10,
        (got, info, ahead, head, gain_row, gain_col, *halo),
    )
    halo = halo_of(faces)
    table, parts, spread, gain_near = call(
        wells_kernel,
        (((2, DEVICES, LANES), VM), (SMALL, VM), (FIELD, VM), (SIX, VM)),
        [VM] * 4 + [HB],
        (got, info, perf, step, gain),
        [sem((1,))],
    )
    step, pay = call(
        third_kernel,
        ((FIELD, VM), PAY),
        [VM] * 12,
        (info, perf, parts, spread, step, start, gain_near, head, *halo),
        [(L, C), (L, C)],
    )
    got = exchange_tiles(pay)
    halo = halo_of(call(step_faces_kernel, FACES, [VM], (step,)))
    end_row, end_col, ahead, slope = call(
        last_grid_kernel,
        (((2, 2, L, C), VM), ((2, R, LANES), VM), (THREE, HB), (TWO, HB)),
        [VM] * 6 + [HB] * 9,
        (coef_row, coef_col, head, step, gain_row, gain_col, pressure, porosity, *fields, diag, residual),
        [FIELD, FIELD, THREE, TWO, TWO, FACED, THREE, TWO, THREE, THREE, TWO, sem((18,)), sem((2, L))],
        flops=150 * L * R * C,
    )
    update, moved = call(
        final_kernel,
        ((THREE, HB), ((1, WELL_DEV), None)),
        [VM] * 13 + [HB] * 2,
        (got, info, table, mine, head, gain_row, gain_col, end_row, end_col, *halo, ahead, slope),
        [THREE, TWO, THREE, sem((2,)), sem((1, L))],
    )
    return residual, well_residual.reshape(WELL_DEV), update, moved.reshape(WELL_DEV)


def solution(mesh):
    return jax.shard_map(
        local,
        mesh=mesh,
        in_specs=(
            P(None, "gx", "gy"),
            P(None, "gx", "gy"),
            P(None, "gx", "gy"),
            P(None, None, "gx", "gy"),
            P(None, None, "gx", "gy"),
            P(None, "gx", "gy"),
            P(("gx", "gy")),
            P(("gx", "gy")),
            P(("gx", "gy")),
            P(("gx", "gy")),
            P(("gx", "gy")),
        ),
        out_specs=(
            P(None, None, "gx", "gy"),
            P(("gx", "gy")),
            P(None, None, "gx", "gy"),
            P(("gx", "gy")),
        ),
        check_vma=False,
    )
```

```python
import jax
import jax.numpy as jnp
from jax import lax
from jax.experimental import pallas as pl
from jax.experimental.pallas import tpu as pltpu
from jax.sharding import PartitionSpec as P

f32 = jnp.float32
bf16 = jnp.bfloat16
i32 = jnp.int32

compress = (0.05, 0.02, 0.2)
viscosity = (0.5, 2.0, 0.1)
volume_scale = 4.0
layer_ratio = 0.1
AXES = ("gx", "gy")
DEVICES = 128
WELL_DEV = 16
REACH = 40
FAR = 64
TAIL = REACH * WELL_DEV
WIDTH = TAIL + 128
TILES = WIDTH // 128
LANES = 128
L, R, C = 8, 64, 256
PERFS = 256
BLOCK = 8
VM = pl.BlockSpec(memory_space=pltpu.VMEM)
HB = pl.BlockSpec(memory_space=pltpu.HBM)


def iota(shape, dim):
    return lax.broadcasted_iota(i32, shape, dim)


def split3(x):
    high = x.astype(bf16)
    rest = x - high.astype(f32)
    middle = rest.astype(bf16)
    low = (rest - middle.astype(f32)).astype(bf16)
    return high, middle, low


def dot(a, b):
    return jnp.dot(a, b, preferred_element_type=f32)


def to_column(row):
    n = row.shape[1]
    return jnp.sum(jnp.where(iota((n, n), 0) == iota((n, n), 1), row, 0.0), axis=1, keepdims=True)


def to_row(column):
    n = column.shape[0]
    return jnp.sum(jnp.where(iota((n, n), 0) == iota((n, n), 1), column, 0.0), axis=0, keepdims=True)


def coeffs_of(p, sw, sg):
    so = 1.0 - sw - sg
    return tuple(
        s * s * (1.0 / viscosity[a]) * (1.0 + compress[a] * p) for a, s in enumerate((sw, so, sg))
    )


def scatter(cell_row, values):
    match = iota((L * R, PERFS), 0) == (cell_row >> 8)
    column = to_column(cell_row.astype(f32)).astype(i32) & (C - 1)
    spread = (iota((PERFS, C), 1) == column).astype(bf16)
    return sum(
        dot(jnp.where(match, part.astype(f32), 0.0).astype(bf16), spread) for part in split3(values)
    )


def gather_cells(cell_column, fields):
    onehot = (iota((PERFS, L * R), 1) == (cell_column >> 8)).astype(bf16)
    here = iota((PERFS, C), 1) == (cell_column & (C - 1))
    picked = []
    for field in fields:
        rows = sum(dot(onehot, part) for part in split3(field))
        picked.append(jnp.sum(jnp.where(here, rows, 0.0), axis=1, keepdims=True))
    return picked


def flat(field):
    return field[...].reshape(L * R, C)


def gather_wells(table, holder, slot):
    onehot = (iota((DEVICES, PERFS), 0) == holder).astype(bf16)
    wide = sum(dot(part, onehot) for part in split3(table.T))
    return jnp.sum(jnp.where(iota((LANES, PERFS), 0) == slot, wide, 0.0), axis=0, keepdims=True)


def to_holders(holder, slot_column, columns):
    lane = iota((PERFS, LANES), 1)
    group = lane >> 4
    values = jnp.zeros((PERFS, LANES), f32)
    for g, column in columns:
        values = jnp.where(group == g, column, values)
    values = jnp.where((lane & 15) == slot_column, values, 0.0)
    onehot = (iota((DEVICES, PERFS), 0) == holder).astype(bf16)
    return sum(dot(onehot, part) for part in split3(values))


def parts_by_offset(me, well_row, values):
    offset = (me - (well_row >> 4)) & (DEVICES - 1)
    lane = jnp.where(offset == FAR, TAIL, offset * WELL_DEV) + (well_row & 15)
    column = to_column(lane.astype(f32)).astype(i32)
    onehot = (iota((PERFS, WIDTH), 1) == column).astype(bf16)
    high, middle, low = split3(values)
    rows = jnp.concatenate([high.astype(f32), middle.astype(f32), low.astype(f32), jnp.zeros((5, PERFS), f32)], axis=0)
    return jnp.sum(dot(rows.astype(bf16), onehot), axis=0, keepdims=True)


def tile_of(got, t):
    return got[pl.ds(t, DEVICES, stride=TILES), :]


def sum_parts(got):
    aligned = tile_of(got, 0)
    for t in range(1, TAIL // LANES):
        aligned = aligned + pltpu.roll(tile_of(got, t), DEVICES - 8 * t, 0)
    total = aligned + pltpu.roll(tile_of(got, 5), DEVICES - FAR, 0)
    for u in range(1, 8):
        total = total + pltpu.roll(pltpu.roll(aligned, DEVICES - u, 0), LANES - 16 * u, 1)
    return total


def to_everyone(pay, rows):
    four = jnp.concatenate([rows] * 4, axis=0)
    pay[...] = jnp.broadcast_to(four[None], (DEVICES // 4, 4 * TILES, LANES)).reshape(TILES * DEVICES, LANES)


def rolled_row(row, shift):
    return pltpu.roll(jnp.broadcast_to(row, (8, LANES)), shift, 1)[0:1]


def shift_rows(x, first, last):
    return (
        jnp.concatenate([first, x[:-1]], axis=0),
        jnp.concatenate([x[1:], last], axis=0),
    )


def shift_columns(x, first, last):
    lane = iota(x.shape, 1)
    return (
        jnp.where(lane == 0, first, pltpu.roll(x, 1, 1)),
        jnp.where(lane == C - 1, last, pltpu.roll(x, C - 1, 1)),
    )


def lane_of(x, index):
    return pltpu.roll(x, (LANES - index) % LANES, 1)[:, 0:1]


def is_even(axis):
    return lax.axis_index(axis) % 2 == 0


def by_partner(axis, low, high):
    even = is_even(axis)
    return jnp.where(even, high, low), jnp.where(even, low, high)


def from_partner(axis, first, second):
    even = is_even(axis)
    return jnp.where(even, second, first), jnp.where(even, first, second)


def pack_columns(columns, first, second):
    n = first.shape[0]
    turned = jnp.concatenate([columns, jnp.zeros((LANES - R, LANES), f32)], axis=0).T
    first[...], second[...] = by_partner("gy", turned[0:n], turned[n : 2 * n])


def unpack_columns(first, second):
    n = first.shape[0]
    low, high = from_partner("gy", first[...], second[...])
    rows = jnp.concatenate([low, high, jnp.zeros((LANES - 2 * n, LANES), f32)], axis=0)
    return rows.T[0:R]


def write_faces(step, outs):
    row_first, row_second, col_first, col_second = outs
    lane = iota((R, LANES), 1)
    columns = jnp.zeros((R, LANES), f32)
    for l in range(L):
        x = step[l]
        pair = by_partner("gx", x[0:1], x[R - 1 : R])
        row_first[l : l + 1, :], row_second[l : l + 1, :] = pair
        columns = jnp.where(lane == l, x[:, 0:1], columns)
        columns = jnp.where(lane == L + l, x[:, C - 1 : C], columns)
    pack_columns(columns, col_first, col_second)


def start_copies(pairs, sems):
    copies = [pltpu.make_async_copy(a, b, sems.at[n]) for n, (a, b) in enumerate(pairs)]
    for c in copies:
        c.start()
    return copies


def wait_copies(copies):
    for c in copies:
        c.wait()


def layer_copies(pairs, sems, l):
    return [pltpu.make_async_copy(a, b, sems.at[n, l]) for n, (a, b) in enumerate(pairs(l))]


def faces_kernel(
    cell_h, well_h, index_h, pressure_h, rate_h, p_h, sw_h, sg_h, perm_h,
    row_first, row_second, col_first, col_second, p, sw, sg, info, own,
    cell_in, well_in, index_in, pressure_in, rate_in, perm, sems, sems_in,
):
    copies = start_copies(((perm_h.at[0:2], perm), (p_h, p), (sw_h, sw), (sg_h, sg)), sems)
    small = start_copies(
        (
            (cell_h, cell_in), (well_h, well_in), (index_h, index_in),
            (pressure_h, pressure_in), (rate_h, rate_in),
        ),
        sems_in,
    )
    me = lax.axis_index("gx") * 16 + lax.axis_index("gy")
    device = jnp.full((1, PERFS), me, i32).astype(f32)
    wait_copies(small)
    numbers = [cell_in[...].astype(f32), well_in[...].astype(f32), index_in[...], device]
    info[...] = jnp.concatenate(numbers + [jnp.zeros((4, PERFS), f32)], axis=0)
    blank = jnp.zeros((1, LANES - WELL_DEV), f32)
    heads = jnp.concatenate([pressure_in[...], blank], axis=1)
    rates = jnp.concatenate([rate_in[...], blank], axis=1)
    own[...] = jnp.concatenate([heads, rates, jnp.zeros((6, LANES), f32)], axis=0)
    lane = iota((R, LANES), 1)
    columns = jnp.zeros((R, LANES), f32)
    wait_copies(copies[:1])
    for l in range(L):
        n = 3 * L + l
        low = perm[0, l, 0:16, :].astype(f32)[0:1]
        high = perm[0, l, R - 16 : R, :].astype(f32)[15:16]
        row_first[n : n + 1, :], row_second[n : n + 1, :] = by_partner("gx", low, high)
        k = perm[1, l].astype(f32)
        columns = jnp.where(lane == n, k[:, 0:1], columns)
        columns = jnp.where(lane == 4 * L + n, k[:, C - 1 : C], columns)
    wait_copies(copies[1:])
    for l in range(L):
        for f, ref in enumerate((p, sw, sg)):
            x = ref[l]
            n = f * L + l
            pair = by_partner("gx", x[0:1], x[R - 1 : R])
            row_first[n : n + 1, :], row_second[n : n + 1, :] = pair
            columns = jnp.where(lane == n, x[:, 0:1], columns)
            columns = jnp.where(lane == 4 * L + n, x[:, C - 1 : C], columns)
    pack_columns(columns, col_first, col_second)


def start_kernel(info, own, p, sw, sg, pay, perf):
    well_row = info[1:2].astype(i32)
    slot_column = to_column(info[1:2]).astype(i32) & 15
    here = gather_cells(to_column(info[0:1]).astype(i32), (flat(p), flat(sw), flat(sg)))
    coeffs = coeffs_of(*here)
    total = to_column(info[2:3]) * (coeffs[0] + coeffs[1] + coeffs[2])
    sums = to_holders(well_row >> 4, slot_column, ((0, total), (1, total * here[0])))
    pay[...] = sums + rolled_row(own[0:1], 32)
    perf[...] = jnp.broadcast_to(to_row(total), (8, PERFS))


def after_kernel(pay, *refs):
    pass


def reciprocal(x):
    r = pl.reciprocal(x, approx=True)
    return r * (2.0 - x * r)


def transmit(k, k_next):
    return k * k_next * reciprocal(k + k_next)


def neighbours(field, l, lo, rows, columns):
    hi = lo + BLOCK
    here = field[l, lo:hi, :]
    if lo > 0:
        before = field[l, lo - 1 : hi - 1, :]
    else:
        before = jnp.concatenate([rows[0], field[l, 0 : hi - 1, :]], axis=0)
    if hi < R:
        after = field[l, lo + 1 : hi + 1, :]
    else:
        after = jnp.concatenate([field[l, lo + 1 : R, :], rows[1]], axis=0)
    sides = (field[jnp.maximum(l - 1, 0), lo:hi, :], field[jnp.minimum(l + 1, L - 1), lo:hi, :])
    return (before, after) + shift_columns(here, *columns) + sides


def coeff_neighbours(coef, coef_row, a, l, lo, columns):
    rows = (coef_row[0, a, pl.ds(l, 1), :], coef_row[1, a, pl.ds(l, 1), :])
    ends = [c[lo : lo + BLOCK] for c in columns[a]]
    return neighbours(coef.at[a], l, lo, rows, ends)


def coeff_columns(coef_col, l):
    return [(lane_of(coef_col[a], l), lane_of(coef_col[a], 4 * L + l)) for a in range(3)]


def inner_neighbours(step, l, lo):
    blank = jnp.zeros((1, C), f32)
    return neighbours(step, l, lo, (blank, blank), (0.0, 0.0))


def face_terms(tx, ty, tz, l, rows):
    return (tx[0, l, rows, :], tx[1, l, rows, :], ty[0, l, rows, :], ty[1, l, rows, :], tz[l, rows, :], tz[l + 1, rows, :])


def halves(pairs):
    parts = []
    for half in range(2):
        for a, b, dim in pairs:
            count = a.shape[dim]
            middle = L // 2 + 1
            span = pl.ds(0, middle) if half == 0 else pl.ds(middle, count - middle)
            index = (slice(None),) * dim + (span,)
            parts.append((a.at[index], b.at[index]))
    return parts


def put_with_faces(field, l, x, low, high, columns):
    lane = iota((R, LANES), 1)
    field[l, :, 0:LANES] = x[:, 0:LANES] + jnp.where(lane == 0, columns[:, l : l + 1], 0.0)
    field[l, :, LANES:C] = x[:, LANES:C] + jnp.where(lane == LANES - 1, columns[:, L + l : L + l + 1], 0.0)
    field[l, 0:1, :] += low
    field[l, R - 1 : R, :] += high


def end_columns(columns, l, first, last):
    lane = iota((R, LANES), 1)
    return jnp.where(lane == l, first, jnp.where(lane == L + l, last, columns))


def setup_kernel(
    info, row_first, row_second, col_first, col_second, p, sw, sg, por_h, mass_h, perm_h,
    coef_row, coef_col, base, head, coef_h, tx_h, ty_h, tz_h, weight_h, res_h, diag_h,
    por, mass, perm, coef, tx, ty, tz, weight, res, diag, index_sum, row_lo, row_hi,
    sems, sems_t, sems_out,
):
    copies = start_copies(((perm_h, perm), (por_h, por), (mass_h, mass)), sems)
    index_sum[...] = scatter(info[0:1].astype(i32), info[2:3]).reshape(L, R, C)
    row_lo[...], row_hi[...] = from_partner("gx", row_first[...], row_second[...])
    for side, ref in enumerate((row_lo, row_hi)):
        for a, c in enumerate(coeffs_of(ref[0:L], ref[L : 2 * L], ref[2 * L : 3 * L])):
            coef_row[side, a] = c
    columns = unpack_columns(col_first, col_second)
    for a, c in enumerate(
        coeffs_of(columns, pltpu.roll(columns, LANES - L, 1), pltpu.roll(columns, LANES - 2 * L, 1))
    ):
        coef_col[a] = c
    lane = iota((R, C), 1)
    me = info[3:4, 0:1].astype(i32)
    gx = me >> 4
    gy = me & 15
    inside = [jnp.where(t, 1.0, 0.0) for t in (gx > 0, gx < 7, gy > 0, gy < 15)]
    wait_copies(copies[:1])

    def first(l, carry):
        for a, c in enumerate(coeffs_of(p[l], sw[l], sg[l])):
            coef[a, l] = c
        k = perm[0, l].astype(f32)
        n = 3 * L + l
        edge = row_lo[pl.ds(n, 1), :] * inside[0]
        before = transmit(k, jnp.concatenate([edge, k[:-1]], axis=0))
        edge = row_hi[pl.ds(n, 1), :] * inside[1]
        tx[0, l] = before
        tx[1, l] = jnp.concatenate([before[1:], transmit(k[R - 1 : R], edge)], axis=0)
        k = perm[1, l].astype(f32)
        edge = lane_of(columns, n) * inside[2]
        before = transmit(k, jnp.where(lane == 0, edge, pltpu.roll(k, 1, 1)))
        edge = lane_of(columns, 4 * L + n) * inside[3]
        ty[0, l] = before
        ty[1, l] = jnp.where(lane == C - 1, transmit(k[:, C - 1 : C], edge), pltpu.roll(before, C - 1, 1))
        k = perm[2, l].astype(f32)
        under = perm[2, jnp.maximum(l - 1, 0)].astype(f32)
        tz[l] = jnp.where(l > 0, layer_ratio, 0.0) * transmit(k, under)
        return carry

    lax.fori_loop(0, L, first, 0)
    tz[L] = jnp.zeros((R, C), f32)
    saved = start_copies(((coef, coef_h), (tx, tx_h), (ty, ty_h), (tz, tz_h)), sems_t)
    wait_copies(copies[1:])

    def outs(l):
        return (
            (weight.at[:, l], weight_h.at[:, l]),
            (res.at[:, l], res_h.at[:, l]), (diag.at[:, l], diag_h.at[:, l]),
        )

    def second(l, carry):
        rows = (row_lo[pl.ds(l, 1), :], row_hi[pl.ds(l, 1), :])
        ends = lane_of(columns, l), lane_of(columns, 4 * L + l)
        sides_of = coeff_columns(coef_col, l)
        for lo in range(0, R, BLOCK):
            at = slice(lo, lo + BLOCK)
            here = p[l, at, :]
            nexts = neighbours(p, l, lo, rows, [e[at] for e in ends])
            faces = face_terms(tx, ty, tz, l, at)
            drops = [t * (here - q) for t, q in zip(faces, nexts)]
            face_sum = sum(faces)
            drop_sum = sum(drops)
            porous = volume_scale * por[l, at, :]
            water, gas = (sw[l, at, :], sg[l, at, :])
            sats = (water, 1.0 - water - gas, gas)
            indices = index_sum[l, at, :]
            diagonals, residuals, inverses, cs = [], [], [], []
            for a in range(3):
                c = coef[a, l, at, :]
                ab = c * face_sum
                net = c * drop_sum
                for t, d, s in zip(faces, drops, coeff_neighbours(coef, coef_row, a, l, lo, sides_of)):
                    ab = ab + t * s
                    net = net + d * s
                b = 1.0 + compress[a] * here
                stored = porous * sats[a]
                diagonals.append(compress[a] * stored + ab + c * indices)
                residuals.append(b * stored - volume_scale * mass[a, l, at, :] + net + c * (indices * here))
                inverses.append(reciprocal(porous * b))
                cs.append(c)
            inverse_total = reciprocal(sum(d * v for d, v in zip(diagonals, inverses)))
            weights = [v * inverse_total for v in inverses]
            base[l, at, :] = -sum(w * r for w, r in zip(weights, residuals))
            head[l, at, :] = sum(w * c for w, c in zip(weights, cs))
            for a in range(3):
                weight[a, l, at, :] = weights[a]
                res[a, l, at, :] = residuals[a]
            diag[0, l, at, :] = diagonals[0]
            diag[1, l, at, :] = diagonals[2]
        for c in layer_copies(outs, sems_out, l):
            c.start()
        return carry

    lax.fori_loop(0, L, second, 0)
    wait_copies(saved)
    for l in range(L):
        wait_copies(layer_copies(outs, sems_out, l))


def first_kernel(
    got, info, own, perf, base, head, mine, well_residual, spread, step, pay,
):
    lane = iota((1, LANES), 1)
    sums = jnp.sum(got[...], axis=0, keepdims=True)
    total = jnp.where(lane < WELL_DEV, sums, 1.0)
    flow = rolled_row(sums, LANES - 16)
    residual = jnp.where(lane < WELL_DEV, flow - total * own[0:1] - own[1:2], 0.0)
    inverse = jnp.where(lane < WELL_DEV, 1.0 / total, 0.0)
    mine[...] = jnp.concatenate([residual, inverse, jnp.zeros((6, LANES), f32)], axis=0)
    well_residual[...] = residual[:, 0:WELL_DEV]
    cell_row = info[0:1].astype(i32)
    well_row = info[1:2].astype(i32)
    heads = gather_wells(got[...], well_row >> 4, (well_row & 15) + 32)
    spread[...] = scatter(cell_row, info[2:3] * heads).reshape(L, R, C)
    step[...] = base[...] + head[...] * spread[...]
    here = to_row(gather_cells(to_column(info[0:1]).astype(i32), (flat(step),))[0])
    parts = parts_by_offset(info[3:4].astype(i32), well_row, perf[0:1] * here)
    packed = parts[:, TAIL:]
    for n, row in enumerate((residual * inverse, residual, inverse)):
        packed = packed + rolled_row(row, 16 * (n + 1))
    tiles = [parts[:, LANES * t : LANES * (t + 1)] for t in range(5)]
    to_everyone(pay, jnp.concatenate(tiles + [packed], axis=0))


def step_faces_kernel(step, row_first, row_second, col_first, col_second):
    write_faces(step, (row_first, row_second, col_first, col_second))


def grid_kernel(
    coef_row, coef_col, head, spread, step,
    coef_h, tx_h, ty_h, tz_h, weight_h, res_h,
    ahead, end_row, end_col, residual_h, gain_h,
    coef, tx, ty, tz, weight, res, residual, gain, sems, sems_out,
):
    copies = start_copies(
        halves(((coef_h, coef, 1), (tx_h, tx, 1), (ty_h, ty, 1), (tz_h, tz, 0), (weight_h, weight, 1), (res_h, res, 1))),
        sems,
    )
    wait_copies(copies[:6])

    def outs(l):
        return (
            (residual.at[:, l], residual_h.at[:, l]), (gain.at[:, l], gain_h.at[:, l]),
        )

    def layer(l, ends):
        sides_of = coeff_columns(coef_col, l)
        for lo in range(0, R, BLOCK):
            at = slice(lo, lo + BLOCK)
            nexts = inner_neighbours(step, l, lo)
            faces = face_terms(tx, ty, tz, l, at)
            wells = spread[l, at, :]
            mixes = [head[l, at, :]] * 6
            for a in range(3):
                w = weight[a, l, at, :]
                sides = coeff_neighbours(coef, coef_row, a, l, lo, sides_of)
                mixes = [m + w * s for m, s in zip(mixes, sides)]
                residual[a, l, at, :] = res[a, l, at, :] - coef[a, l, at, :] * wells
            total = step[l, at, :]
            for j in range(6):
                g = faces[j] * mixes[j]
                gain[j, l, at, :] = g
                total = total + g * nexts[j]
            ahead[l, at, :] = total
        end_row[0, pl.ds(l, 1), :] = gain[0, l, 0:1, :]
        end_row[1, pl.ds(l, 1), :] = gain[1, l, R - 1 : R, :]
        for c in layer_copies(outs, sems_out, l):
            c.start()
        return end_columns(ends, l, gain[2, l, :, 0:LANES][:, 0:1], gain[3, l, :, C - LANES : C][:, LANES - 1 : LANES])

    ends = lax.fori_loop(0, L // 2, layer, jnp.zeros((R, LANES), f32))
    wait_copies(copies[6:])
    end_col[...] = lax.fori_loop(L // 2, L, layer, ends)
    for l in range(L):
        wait_copies(layer_copies(outs, sems_out, l))


def second_kernel(
    got, info, ahead, head, end_row, end_col, row_first, row_second, col_first, col_second,
    out_row_first, out_row_second, out_col_first, out_col_second, step,
):
    cell_row = info[0:1].astype(i32)
    well_row = info[1:2].astype(i32)
    moves = gather_wells(tile_of(got, 5), well_row >> 4, (well_row & 15) + 16)
    wells = scatter(cell_row, info[2:3] * moves).reshape(L, R, C)
    columns = end_col[...] * unpack_columns(col_first, col_second)
    low, high = from_partner("gx", row_first[...], row_second[...])
    low = end_row[0] * low
    high = end_row[1] * high
    for l in range(L):
        put_with_faces(step, l, ahead[l] + head[l] * wells[l], low[l : l + 1], high[l : l + 1], columns)
    write_faces(step, (out_row_first, out_row_second, out_col_first, out_col_second))


def wells_kernel(
    got, info, perf, step, base, head, gain_h, table, parts, near, gain, spread, sems,
):
    copies = start_copies(((gain_h, gain),), sems)
    tail = tile_of(got, 5)
    residuals = pltpu.roll(tail, LANES - 32, 1)
    inverses = pltpu.roll(tail, LANES - 48, 1)
    table[0] = residuals
    table[1] = inverses
    cell_row = info[0:1].astype(i32)
    well_row = info[1:2].astype(i32)
    valid = iota((DEVICES, LANES), 1) < WELL_DEV
    moves = jnp.where(valid, (sum_parts(got) + residuals) * inverses, 0.0)
    values = gather_wells(moves, well_row >> 4, well_row & 15)
    spread[...] = scatter(cell_row, info[2:3] * values).reshape(L, R, C)
    here = to_row(gather_cells(to_column(info[0:1]).astype(i32), (flat(step),))[0])
    flows = parts_by_offset(info[3:4].astype(i32), well_row, perf[0:1] * here)
    tiles = [flows[:, LANES * t : LANES * (t + 1)] for t in range(6)]
    parts[...] = jnp.concatenate(tiles + [jnp.zeros((2, LANES), f32)], axis=0)
    wait_copies(copies)

    def layer(l, carry):
        for lo in range(0, R, BLOCK):
            at = slice(lo, lo + BLOCK)
            total = base[l, at, :] + head[l, at, :] * spread[l, at, :]
            for j, q in enumerate(inner_neighbours(step, l, lo)):
                total = total + gain[j, l, at, :] * q
            near[l, at, :] = total
        return carry

    lax.fori_loop(0, L, layer, 0)


def third_kernel(info, perf, parts, near, end_row, end_col, row_first, row_second, col_first, col_second, step, pay):
    columns = end_col[...] * unpack_columns(col_first, col_second)
    low, high = from_partner("gx", row_first[...], row_second[...])
    low = end_row[0] * low
    high = end_row[1] * high
    for l in range(L):
        put_with_faces(step, l, near[l], low[l : l + 1], high[l : l + 1], columns)
    here = gather_cells(to_column(info[0:1]).astype(i32), (flat(step),))[0]
    well_row = info[1:2].astype(i32)
    slot_column = to_column(info[1:2]).astype(i32) & 15
    sums = to_holders(well_row >> 4, slot_column, ((1, to_column(perf[0:1]) * here),))
    to_everyone(pay, parts[0:TILES])
    pay[pl.ds(TILES - 1, DEVICES, stride=TILES), :] = sums + parts[TILES - 1 : TILES]


def last_grid_kernel(
    coef_row, coef_col, head, step, gain_row, gain_col,
    p_h, por_h, coef_h, tx_h, ty_h, tz_h, weight_h, diag_h, residual_h,
    end_row, end_col, ahead_h, slope_h,
    p, por, coef, tx, ty, tz, weight, diag, residual, ahead, slope, sems, sems_out,
):
    copies = start_copies(
        halves(
            (
                (p_h, p, 0), (por_h, por, 0), (coef_h, coef, 1), (tx_h, tx, 1), (ty_h, ty, 1), (tz_h, tz, 0),
                (weight_h, weight, 1), (diag_h, diag, 1), (residual_h, residual, 1),
            )
        ),
        sems,
    )
    wait_copies(copies[:9])

    def outs(l):
        return ((ahead.at[:, l], ahead_h.at[:, l]), (slope.at[:, l], slope_h.at[:, l]))

    def layer(l, ends):
        sides_of = coeff_columns(coef_col, l)
        gains = lane_of(gain_col[...], l), lane_of(gain_col[...], L + l)
        pairs = [([], []), ([], [])]
        for lo in range(0, R, BLOCK):
            at = slice(lo, lo + BLOCK)
            nexts = inner_neighbours(step, l, lo)
            faces = face_terms(tx, ty, tz, l, at)
            flows = [t * q for t, q in zip(faces, nexts)]
            flow_sum = sum(flows)
            rights, cs, sides = [], [], []
            for a in range(3):
                c = coef[a, l, at, :]
                total = c * flow_sum - residual[a, l, at, :]
                sides.append(coeff_neighbours(coef, coef_row, a, l, lo, sides_of))
                for v, s in zip(flows, sides[a]):
                    total = total + v * s
                rights.append(total)
                cs.append(c)
            z = sum(weight[a, l, at, :] * rights[a] for a in range(3))
            h = head[l, at, :]
            porous = volume_scale * por[l, at, :]
            inverses = [reciprocal(porous * (1.0 + compress[a] * p[l, at, :])) for a in (0, 2)]
            ahead[0, l, at, :] = z
            for n, a in enumerate((0, 2)):
                d = diag[n, l, at, :]
                inverse = inverses[n]
                ahead[1 + n, l, at, :] = (rights[a] - d * z) * inverse
                slope[n, l, at, :] = (cs[a] - d * h) * inverse
                for side in range(2):
                    if lo == (0, R - BLOCK)[side]:
                        row = slice(0, 1) if side == 0 else slice(BLOCK - 1, BLOCK)
                        face = faces[side][row] * (cs[a][row] + sides[a][side][row])
                        end_row[side, n, pl.ds(l, 1), :] = (
                            face - d[row] * gain_row[side, pl.ds(l, 1), :]
                        ) * inverse[row]
                    col = slice(0, 1) if side == 0 else slice(C - 1, C)
                    face = faces[2 + side][:, col] * (cs[a][:, col] + sides_of[a][side][at])
                    pairs[n][side].append((face - d[:, col] * gains[side][at]) * inverse[:, col])
        for c in layer_copies(outs, sems_out, l):
            c.start()
        return tuple(
            end_columns(ends[n], l, *(jnp.concatenate(part, axis=0) for part in pairs[n])) for n in range(2)
        )

    blank = jnp.zeros((R, LANES), f32)
    ends = lax.fori_loop(0, L // 2, layer, (blank, blank))
    wait_copies(copies[9:])
    end_col[0], end_col[1] = lax.fori_loop(L // 2, L, layer, ends)
    for l in range(L):
        wait_copies(layer_copies(outs, sems_out, l))


def final_kernel(
    got, info, table, mine, head, gain_row, gain_col, end_row, end_col, row_first, row_second, col_first, col_second,
    ahead_h, slope_h, update_h, moved, ahead, slope, update, sems, sems_out,
):
    copies = start_copies(((ahead_h, ahead), (slope_h, slope)), sems)
    flow = rolled_row(jnp.sum(tile_of(got, TILES - 1), axis=0, keepdims=True), LANES - 16)
    moved[...] = ((flow + mine[0:1]) * mine[1:2])[:, 0:WELL_DEV]
    cell_row = info[0:1].astype(i32)
    well_row = info[1:2].astype(i32)
    valid = iota((DEVICES, LANES), 1) < WELL_DEV
    moves = jnp.where(valid, (sum_parts(got) + table[0]) * table[1], 0.0)
    values = gather_wells(moves, well_row >> 4, well_row & 15)
    wells = scatter(cell_row, info[2:3] * values).reshape(L, R, C)
    halo = unpack_columns(col_first, col_second)
    lows, highs = from_partner("gx", row_first[...], row_second[...])
    columns = (gain_col[...] * halo, end_col[0] * halo, end_col[1] * halo)
    wait_copies(copies)

    def outs(l):
        return ((update.at[:, l], update_h.at[:, l]),)

    for l in range(L):
        low = lows[l : l + 1]
        high = highs[l : l + 1]
        for n in range(3):
            rows = [gain_row[side, l : l + 1, :] if n == 0 else end_row[side, n - 1, l : l + 1, :] for side in range(2)]
            x = ahead[n, l] + (head[l] if n == 0 else slope[n - 1, l]) * wells[l]
            put_with_faces(update.at[n], l, x, rows[0] * low, rows[1] * high, columns[n])
        layer_copies(outs, sems_out, l)[0].start()
    for l in range(L):
        wait_copies(layer_copies(outs, sems_out, l))


def call(kernel, outs, ins, operands, scratch=(), flops=0):
    shapes = tuple(
        pltpu.VMEM(s, f32) if w is VM else pltpu.HBM(s, f32) if w is HB else jax.ShapeDtypeStruct(s, f32)
        for s, w in outs
    )
    moved = 4 * sum(int(x.size) for x in operands)
    operands = [
        pltpu.with_memory_space_constraint(x, pltpu.HBM) if w is HB else x for x, w in zip(operands, ins)
    ]
    return pl.pallas_call(
        kernel,
        out_shape=shapes,
        in_specs=ins,
        out_specs=tuple(w or VM for _, w in outs),
        scratch_shapes=[pltpu.VMEM(x, f32) if type(x) is tuple else x for x in scratch],
        compiler_params=pltpu.CompilerParams(vmem_limit_bytes=40 * 1024 * 1024),
        cost_estimate=pl.CostEstimate(flops=flops, bytes_accessed=moved, transcendentals=0),
    )(*operands)


FIELD = (L, R, C)
TWO, THREE, SIX, FACED = ((2,) + FIELD, (3,) + FIELD, (6,) + FIELD, (L + 1, R, C))
FACES = (((L, C), VM), ((L, C), VM), ((L, LANES), VM), ((L, LANES), VM))
WIDE_FACES = (((4 * L, C), VM), ((4 * L, C), VM), ((4 * L, LANES), VM), ((4 * L, LANES), VM))
SMALL = (8, LANES)
PAY = ((TILES * DEVICES, LANES), None)
sem = pltpu.SemaphoreType.DMA


def exchange(array):
    return lax.all_to_all(array, AXES, split_axis=0, concat_axis=0, tiled=True)


def exchange_tiles(array):
    return exchange(array.reshape(DEVICES, WIDTH)).reshape(TILES * DEVICES, LANES)


def partners():
    rows, columns = (lax.axis_size(axis) for axis in AXES)
    swaps = [[], [], [], []]
    for x in range(rows):
        for y in range(columns):
            here = x * columns + y
            x_next = x - 1 + 2 * (x % 2)
            y_next = y - 1 + 2 * (y % 2)
            swaps[0].append((here, (x ^ 1) * columns + y))
            swaps[1].append((here, x_next * columns + y if 0 <= x_next < rows else x * columns + (y ^ 1)))
            swaps[2].append((here, x * columns + (y ^ 1)))
            swaps[3].append((here, x * columns + y_next if 0 <= y_next < columns else (x ^ 1) * columns + y))
    return swaps


def halo_of(faces):
    swaps = partners()
    got = {n: lax.ppermute(faces[n], AXES, swaps[n]) for n in (3, 1, 2, 0)}
    return [got[n] for n in range(4)]


def local(
    pressure, sat_water, sat_gas, old_mass, perm, porosity,
    perf_well, perf_cell, perf_index, well_pressure, well_rate,
):
    *faces, p, sw, sg, info, own = call(
        faces_kernel,
        WIDE_FACES + ((FIELD, VM), (FIELD, VM), (FIELD, VM), ((8, PERFS), VM), (SMALL, VM)),
        [HB] * 9,
        (
            perf_cell.reshape(1, PERFS), perf_well.reshape(1, PERFS), perf_index.reshape(1, PERFS),
            well_pressure.reshape(1, WELL_DEV), well_rate.reshape(1, WELL_DEV), pressure, sat_water, sat_gas, perm,
        ),
        [
            pltpu.VMEM((1, PERFS), i32), pltpu.VMEM((1, PERFS), i32), (1, PERFS),
            (1, WELL_DEV), (1, WELL_DEV), pltpu.VMEM(TWO, bf16), sem((4,)), sem((5,)),
        ],
    )
    halo = halo_of(faces)
    pay, perf = call(
        start_kernel, (((DEVICES, LANES), VM), ((8, PERFS), VM)), [VM] * 5, (info, own, p, sw, sg)
    )
    pay, *halo = pl.pallas_call(
        after_kernel,
        out_shape=tuple(pltpu.VMEM(x.shape, f32) for x in (pay, *halo)),
        in_specs=[pl.BlockSpec(memory_space=pl.ANY)] * 5,
        out_specs=(pl.BlockSpec(memory_space=pl.ANY),) * 5,
        input_output_aliases={n: n for n in range(5)},
    )(pay, *halo)
    got = exchange(pay)
    coef_row, coef_col, base, head, coef, tx, ty, tz, weight, res, diag = call(
        setup_kernel,
        (
            ((2, 3, L, C), VM), ((3, R, LANES), VM), (FIELD, VM), (FIELD, VM), (THREE, HB), (TWO, HB), (TWO, HB),
            (FACED, HB), (THREE, HB), (THREE, HB), (TWO, HB),
        ),
        [VM] * 8 + [HB] * 3,
        (info, *halo, p, sw, sg, porosity, old_mass, perm),
        [
            FIELD, THREE, pltpu.VMEM(THREE, bf16), THREE, TWO, TWO, FACED,
            THREE, THREE, TWO, FIELD, (4 * L, C), (4 * L, C), sem((3,)), sem((4,)), sem((3, L)),
        ],
        flops=400 * L * R * C,
    )
    mine, well_residual, spread, start, pay = call(
        first_kernel,
        ((SMALL, VM), ((1, WELL_DEV), None), (FIELD, VM), (FIELD, VM), PAY),
        [VM] * 6,
        (got, info, own, perf, base, head),
    )
    got = exchange_tiles(pay)
    halo = halo_of(call(step_faces_kernel, FACES, [VM], (start,)))
    fields = (coef, tx, ty, tz, weight)
    ahead, gain_row, gain_col, residual, gain = call(
        grid_kernel,
        ((FIELD, VM), ((2, L, C), VM), ((R, LANES), VM), (THREE, HB), (SIX, HB)),
        [VM] * 5 + [HB] * 6,
        (coef_row, coef_col, head, spread, start, *fields, res),
        [THREE, TWO, TWO, FACED, THREE, THREE, THREE, SIX, sem((12,)), sem((2, L))],
        flops=100 * L * R * C,
    )
    *faces, step = call(
        second_kernel,
        FACES + ((FIELD, VM),),
        [VM] * 10,
        (got, info, ahead, head, gain_row, gain_col, *halo),
    )
    halo = halo_of(faces)
    table, parts, near = call(
        wells_kernel,
        (((2, DEVICES, LANES), VM), (SMALL, VM), (FIELD, VM)),
        [VM] * 6 + [HB],
        (got, info, perf, step, start, head, gain),
        [SIX, FIELD, sem((1,))],
    )
    step, pay = call(
        third_kernel,
        ((FIELD, VM), PAY),
        [VM] * 10,
        (info, perf, parts, near, gain_row, gain_col, *halo),
    )
    got = exchange_tiles(pay)
    halo = halo_of(call(step_faces_kernel, FACES, [VM], (step,)))
    end_row, end_col, ahead, slope = call(
        last_grid_kernel,
        (((2, 2, L, C), VM), ((2, R, LANES), VM), (THREE, HB), (TWO, HB)),
        [VM] * 6 + [HB] * 9,
        (coef_row, coef_col, head, step, gain_row, gain_col, pressure, porosity, *fields, diag, residual),
        [FIELD, FIELD, THREE, TWO, TWO, FACED, THREE, TWO, THREE, THREE, TWO, sem((18,)), sem((2, L))],
        flops=150 * L * R * C,
    )
    update, moved = call(
        final_kernel,
        ((THREE, HB), ((1, WELL_DEV), None)),
        [VM] * 13 + [HB] * 2,
        (got, info, table, mine, head, gain_row, gain_col, end_row, end_col, *halo, ahead, slope),
        [THREE, TWO, THREE, sem((2,)), sem((1, L))],
    )
    return residual, well_residual.reshape(WELL_DEV), update, moved.reshape(WELL_DEV)


def solution(mesh):
    return jax.shard_map(
        local,
        mesh=mesh,
        in_specs=(
            P(None, "gx", "gy"),
            P(None, "gx", "gy"),
            P(None, "gx", "gy"),
            P(None, None, "gx", "gy"),
            P(None, None, "gx", "gy"),
            P(None, "gx", "gy"),
            P(("gx", "gy")),
            P(("gx", "gy")),
            P(("gx", "gy")),
            P(("gx", "gy")),
            P(("gx", "gy")),
        ),
        out_specs=(
            P(None, None, "gx", "gy"),
            P(("gx", "gy")),
            P(None, None, "gx", "gy"),
            P(("gx", "gy")),
        ),
        check_vma=False,
    )
```

```python
import jax
import jax.numpy as jnp
from jax import lax
from jax.experimental import pallas as pl
from jax.experimental.pallas import tpu as pltpu
from jax.sharding import PartitionSpec as P

f32 = jnp.float32
bf16 = jnp.bfloat16
i32 = jnp.int32

compress = (0.05, 0.02, 0.2)
viscosity = (0.5, 2.0, 0.1)
volume_scale = 4.0
layer_ratio = 0.1
AXES = ("gx", "gy")
DEVICES = 128
WELL_DEV = 16
REACH = 40
FAR = 64
TAIL = REACH * WELL_DEV
WIDTH = TAIL + 128
TILES = WIDTH // 128
LANES = 128
L, R, C = 8, 64, 256
PERFS = 256
BLOCK = 8
VM = pl.BlockSpec(memory_space=pltpu.VMEM)
HB = pl.BlockSpec(memory_space=pltpu.HBM)


def iota(shape, dim):
    return lax.broadcasted_iota(i32, shape, dim)


def split3(x):
    high = x.astype(bf16)
    rest = x - high.astype(f32)
    middle = rest.astype(bf16)
    low = (rest - middle.astype(f32)).astype(bf16)
    return high, middle, low


def dot(a, b):
    return jnp.dot(a, b, preferred_element_type=f32)


def to_column(row):
    n = row.shape[1]
    return jnp.sum(jnp.where(iota((n, n), 0) == iota((n, n), 1), row, 0.0), axis=1, keepdims=True)


def to_row(column):
    n = column.shape[0]
    return jnp.sum(jnp.where(iota((n, n), 0) == iota((n, n), 1), column, 0.0), axis=0, keepdims=True)


def coeffs_of(p, sw, sg):
    so = 1.0 - sw - sg
    return tuple(
        s * s * (1.0 / viscosity[a]) * (1.0 + compress[a] * p) for a, s in enumerate((sw, so, sg))
    )


def scatter(cell_row, values):
    match = iota((L * R, PERFS), 0) == (cell_row >> 8)
    column = to_column(cell_row.astype(f32)).astype(i32) & (C - 1)
    spread = (iota((PERFS, C), 1) == column).astype(bf16)
    parts = [jnp.where(match, part.astype(f32), 0.0).astype(bf16) for part in split3(values)]
    return dot(jnp.concatenate(parts, axis=1), jnp.concatenate([spread] * 3, axis=0))


def gather_cells(cell_column, fields):
    onehot = (iota((PERFS, L * R), 1) == (cell_column >> 8)).astype(bf16)
    onehot = jnp.concatenate([onehot] * 3, axis=1)
    here = iota((PERFS, C), 1) == (cell_column & (C - 1))
    picked = []
    for field in fields:
        rows = dot(onehot, jnp.concatenate(split3(field), axis=0))
        picked.append(jnp.sum(jnp.where(here, rows, 0.0), axis=1, keepdims=True))
    return picked


def flat(field):
    return field[...].reshape(L * R, C)


def gather_wells(table, holder, slot):
    onehot = (iota((DEVICES, PERFS), 0) == holder).astype(bf16)
    wide = dot(jnp.concatenate(split3(table.T), axis=1), jnp.concatenate([onehot] * 3, axis=0))
    return jnp.sum(jnp.where(iota((LANES, PERFS), 0) == slot, wide, 0.0), axis=0, keepdims=True)


def to_holders(holder, slot_column, columns):
    lane = iota((PERFS, LANES), 1)
    group = lane >> 4
    values = jnp.zeros((PERFS, LANES), f32)
    for g, column in columns:
        values = jnp.where(group == g, column, values)
    values = jnp.where((lane & 15) == slot_column, values, 0.0)
    onehot = (iota((DEVICES, PERFS), 0) == holder).astype(bf16)
    return dot(jnp.concatenate([onehot] * 3, axis=1), jnp.concatenate(split3(values), axis=0))


def parts_by_offset(me, well_row, values):
    offset = (me - (well_row >> 4)) & (DEVICES - 1)
    lane = jnp.where(offset == FAR, TAIL, offset * WELL_DEV) + (well_row & 15)
    column = to_column(lane.astype(f32)).astype(i32)
    onehot = (iota((PERFS, WIDTH), 1) == column).astype(bf16)
    high, middle, low = split3(values)
    rows = jnp.concatenate([high.astype(f32), middle.astype(f32), low.astype(f32), jnp.zeros((5, PERFS), f32)], axis=0)
    return jnp.sum(dot(rows.astype(bf16), onehot), axis=0, keepdims=True)


def tile_of(got, t):
    return got[pl.ds(t, DEVICES, stride=TILES), :]


def sum_parts(got):
    aligned = tile_of(got, 0)
    for t in range(1, TAIL // LANES):
        aligned = aligned + pltpu.roll(tile_of(got, t), DEVICES - 8 * t, 0)
    total = aligned + pltpu.roll(tile_of(got, 5), DEVICES - FAR, 0)
    for u in range(1, 8):
        total = total + pltpu.roll(pltpu.roll(aligned, DEVICES - u, 0), LANES - 16 * u, 1)
    return total


def to_everyone(pay, rows):
    four = jnp.concatenate([rows] * 4, axis=0)
    pay[...] = jnp.broadcast_to(four[None], (DEVICES // 4, 4 * TILES, LANES)).reshape(TILES * DEVICES, LANES)


def rolled_row(row, shift):
    return pltpu.roll(jnp.broadcast_to(row, (8, LANES)), shift, 1)[0:1]


def shift_rows(x, first, last):
    return (
        jnp.concatenate([first, x[:-1]], axis=0),
        jnp.concatenate([x[1:], last], axis=0),
    )


def shift_columns(x, first, last):
    lane = iota(x.shape, 1)
    return (
        jnp.where(lane == 0, first, pltpu.roll(x, 1, 1)),
        jnp.where(lane == C - 1, last, pltpu.roll(x, C - 1, 1)),
    )


def lane_of(x, index):
    return pltpu.roll(x, (LANES - index) % LANES, 1)[:, 0:1]


def is_even(axis):
    return lax.axis_index(axis) % 2 == 0


def by_partner(axis, low, high):
    even = is_even(axis)
    return jnp.where(even, high, low), jnp.where(even, low, high)


def from_partner(axis, first, second):
    even = is_even(axis)
    return jnp.where(even, second, first), jnp.where(even, first, second)


def pack_columns(columns, first, second):
    n = first.shape[0]
    turned = jnp.concatenate([columns, jnp.zeros((LANES - R, LANES), f32)], axis=0).T
    first[...], second[...] = by_partner("gy", turned[0:n], turned[n : 2 * n])


def unpack_columns(first, second):
    n = first.shape[0]
    low, high = from_partner("gy", first[...], second[...])
    rows = jnp.concatenate([low, high, jnp.zeros((LANES - 2 * n, LANES), f32)], axis=0)
    return rows.T[0:R]


def write_faces(step, outs):
    row_first, row_second, col_first, col_second = outs
    lane = iota((R, LANES), 1)
    columns = jnp.zeros((R, LANES), f32)
    for l in range(L):
        x = step[l]
        pair = by_partner("gx", x[0:1], x[R - 1 : R])
        row_first[l : l + 1, :], row_second[l : l + 1, :] = pair
        columns = jnp.where(lane == l, x[:, 0:1], columns)
        columns = jnp.where(lane == L + l, x[:, C - 1 : C], columns)
    pack_columns(columns, col_first, col_second)


def start_copies(pairs, sems):
    copies = [pltpu.make_async_copy(a, b, sems.at[n]) for n, (a, b) in enumerate(pairs)]
    for c in copies:
        c.start()
    return copies


def wait_copies(copies):
    for c in copies:
        c.wait()


def layer_copies(pairs, sems, l):
    return [pltpu.make_async_copy(a, b, sems.at[n, l]) for n, (a, b) in enumerate(pairs(l))]


def faces_kernel(
    cell_h, well_h, index_h, pressure_h, rate_h, p_h, sw_h, sg_h, perm_h,
    row_first, row_second, col_first, col_second, p, sw, sg, info, own,
    cell_in, well_in, index_in, pressure_in, rate_in, perm, sems, sems_in,
):
    copies = start_copies(((perm_h.at[0:2], perm), (p_h, p), (sw_h, sw), (sg_h, sg)), sems)
    small = start_copies(
        (
            (cell_h, cell_in), (well_h, well_in), (index_h, index_in),
            (pressure_h, pressure_in), (rate_h, rate_in),
        ),
        sems_in,
    )
    me = lax.axis_index("gx") * 16 + lax.axis_index("gy")
    device = jnp.full((1, PERFS), me, i32).astype(f32)
    wait_copies(small)
    numbers = [cell_in[...].astype(f32), well_in[...].astype(f32), index_in[...], device]
    info[...] = jnp.concatenate(numbers + [jnp.zeros((4, PERFS), f32)], axis=0)
    blank = jnp.zeros((1, LANES - WELL_DEV), f32)
    heads = jnp.concatenate([pressure_in[...], blank], axis=1)
    rates = jnp.concatenate([rate_in[...], blank], axis=1)
    own[...] = jnp.concatenate([heads, rates, jnp.zeros((6, LANES), f32)], axis=0)
    lane = iota((R, LANES), 1)
    columns = jnp.zeros((R, LANES), f32)
    wait_copies(copies[:1])
    for l in range(L):
        n = 3 * L + l
        low = perm[0, l, 0:16, :].astype(f32)[0:1]
        high = perm[0, l, R - 16 : R, :].astype(f32)[15:16]
        row_first[n : n + 1, :], row_second[n : n + 1, :] = by_partner("gx", low, high)
        k = perm[1, l].astype(f32)
        columns = jnp.where(lane == n, k[:, 0:1], columns)
        columns = jnp.where(lane == 4 * L + n, k[:, C - 1 : C], columns)
    wait_copies(copies[1:])
    for l in range(L):
        for f, ref in enumerate((p, sw, sg)):
            x = ref[l]
            n = f * L + l
            pair = by_partner("gx", x[0:1], x[R - 1 : R])
            row_first[n : n + 1, :], row_second[n : n + 1, :] = pair
            columns = jnp.where(lane == n, x[:, 0:1], columns)
            columns = jnp.where(lane == 4 * L + n, x[:, C - 1 : C], columns)
    pack_columns(columns, col_first, col_second)


def start_kernel(info, own, p, sw, sg, pay, perf):
    well_row = info[1:2].astype(i32)
    slot_column = to_column(info[1:2]).astype(i32) & 15
    here = gather_cells(to_column(info[0:1]).astype(i32), (flat(p), flat(sw), flat(sg)))
    coeffs = coeffs_of(*here)
    total = to_column(info[2:3]) * (coeffs[0] + coeffs[1] + coeffs[2])
    sums = to_holders(well_row >> 4, slot_column, ((0, total), (1, total * here[0])))
    pay[...] = sums + rolled_row(own[0:1], 32)
    perf[...] = jnp.broadcast_to(to_row(total), (8, PERFS))


def after_kernel(pay, *refs):
    pass


def reciprocal(x):
    r = pl.reciprocal(x, approx=True)
    return r * (2.0 - x * r)


def transmit(k, k_next):
    return k * k_next * reciprocal(k + k_next)


def neighbours(field, l, lo, rows, columns):
    hi = lo + BLOCK
    here = field[l, lo:hi, :]
    if lo > 0:
        before = field[l, lo - 1 : hi - 1, :]
    else:
        before = jnp.concatenate([rows[0], field[l, 0 : hi - 1, :]], axis=0)
    if hi < R:
        after = field[l, lo + 1 : hi + 1, :]
    else:
        after = jnp.concatenate([field[l, lo + 1 : R, :], rows[1]], axis=0)
    sides = (field[jnp.maximum(l - 1, 0), lo:hi, :], field[jnp.minimum(l + 1, L - 1), lo:hi, :])
    return (before, after) + shift_columns(here, *columns) + sides


def coeff_neighbours(coef, coef_row, a, l, lo, columns):
    rows = (coef_row[0, a, pl.ds(l, 1), :], coef_row[1, a, pl.ds(l, 1), :])
    ends = [c[lo : lo + BLOCK] for c in columns[a]]
    return neighbours(coef.at[a], l, lo, rows, ends)


def coeff_columns(coef_col, l):
    return [(lane_of(coef_col[a], l), lane_of(coef_col[a], 4 * L + l)) for a in range(3)]


def inner_neighbours(step, l, lo):
    blank = jnp.zeros((1, C), f32)
    return neighbours(step, l, lo, (blank, blank), (0.0, 0.0))


def face_terms(tx, ty, tz, l, rows):
    return (tx[0, l, rows, :], tx[1, l, rows, :], ty[0, l, rows, :], ty[1, l, rows, :], tz[l, rows, :], tz[l + 1, rows, :])


def halves(pairs):
    parts = []
    for half in range(2):
        for a, b, dim in pairs:
            count = a.shape[dim]
            middle = L // 2 + 1
            span = pl.ds(0, middle) if half == 0 else pl.ds(middle, count - middle)
            index = (slice(None),) * dim + (span,)
            parts.append((a.at[index], b.at[index]))
    return parts


def put_with_faces(field, l, x, low, high, columns):
    lane = iota((R, LANES), 1)
    field[l, :, 0:LANES] = x[:, 0:LANES] + jnp.where(lane == 0, columns[:, l : l + 1], 0.0)
    field[l, :, LANES:C] = x[:, LANES:C] + jnp.where(lane == LANES - 1, columns[:, L + l : L + l + 1], 0.0)
    field[l, 0:1, :] += low
    field[l, R - 1 : R, :] += high


def end_columns(columns, l, first, last):
    lane = iota((R, LANES), 1)
    return jnp.where(lane == l, first, jnp.where(lane == L + l, last, columns))


def setup_kernel(
    info, row_first, row_second, col_first, col_second, p, sw, sg, por_h, mass_h, perm_h,
    coef_row, coef_col, base, head, coef_h, tx_h, ty_h, tz_h, weight_h, res_h, diag_h,
    por, mass, perm, coef, tx, ty, tz, weight, res, diag, index_sum, row_lo, row_hi,
    sems, sems_t, sems_out,
):
    copies = start_copies(((perm_h, perm), (por_h, por), (mass_h, mass)), sems)
    index_sum[...] = scatter(info[0:1].astype(i32), info[2:3]).reshape(L, R, C)
    row_lo[...], row_hi[...] = from_partner("gx", row_first[...], row_second[...])
    for side, ref in enumerate((row_lo, row_hi)):
        for a, c in enumerate(coeffs_of(ref[0:L], ref[L : 2 * L], ref[2 * L : 3 * L])):
            coef_row[side, a] = c
    columns = unpack_columns(col_first, col_second)
    for a, c in enumerate(
        coeffs_of(columns, pltpu.roll(columns, LANES - L, 1), pltpu.roll(columns, LANES - 2 * L, 1))
    ):
        coef_col[a] = c
    lane = iota((R, C), 1)
    me = info[3:4, 0:1].astype(i32)
    gx = me >> 4
    gy = me & 15
    inside = [jnp.where(t, 1.0, 0.0) for t in (gx > 0, gx < 7, gy > 0, gy < 15)]
    wait_copies(copies[:1])

    def first(l, carry):
        for a, c in enumerate(coeffs_of(p[l], sw[l], sg[l])):
            coef[a, l] = c
        k = perm[0, l].astype(f32)
        n = 3 * L + l
        edge = row_lo[pl.ds(n, 1), :] * inside[0]
        before = transmit(k, jnp.concatenate([edge, k[:-1]], axis=0))
        edge = row_hi[pl.ds(n, 1), :] * inside[1]
        tx[0, l] = before
        tx[1, l] = jnp.concatenate([before[1:], transmit(k[R - 1 : R], edge)], axis=0)
        k = perm[1, l].astype(f32)
        edge = lane_of(columns, n) * inside[2]
        before = transmit(k, jnp.where(lane == 0, edge, pltpu.roll(k, 1, 1)))
        edge = lane_of(columns, 4 * L + n) * inside[3]
        ty[0, l] = before
        ty[1, l] = jnp.where(lane == C - 1, transmit(k[:, C - 1 : C], edge), pltpu.roll(before, C - 1, 1))
        k = perm[2, l].astype(f32)
        under = perm[2, jnp.maximum(l - 1, 0)].astype(f32)
        tz[l] = jnp.where(l > 0, layer_ratio, 0.0) * transmit(k, under)
        return carry

    lax.fori_loop(0, L, first, 0)
    tz[L] = jnp.zeros((R, C), f32)
    saved = start_copies(((coef, coef_h), (tx, tx_h), (ty, ty_h), (tz, tz_h)), sems_t)
    wait_copies(copies[1:])

    def outs(l):
        return (
            (weight.at[:, l], weight_h.at[:, l]),
            (res.at[:, l], res_h.at[:, l]), (diag.at[:, l], diag_h.at[:, l]),
        )

    def second(l, carry):
        rows = (row_lo[pl.ds(l, 1), :], row_hi[pl.ds(l, 1), :])
        ends = lane_of(columns, l), lane_of(columns, 4 * L + l)
        sides_of = coeff_columns(coef_col, l)
        for lo in range(0, R, BLOCK):
            at = slice(lo, lo + BLOCK)
            here = p[l, at, :]
            nexts = neighbours(p, l, lo, rows, [e[at] for e in ends])
            faces = face_terms(tx, ty, tz, l, at)
            drops = [t * (here - q) for t, q in zip(faces, nexts)]
            face_sum = sum(faces)
            drop_sum = sum(drops)
            porous = volume_scale * por[l, at, :]
            water, gas = (sw[l, at, :], sg[l, at, :])
            sats = (water, 1.0 - water - gas, gas)
            indices = index_sum[l, at, :]
            diagonals, residuals, inverses, cs = [], [], [], []
            for a in range(3):
                c = coef[a, l, at, :]
                ab = c * face_sum
                net = c * drop_sum
                for t, d, s in zip(faces, drops, coeff_neighbours(coef, coef_row, a, l, lo, sides_of)):
                    ab = ab + t * s
                    net = net + d * s
                b = 1.0 + compress[a] * here
                stored = porous * sats[a]
                diagonals.append(compress[a] * stored + ab + c * indices)
                residuals.append(b * stored - volume_scale * mass[a, l, at, :] + net + c * (indices * here))
                inverses.append(reciprocal(porous * b))
                cs.append(c)
            inverse_total = reciprocal(sum(d * v for d, v in zip(diagonals, inverses)))
            weights = [v * inverse_total for v in inverses]
            base[l, at, :] = -sum(w * r for w, r in zip(weights, residuals))
            head[l, at, :] = sum(w * c for w, c in zip(weights, cs))
            for a in range(3):
                weight[a, l, at, :] = weights[a]
                res[a, l, at, :] = residuals[a]
            diag[0, l, at, :] = diagonals[0]
            diag[1, l, at, :] = diagonals[2]
        for c in layer_copies(outs, sems_out, l):
            c.start()
        return carry

    lax.fori_loop(0, L, second, 0)
    wait_copies(saved)
    for l in range(L):
        wait_copies(layer_copies(outs, sems_out, l))


def first_kernel(
    got, info, own, perf, base, head, mine, well_residual, spread, step, pay,
):
    lane = iota((1, LANES), 1)
    sums = jnp.sum(got[...], axis=0, keepdims=True)
    total = jnp.where(lane < WELL_DEV, sums, 1.0)
    flow = rolled_row(sums, LANES - 16)
    residual = jnp.where(lane < WELL_DEV, flow - total * own[0:1] - own[1:2], 0.0)
    inverse = jnp.where(lane < WELL_DEV, 1.0 / total, 0.0)
    mine[...] = jnp.concatenate([residual, inverse, jnp.zeros((6, LANES), f32)], axis=0)
    well_residual[...] = residual[:, 0:WELL_DEV]
    cell_row = info[0:1].astype(i32)
    well_row = info[1:2].astype(i32)
    heads = gather_wells(got[...], well_row >> 4, (well_row & 15) + 32)
    spread[...] = scatter(cell_row, info[2:3] * heads).reshape(L, R, C)
    step[...] = base[...] + head[...] * spread[...]
    here = to_row(gather_cells(to_column(info[0:1]).astype(i32), (flat(step),))[0])
    parts = parts_by_offset(info[3:4].astype(i32), well_row, perf[0:1] * here)
    packed = parts[:, TAIL:]
    for n, row in enumerate((residual * inverse, residual, inverse)):
        packed = packed + rolled_row(row, 16 * (n + 1))
    tiles = [parts[:, LANES * t : LANES * (t + 1)] for t in range(5)]
    to_everyone(pay, jnp.concatenate(tiles + [packed], axis=0))


def step_faces_kernel(step, row_first, row_second, col_first, col_second):
    write_faces(step, (row_first, row_second, col_first, col_second))


def grid_kernel(
    coef_row, coef_col, head, spread, step,
    coef_h, tx_h, ty_h, tz_h, weight_h, res_h,
    ahead, end_row, end_col, residual_h, gain_h,
    coef, tx, ty, tz, weight, res, residual, gain, sems, sems_out,
):
    copies = start_copies(
        halves(((coef_h, coef, 1), (tx_h, tx, 1), (ty_h, ty, 1), (tz_h, tz, 0), (weight_h, weight, 1), (res_h, res, 1))),
        sems,
    )
    wait_copies(copies[:6])

    def outs(l):
        return (
            (residual.at[:, l], residual_h.at[:, l]), (gain.at[:, l], gain_h.at[:, l]),
        )

    def layer(l, ends):
        sides_of = coeff_columns(coef_col, l)
        for lo in range(0, R, BLOCK):
            at = slice(lo, lo + BLOCK)
            nexts = inner_neighbours(step, l, lo)
            faces = face_terms(tx, ty, tz, l, at)
            wells = spread[l, at, :]
            mixes = [head[l, at, :]] * 6
            for a in range(3):
                w = weight[a, l, at, :]
                sides = coeff_neighbours(coef, coef_row, a, l, lo, sides_of)
                mixes = [m + w * s for m, s in zip(mixes, sides)]
                residual[a, l, at, :] = res[a, l, at, :] - coef[a, l, at, :] * wells
            total = step[l, at, :]
            for j in range(6):
                g = faces[j] * mixes[j]
                gain[j, l, at, :] = g
                total = total + g * nexts[j]
            ahead[l, at, :] = total
        end_row[0, pl.ds(l, 1), :] = gain[0, l, 0:1, :]
        end_row[1, pl.ds(l, 1), :] = gain[1, l, R - 1 : R, :]
        for c in layer_copies(outs, sems_out, l):
            c.start()
        return end_columns(ends, l, gain[2, l, :, 0:LANES][:, 0:1], gain[3, l, :, C - LANES : C][:, LANES - 1 : LANES])

    ends = lax.fori_loop(0, L // 2, layer, jnp.zeros((R, LANES), f32))
    wait_copies(copies[6:])
    end_col[...] = lax.fori_loop(L // 2, L, layer, ends)
    for l in range(L):
        wait_copies(layer_copies(outs, sems_out, l))


def second_kernel(
    got, info, ahead, head, end_row, end_col, row_first, row_second, col_first, col_second,
    out_row_first, out_row_second, out_col_first, out_col_second, step,
):
    cell_row = info[0:1].astype(i32)
    well_row = info[1:2].astype(i32)
    moves = gather_wells(tile_of(got, 5), well_row >> 4, (well_row & 15) + 16)
    wells = scatter(cell_row, info[2:3] * moves).reshape(L, R, C)
    columns = end_col[...] * unpack_columns(col_first, col_second)
    low, high = from_partner("gx", row_first[...], row_second[...])
    low = end_row[0] * low
    high = end_row[1] * high
    for l in range(L):
        put_with_faces(step, l, ahead[l] + head[l] * wells[l], low[l : l + 1], high[l : l + 1], columns)
    write_faces(step, (out_row_first, out_row_second, out_col_first, out_col_second))


def wells_kernel(
    got, info, perf, step, base, head, gain_h, table, parts, near, gain, spread, sems,
):
    copies = start_copies(((gain_h, gain),), sems)
    tail = tile_of(got, 5)
    residuals = pltpu.roll(tail, LANES - 32, 1)
    inverses = pltpu.roll(tail, LANES - 48, 1)
    table[0] = residuals
    table[1] = inverses
    cell_row = info[0:1].astype(i32)
    well_row = info[1:2].astype(i32)
    valid = iota((DEVICES, LANES), 1) < WELL_DEV
    moves = jnp.where(valid, (sum_parts(got) + residuals) * inverses, 0.0)
    values = gather_wells(moves, well_row >> 4, well_row & 15)
    spread[...] = scatter(cell_row, info[2:3] * values).reshape(L, R, C)
    here = to_row(gather_cells(to_column(info[0:1]).astype(i32), (flat(step),))[0])
    flows = parts_by_offset(info[3:4].astype(i32), well_row, perf[0:1] * here)
    tiles = [flows[:, LANES * t : LANES * (t + 1)] for t in range(6)]
    parts[...] = jnp.concatenate(tiles + [jnp.zeros((2, LANES), f32)], axis=0)
    wait_copies(copies)

    def layer(l, carry):
        for lo in range(0, R, BLOCK):
            at = slice(lo, lo + BLOCK)
            total = base[l, at, :] + head[l, at, :] * spread[l, at, :]
            for j, q in enumerate(inner_neighbours(step, l, lo)):
                total = total + gain[j, l, at, :] * q
            near[l, at, :] = total
        return carry

    lax.fori_loop(0, L, layer, 0)


def third_kernel(info, perf, parts, near, end_row, end_col, row_first, row_second, col_first, col_second, step, pay):
    columns = end_col[...] * unpack_columns(col_first, col_second)
    low, high = from_partner("gx", row_first[...], row_second[...])
    low = end_row[0] * low
    high = end_row[1] * high
    for l in range(L):
        put_with_faces(step, l, near[l], low[l : l + 1], high[l : l + 1], columns)
    here = gather_cells(to_column(info[0:1]).astype(i32), (flat(step),))[0]
    well_row = info[1:2].astype(i32)
    slot_column = to_column(info[1:2]).astype(i32) & 15
    sums = to_holders(well_row >> 4, slot_column, ((1, to_column(perf[0:1]) * here),))
    to_everyone(pay, parts[0:TILES])
    pay[pl.ds(TILES - 1, DEVICES, stride=TILES), :] = sums + parts[TILES - 1 : TILES]


def last_grid_kernel(
    coef_row, coef_col, head, step, gain_row, gain_col,
    p_h, por_h, coef_h, tx_h, ty_h, tz_h, weight_h, diag_h, residual_h,
    end_row, end_col, ahead_h, slope_h,
    p, por, coef, tx, ty, tz, weight, diag, residual, ahead, slope, sems, sems_out,
):
    copies = start_copies(
        halves(
            (
                (p_h, p, 0), (por_h, por, 0), (coef_h, coef, 1), (tx_h, tx, 1), (ty_h, ty, 1), (tz_h, tz, 0),
                (weight_h, weight, 1), (diag_h, diag, 1), (residual_h, residual, 1),
            )
        ),
        sems,
    )
    wait_copies(copies[:9])

    def outs(l):
        return ((ahead.at[:, l], ahead_h.at[:, l]), (slope.at[:, l], slope_h.at[:, l]))

    def layer(l, ends):
        sides_of = coeff_columns(coef_col, l)
        gains = lane_of(gain_col[...], l), lane_of(gain_col[...], L + l)
        pairs = [([], []), ([], [])]
        for lo in range(0, R, BLOCK):
            at = slice(lo, lo + BLOCK)
            nexts = inner_neighbours(step, l, lo)
            faces = face_terms(tx, ty, tz, l, at)
            flows = [t * q for t, q in zip(faces, nexts)]
            flow_sum = sum(flows)
            rights, cs, sides = [], [], []
            for a in range(3):
                c = coef[a, l, at, :]
                total = c * flow_sum - residual[a, l, at, :]
                sides.append(coeff_neighbours(coef, coef_row, a, l, lo, sides_of))
                for v, s in zip(flows, sides[a]):
                    total = total + v * s
                rights.append(total)
                cs.append(c)
            z = sum(weight[a, l, at, :] * rights[a] for a in range(3))
            h = head[l, at, :]
            porous = volume_scale * por[l, at, :]
            inverses = [reciprocal(porous * (1.0 + compress[a] * p[l, at, :])) for a in (0, 2)]
            ahead[0, l, at, :] = z
            for n, a in enumerate((0, 2)):
                d = diag[n, l, at, :]
                inverse = inverses[n]
                ahead[1 + n, l, at, :] = (rights[a] - d * z) * inverse
                slope[n, l, at, :] = (cs[a] - d * h) * inverse
                for side in range(2):
                    if lo == (0, R - BLOCK)[side]:
                        row = slice(0, 1) if side == 0 else slice(BLOCK - 1, BLOCK)
                        face = faces[side][row] * (cs[a][row] + sides[a][side][row])
                        end_row[side, n, pl.ds(l, 1), :] = (
                            face - d[row] * gain_row[side, pl.ds(l, 1), :]
                        ) * inverse[row]
                    col = slice(0, 1) if side == 0 else slice(C - 1, C)
                    face = faces[2 + side][:, col] * (cs[a][:, col] + sides_of[a][side][at])
                    pairs[n][side].append((face - d[:, col] * gains[side][at]) * inverse[:, col])
        for c in layer_copies(outs, sems_out, l):
            c.start()
        return tuple(
            end_columns(ends[n], l, *(jnp.concatenate(part, axis=0) for part in pairs[n])) for n in range(2)
        )

    blank = jnp.zeros((R, LANES), f32)
    ends = lax.fori_loop(0, L // 2, layer, (blank, blank))
    wait_copies(copies[9:])
    end_col[0], end_col[1] = lax.fori_loop(L // 2, L, layer, ends)
    for l in range(L):
        wait_copies(layer_copies(outs, sems_out, l))


def final_kernel(
    got, info, table, mine, head, gain_row, gain_col, end_row, end_col, row_first, row_second, col_first, col_second,
    ahead_h, slope_h, update_h, moved, ahead, slope, update, sems, sems_out,
):
    copies = start_copies(((ahead_h, ahead), (slope_h, slope)), sems)
    flow = rolled_row(jnp.sum(tile_of(got, TILES - 1), axis=0, keepdims=True), LANES - 16)
    moved[...] = ((flow + mine[0:1]) * mine[1:2])[:, 0:WELL_DEV]
    cell_row = info[0:1].astype(i32)
    well_row = info[1:2].astype(i32)
    valid = iota((DEVICES, LANES), 1) < WELL_DEV
    moves = jnp.where(valid, (sum_parts(got) + table[0]) * table[1], 0.0)
    values = gather_wells(moves, well_row >> 4, well_row & 15)
    wells = scatter(cell_row, info[2:3] * values).reshape(L, R, C)
    halo = unpack_columns(col_first, col_second)
    lows, highs = from_partner("gx", row_first[...], row_second[...])
    columns = (gain_col[...] * halo, end_col[0] * halo, end_col[1] * halo)
    wait_copies(copies)

    def outs(l):
        return ((update.at[:, l], update_h.at[:, l]),)

    for l in range(L):
        low = lows[l : l + 1]
        high = highs[l : l + 1]
        for n in range(3):
            rows = [gain_row[side, l : l + 1, :] if n == 0 else end_row[side, n - 1, l : l + 1, :] for side in range(2)]
            x = ahead[n, l] + (head[l] if n == 0 else slope[n - 1, l]) * wells[l]
            put_with_faces(update.at[n], l, x, rows[0] * low, rows[1] * high, columns[n])
        layer_copies(outs, sems_out, l)[0].start()
    for l in range(L):
        wait_copies(layer_copies(outs, sems_out, l))


def call(kernel, outs, ins, operands, scratch=(), flops=0):
    shapes = tuple(
        pltpu.VMEM(s, f32) if w is VM else pltpu.HBM(s, f32) if w is HB else jax.ShapeDtypeStruct(s, f32)
        for s, w in outs
    )
    moved = 4 * sum(int(x.size) for x in operands)
    operands = [
        pltpu.with_memory_space_constraint(x, pltpu.HBM) if w is HB else x for x, w in zip(operands, ins)
    ]
    return pl.pallas_call(
        kernel,
        out_shape=shapes,
        in_specs=ins,
        out_specs=tuple(w or VM for _, w in outs),
        scratch_shapes=[pltpu.VMEM(x, f32) if type(x) is tuple else x for x in scratch],
        compiler_params=pltpu.CompilerParams(vmem_limit_bytes=40 * 1024 * 1024),
        cost_estimate=pl.CostEstimate(flops=flops, bytes_accessed=moved, transcendentals=0),
    )(*operands)


FIELD = (L, R, C)
TWO, THREE, SIX, FACED = ((2,) + FIELD, (3,) + FIELD, (6,) + FIELD, (L + 1, R, C))
FACES = (((L, C), VM), ((L, C), VM), ((L, LANES), VM), ((L, LANES), VM))
WIDE_FACES = (((4 * L, C), VM), ((4 * L, C), VM), ((4 * L, LANES), VM), ((4 * L, LANES), VM))
SMALL = (8, LANES)
PAY = ((TILES * DEVICES, LANES), None)
sem = pltpu.SemaphoreType.DMA


def exchange(array):
    return lax.all_to_all(array, AXES, split_axis=0, concat_axis=0, tiled=True)


def exchange_tiles(array):
    return exchange(array.reshape(DEVICES, WIDTH)).reshape(TILES * DEVICES, LANES)


def partners():
    rows, columns = (lax.axis_size(axis) for axis in AXES)
    swaps = [[], [], [], []]
    for x in range(rows):
        for y in range(columns):
            here = x * columns + y
            x_next = x - 1 + 2 * (x % 2)
            y_next = y - 1 + 2 * (y % 2)
            swaps[0].append((here, (x ^ 1) * columns + y))
            swaps[1].append((here, x_next * columns + y if 0 <= x_next < rows else x * columns + (y ^ 1)))
            swaps[2].append((here, x * columns + (y ^ 1)))
            swaps[3].append((here, x * columns + y_next if 0 <= y_next < columns else (x ^ 1) * columns + y))
    return swaps


def halo_of(faces):
    swaps = partners()
    got = {n: lax.ppermute(faces[n], AXES, swaps[n]) for n in (3, 1, 2, 0)}
    return [got[n] for n in range(4)]


def local(
    pressure, sat_water, sat_gas, old_mass, perm, porosity,
    perf_well, perf_cell, perf_index, well_pressure, well_rate,
):
    *faces, p, sw, sg, info, own = call(
        faces_kernel,
        WIDE_FACES + ((FIELD, VM), (FIELD, VM), (FIELD, VM), ((8, PERFS), VM), (SMALL, VM)),
        [HB] * 9,
        (
            perf_cell.reshape(1, PERFS), perf_well.reshape(1, PERFS), perf_index.reshape(1, PERFS),
            well_pressure.reshape(1, WELL_DEV), well_rate.reshape(1, WELL_DEV), pressure, sat_water, sat_gas, perm,
        ),
        [
            pltpu.VMEM((1, PERFS), i32), pltpu.VMEM((1, PERFS), i32), (1, PERFS),
            (1, WELL_DEV), (1, WELL_DEV), pltpu.VMEM(TWO, bf16), sem((4,)), sem((5,)),
        ],
    )
    halo = halo_of(faces)
    pay, perf = call(
        start_kernel, (((DEVICES, LANES), VM), ((8, PERFS), VM)), [VM] * 5, (info, own, p, sw, sg)
    )
    pay, *halo = pl.pallas_call(
        after_kernel,
        out_shape=tuple(pltpu.VMEM(x.shape, f32) for x in (pay, *halo)),
        in_specs=[pl.BlockSpec(memory_space=pl.ANY)] * 5,
        out_specs=(pl.BlockSpec(memory_space=pl.ANY),) * 5,
        input_output_aliases={n: n for n in range(5)},
    )(pay, *halo)
    got = exchange(pay)
    coef_row, coef_col, base, head, coef, tx, ty, tz, weight, res, diag = call(
        setup_kernel,
        (
            ((2, 3, L, C), VM), ((3, R, LANES), VM), (FIELD, VM), (FIELD, VM), (THREE, HB), (TWO, HB), (TWO, HB),
            (FACED, HB), (THREE, HB), (THREE, HB), (TWO, HB),
        ),
        [VM] * 8 + [HB] * 3,
        (info, *halo, p, sw, sg, porosity, old_mass, perm),
        [
            FIELD, THREE, pltpu.VMEM(THREE, bf16), THREE, TWO, TWO, FACED,
            THREE, THREE, TWO, FIELD, (4 * L, C), (4 * L, C), sem((3,)), sem((4,)), sem((3, L)),
        ],
        flops=400 * L * R * C,
    )
    mine, well_residual, spread, start, pay = call(
        first_kernel,
        ((SMALL, VM), ((1, WELL_DEV), None), (FIELD, VM), (FIELD, VM), PAY),
        [VM] * 6,
        (got, info, own, perf, base, head),
    )
    got = exchange_tiles(pay)
    halo = halo_of(call(step_faces_kernel, FACES, [VM], (start,)))
    fields = (coef, tx, ty, tz, weight)
    ahead, gain_row, gain_col, residual, gain = call(
        grid_kernel,
        ((FIELD, VM), ((2, L, C), VM), ((R, LANES), VM), (THREE, HB), (SIX, HB)),
        [VM] * 5 + [HB] * 6,
        (coef_row, coef_col, head, spread, start, *fields, res),
        [THREE, TWO, TWO, FACED, THREE, THREE, THREE, SIX, sem((12,)), sem((2, L))],
        flops=100 * L * R * C,
    )
    *faces, step = call(
        second_kernel,
        FACES + ((FIELD, VM),),
        [VM] * 10,
        (got, info, ahead, head, gain_row, gain_col, *halo),
    )
    halo = halo_of(faces)
    table, parts, near = call(
        wells_kernel,
        (((2, DEVICES, LANES), VM), (SMALL, VM), (FIELD, VM)),
        [VM] * 6 + [HB],
        (got, info, perf, step, start, head, gain),
        [SIX, FIELD, sem((1,))],
    )
    step, pay = call(
        third_kernel,
        ((FIELD, VM), PAY),
        [VM] * 10,
        (info, perf, parts, near, gain_row, gain_col, *halo),
    )
    got = exchange_tiles(pay)
    halo = halo_of(call(step_faces_kernel, FACES, [VM], (step,)))
    end_row, end_col, ahead, slope = call(
        last_grid_kernel,
        (((2, 2, L, C), VM), ((2, R, LANES), VM), (THREE, HB), (TWO, HB)),
        [VM] * 6 + [HB] * 9,
        (coef_row, coef_col, head, step, gain_row, gain_col, pressure, porosity, *fields, diag, residual),
        [FIELD, FIELD, THREE, TWO, TWO, FACED, THREE, TWO, THREE, THREE, TWO, sem((18,)), sem((2, L))],
        flops=150 * L * R * C,
    )
    update, moved = call(
        final_kernel,
        ((THREE, HB), ((1, WELL_DEV), None)),
        [VM] * 13 + [HB] * 2,
        (got, info, table, mine, head, gain_row, gain_col, end_row, end_col, *halo, ahead, slope),
        [THREE, TWO, THREE, sem((2,)), sem((1, L))],
    )
    return residual, well_residual.reshape(WELL_DEV), update, moved.reshape(WELL_DEV)


def solution(mesh):
    return jax.shard_map(
        local,
        mesh=mesh,
        in_specs=(
            P(None, "gx", "gy"),
            P(None, "gx", "gy"),
            P(None, "gx", "gy"),
            P(None, None, "gx", "gy"),
            P(None, None, "gx", "gy"),
            P(None, "gx", "gy"),
            P(("gx", "gy")),
            P(("gx", "gy")),
            P(("gx", "gy")),
            P(("gx", "gy")),
            P(("gx", "gy")),
        ),
        out_specs=(
            P(None, None, "gx", "gy"),
            P(("gx", "gy")),
            P(None, None, "gx", "gy"),
            P(("gx", "gy")),
        ),
        check_vma=False,
    )
```

```python
import jax
import jax.numpy as jnp
from jax import lax
from jax.experimental import pallas as pl
from jax.experimental.pallas import tpu as pltpu
from jax.sharding import PartitionSpec as P

f32 = jnp.float32
bf16 = jnp.bfloat16
i32 = jnp.int32

compress = (0.05, 0.02, 0.2)
viscosity = (0.5, 2.0, 0.1)
volume_scale = 4.0
layer_ratio = 0.1
AXES = ("gx", "gy")
DEVICES = 128
WELL_DEV = 16
REACH = 40
FAR = 64
TAIL = REACH * WELL_DEV
WIDTH = TAIL + 128
TILES = WIDTH // 128
LANES = 128
L, R, C = 8, 64, 256
PERFS = 256
BLOCK = 32
VM = pl.BlockSpec(memory_space=pltpu.VMEM)
HB = pl.BlockSpec(memory_space=pltpu.HBM)


def iota(shape, dim):
    return lax.broadcasted_iota(i32, shape, dim)


def split3(x):
    high = x.astype(bf16)
    rest = x - high.astype(f32)
    middle = rest.astype(bf16)
    low = (rest - middle.astype(f32)).astype(bf16)
    return high, middle, low


def dot(a, b):
    return jnp.dot(a, b, preferred_element_type=f32)


def to_column(row):
    n = row.shape[1]
    return jnp.sum(jnp.where(iota((n, n), 0) == iota((n, n), 1), row, 0.0), axis=1, keepdims=True)


def to_row(column):
    n = column.shape[0]
    return jnp.sum(jnp.where(iota((n, n), 0) == iota((n, n), 1), column, 0.0), axis=0, keepdims=True)


def coeffs_of(p, sw, sg):
    so = 1.0 - sw - sg
    return tuple(
        s * s * (1.0 / viscosity[a]) * (1.0 + compress[a] * p) for a, s in enumerate((sw, so, sg))
    )


def scatter(cell_row, values):
    match = iota((L * R, PERFS), 0) == (cell_row >> 8)
    column = to_column(cell_row.astype(f32)).astype(i32) & (C - 1)
    spread = (iota((PERFS, C), 1) == column).astype(bf16)
    parts = [jnp.where(match, part.astype(f32), 0.0).astype(bf16) for part in split3(values)]
    return dot(jnp.concatenate(parts, axis=1), jnp.concatenate([spread] * 3, axis=0))


def gather_cells(cell_column, fields):
    onehot = (iota((PERFS, L * R), 1) == (cell_column >> 8)).astype(bf16)
    onehot = jnp.concatenate([onehot] * 3, axis=1)
    here = iota((PERFS, C), 1) == (cell_column & (C - 1))
    picked = []
    for field in fields:
        rows = dot(onehot, jnp.concatenate(split3(field), axis=0))
        picked.append(jnp.sum(jnp.where(here, rows, 0.0), axis=1, keepdims=True))
    return picked


def flat(field):
    return field[...].reshape(L * R, C)


def gather_wells(table, holder, slot):
    onehot = (iota((DEVICES, PERFS), 0) == holder).astype(bf16)
    wide = dot(jnp.concatenate(split3(table.T), axis=1), jnp.concatenate([onehot] * 3, axis=0))
    return jnp.sum(jnp.where(iota((LANES, PERFS), 0) == slot, wide, 0.0), axis=0, keepdims=True)


def to_holders(holder, slot_column, columns):
    lane = iota((PERFS, LANES), 1)
    group = lane >> 4
    values = jnp.zeros((PERFS, LANES), f32)
    for g, column in columns:
        values = jnp.where(group == g, column, values)
    values = jnp.where((lane & 15) == slot_column, values, 0.0)
    onehot = (iota((DEVICES, PERFS), 0) == holder).astype(bf16)
    return dot(jnp.concatenate([onehot] * 3, axis=1), jnp.concatenate(split3(values), axis=0))


def parts_by_offset(me, well_row, values):
    offset = (me - (well_row >> 4)) & (DEVICES - 1)
    lane = jnp.where(offset == FAR, TAIL, offset * WELL_DEV) + (well_row & 15)
    column = to_column(lane.astype(f32)).astype(i32)
    onehot = (iota((PERFS, WIDTH), 1) == column).astype(bf16)
    high, middle, low = split3(values)
    rows = jnp.concatenate([high.astype(f32), middle.astype(f32), low.astype(f32), jnp.zeros((5, PERFS), f32)], axis=0)
    return jnp.sum(dot(rows.astype(bf16), onehot), axis=0, keepdims=True)


def tile_of(got, t):
    return got[pl.ds(t, DEVICES, stride=TILES), :]


def sum_parts(got):
    aligned = tile_of(got, 0)
    for t in range(1, TAIL // LANES):
        aligned = aligned + pltpu.roll(tile_of(got, t), DEVICES - 8 * t, 0)
    total = aligned + pltpu.roll(tile_of(got, 5), DEVICES - FAR, 0)
    for u in range(1, 8):
        total = total + pltpu.roll(pltpu.roll(aligned, DEVICES - u, 0), LANES - 16 * u, 1)
    return total


def to_everyone(pay, rows):
    four = jnp.concatenate([rows] * 4, axis=0)
    pay[...] = jnp.broadcast_to(four[None], (DEVICES // 4, 4 * TILES, LANES)).reshape(TILES * DEVICES, LANES)


def rolled_row(row, shift):
    return pltpu.roll(jnp.broadcast_to(row, (8, LANES)), shift, 1)[0:1]


def shift_rows(x, first, last):
    return (
        jnp.concatenate([first, x[:-1]], axis=0),
        jnp.concatenate([x[1:], last], axis=0),
    )


def shift_columns(x, first, last):
    lane = iota(x.shape, 1)
    return (
        jnp.where(lane == 0, first, pltpu.roll(x, 1, 1)),
        jnp.where(lane == C - 1, last, pltpu.roll(x, C - 1, 1)),
    )


def lane_of(x, index):
    return pltpu.roll(x, (LANES - index) % LANES, 1)[:, 0:1]


def is_even(axis):
    return lax.axis_index(axis) % 2 == 0


def by_partner(axis, low, high):
    even = is_even(axis)
    return jnp.where(even, high, low), jnp.where(even, low, high)


def from_partner(axis, first, second):
    even = is_even(axis)
    return jnp.where(even, second, first), jnp.where(even, first, second)


def pack_columns(columns, first, second):
    n = first.shape[0]
    turned = jnp.concatenate([columns, jnp.zeros((LANES - R, LANES), f32)], axis=0).T
    first[...], second[...] = by_partner("gy", turned[0:n], turned[n : 2 * n])


def unpack_columns(first, second):
    n = first.shape[0]
    low, high = from_partner("gy", first[...], second[...])
    rows = jnp.concatenate([low, high, jnp.zeros((LANES - 2 * n, LANES), f32)], axis=0)
    return rows.T[0:R]


def write_faces(step, outs):
    row_first, row_second, col_first, col_second = outs
    lane = iota((R, LANES), 1)
    columns = jnp.zeros((R, LANES), f32)
    for l in range(L):
        x = step[l]
        pair = by_partner("gx", x[0:1], x[R - 1 : R])
        row_first[l : l + 1, :], row_second[l : l + 1, :] = pair
        columns = jnp.where(lane == l, x[:, 0:1], columns)
        columns = jnp.where(lane == L + l, x[:, C - 1 : C], columns)
    pack_columns(columns, col_first, col_second)


def start_copies(pairs, sems):
    copies = [pltpu.make_async_copy(a, b, sems.at[n]) for n, (a, b) in enumerate(pairs)]
    for c in copies:
        c.start()
    return copies


def wait_copies(copies):
    for c in copies:
        c.wait()


def layer_copies(pairs, sems, l):
    return [pltpu.make_async_copy(a, b, sems.at[n, l]) for n, (a, b) in enumerate(pairs(l))]


def faces_kernel(
    cell_h, well_h, index_h, pressure_h, rate_h, p_h, sw_h, sg_h, perm_h,
    row_first, row_second, col_first, col_second, p, sw, sg, info, own,
    cell_in, well_in, index_in, pressure_in, rate_in, perm, sems, sems_in,
):
    copies = start_copies(((perm_h.at[0:2], perm), (p_h, p), (sw_h, sw), (sg_h, sg)), sems)
    small = start_copies(
        (
            (cell_h, cell_in), (well_h, well_in), (index_h, index_in),
            (pressure_h, pressure_in), (rate_h, rate_in),
        ),
        sems_in,
    )
    me = lax.axis_index("gx") * 16 + lax.axis_index("gy")
    device = jnp.full((1, PERFS), me, i32).astype(f32)
    wait_copies(small)
    numbers = [cell_in[...].astype(f32), well_in[...].astype(f32), index_in[...], device]
    info[...] = jnp.concatenate(numbers + [jnp.zeros((4, PERFS), f32)], axis=0)
    blank = jnp.zeros((1, LANES - WELL_DEV), f32)
    heads = jnp.concatenate([pressure_in[...], blank], axis=1)
    rates = jnp.concatenate([rate_in[...], blank], axis=1)
    own[...] = jnp.concatenate([heads, rates, jnp.zeros((6, LANES), f32)], axis=0)
    lane = iota((R, LANES), 1)
    columns = jnp.zeros((R, LANES), f32)
    wait_copies(copies[:1])
    for l in range(L):
        n = 3 * L + l
        low = perm[0, l, 0:16, :].astype(f32)[0:1]
        high = perm[0, l, R - 16 : R, :].astype(f32)[15:16]
        row_first[n : n + 1, :], row_second[n : n + 1, :] = by_partner("gx", low, high)
        k = perm[1, l].astype(f32)
        columns = jnp.where(lane == n, k[:, 0:1], columns)
        columns = jnp.where(lane == 4 * L + n, k[:, C - 1 : C], columns)
    wait_copies(copies[1:])
    for l in range(L):
        for f, ref in enumerate((p, sw, sg)):
            x = ref[l]
            n = f * L + l
            pair = by_partner("gx", x[0:1], x[R - 1 : R])
            row_first[n : n + 1, :], row_second[n : n + 1, :] = pair
            columns = jnp.where(lane == n, x[:, 0:1], columns)
            columns = jnp.where(lane == 4 * L + n, x[:, C - 1 : C], columns)
    pack_columns(columns, col_first, col_second)


def start_kernel(info, own, p, sw, sg, pay, perf):
    well_row = info[1:2].astype(i32)
    slot_column = to_column(info[1:2]).astype(i32) & 15
    here = gather_cells(to_column(info[0:1]).astype(i32), (flat(p), flat(sw), flat(sg)))
    coeffs = coeffs_of(*here)
    total = to_column(info[2:3]) * (coeffs[0] + coeffs[1] + coeffs[2])
    sums = to_holders(well_row >> 4, slot_column, ((0, total), (1, total * here[0])))
    pay[...] = sums + rolled_row(own[0:1], 32)
    perf[...] = jnp.broadcast_to(to_row(total), (8, PERFS))


def after_kernel(pay, *refs):
    pass


def reciprocal(x):
    r = pl.reciprocal(x, approx=True)
    return r * (2.0 - x * r)


def transmit(k, k_next):
    return k * k_next * reciprocal(k + k_next)


def neighbours(field, l, lo, rows, columns):
    hi = lo + BLOCK
    here = field[l, lo:hi, :]
    if lo > 0:
        before = field[l, lo - 1 : hi - 1, :]
    else:
        before = jnp.concatenate([rows[0], field[l, 0 : hi - 1, :]], axis=0)
    if hi < R:
        after = field[l, lo + 1 : hi + 1, :]
    else:
        after = jnp.concatenate([field[l, lo + 1 : R, :], rows[1]], axis=0)
    sides = (field[jnp.maximum(l - 1, 0), lo:hi, :], field[jnp.minimum(l + 1, L - 1), lo:hi, :])
    return (before, after) + shift_columns(here, *columns) + sides


def coeff_neighbours(coef, coef_row, a, l, lo, columns):
    rows = (coef_row[0, a, pl.ds(l, 1), :], coef_row[1, a, pl.ds(l, 1), :])
    ends = [c[lo : lo + BLOCK] for c in columns[a]]
    return neighbours(coef.at[a], l, lo, rows, ends)


def coeff_columns(coef_col, l):
    return [(lane_of(coef_col[a], l), lane_of(coef_col[a], 4 * L + l)) for a in range(3)]


def inner_neighbours(step, l, lo):
    blank = jnp.zeros((1, C), f32)
    return neighbours(step, l, lo, (blank, blank), (0.0, 0.0))


def face_terms(tx, ty, tz, l, rows):
    return (tx[0, l, rows, :], tx[1, l, rows, :], ty[0, l, rows, :], ty[1, l, rows, :], tz[l, rows, :], tz[l + 1, rows, :])


def halves(pairs):
    parts = []
    for half in range(2):
        for a, b, dim in pairs:
            count = a.shape[dim]
            middle = L // 2 + 1
            span = pl.ds(0, middle) if half == 0 else pl.ds(middle, count - middle)
            index = (slice(None),) * dim + (span,)
            parts.append((a.at[index], b.at[index]))
    return parts


def put_with_faces(field, l, x, low, high, columns):
    lane = iota((R, LANES), 1)
    field[l, :, 0:LANES] = x[:, 0:LANES] + jnp.where(lane == 0, columns[:, l : l + 1], 0.0)
    field[l, :, LANES:C] = x[:, LANES:C] + jnp.where(lane == LANES - 1, columns[:, L + l : L + l + 1], 0.0)
    field[l, 0:1, :] += low
    field[l, R - 1 : R, :] += high


def end_columns(columns, l, first, last):
    lane = iota((R, LANES), 1)
    return jnp.where(lane == l, first, jnp.where(lane == L + l, last, columns))


def setup_kernel(
    info, row_first, row_second, col_first, col_second, p, sw, sg, por_h, mass_h, perm_h,
    coef_row, coef_col, base, head, coef_h, tx_h, ty_h, tz_h, weight_h, res_h, diag_h,
    por, mass, perm, coef, tx, ty, tz, weight, res, diag, index_sum, row_lo, row_hi,
    sems, sems_t, sems_out,
):
    copies = start_copies(((perm_h, perm), (por_h, por), (mass_h, mass)), sems)
    index_sum[...] = scatter(info[0:1].astype(i32), info[2:3]).reshape(L, R, C)
    row_lo[...], row_hi[...] = from_partner("gx", row_first[...], row_second[...])
    for side, ref in enumerate((row_lo, row_hi)):
        for a, c in enumerate(coeffs_of(ref[0:L], ref[L : 2 * L], ref[2 * L : 3 * L])):
            coef_row[side, a] = c
    columns = unpack_columns(col_first, col_second)
    for a, c in enumerate(
        coeffs_of(columns, pltpu.roll(columns, LANES - L, 1), pltpu.roll(columns, LANES - 2 * L, 1))
    ):
        coef_col[a] = c
    lane = iota((R, C), 1)
    me = info[3:4, 0:1].astype(i32)
    gx = me >> 4
    gy = me & 15
    inside = [jnp.where(t, 1.0, 0.0) for t in (gx > 0, gx < 7, gy > 0, gy < 15)]
    wait_copies(copies[:1])

    def first(l, carry):
        for a, c in enumerate(coeffs_of(p[l], sw[l], sg[l])):
            coef[a, l] = c
        k = perm[0, l].astype(f32)
        n = 3 * L + l
        edge = row_lo[pl.ds(n, 1), :] * inside[0]
        before = transmit(k, jnp.concatenate([edge, k[:-1]], axis=0))
        edge = row_hi[pl.ds(n, 1), :] * inside[1]
        tx[0, l] = before
        tx[1, l] = jnp.concatenate([before[1:], transmit(k[R - 1 : R], edge)], axis=0)
        k = perm[1, l].astype(f32)
        edge = lane_of(columns, n) * inside[2]
        before = transmit(k, jnp.where(lane == 0, edge, pltpu.roll(k, 1, 1)))
        edge = lane_of(columns, 4 * L + n) * inside[3]
        ty[0, l] = before
        ty[1, l] = jnp.where(lane == C - 1, transmit(k[:, C - 1 : C], edge), pltpu.roll(before, C - 1, 1))
        k = perm[2, l].astype(f32)
        under = perm[2, jnp.maximum(l - 1, 0)].astype(f32)
        tz[l] = jnp.where(l > 0, layer_ratio, 0.0) * transmit(k, under)
        return carry

    lax.fori_loop(0, L, first, 0)
    tz[L] = jnp.zeros((R, C), f32)
    saved = start_copies(((coef, coef_h), (tx, tx_h), (ty, ty_h), (tz, tz_h)), sems_t)
    wait_copies(copies[1:])

    def outs(l):
        return (
            (weight.at[:, l], weight_h.at[:, l]),
            (res.at[:, l], res_h.at[:, l]), (diag.at[:, l], diag_h.at[:, l]),
        )

    def second(l, carry):
        rows = (row_lo[pl.ds(l, 1), :], row_hi[pl.ds(l, 1), :])
        ends = lane_of(columns, l), lane_of(columns, 4 * L + l)
        sides_of = coeff_columns(coef_col, l)
        for lo in range(0, R, BLOCK):
            at = slice(lo, lo + BLOCK)
            here = p[l, at, :]
            nexts = neighbours(p, l, lo, rows, [e[at] for e in ends])
            faces = face_terms(tx, ty, tz, l, at)
            drops = [t * (here - q) for t, q in zip(faces, nexts)]
            face_sum = sum(faces)
            drop_sum = sum(drops)
            porous = volume_scale * por[l, at, :]
            water, gas = (sw[l, at, :], sg[l, at, :])
            sats = (water, 1.0 - water - gas, gas)
            indices = index_sum[l, at, :]
            diagonals, residuals, inverses, cs = [], [], [], []
            for a in range(3):
                c = coef[a, l, at, :]
                ab = c * face_sum
                net = c * drop_sum
                for t, d, s in zip(faces, drops, coeff_neighbours(coef, coef_row, a, l, lo, sides_of)):
                    ab = ab + t * s
                    net = net + d * s
                b = 1.0 + compress[a] * here
                stored = porous * sats[a]
                diagonals.append(compress[a] * stored + ab + c * indices)
                residuals.append(b * stored - volume_scale * mass[a, l, at, :] + net + c * (indices * here))
                inverses.append(reciprocal(porous * b))
                cs.append(c)
            inverse_total = reciprocal(sum(d * v for d, v in zip(diagonals, inverses)))
            weights = [v * inverse_total for v in inverses]
            base[l, at, :] = -sum(w * r for w, r in zip(weights, residuals))
            head[l, at, :] = sum(w * c for w, c in zip(weights, cs))
            for a in range(3):
                weight[a, l, at, :] = weights[a]
                res[a, l, at, :] = residuals[a]
            diag[0, l, at, :] = diagonals[0]
            diag[1, l, at, :] = diagonals[2]
        for c in layer_copies(outs, sems_out, l):
            c.start()
        return carry

    lax.fori_loop(0, L, second, 0)
    wait_copies(saved)
    for l in range(L):
        wait_copies(layer_copies(outs, sems_out, l))


def first_kernel(
    got, info, own, perf, base, head, mine, well_residual, spread, step, pay,
):
    lane = iota((1, LANES), 1)
    sums = jnp.sum(got[...], axis=0, keepdims=True)
    total = jnp.where(lane < WELL_DEV, sums, 1.0)
    flow = rolled_row(sums, LANES - 16)
    residual = jnp.where(lane < WELL_DEV, flow - total * own[0:1] - own[1:2], 0.0)
    inverse = jnp.where(lane < WELL_DEV, 1.0 / total, 0.0)
    mine[...] = jnp.concatenate([residual, inverse, jnp.zeros((6, LANES), f32)], axis=0)
    well_residual[...] = residual[:, 0:WELL_DEV]
    cell_row = info[0:1].astype(i32)
    well_row = info[1:2].astype(i32)
    heads = gather_wells(got[...], well_row >> 4, (well_row & 15) + 32)
    spread[...] = scatter(cell_row, info[2:3] * heads).reshape(L, R, C)
    step[...] = base[...] + head[...] * spread[...]
    here = to_row(gather_cells(to_column(info[0:1]).astype(i32), (flat(step),))[0])
    parts = parts_by_offset(info[3:4].astype(i32), well_row, perf[0:1] * here)
    packed = parts[:, TAIL:]
    for n, row in enumerate((residual * inverse, residual, inverse)):
        packed = packed + rolled_row(row, 16 * (n + 1))
    tiles = [parts[:, LANES * t : LANES * (t + 1)] for t in range(5)]
    to_everyone(pay, jnp.concatenate(tiles + [packed], axis=0))


def step_faces_kernel(step, row_first, row_second, col_first, col_second):
    write_faces(step, (row_first, row_second, col_first, col_second))


def grid_kernel(
    coef_row, coef_col, head, spread, step,
    coef_h, tx_h, ty_h, tz_h, weight_h, res_h,
    ahead, end_row, end_col, residual_h, gain_h,
    coef, tx, ty, tz, weight, res, residual, gain, sems, sems_out,
):
    copies = start_copies(
        halves(((coef_h, coef, 1), (tx_h, tx, 1), (ty_h, ty, 1), (tz_h, tz, 0), (weight_h, weight, 1), (res_h, res, 1))),
        sems,
    )
    wait_copies(copies[:6])

    def outs(l):
        return (
            (residual.at[:, l], residual_h.at[:, l]), (gain.at[:, l], gain_h.at[:, l]),
        )

    def layer(l, ends):
        sides_of = coeff_columns(coef_col, l)
        for lo in range(0, R, BLOCK):
            at = slice(lo, lo + BLOCK)
            nexts = inner_neighbours(step, l, lo)
            faces = face_terms(tx, ty, tz, l, at)
            wells = spread[l, at, :]
            mixes = [head[l, at, :]] * 6
            for a in range(3):
                w = weight[a, l, at, :]
                sides = coeff_neighbours(coef, coef_row, a, l, lo, sides_of)
                mixes = [m + w * s for m, s in zip(mixes, sides)]
                residual[a, l, at, :] = res[a, l, at, :] - coef[a, l, at, :] * wells
            total = step[l, at, :]
            for j in range(6):
                g = faces[j] * mixes[j]
                gain[j, l, at, :] = g
                total = total + g * nexts[j]
            ahead[l, at, :] = total
        end_row[0, pl.ds(l, 1), :] = gain[0, l, 0:1, :]
        end_row[1, pl.ds(l, 1), :] = gain[1, l, R - 1 : R, :]
        for c in layer_copies(outs, sems_out, l):
            c.start()
        return end_columns(ends, l, gain[2, l, :, 0:LANES][:, 0:1], gain[3, l, :, C - LANES : C][:, LANES - 1 : LANES])

    ends = lax.fori_loop(0, L // 2, layer, jnp.zeros((R, LANES), f32))
    wait_copies(copies[6:])
    end_col[...] = lax.fori_loop(L // 2, L, layer, ends)
    for l in range(L):
        wait_copies(layer_copies(outs, sems_out, l))


def second_kernel(
    got, info, ahead, head, end_row, end_col, row_first, row_second, col_first, col_second,
    out_row_first, out_row_second, out_col_first, out_col_second, step,
):
    cell_row = info[0:1].astype(i32)
    well_row = info[1:2].astype(i32)
    moves = gather_wells(tile_of(got, 5), well_row >> 4, (well_row & 15) + 16)
    wells = scatter(cell_row, info[2:3] * moves).reshape(L, R, C)
    columns = end_col[...] * unpack_columns(col_first, col_second)
    low, high = from_partner("gx", row_first[...], row_second[...])
    low = end_row[0] * low
    high = end_row[1] * high
    for l in range(L):
        put_with_faces(step, l, ahead[l] + head[l] * wells[l], low[l : l + 1], high[l : l + 1], columns)
    write_faces(step, (out_row_first, out_row_second, out_col_first, out_col_second))


def wells_kernel(
    got, info, perf, step, base, head, gain_h, table, parts, near, gain, spread, sems,
):
    copies = start_copies(((gain_h, gain),), sems)
    tail = tile_of(got, 5)
    residuals = pltpu.roll(tail, LANES - 32, 1)
    inverses = pltpu.roll(tail, LANES - 48, 1)
    table[0] = residuals
    table[1] = inverses
    cell_row = info[0:1].astype(i32)
    well_row = info[1:2].astype(i32)
    valid = iota((DEVICES, LANES), 1) < WELL_DEV
    moves = jnp.where(valid, (sum_parts(got) + residuals) * inverses, 0.0)
    values = gather_wells(moves, well_row >> 4, well_row & 15)
    spread[...] = scatter(cell_row, info[2:3] * values).reshape(L, R, C)
    here = to_row(gather_cells(to_column(info[0:1]).astype(i32), (flat(step),))[0])
    flows = parts_by_offset(info[3:4].astype(i32), well_row, perf[0:1] * here)
    tiles = [flows[:, LANES * t : LANES * (t + 1)] for t in range(6)]
    parts[...] = jnp.concatenate(tiles + [jnp.zeros((2, LANES), f32)], axis=0)
    wait_copies(copies)

    def layer(l, carry):
        for lo in range(0, R, BLOCK):
            at = slice(lo, lo + BLOCK)
            total = base[l, at, :] + head[l, at, :] * spread[l, at, :]
            for j, q in enumerate(inner_neighbours(step, l, lo)):
                total = total + gain[j, l, at, :] * q
            near[l, at, :] = total
        return carry

    lax.fori_loop(0, L, layer, 0)


def third_kernel(info, perf, parts, near, end_row, end_col, row_first, row_second, col_first, col_second, step, pay):
    columns = end_col[...] * unpack_columns(col_first, col_second)
    low, high = from_partner("gx", row_first[...], row_second[...])
    low = end_row[0] * low
    high = end_row[1] * high
    for l in range(L):
        put_with_faces(step, l, near[l], low[l : l + 1], high[l : l + 1], columns)
    here = gather_cells(to_column(info[0:1]).astype(i32), (flat(step),))[0]
    well_row = info[1:2].astype(i32)
    slot_column = to_column(info[1:2]).astype(i32) & 15
    sums = to_holders(well_row >> 4, slot_column, ((1, to_column(perf[0:1]) * here),))
    to_everyone(pay, parts[0:TILES])
    pay[pl.ds(TILES - 1, DEVICES, stride=TILES), :] = sums + parts[TILES - 1 : TILES]


def last_grid_kernel(
    coef_row, coef_col, head, step, gain_row, gain_col,
    p_h, por_h, coef_h, tx_h, ty_h, tz_h, weight_h, diag_h, residual_h,
    end_row, end_col, ahead_h, slope_h,
    p, por, coef, tx, ty, tz, weight, diag, residual, ahead, slope, sems, sems_out,
):
    copies = start_copies(
        halves(
            (
                (p_h, p, 0), (por_h, por, 0), (coef_h, coef, 1), (tx_h, tx, 1), (ty_h, ty, 1), (tz_h, tz, 0),
                (weight_h, weight, 1), (diag_h, diag, 1), (residual_h, residual, 1),
            )
        ),
        sems,
    )
    wait_copies(copies[:9])

    def outs(l):
        return ((ahead.at[:, l], ahead_h.at[:, l]), (slope.at[:, l], slope_h.at[:, l]))

    def layer(l, ends):
        sides_of = coeff_columns(coef_col, l)
        gains = lane_of(gain_col[...], l), lane_of(gain_col[...], L + l)
        pairs = [([], []), ([], [])]
        for lo in range(0, R, BLOCK):
            at = slice(lo, lo + BLOCK)
            nexts = inner_neighbours(step, l, lo)
            faces = face_terms(tx, ty, tz, l, at)
            flows = [t * q for t, q in zip(faces, nexts)]
            flow_sum = sum(flows)
            rights, cs, sides = [], [], []
            for a in range(3):
                c = coef[a, l, at, :]
                total = c * flow_sum - residual[a, l, at, :]
                sides.append(coeff_neighbours(coef, coef_row, a, l, lo, sides_of))
                for v, s in zip(flows, sides[a]):
                    total = total + v * s
                rights.append(total)
                cs.append(c)
            z = sum(weight[a, l, at, :] * rights[a] for a in range(3))
            h = head[l, at, :]
            porous = volume_scale * por[l, at, :]
            inverses = [reciprocal(porous * (1.0 + compress[a] * p[l, at, :])) for a in (0, 2)]
            ahead[0, l, at, :] = z
            for n, a in enumerate((0, 2)):
                d = diag[n, l, at, :]
                inverse = inverses[n]
                ahead[1 + n, l, at, :] = (rights[a] - d * z) * inverse
                slope[n, l, at, :] = (cs[a] - d * h) * inverse
                for side in range(2):
                    if lo == (0, R - BLOCK)[side]:
                        row = slice(0, 1) if side == 0 else slice(BLOCK - 1, BLOCK)
                        face = faces[side][row] * (cs[a][row] + sides[a][side][row])
                        end_row[side, n, pl.ds(l, 1), :] = (
                            face - d[row] * gain_row[side, pl.ds(l, 1), :]
                        ) * inverse[row]
                    col = slice(0, 1) if side == 0 else slice(C - 1, C)
                    face = faces[2 + side][:, col] * (cs[a][:, col] + sides_of[a][side][at])
                    pairs[n][side].append((face - d[:, col] * gains[side][at]) * inverse[:, col])
        for c in layer_copies(outs, sems_out, l):
            c.start()
        return tuple(
            end_columns(ends[n], l, *(jnp.concatenate(part, axis=0) for part in pairs[n])) for n in range(2)
        )

    blank = jnp.zeros((R, LANES), f32)
    ends = lax.fori_loop(0, L // 2, layer, (blank, blank))
    wait_copies(copies[9:])
    end_col[0], end_col[1] = lax.fori_loop(L // 2, L, layer, ends)
    for l in range(L):
        wait_copies(layer_copies(outs, sems_out, l))


def final_kernel(
    got, info, table, mine, head, gain_row, gain_col, end_row, end_col, row_first, row_second, col_first, col_second,
    ahead_h, slope_h, update_h, moved, ahead, slope, update, sems, sems_out,
):
    copies = start_copies(((ahead_h, ahead), (slope_h, slope)), sems)
    flow = rolled_row(jnp.sum(tile_of(got, TILES - 1), axis=0, keepdims=True), LANES - 16)
    moved[...] = ((flow + mine[0:1]) * mine[1:2])[:, 0:WELL_DEV]
    cell_row = info[0:1].astype(i32)
    well_row = info[1:2].astype(i32)
    valid = iota((DEVICES, LANES), 1) < WELL_DEV
    moves = jnp.where(valid, (sum_parts(got) + table[0]) * table[1], 0.0)
    values = gather_wells(moves, well_row >> 4, well_row & 15)
    wells = scatter(cell_row, info[2:3] * values).reshape(L, R, C)
    halo = unpack_columns(col_first, col_second)
    lows, highs = from_partner("gx", row_first[...], row_second[...])
    columns = (gain_col[...] * halo, end_col[0] * halo, end_col[1] * halo)
    wait_copies(copies)

    def outs(l):
        return ((update.at[:, l], update_h.at[:, l]),)

    for l in range(L):
        low = lows[l : l + 1]
        high = highs[l : l + 1]
        for n in range(3):
            rows = [gain_row[side, l : l + 1, :] if n == 0 else end_row[side, n - 1, l : l + 1, :] for side in range(2)]
            x = ahead[n, l] + (head[l] if n == 0 else slope[n - 1, l]) * wells[l]
            put_with_faces(update.at[n], l, x, rows[0] * low, rows[1] * high, columns[n])
        layer_copies(outs, sems_out, l)[0].start()
    for l in range(L):
        wait_copies(layer_copies(outs, sems_out, l))


def call(kernel, outs, ins, operands, scratch=(), flops=0):
    shapes = tuple(
        pltpu.VMEM(s, f32) if w is VM else pltpu.HBM(s, f32) if w is HB else jax.ShapeDtypeStruct(s, f32)
        for s, w in outs
    )
    moved = 4 * sum(int(x.size) for x in operands)
    operands = [
        pltpu.with_memory_space_constraint(x, pltpu.HBM) if w is HB else x for x, w in zip(operands, ins)
    ]
    return pl.pallas_call(
        kernel,
        out_shape=shapes,
        in_specs=ins,
        out_specs=tuple(w or VM for _, w in outs),
        scratch_shapes=[pltpu.VMEM(x, f32) if type(x) is tuple else x for x in scratch],
        compiler_params=pltpu.CompilerParams(vmem_limit_bytes=40 * 1024 * 1024),
        cost_estimate=pl.CostEstimate(flops=flops, bytes_accessed=moved, transcendentals=0),
    )(*operands)


FIELD = (L, R, C)
TWO, THREE, SIX, FACED = ((2,) + FIELD, (3,) + FIELD, (6,) + FIELD, (L + 1, R, C))
FACES = (((L, C), VM), ((L, C), VM), ((L, LANES), VM), ((L, LANES), VM))
WIDE_FACES = (((4 * L, C), VM), ((4 * L, C), VM), ((4 * L, LANES), VM), ((4 * L, LANES), VM))
SMALL = (8, LANES)
PAY = ((TILES * DEVICES, LANES), None)
sem = pltpu.SemaphoreType.DMA


def exchange(array):
    return lax.all_to_all(array, AXES, split_axis=0, concat_axis=0, tiled=True)


def exchange_tiles(array):
    return exchange(array.reshape(DEVICES, WIDTH)).reshape(TILES * DEVICES, LANES)


def partners():
    rows, columns = (lax.axis_size(axis) for axis in AXES)
    swaps = [[], [], [], []]
    for x in range(rows):
        for y in range(columns):
            here = x * columns + y
            x_next = x - 1 + 2 * (x % 2)
            y_next = y - 1 + 2 * (y % 2)
            swaps[0].append((here, (x ^ 1) * columns + y))
            swaps[1].append((here, x_next * columns + y if 0 <= x_next < rows else x * columns + (y ^ 1)))
            swaps[2].append((here, x * columns + (y ^ 1)))
            swaps[3].append((here, x * columns + y_next if 0 <= y_next < columns else (x ^ 1) * columns + y))
    return swaps


def halo_of(faces):
    swaps = partners()
    got = {n: lax.ppermute(faces[n], AXES, swaps[n]) for n in (3, 1, 2, 0)}
    return [got[n] for n in range(4)]


def local(
    pressure, sat_water, sat_gas, old_mass, perm, porosity,
    perf_well, perf_cell, perf_index, well_pressure, well_rate,
):
    *faces, p, sw, sg, info, own = call(
        faces_kernel,
        WIDE_FACES + ((FIELD, VM), (FIELD, VM), (FIELD, VM), ((8, PERFS), VM), (SMALL, VM)),
        [HB] * 9,
        (
            perf_cell.reshape(1, PERFS), perf_well.reshape(1, PERFS), perf_index.reshape(1, PERFS),
            well_pressure.reshape(1, WELL_DEV), well_rate.reshape(1, WELL_DEV), pressure, sat_water, sat_gas, perm,
        ),
        [
            pltpu.VMEM((1, PERFS), i32), pltpu.VMEM((1, PERFS), i32), (1, PERFS),
            (1, WELL_DEV), (1, WELL_DEV), pltpu.VMEM(TWO, bf16), sem((4,)), sem((5,)),
        ],
    )
    halo = halo_of(faces)
    pay, perf = call(
        start_kernel, (((DEVICES, LANES), VM), ((8, PERFS), VM)), [VM] * 5, (info, own, p, sw, sg)
    )
    pay, *halo = pl.pallas_call(
        after_kernel,
        out_shape=tuple(pltpu.VMEM(x.shape, f32) for x in (pay, *halo)),
        in_specs=[pl.BlockSpec(memory_space=pl.ANY)] * 5,
        out_specs=(pl.BlockSpec(memory_space=pl.ANY),) * 5,
        input_output_aliases={n: n for n in range(5)},
    )(pay, *halo)
    got = exchange(pay)
    coef_row, coef_col, base, head, coef, tx, ty, tz, weight, res, diag = call(
        setup_kernel,
        (
            ((2, 3, L, C), VM), ((3, R, LANES), VM), (FIELD, VM), (FIELD, VM), (THREE, HB), (TWO, HB), (TWO, HB),
            (FACED, HB), (THREE, HB), (THREE, HB), (TWO, HB),
        ),
        [VM] * 8 + [HB] * 3,
        (info, *halo, p, sw, sg, porosity, old_mass, perm),
        [
            FIELD, THREE, pltpu.VMEM(THREE, bf16), THREE, TWO, TWO, FACED,
            THREE, THREE, TWO, FIELD, (4 * L, C), (4 * L, C), sem((3,)), sem((4,)), sem((3, L)),
        ],
        flops=400 * L * R * C,
    )
    mine, well_residual, spread, start, pay = call(
        first_kernel,
        ((SMALL, VM), ((1, WELL_DEV), None), (FIELD, VM), (FIELD, VM), PAY),
        [VM] * 6,
        (got, info, own, perf, base, head),
    )
    got = exchange_tiles(pay)
    halo = halo_of(call(step_faces_kernel, FACES, [VM], (start,)))
    fields = (coef, tx, ty, tz, weight)
    ahead, gain_row, gain_col, residual, gain = call(
        grid_kernel,
        ((FIELD, VM), ((2, L, C), VM), ((R, LANES), VM), (THREE, HB), (SIX, HB)),
        [VM] * 5 + [HB] * 6,
        (coef_row, coef_col, head, spread, start, *fields, res),
        [THREE, TWO, TWO, FACED, THREE, THREE, THREE, SIX, sem((12,)), sem((2, L))],
        flops=100 * L * R * C,
    )
    *faces, step = call(
        second_kernel,
        FACES + ((FIELD, VM),),
        [VM] * 10,
        (got, info, ahead, head, gain_row, gain_col, *halo),
    )
    halo = halo_of(faces)
    table, parts, near = call(
        wells_kernel,
        (((2, DEVICES, LANES), VM), (SMALL, VM), (FIELD, VM)),
        [VM] * 6 + [HB],
        (got, info, perf, step, start, head, gain),
        [SIX, FIELD, sem((1,))],
    )
    step, pay = call(
        third_kernel,
        ((FIELD, VM), PAY),
        [VM] * 10,
        (info, perf, parts, near, gain_row, gain_col, *halo),
    )
    got = exchange_tiles(pay)
    halo = halo_of(call(step_faces_kernel, FACES, [VM], (step,)))
    end_row, end_col, ahead, slope = call(
        last_grid_kernel,
        (((2, 2, L, C), VM), ((2, R, LANES), VM), (THREE, HB), (TWO, HB)),
        [VM] * 6 + [HB] * 9,
        (coef_row, coef_col, head, step, gain_row, gain_col, pressure, porosity, *fields, diag, residual),
        [FIELD, FIELD, THREE, TWO, TWO, FACED, THREE, TWO, THREE, THREE, TWO, sem((18,)), sem((2, L))],
        flops=150 * L * R * C,
    )
    update, moved = call(
        final_kernel,
        ((THREE, HB), ((1, WELL_DEV), None)),
        [VM] * 13 + [HB] * 2,
        (got, info, table, mine, head, gain_row, gain_col, end_row, end_col, *halo, ahead, slope),
        [THREE, TWO, THREE, sem((2,)), sem((1, L))],
    )
    return residual, well_residual.reshape(WELL_DEV), update, moved.reshape(WELL_DEV)


def solution(mesh):
    return jax.shard_map(
        local,
        mesh=mesh,
        in_specs=(
            P(None, "gx", "gy"),
            P(None, "gx", "gy"),
            P(None, "gx", "gy"),
            P(None, None, "gx", "gy"),
            P(None, None, "gx", "gy"),
            P(None, "gx", "gy"),
            P(("gx", "gy")),
            P(("gx", "gy")),
            P(("gx", "gy")),
            P(("gx", "gy")),
            P(("gx", "gy")),
        ),
        out_specs=(
            P(None, None, "gx", "gy"),
            P(("gx", "gy")),
            P(None, None, "gx", "gy"),
            P(("gx", "gy")),
        ),
        check_vma=False,
    )
```
